256 devices in a mesh: space: 64 (over y, z, core), rep: 4 (over x).
Axes of the slice: x: 4, y: 4, z: 8, core: 2. Of those that a mesh axis runs over, the one named last changes fastest.
Arguments:
- features: bfloat16 [512, 96, 512], P(('rep', 'space')), parts along dimension 0, may hold values from -6 to 6
- occupancy: int32 [512, 16], P(('rep', 'space')), parts along dimension 0, may hold values from -2147483647 to 2147483646, as said below
- neighbours: int32 [512, 27], P(('rep', 'space')), parts along dimension 0, may hold values from 0 to 6, as said below
- live_count: int32 [256], P(('rep', 'space')), parts along dimension 0, may hold values from 1 to 2, as said below
- w_subm: bfloat16 [27, 96, 96], replicated, may hold values from -0.15625 to 0.15625
- w_down: bfloat16 [8, 96, 96], replicated, may hold values from -0.3125 to 0.3125
- grad_coarse: bfloat16 [16384, 768], P(('rep', 'space')), parts along dimension 0, may hold values from -6 to 6
Outputs:
- coarse_out: bfloat16 [16384, 768], P(('rep', 'space')), parts along dimension 0
- grad_features: bfloat16 [512, 96, 512], P(('rep', 'space')), parts along dimension 0
- grad_subm: float32 [108, 96, 96], P('rep'), parts along dimension 0
- grad_down: float32 [32, 96, 96], P('rep'), parts along dimension 0
The draws below stay inside these ranges and needn't reach their ends.
There are 4 independent parts, one for each index of `rep`. The reference program is written for one: setup_inputs(seed, part) draws one part's arguments, and reference() takes and returns one part's arrays. A program takes and returns all parts, laid end to end along the dimension named above; an argument that names none is the same for every part. Nothing has to cross between parts.
Inputs may be any that keep to these rules, and one draw needn't show every extreme that they name: `neighbours`: entry 13 of each block's row is 2 plus its own slot; 6 means empty. `live_count`: some device has all 2 slots live; live slots are the lowest ones. `occupancy`: any 32-bit pattern.
All inputs are finite; a program needn't handle non-finite values.
Results may differ from the reference program's by a relative error of at most 0.0054.
Values may be sent and summed in bfloat16 or wider, within the bound.
A program may use at most 128 MiB of HBM per device.

```python
import jax
import jax.numpy as jnp
from jax import lax

C = 96
B_DEV = 2
BLOCKS = 128
CAP = 1
N_SPACE = 64


def draw_occupancy(key, part):
    key = jax.random.fold_in(key, 11)
    return jax.random.randint(key, (BLOCKS, 16), -2147483647, 2147483647, dtype=jnp.int32)


def draw_neighbours(key, part):
    key = jax.random.fold_in(key, 12)
    table = jax.random.randint(key, (BLOCKS, 27), 0, 3 * B_DEV + 1, dtype=jnp.int32)
    center = B_DEV + jnp.arange(BLOCKS, dtype=jnp.int32) % B_DEV
    table = table.at[:, 13].set(center)
    table = table.at[0, 0].set(3 * B_DEV)
    return table.at[1, 0].set(0)


def draw_live_count(key, part):
    key = jax.random.fold_in(key, 13)
    first_key, third_key = jax.random.split(key, 2)
    spread = max(B_DEV // 4, 1)
    counts = B_DEV - jax.random.randint(first_key, (N_SPACE,), 0, spread + 1, dtype=jnp.int32)
    where_full = jax.random.randint(third_key, (), 0, N_SPACE, dtype=jnp.int32)
    return counts.at[where_full].set(B_DEV)


def block_scale(rng, dims, cuts, smallest, largest):
    loudness, own = 1.0, jax.random.fold_in(rng, 6)
    for dim, shards_of in cuts:
        heights = jnp.exp(jax.random.uniform(jax.random.fold_in(own, dim), (shards_of,), jnp.float32, smallest / len(cuts), largest / len(cuts)))
        loudness = loudness * jnp.repeat(heights, dims[dim] // shards_of).reshape([-1 if axis == dim else 1 for axis in range(len(dims))])
    return loudness


def centred(stream_key, dims, deviation, limit, cuts=(), kind=jnp.bfloat16):
    level = block_scale(stream_key, dims, cuts, -0.22, 0.18) if cuts else 1.0
    drawn = jax.random.normal(stream_key, dims, jnp.float32) * deviation * level
    return jnp.minimum(jnp.maximum(drawn, -limit), limit).astype(kind)


def setup_inputs(seed: int = 0, part: int = 0) -> dict:
    arg_keys = jax.random.split(jax.random.key(seed), 8)
    part_keys = jax.random.split(jax.random.fold_in(arg_keys[7], part), 8)
    return {
        "features": centred(part_keys[0], (BLOCKS, C, 512), 1.0, 6.0, ((0, 64),)),
        "occupancy": draw_occupancy(jax.random.fold_in(jax.random.fold_in(arg_keys[7], part), 71), part),
        "neighbours": draw_neighbours(jax.random.fold_in(jax.random.fold_in(arg_keys[7], part), 71), part),
        "live_count": draw_live_count(jax.random.fold_in(jax.random.fold_in(arg_keys[7], part), 71), part),
        "w_subm": centred(arg_keys[4], (27, C, C), (14 * C) ** -0.5, 0.15625),
        "w_down": centred(arg_keys[5], (8, C, C), (4 * C) ** -0.5, 0.3125),
        "grad_coarse": centred(part_keys[6], (N_SPACE * N_SPACE * CAP, C * 8), 1.0, 6.0, ((0, 64),)),
    }


stencil_offsets = [(first, second, third) for first in (-1, 0, 1) for second in (-1, 0, 1) for third in (-1, 0, 1)]
slab_spans = {-1: (7, 8, 0, 1), 0: (0, 8, 1, 9), 1: (0, 1, 9, 10)}

def source_slices(first, second, third):
    return tuple((slice(slab_spans[offset][0], slab_spans[offset][1]) for offset in (first, second, third)))

def target_slices(first, second, third):
    return tuple((slice(slab_spans[offset][2], slab_spans[offset][3]) for offset in (first, second, third)))

def unpack_bits(words):
    position = jnp.arange(512, dtype=jnp.int32)
    chosen = words[:, position // 32]
    return jnp.bitwise_and(jnp.right_shift(chosen, position % 32), 1)

def build_pad(source, table):
    count = table.shape[0]
    chans = source.shape[1]
    padded = jnp.zeros((count, chans, 10, 10, 10), source.dtype)
    for index, (first, second, third) in enumerate(stencil_offsets):
        piece = source[(slice(None), slice(None)) + source_slices(first, second, third)]
        piece = jnp.take(piece, table[:, index], axis=0)
        padded = padded.at[(slice(None), slice(None)) + target_slices(first, second, third)].set(piece)
    return padded

def window(padded, first, second, third):
    count, chans = (padded.shape[0], padded.shape[1])
    return padded[:, :, 1 + first:9 + first, 1 + second:9 + second, 1 + third:9 + third].reshape(count, chans, 512)

def child(hidden, index):
    count, chans = (hidden.shape[0], hidden.shape[1])
    return hidden.reshape(count, chans, 4, 2, 4, 2, 4, 2)[:, :, :, index // 4, :, index // 2 % 2, :, index % 2].reshape(count, chans, 64)

def place_children(pieces):
    count, chans = (pieces[0].shape[0], pieces[0].shape[1])
    stacked = jnp.stack(pieces, axis=-1).reshape(count, chans, 4, 4, 4, 2, 2, 2)
    return jnp.transpose(stacked, (0, 1, 2, 5, 3, 6, 4, 7)).reshape(count, chans, 512)

def gelu_tanh(values):
    return jax.nn.gelu(values, approximate=True)

def reference(features, occupancy, neighbours, live_count, w_subm, w_down, grad_coarse):
    peers = N_SPACE
    per_dev = B_DEV
    total = BLOCKS
    chans = C
    capacity = CAP
    blockid = jnp.arange(total, dtype=jnp.int32)
    owner = blockid // per_dev
    slot = blockid % per_dev
    alive = (slot < live_count[owner]).astype(jnp.int32)
    mask = unpack_bits(occupancy) * alive[:, None]
    mask_f = mask.astype(jnp.float32)
    masked = jnp.where(mask[:, None, :] > 0, features, jnp.zeros_like(features))
    device = owner[:, None] + neighbours // per_dev - 1
    valid_nb = (neighbours < 3 * per_dev) & (device >= 0) & (device < peers)
    global_table = jnp.where(valid_nb, device * per_dev + neighbours % per_dev, total).astype(jnp.int32)
    source = jnp.concatenate([masked.reshape(total, chans, 8, 8, 8), jnp.zeros((1, chans, 8, 8, 8), masked.dtype)], axis=0)
    padded = build_pad(source, global_table)
    pre = jnp.zeros((total, chans, 512), jnp.float32)
    for index, (first, second, third) in enumerate(stencil_offsets):
        pre = pre + jnp.einsum('bcv,cd->bdv', window(padded, first, second, third).astype(jnp.float32), w_subm[index].astype(jnp.float32))
    hidden = (gelu_tanh(pre) * mask_f[:, None, :]).astype(jnp.bfloat16)
    cmask = lax.optimization_barrier(jnp.max(mask_f.reshape(total, 4, 2, 4, 2, 4, 2), axis=(2, 4, 6))).reshape(total, 64)
    coarse = jnp.zeros((total, chans, 64), jnp.float32)
    for index in range(8):
        coarse = coarse + jnp.einsum('bcu,cd->bdu', child(hidden, index).astype(jnp.float32), w_down[index].astype(jnp.float32))
    coarse = (coarse * cmask[:, None, :]).astype(jnp.bfloat16)
    pieces = jnp.transpose(coarse.reshape(total, chans, 8, 8), (0, 2, 1, 3)).reshape(total, 8, chans * 8)
    start = (jnp.cumsum(live_count) - live_count).astype(jnp.int32)
    dest = jnp.arange(peers, dtype=jnp.int32)[:, None, None]
    srcdev = jnp.arange(peers, dtype=jnp.int32)[None, :, None]
    place = jnp.arange(capacity, dtype=jnp.int32)[None, None, :]
    which = place * peers + jnp.mod(dest - 8 * start[srcdev], peers)
    usable = which < 8 * live_count[srcdev]
    rows = srcdev * per_dev + jnp.clip(which // 8, 0, per_dev - 1)
    chosen = pieces[rows, which % 8]
    coarse_out = jnp.where(usable[..., None], chosen, jnp.zeros((), chosen.dtype)).reshape(peers * peers * capacity, chans * 8)
    back = grad_coarse.reshape(peers, peers, capacity, chans * 8)
    stream = 8 * slot[:, None] + jnp.arange(8, dtype=jnp.int32)[None, :]
    target = jnp.mod(8 * start[owner][:, None] + stream, peers)
    taken = back[target, owner[:, None], stream // peers]
    taken = jnp.where(alive[:, None, None] > 0, taken, jnp.zeros((), taken.dtype))
    dz = jnp.transpose(taken.reshape(total, 8, chans, 8), (0, 2, 1, 3)).reshape(total, chans, 64)
    dz = jnp.where(cmask[:, None, :] > 0, dz, jnp.zeros((), dz.dtype))
    grad_down = jnp.stack([jnp.einsum('bcu,bdu->cd', child(hidden, index).astype(jnp.float32), dz.astype(jnp.float32)) for index in range(8)])
    dh = place_children([jnp.einsum('bdu,cd->bcu', dz.astype(jnp.float32), w_down[index].astype(jnp.float32)) for index in range(8)])
    _, pull = jax.vjp(gelu_tanh, pre)
    dpre = pull(dh * mask_f[:, None, :])[0].astype(jnp.bfloat16)
    grad_subm = jnp.stack([jnp.einsum('bcv,bdv->cd', window(padded, first, second, third).astype(jnp.float32), dpre.astype(jnp.float32)) for first, second, third in stencil_offsets])
    gpad = jnp.zeros((total, chans, 10, 10, 10), jnp.float32)
    for index, (first, second, third) in enumerate(stencil_offsets):
        term = jnp.einsum('cd,bdv->bcv', w_subm[index].astype(jnp.float32), dpre.astype(jnp.float32)).reshape(total, chans, 8, 8, 8)
        gpad = gpad.at[:, :, 1 + first:9 + first, 1 + second:9 + second, 1 + third:9 + third].add(term)
    gsource = jnp.zeros((total + 1, chans, 8, 8, 8), jnp.float32)
    for index, (first, second, third) in enumerate(stencil_offsets):
        gsource = gsource.at[(global_table[:, index], slice(None)) + source_slices(first, second, third)].add(gpad[(slice(None), slice(None)) + target_slices(first, second, third)])
    grad_features = (gsource[:total].reshape(total, chans, 512) * mask_f[:, None, :]).astype(jnp.bfloat16)
    return (coarse_out, grad_features, grad_subm, grad_down)
```

```python
import functools

import jax
import jax.numpy as jnp
from jax import lax
from jax.experimental import pallas as pl
from jax.experimental.pallas import tpu as pltpu
from jax.sharding import PartitionSpec as P

C, L, V = 96, 128, 512
OFFSETS = [(a, b, c) for a in (-1, 0, 1) for b in (-1, 0, 1) for c in (-1, 0, 1)]
VMEM_LIMIT = 50 * 2**20
F32, BF16 = jnp.float32, jnp.bfloat16
NT = (((1,), (1,)), ((), ()))


def segments(a, b, c):
    span = {-1: [(7, 0)], 0: [(i, i + 1) for i in range(8)], 1: [(0, 9)]}
    xs, ys, zs = span[a], span[b], span[c]
    if c == 0:
        return [(x * 64 + y * 8, 1, tx * 100 + ty * 10 + 1, 1, 8) for x, tx in xs for y, ty in ys]
    z, tz = zs[0]
    if b == 0:
        return [(x * 64 + z, 8, tx * 100 + 10 + tz, 10, 8) for x, tx in xs]
    y, ty = ys[0]
    if a == 0:
        return [(y * 8 + z, 64, 100 + ty * 10 + tz, 100, 8)]
    x, tx = xs[0]
    return [(x * 64 + y * 8 + z, 1, tx * 100 + ty * 10 + tz, 1, 1)]


def rows(start, count, stride):
    return pl.ds(start, count) if stride == 1 else pl.ds(start, count, stride=stride)


def mask_row(words, live, g):
    lane = lax.broadcasted_iota(jnp.int32, (1, V), 1)
    word = jnp.zeros((1, V), jnp.int32)
    for w in range(16):
        word = jnp.where(lane // 32 == w, words[g, w], word)
    bit = jnp.bitwise_and(jnp.right_shift(word, jnp.bitwise_and(lane, 31)), 1)
    return jnp.where(g < live, bit, 0)


def masked_rows(features, words, live, g):
    bit = mask_row(words, live, g)
    values = jnp.where(bit > 0, features[g].astype(F32), 0.0)
    marks = jnp.broadcast_to(bit.astype(F32), (L - C, V))
    return jnp.transpose(jnp.concatenate([values, marks], axis=0)).astype(BF16)


def mask_kernel(live_ref, occupancy_ref, features_ref, out_ref):
    for g in range(2):
        out_ref[g] = masked_rows(features_ref, occupancy_ref, live_ref[0], g)


def block_kernel(
    table, live_ref, lower, own, upper, inbox, w_subm, w_down,
    outbox, part_own, part_lower, part_upper, sums,
    source, pad, cols, wf, wb, wd, perm, spread, pre, hid, dpre3, u, gpad, gsource,
):
    me = lax.axis_index("space")
    wf[...] = jnp.zeros_like(wf)
    wb[...] = jnp.zeros_like(wb)
    wd[...] = jnp.zeros_like(wd)
    for k in range(27):
        a, bc = divmod(k, 9)
        w = w_subm[k]
        wf[k * L : k * L + C, :C] = w
        wb[bc * L : bc * L + C, a * L : a * L + C] = w
    for j in range(8):
        wd[j * L : j * L + C, :C] = w_down[j]
    i = lax.broadcasted_iota(jnp.int32, (V, V), 0)
    v = lax.broadcasted_iota(jnp.int32, (V, V), 1)
    j, t = i // 64, i % 64
    x, y, z = 2 * (t // 16) + j // 4, 2 * (t // 4 % 4) + j // 2 % 2, 2 * (t % 4) + j % 2
    perm[...] = jnp.where(x * 64 + y * 8 + z == v, 1.0, 0.0).astype(BF16)
    spread[...] = jnp.where(
        lax.broadcasted_iota(jnp.int32, (L, 6 * L), 1) // 8
        == lax.broadcasted_iota(jnp.int32, (L, 6 * L), 0),
        1.0, 0.0,
    ).astype(BF16)
    pick = (
        lax.broadcasted_iota(jnp.int32, (8, L), 1) % 8 == lax.broadcasted_iota(jnp.int32, (8, L), 0)
    )

    for n, ref in enumerate((lower, own, upper)):
        for g in range(2):
            source[(2 * n + g) * V : (2 * n + g + 1) * V, :] = ref[g].astype(F32)
    source[6 * V :, :] = jnp.zeros((V, L), F32)

    for g in range(2):
        for k, offset in enumerate(OFFSETS):
            base = table[g, k] * V
            for s0, ss, p0, ps, count in segments(*offset):
                pad[rows(g * 1000 + p0, count, ps), :] = source[rows(base + s0, count, ss), :]

    def columns(gx, carry):
        for b in range(3):
            for c in range(3):
                piece = jnp.concatenate(
                    [pad[pl.ds(gx * 100 + (yy + b) * 10 + c, 8), :] for yy in range(8)], axis=0
                )
                bc = 3 * b + c
                cols[pl.ds(gx * 64, 64), bc * L : (bc + 1) * L] = piece.astype(BF16)
        return carry

    lax.fori_loop(0, 20, columns, 0)

    for g in range(2):
        acc = jnp.zeros((V, L), F32)
        for a in range(3):
            acc += jnp.dot(
                cols[g * 640 + a * 64 : g * 640 + a * 64 + V, :],
                wf[a * 9 * L : (a + 1) * 9 * L, :],
                preferred_element_type=F32,
            )
        pre[g * V : (g + 1) * V, :] = acc

    counts = inbox[:, 6, :]
    place = lax.broadcasted_iota(jnp.int32, (64, L), 0)
    start = jnp.sum(jnp.where(place < me, counts, 0.0), axis=0, keepdims=True)[0, 0].astype(jnp.int32)
    live = live_ref[0]
    outbox[...] = jnp.zeros_like(outbox)
    s, q = 0.7978845608028654, 0.044715
    dpre3[...] = jnp.zeros_like(dpre3)
    down = jnp.zeros((L, 8 * L), F32)
    for g in range(2):
        mask = jnp.broadcast_to(own[g, :, C : C + 1].astype(F32), (V, L))
        tt = pre[g * V : (g + 1) * V, :]
        th = jnp.tanh(s * (tt + q * tt * tt * tt))
        hidden = (0.5 * tt * (1.0 + th) * mask).astype(BF16)
        slope = (0.5 * (1.0 + th) + 0.5 * tt * (1.0 - th * th) * (s * (1.0 + 3.0 * q * tt * tt))) * mask
        both = jnp.dot(
            perm[...], jnp.concatenate([hidden, mask.astype(BF16)], axis=1),
            preferred_element_type=F32,
        )
        kids = both[:, :L].astype(BF16)
        hid[...] = kids
        cmask = both[:64, L:]
        coarse = jnp.dot(kids[:64], wd[:L, :], preferred_element_type=F32)
        for j in range(1, 8):
            cmask = jnp.maximum(cmask, both[j * 64 : (j + 1) * 64, L:])
            coarse += jnp.dot(
                kids[j * 64 : (j + 1) * 64], wd[j * L : (j + 1) * L, :], preferred_element_type=F32
            )
        coarse = (coarse * cmask).astype(BF16)
        group = jnp.bitwise_and(start + g, 7)
        alive = g < live
        flat = jnp.dot(coarse, spread[...], preferred_element_type=F32)
        for t in range(8):
            for n in range(6):
                tile = jnp.where(pick, flat[t * 8 : t * 8 + 8, n * L : (n + 1) * L], 0.0)
                line = jnp.where(alive, jnp.sum(tile, axis=0, keepdims=True), 0.0)

                @pl.when(alive)
                def _():
                    outbox[group * 8 + t, n : n + 1, :] = line

        dz = []
        for t in range(8):
            dz.append(
                jnp.concatenate(
                    [
                        jnp.where(pick, jnp.broadcast_to(inbox[group * 8 + t, n : n + 1, :], (8, L)), 0.0)
                        for n in range(6)
                    ],
                    axis=1,
                )
            )
        dz = jnp.concatenate(dz, axis=0).astype(BF16)
        dz = lax.dot_general(dz, spread[...], NT, preferred_element_type=F32)
        dz = jnp.where(alive & (cmask > 0), dz, 0.0).astype(BF16)
        dzt = jnp.transpose(dz.astype(F32)).astype(BF16)
        down += jnp.dot(
            dzt, jnp.concatenate([kids[j * 64 : (j + 1) * 64] for j in range(8)], axis=1),
            preferred_element_type=F32,
        )
        dh = jnp.concatenate(
            [
                lax.dot_general(dz, wd[j * L : (j + 1) * L, :], NT, preferred_element_type=F32)
                for j in range(8)
            ],
            axis=0,
        )
        high = dh.astype(BF16)
        low = (dh - high.astype(F32)).astype(BF16)
        dh = lax.dot_general(
            perm[...], jnp.concatenate([high, low], axis=1), (((0,), (0,)), ((), ())),
            preferred_element_type=F32,
        )
        dh = dh[:, :L] + dh[:, L:]
        dpre = slope * dh
        dpre16 = dpre.astype(BF16)
        for a in range(3):
            dpre3[g * 640 + a * 64 : g * 640 + a * 64 + V, a * L : (a + 1) * L] = dpre16
        hid[...] = dpre16
        pre[g * V : (g + 1) * V, :] = dpre
    for j in range(8):
        sums[27 + j] = down[:C, j * L : (j + 1) * L].astype(sums.dtype)

    dt = jnp.transpose(pre[...]).astype(BF16)
    for a in range(3):
        for bc in range(0, 9, 2):
            lanes = slice(bc * L, min(bc + 2, 9) * L)
            total = jnp.dot(
                dt[:, :V], cols[a * 64 : a * 64 + V, lanes], preferred_element_type=F32
            ) + jnp.dot(
                dt[:, V:], cols[640 + a * 64 : 640 + a * 64 + V, lanes], preferred_element_type=F32
            )
            for n in range(min(2, 9 - bc)):
                sums[a * 9 + bc + n] = total[:C, n * L : (n + 1) * L].astype(sums.dtype)

    gpad[...] = jnp.zeros_like(gpad)
    for bc in range(0, 9, 2):
        width = min(2, 9 - bc)
        u[:, : width * L] = lax.dot_general(
            dpre3[...], wb[bc * L : (bc + width) * L, :], NT, preferred_element_type=F32
        )

        def add(gx, carry):
            for n in range(width):
                b, c = divmod(bc + n, 3)
                for yy in range(8):
                    at = pl.ds(gx * 100 + (yy + b) * 10 + c, 8)
                    gpad[at, :] += u[pl.ds(gx * 64 + yy * 8, 8), n * L : (n + 1) * L]
            return carry

        lax.fori_loop(0, 20, add, 0)

    gsource[...] = jnp.zeros_like(gsource)
    for g in range(2):
        for k, offset in enumerate(OFFSETS):
            base = table[g, k] * V
            for s0, ss, p0, ps, count in segments(*offset):
                gsource[rows(base + s0, count, ss), :] += gpad[rows(g * 1000 + p0, count, ps), :]
    for g in range(2):
        part_lower[g] = gsource[g * V : (g + 1) * V, :].astype(BF16)
        part_own[g] = gsource[(2 + g) * V : (3 + g) * V, :]
        part_upper[g] = gsource[(4 + g) * V : (5 + g) * V, :].astype(BF16)


def smem():
    return pl.BlockSpec(memory_space=pltpu.SMEM)


def vmem(n):
    return [pl.BlockSpec(memory_space=pltpu.VMEM)] * n


def run_blocks(neighbours, live_count, lower, own, upper, inbox, w_subm, w_down, kind=F32):
    return pl.pallas_call(
        block_kernel,
        out_shape=(
            jax.ShapeDtypeStruct((64, 8, L), F32),
            jax.ShapeDtypeStruct((2, V, L), F32),
            jax.ShapeDtypeStruct((2, V, L), BF16),
            jax.ShapeDtypeStruct((2, V, L), BF16),
            jax.ShapeDtypeStruct((35, C, L), kind),
        ),
        in_specs=[smem(), smem()] + vmem(6),
        out_specs=tuple(vmem(5)),
        scratch_shapes=[
            pltpu.VMEM((7 * V, L), F32),
            pltpu.VMEM((2000, L), F32),
            pltpu.VMEM((1280, 9 * L), BF16),
            pltpu.VMEM((27 * L, L), BF16),
            pltpu.VMEM((9 * L, 3 * L), BF16),
            pltpu.VMEM((8 * L, L), BF16),
            pltpu.VMEM((V, V), BF16),
            pltpu.VMEM((L, 6 * L), BF16),
            pltpu.VMEM((2 * V, L), F32),
            pltpu.VMEM((V, L), BF16),
            pltpu.VMEM((1280, 3 * L), BF16),
            pltpu.VMEM((1280, 2 * L), F32),
            pltpu.VMEM((2000, L), F32),
            pltpu.VMEM((7 * V, L), F32),
        ],
        compiler_params=pltpu.CompilerParams(vmem_limit_bytes=VMEM_LIMIT),
    )(neighbours, live_count, lower, own, upper, inbox, w_subm, w_down)


def run_mask(features, occupancy, live_count):
    return pl.pallas_call(
        mask_kernel,
        out_shape=jax.ShapeDtypeStruct((2, V, L), BF16),
        in_specs=[smem(), smem()] + vmem(1),
        out_specs=vmem(1)[0],
        compiler_params=pltpu.CompilerParams(vmem_limit_bytes=VMEM_LIMIT),
    )(live_count, occupancy, features)


def finish_kernel(part_own, from_lower, from_upper, own, out):
    for g in range(2):
        total = part_own[g] + from_lower[g].astype(F32) + from_upper[g].astype(F32)
        total = total * jnp.broadcast_to(own[g, :, C : C + 1].astype(F32), (V, L))
        out[g] = jnp.transpose(total)[:C, :].astype(BF16)


def run_finish(part_own, from_lower, from_upper, own):
    return pl.pallas_call(
        finish_kernel,
        out_shape=jax.ShapeDtypeStruct((2, C, V), BF16),
        in_specs=vmem(4),
        out_specs=vmem(1)[0],
        compiler_params=pltpu.CompilerParams(vmem_limit_bytes=VMEM_LIMIT),
    )(part_own, from_lower, from_upper, own)


def shifted(block, distance):
    devices = range(lax.axis_size("space"))
    route = [(i - distance, i) for i in devices if i - distance in devices]
    return lax.ppermute(block, "space", route)


def exchanged(boxes):
    return lax.all_to_all(boxes, "space", split_axis=0, concat_axis=0, tiled=True)


def per_device(features, occupancy, neighbours, live_count, w_subm, w_down, grad_coarse):
    own = run_mask(features, occupancy, live_count)
    counts = jnp.broadcast_to(live_count.astype(F32)[:, None, None], (64, 2, L))
    inbox = exchanged(
        jnp.concatenate([grad_coarse.reshape(64, 6, L).astype(F32), counts], axis=1)
    )
    lower, upper = shifted(own, 1), shifted(own, -1)
    outbox, part_own, part_lower, part_upper, sums = run_blocks(
        neighbours, live_count, lower, own, upper, inbox, w_subm, w_down
    )
    coarse_out = exchanged(outbox)[:, :6, :].reshape(64, 6 * L).astype(BF16)
    grad_features = run_finish(part_own, shifted(part_upper, 1), shifted(part_lower, -1), own)
    sums = jnp.transpose(lax.psum(sums, "space")[:, :, :C], (0, 2, 1))
    return coarse_out, grad_features, sums[:27], sums[27:]


def solution(mesh):
    blocks = P(("rep", "space"), None)
    return jax.shard_map(
        per_device,
        mesh=mesh,
        in_specs=(
            P(("rep", "space"), None, None), blocks, blocks, P(("rep", "space")), P(), P(), blocks,
        ),
        out_specs=(
            blocks, P(("rep", "space"), None, None), P("rep", None, None), P("rep", None, None),
        ),
        check_vma=False,
    )
```

```python
import functools

import jax
import jax.numpy as jnp
from jax import lax
from jax.experimental import pallas as pl
from jax.experimental.pallas import tpu as pltpu
from jax.sharding import PartitionSpec as P

C, L, V = 96, 128, 512
OFFSETS = [(a, b, c) for a in (-1, 0, 1) for b in (-1, 0, 1) for c in (-1, 0, 1)]
PEERS, SHARDS, CHIPS, SHARD = 64, 27, 32, 48
VMEM_LIMIT = 50 * 2**20
F32, BF16 = jnp.float32, jnp.bfloat16
NT = (((1,), (1,)), ((), ()))


def segments(a, b, c):
    span = {-1: [(7, 0)], 0: [(i, i + 1) for i in range(8)], 1: [(0, 9)]}
    xs, ys, zs = span[a], span[b], span[c]
    if c == 0:
        return [(x * 64 + y * 8, 1, tx * 100 + ty * 10 + 1, 1, 8) for x, tx in xs for y, ty in ys]
    z, tz = zs[0]
    if b == 0:
        return [(x * 64 + z, 8, tx * 100 + 10 + tz, 10, 8) for x, tx in xs]
    y, ty = ys[0]
    if a == 0:
        return [(y * 8 + z, 64, 100 + ty * 10 + tz, 100, 8)]
    x, tx = xs[0]
    return [(x * 64 + y * 8 + z, 1, tx * 100 + ty * 10 + tz, 1, 1)]


def rows(start, count, stride):
    return pl.ds(start, count) if stride == 1 else pl.ds(start, count, stride=stride)


def mask_row(words, live, g):
    lane = lax.broadcasted_iota(jnp.int32, (1, V), 1)
    word = jnp.zeros((1, V), jnp.int32)
    for w in range(16):
        word = jnp.where(lane // 32 == w, words[g, w], word)
    bit = jnp.bitwise_and(jnp.right_shift(word, jnp.bitwise_and(lane, 31)), 1)
    return jnp.where(g < live, bit, 0)


def masked_rows(features, words, live, g):
    bit = mask_row(words, live, g)
    values = jnp.where(bit > 0, features[g].astype(F32), 0.0)
    marks = jnp.broadcast_to(bit.astype(F32), (L - C, V))
    return jnp.transpose(jnp.concatenate([values, marks], axis=0)).astype(BF16)


def remote(source, target, sent, arrived, peer):
    return pltpu.make_async_remote_copy(
        src_ref=source, dst_ref=target, send_sem=sent, recv_sem=arrived,
        device_id={"space": peer}, device_id_type=pl.DeviceIdType.MESH,
    )


def greet_all(me):
    barrier = pltpu.get_barrier_semaphore()

    def tell(i, carry):
        pl.semaphore_signal(
            barrier, inc=1, device_id={"space": lax.rem(me + i, PEERS)},
            device_id_type=pl.DeviceIdType.MESH,
        )
        return carry

    lax.fori_loop(1, PEERS, tell, 0)


def greeted():
    pl.semaphore_wait(pltpu.get_barrier_semaphore(), PEERS - 1)


def swap(me, outbox, inbox, sent, arrived):
    def box(i):
        peer = lax.rem(me + i, PEERS)
        return pl.ds(pl.multiple_of(peer * 8, 8), 8), peer

    def start(i, carry):
        at, peer = box(i)
        mine = pl.ds(pl.multiple_of(me * 8, 8), 8)
        remote(outbox.at[at], inbox.at[mine], sent.at[peer], arrived.at[me], peer).start()
        return carry

    def finish(i, carry):
        at, peer = box(i)
        remote(outbox.at[at], inbox.at[at], sent.at[peer], arrived.at[peer], peer).wait()
        return carry

    return (
        lambda: lax.fori_loop(1, PEERS, start, 0),
        lambda: lax.fori_loop(1, PEERS, finish, 0),
    )


def spread_kernel(
    live_ref, occupancy_ref, features_ref, cotangent_ref,
    own, lower, upper, inbox,
    outbox, box_sent, box_arrived, halo_sent, halo_arrived,
):
    me = lax.axis_index("space")
    greet_all(me)
    for n in range(6):
        outbox[pl.ds(n, PEERS, stride=8), :] = cotangent_ref[:, n * L : (n + 1) * L].astype(F32)
    live = jnp.broadcast_to(live_ref[0].astype(F32), (PEERS, L))
    for n in (6, 7):
        outbox[pl.ds(n, PEERS, stride=8), :] = live
    for g in range(2):
        own[g] = masked_rows(features_ref, occupancy_ref, live_ref[0], g)
    greeted()
    up = remote(own, lower, halo_sent.at[0], halo_arrived.at[0], lax.min(me + 1, PEERS - 1))
    down = remote(own, upper, halo_sent.at[1], halo_arrived.at[1], lax.max(me - 1, 0))
    has_up, has_down = me < PEERS - 1, me > 0
    start, finish = swap(me, outbox, inbox, box_sent, box_arrived)

    @pl.when(has_up)
    def _():
        up.start()

    @pl.when(has_down)
    def _():
        down.start()

    start()
    mine = pl.ds(pl.multiple_of(me * 8, 8), 8)
    inbox[mine, :] = outbox[mine, :]

    @pl.when(has_down)
    def _():
        up.wait_recv()

    @pl.when(jnp.logical_not(has_down))
    def _():
        lower[...] = jnp.zeros_like(lower)

    @pl.when(has_up)
    def _():
        down.wait_recv()

    @pl.when(jnp.logical_not(has_up))
    def _():
        upper[...] = jnp.zeros_like(upper)

    finish()

    @pl.when(has_up)
    def _():
        up.wait_send()

    @pl.when(has_down)
    def _():
        down.wait_send()


def block_kernel(
    table, live_ref, lower, own, upper, inbox, w_subm, w_down,
    outbox, part_own, part_lower, part_upper, sums,
    source, pad, cols, wf, wb, wd, perm, spread, pre, hid, dpre3, u, gpad, gsource,
):
    me = lax.axis_index("space")
    wf[...] = jnp.zeros_like(wf)
    wb[...] = jnp.zeros_like(wb)
    wd[...] = jnp.zeros_like(wd)
    for k in range(27):
        a, bc = divmod(k, 9)
        w = w_subm[k]
        wf[k * L : k * L + C, :C] = w
        wb[bc * L : bc * L + C, a * L : a * L + C] = w
    for j in range(8):
        wd[j * L : j * L + C, :C] = w_down[j]
    i = lax.broadcasted_iota(jnp.int32, (V, V), 0)
    v = lax.broadcasted_iota(jnp.int32, (V, V), 1)
    j, t = i // 64, i % 64
    x, y, z = 2 * (t // 16) + j // 4, 2 * (t // 4 % 4) + j // 2 % 2, 2 * (t % 4) + j % 2
    perm[...] = jnp.where(x * 64 + y * 8 + z == v, 1.0, 0.0).astype(BF16)
    spread[...] = jnp.where(
        lax.broadcasted_iota(jnp.int32, (L, 6 * L), 1) // 8
        == lax.broadcasted_iota(jnp.int32, (L, 6 * L), 0),
        1.0, 0.0,
    ).astype(BF16)
    pick = (
        lax.broadcasted_iota(jnp.int32, (8, L), 1) % 8 == lax.broadcasted_iota(jnp.int32, (8, L), 0)
    )

    for n, ref in enumerate((lower, own, upper)):
        for g in range(2):
            source[(2 * n + g) * V : (2 * n + g + 1) * V, :] = ref[g].astype(F32)
    source[6 * V :, :] = jnp.zeros((V, L), F32)

    for g in range(2):
        for k, offset in enumerate(OFFSETS):
            base = table[g, k] * V
            for s0, ss, p0, ps, count in segments(*offset):
                pad[rows(g * 1000 + p0, count, ps), :] = source[rows(base + s0, count, ss), :]

    def columns(gx, carry):
        for b in range(3):
            for c in range(3):
                piece = jnp.concatenate(
                    [pad[pl.ds(gx * 100 + (yy + b) * 10 + c, 8), :] for yy in range(8)], axis=0
                )
                bc = 3 * b + c
                cols[pl.ds(gx * 64, 64), bc * L : (bc + 1) * L] = piece.astype(BF16)
        return carry

    lax.fori_loop(0, 20, columns, 0)

    for g in range(2):
        acc = jnp.zeros((V, L), F32)
        for a in range(3):
            acc += jnp.dot(
                cols[g * 640 + a * 64 : g * 640 + a * 64 + V, :],
                wf[a * 9 * L : (a + 1) * 9 * L, :],
                preferred_element_type=F32,
            )
        pre[g * V : (g + 1) * V, :] = acc

    counts = inbox[:, 6, :]
    place = lax.broadcasted_iota(jnp.int32, (64, L), 0)
    start = jnp.sum(jnp.where(place < me, counts, 0.0), axis=0, keepdims=True)[0, 0].astype(jnp.int32)
    live = live_ref[0]
    outbox[...] = jnp.zeros_like(outbox)
    s, q = 0.7978845608028654, 0.044715
    dpre3[...] = jnp.zeros_like(dpre3)
    down = jnp.zeros((L, 8 * L), F32)
    for g in range(2):
        mask = jnp.broadcast_to(own[g, :, C : C + 1].astype(F32), (V, L))
        tt = pre[g * V : (g + 1) * V, :]
        th = jnp.tanh(s * (tt + q * tt * tt * tt))
        hidden = (0.5 * tt * (1.0 + th) * mask).astype(BF16)
        slope = (0.5 * (1.0 + th) + 0.5 * tt * (1.0 - th * th) * (s * (1.0 + 3.0 * q * tt * tt))) * mask
        both = jnp.dot(
            perm[...], jnp.concatenate([hidden, mask.astype(BF16)], axis=1),
            preferred_element_type=F32,
        )
        kids = both[:, :L].astype(BF16)
        hid[...] = kids
        cmask = both[:64, L:]
        coarse = jnp.dot(kids[:64], wd[:L, :], preferred_element_type=F32)
        for j in range(1, 8):
            cmask = jnp.maximum(cmask, both[j * 64 : (j + 1) * 64, L:])
            coarse += jnp.dot(
                kids[j * 64 : (j + 1) * 64], wd[j * L : (j + 1) * L, :], preferred_element_type=F32
            )
        coarse = (coarse * cmask).astype(BF16)
        group = jnp.bitwise_and(start + g, 7)
        alive = g < live
        flat = jnp.dot(coarse, spread[...], preferred_element_type=F32)
        for t in range(8):
            for n in range(6):
                tile = jnp.where(pick, flat[t * 8 : t * 8 + 8, n * L : (n + 1) * L], 0.0)
                line = jnp.where(alive, jnp.sum(tile, axis=0, keepdims=True), 0.0)

                @pl.when(alive)
                def _():
                    outbox[group * 8 + t, n : n + 1, :] = line

        dz = []
        for t in range(8):
            dz.append(
                jnp.concatenate(
                    [
                        jnp.where(pick, jnp.broadcast_to(inbox[group * 8 + t, n : n + 1, :], (8, L)), 0.0)
                        for n in range(6)
                    ],
                    axis=1,
                )
            )
        dz = jnp.concatenate(dz, axis=0).astype(BF16)
        dz = lax.dot_general(dz, spread[...], NT, preferred_element_type=F32)
        dz = jnp.where(alive & (cmask > 0), dz, 0.0).astype(BF16)
        dzt = jnp.transpose(dz.astype(F32)).astype(BF16)
        down += jnp.dot(
            dzt, jnp.concatenate([kids[j * 64 : (j + 1) * 64] for j in range(8)], axis=1),
            preferred_element_type=F32,
        )
        dh = jnp.concatenate(
            [
                lax.dot_general(dz, wd[j * L : (j + 1) * L, :], NT, preferred_element_type=F32)
                for j in range(8)
            ],
            axis=0,
        )
        high = dh.astype(BF16)
        low = (dh - high.astype(F32)).astype(BF16)
        dh = lax.dot_general(
            perm[...], jnp.concatenate([high, low], axis=1), (((0,), (0,)), ((), ())),
            preferred_element_type=F32,
        )
        dh = dh[:, :L] + dh[:, L:]
        dpre = slope * dh
        dpre16 = dpre.astype(BF16)
        for a in range(3):
            dpre3[g * 640 + a * 64 : g * 640 + a * 64 + V, a * L : (a + 1) * L] = dpre16
        hid[...] = dpre16
        pre[g * V : (g + 1) * V, :] = dpre
    lane = lax.broadcasted_iota(jnp.int32, (C, L), 1)
    held = {}

    def keep(k, product):
        held[k % 4] = jnp.transpose(product)[:C]
        if k % 4 == 3 or k == 34:
            last = held.get(3)
            for n in range(3):
                slab = held[n]
                if last is not None:
                    slab = jnp.where(lane < C, slab, pltpu.roll(last, C - 32 * n, 1))
                at = (3 * (k // 4) + n) * C
                sums[at : at + C, :] = slab.astype(BF16)
            held.clear()

    dt = jnp.transpose(pre[...]).astype(BF16)
    for a in range(3):
        for bc in range(0, 9, 2):
            lanes = slice(bc * L, min(bc + 2, 9) * L)
            total = jnp.dot(
                dt[:, :V], cols[a * 64 : a * 64 + V, lanes], preferred_element_type=F32
            ) + jnp.dot(
                dt[:, V:], cols[640 + a * 64 : 640 + a * 64 + V, lanes], preferred_element_type=F32
            )
            for n in range(min(2, 9 - bc)):
                keep(a * 9 + bc + n, total[:, n * L : (n + 1) * L])
    for j in range(8):
        keep(27 + j, down[:, j * L : (j + 1) * L])

    gpad[...] = jnp.zeros_like(gpad)
    for bc in range(0, 9, 2):
        width = min(2, 9 - bc)
        u[:, : width * L] = lax.dot_general(
            dpre3[...], wb[bc * L : (bc + width) * L, :], NT, preferred_element_type=F32
        )

        def add(gx, carry):
            for n in range(width):
                b, c = divmod(bc + n, 3)
                for yy in range(8):
                    at = pl.ds(gx * 100 + (yy + b) * 10 + c, 8)
                    gpad[at, :] += u[pl.ds(gx * 64 + yy * 8, 8), n * L : (n + 1) * L]
            return carry

        lax.fori_loop(0, 20, add, 0)

    gsource[...] = jnp.zeros_like(gsource)
    for g in range(2):
        for k, offset in enumerate(OFFSETS):
            base = table[g, k] * V
            for s0, ss, p0, ps, count in segments(*offset):
                gsource[rows(base + s0, count, ss), :] += gpad[rows(g * 1000 + p0, count, ps), :]
    for g in range(2):
        part_lower[g] = gsource[g * V : (g + 1) * V, :].astype(BF16)
        part_own[g] = gsource[(2 + g) * V : (3 + g) * V, :]
        part_upper[g] = gsource[(4 + g) * V : (5 + g) * V, :].astype(BF16)


def smem():
    return pl.BlockSpec(memory_space=pltpu.SMEM)


def vmem(n):
    return [pl.BlockSpec(memory_space=pltpu.VMEM)] * n


def run_blocks(neighbours, live_count, lower, own, upper, inbox, w_subm, w_down):
    return pl.pallas_call(
        block_kernel,
        out_shape=(
            jax.ShapeDtypeStruct((64, 8, L), F32),
            jax.ShapeDtypeStruct((2, V, L), F32),
            jax.ShapeDtypeStruct((2, V, L), BF16),
            jax.ShapeDtypeStruct((2, V, L), BF16),
            jax.ShapeDtypeStruct((27 * C, L), BF16),
        ),
        in_specs=[smem(), smem()] + vmem(6),
        out_specs=tuple(vmem(5)),
        scratch_shapes=[
            pltpu.VMEM((7 * V, L), F32),
            pltpu.VMEM((2000, L), F32),
            pltpu.VMEM((1280, 9 * L), BF16),
            pltpu.VMEM((27 * L, L), BF16),
            pltpu.VMEM((9 * L, 3 * L), BF16),
            pltpu.VMEM((8 * L, L), BF16),
            pltpu.VMEM((V, V), BF16),
            pltpu.VMEM((L, 6 * L), BF16),
            pltpu.VMEM((2 * V, L), F32),
            pltpu.VMEM((V, L), BF16),
            pltpu.VMEM((1280, 3 * L), BF16),
            pltpu.VMEM((1280, 2 * L), F32),
            pltpu.VMEM((2000, L), F32),
            pltpu.VMEM((7 * V, L), F32),
        ],
        compiler_params=pltpu.CompilerParams(vmem_limit_bytes=VMEM_LIMIT),
    )(neighbours, live_count, lower, own, upper, inbox, w_subm, w_down)


def run_spread(features, occupancy, live_count, grad_coarse):
    halo = jax.ShapeDtypeStruct((2, V, L), BF16)
    return pl.pallas_call(
        spread_kernel,
        out_shape=(halo, halo, halo, jax.ShapeDtypeStruct((8 * PEERS, L), F32)),
        in_specs=[smem(), smem()] + vmem(2),
        out_specs=tuple(vmem(4)),
        scratch_shapes=[
            pltpu.VMEM((8 * PEERS, L), F32),
            pltpu.SemaphoreType.DMA((PEERS,)),
            pltpu.SemaphoreType.DMA((PEERS,)),
            pltpu.SemaphoreType.DMA((2,)),
            pltpu.SemaphoreType.DMA((2,)),
        ],
        compiler_params=pltpu.CompilerParams(
            vmem_limit_bytes=VMEM_LIMIT, collective_id=0, has_side_effects=True
        ),
    )(live_count, occupancy, features, grad_coarse)


def gather_kernel(
    outbox, part_own, part_lower, part_upper, own, sums,
    coarse_out, grad_features, grad_subm, grad_down,
    inbox, from_lower, from_upper, other, chip, shares, total,
    box_sent, box_arrived, halo_sent, halo_arrived, pair_sent, pair_arrived,
    share_sent, share_arrived, total_sent, total_arrived, copy_sent, copy_arrived,
):
    me = lax.axis_index("space")
    here, core = me // 2, lax.rem(me, 2)
    partner = me + 1 - 2 * core
    half = SHARDS * SHARD

    def rows_of(shard):
        return pl.ds(pl.multiple_of(shard * SHARD, SHARD), SHARD)

    def chip_of(shard):
        return shard + shard // 6

    mine = here - here // 7
    owns = (lax.rem(here, 7) != 6) & (here < CHIPS - 1)

    greet_all(me)
    greeted()

    def half_of(which):
        return pl.ds(pl.multiple_of(which * half, half), half)

    pair = remote(sums.at[half_of(1 - core)], other, pair_sent, pair_arrived, partner)
    pair.start()
    up = remote(part_upper, from_lower, halo_sent.at[0], halo_arrived.at[0], lax.min(me + 1, PEERS - 1))
    down = remote(part_lower, from_upper, halo_sent.at[1], halo_arrived.at[1], lax.max(me - 1, 0))
    has_up, has_down = me < PEERS - 1, me > 0
    start, finish = swap(me, outbox, inbox, box_sent, box_arrived)

    @pl.when(has_up)
    def _():
        up.start()

    @pl.when(has_down)
    def _():
        down.start()

    pair.wait_recv()
    chip[...] = (sums[half_of(core), :].astype(F32) + other[...].astype(F32)).astype(BF16)

    def share(shard):
        peer = chip_of(shard) * 2 + core
        return peer, remote(
            chip.at[rows_of(shard)], shares.at[rows_of(here)],
            share_sent.at[shard], share_arrived.at[here], peer,
        )

    def share_start(i, carry):
        shard = lax.rem(mine + i, SHARDS)
        peer, copy = share(shard)

        @pl.when(peer != me)
        def _():
            copy.start()

        return carry

    lax.fori_loop(0, SHARDS, share_start, 0)
    start()
    box = pl.ds(pl.multiple_of(me * 8, 8), 8)
    inbox[box, :] = outbox[box, :]

    @pl.when(has_down)
    def _():
        up.wait_recv()

    @pl.when(jnp.logical_not(has_down))
    def _():
        from_lower[...] = jnp.zeros_like(from_lower)

    @pl.when(has_up)
    def _():
        down.wait_recv()

    @pl.when(jnp.logical_not(has_up))
    def _():
        from_upper[...] = jnp.zeros_like(from_upper)

    for g in range(2):
        value = part_own[g] + from_lower[g].astype(F32) + from_upper[g].astype(F32)
        value = value * jnp.broadcast_to(own[g, :, C : C + 1].astype(F32), (V, L))
        grad_features[g] = jnp.transpose(value)[:C, :].astype(BF16)

    def handed(shard, peer):
        at = pl.ds(pl.multiple_of(core * half + shard * SHARD, SHARD), SHARD)
        return remote(total.at[at], total.at[at], total_sent.at[peer // 2], total_arrived.at[shard], peer)

    def copied(shard, which):
        at = pl.ds(pl.multiple_of(which * half + shard * SHARD, SHARD), SHARD)
        return remote(total.at[at], total.at[at], copy_sent.at[shard], copy_arrived.at[shard], partner)

    @pl.when(owns)
    def _():
        shares[rows_of(here), :] = chip[rows_of(mine), :]

        def arrived(i, carry):
            there = lax.rem(here + i, CHIPS)
            remote(
                chip.at[rows_of(0)], shares.at[rows_of(there)],
                share_sent.at[0], share_arrived.at[there], there * 2 + core,
            ).wait_recv()
            return carry

        lax.fori_loop(1, CHIPS, arrived, 0)

        def plus(i, value):
            return value + shares[rows_of(i), :].astype(F32)

        value = lax.fori_loop(0, CHIPS, plus, jnp.zeros((SHARD, L), F32))
        at = pl.ds(pl.multiple_of(core * half + mine * SHARD, SHARD), SHARD)
        total[at, :] = value.astype(BF16)

        def hand(i, carry):
            handed(mine, lax.rem(here + i, CHIPS) * 2 + core).start()
            return carry

        lax.fori_loop(1, CHIPS, hand, 0)
        copied(mine, core).start()

    def pass_on(i, carry):
        shard = lax.rem(mine + i, SHARDS)

        @pl.when(chip_of(shard) != here)
        def _():
            handed(shard, chip_of(shard) * 2 + core).wait_recv()
            copied(shard, core).start()

        return carry

    lax.fori_loop(0, SHARDS, pass_on, 0)

    finish()
    for n in range(6):
        coarse_out[:, n * L : (n + 1) * L] = inbox[pl.ds(n, PEERS, stride=8), :].astype(BF16)

    def copied_in(i, carry):
        copied(i, 1 - core).wait_recv()
        return carry

    lax.fori_loop(0, SHARDS, copied_in, 0)

    for k in range(35):
        quad, n = divmod(k, 4)
        if n < 3:
            at = (3 * quad + n) * C
            value = total[at : at + C, :].astype(F32)[:, :C]
        else:
            lane = lax.broadcasted_iota(jnp.int32, (C, L), 1)
            value = jnp.zeros((C, L), F32)
            for m in range(3):
                at = (3 * quad + m) * C
                piece = pltpu.roll(total[at : at + C, :].astype(F32), 32 + 32 * m, 1)
                value = jnp.where(lane // 32 == m, piece, value)
            value = value[:, :C]
        if k < 27:
            grad_subm[k] = value
        else:
            grad_down[k - 27] = value

    pair.wait_send()

    @pl.when(has_up)
    def _():
        up.wait_send()

    @pl.when(has_down)
    def _():
        down.wait_send()

    def share_done(i, carry):
        peer, copy = share(i)

        @pl.when(peer != me)
        def _():
            copy.wait_send()

        return carry

    lax.fori_loop(0, SHARDS, share_done, 0)

    @pl.when(owns)
    def _():
        def done(i, carry):
            handed(mine, lax.rem(here + i, CHIPS) * 2 + core).wait_send()
            return carry

        lax.fori_loop(1, CHIPS, done, 0)

    def copied_out(i, carry):
        copied(i, core).wait_send()
        return carry

    lax.fori_loop(0, SHARDS, copied_out, 0)


def run_gather(outbox, part_own, part_lower, part_upper, own, sums):
    dma = pltpu.SemaphoreType.DMA
    return pl.pallas_call(
        gather_kernel,
        out_shape=(
            jax.ShapeDtypeStruct((PEERS, 6 * L), BF16),
            jax.ShapeDtypeStruct((2, C, V), BF16),
            jax.ShapeDtypeStruct((27, C, C), F32),
            jax.ShapeDtypeStruct((8, C, C), F32),
        ),
        in_specs=vmem(6),
        out_specs=tuple(vmem(4)),
        scratch_shapes=[
            pltpu.VMEM((8 * PEERS, L), F32),
            pltpu.VMEM((2, V, L), BF16),
            pltpu.VMEM((2, V, L), BF16),
            pltpu.VMEM((SHARDS * SHARD, L), BF16),
            pltpu.VMEM((SHARDS * SHARD, L), BF16),
            pltpu.VMEM((CHIPS * SHARD, L), BF16),
            pltpu.VMEM((2 * SHARDS * SHARD, L), BF16),
            dma((PEERS,)), dma((PEERS,)), dma((2,)), dma((2,)), dma(()), dma(()),
            dma((SHARDS,)), dma((CHIPS,)), dma((CHIPS,)), dma((SHARDS,)), dma((SHARDS,)), dma((SHARDS,)),
        ],
        compiler_params=pltpu.CompilerParams(
            vmem_limit_bytes=VMEM_LIMIT, collective_id=1, has_side_effects=True
        ),
    )(outbox, part_own, part_lower, part_upper, own, sums)


def per_device(features, occupancy, neighbours, live_count, w_subm, w_down, grad_coarse):
    own, lower, upper, inbox = run_spread(features, occupancy, live_count, grad_coarse)
    outbox, part_own, part_lower, part_upper, sums = run_blocks(
        neighbours, live_count, lower, own, upper, inbox.reshape(PEERS, 8, L), w_subm, w_down
    )
    return run_gather(outbox.reshape(8 * PEERS, L), part_own, part_lower, part_upper, own, sums)


def solution(mesh):
    blocks = P(("rep", "space"), None)
    return jax.shard_map(
        per_device,
        mesh=mesh,
        in_specs=(
            P(("rep", "space"), None, None), blocks, blocks, P(("rep", "space")), P(), P(), blocks,
        ),
        out_specs=(
            blocks, P(("rep", "space"), None, None), P("rep", None, None), P("rep", None, None),
        ),
        check_vma=False,
    )
```

```python
import functools

import jax
import jax.numpy as jnp
from jax import lax
from jax.experimental import pallas as pl
from jax.experimental.pallas import tpu as pltpu
from jax.sharding import PartitionSpec as P

C, L, V = 96, 128, 512
OFFSETS = [(a, b, c) for a in (-1, 0, 1) for b in (-1, 0, 1) for c in (-1, 0, 1)]
PEERS = 64
HALF, YPART, ZPART = 1344, 336, 48
VMEM_LIMIT = 50 * 2**20
F32, BF16 = jnp.float32, jnp.bfloat16
NT = (((1,), (1,)), ((), ()))


def segments(a, b, c):
    span = {-1: [(7, 0)], 0: [(i, i + 1) for i in range(8)], 1: [(0, 9)]}
    xs, ys, zs = span[a], span[b], span[c]
    if c == 0:
        return [(x * 64 + y * 8, 1, tx * 100 + ty * 10 + 1, 1, 8) for x, tx in xs for y, ty in ys]
    z, tz = zs[0]
    if b == 0:
        return [(x * 64 + z, 8, tx * 100 + 10 + tz, 10, 8) for x, tx in xs]
    y, ty = ys[0]
    if a == 0:
        return [(y * 8 + z, 64, 100 + ty * 10 + tz, 100, 8)]
    x, tx = xs[0]
    return [(x * 64 + y * 8 + z, 1, tx * 100 + ty * 10 + tz, 1, 1)]


def rows(start, count, stride):
    return pl.ds(start, count) if stride == 1 else pl.ds(start, count, stride=stride)


def mask_row(words, live, g):
    lane = lax.broadcasted_iota(jnp.int32, (1, V), 1)
    word = jnp.zeros((1, V), jnp.int32)
    for w in range(16):
        word = jnp.where(lane // 32 == w, words[g, w], word)
    bit = jnp.bitwise_and(jnp.right_shift(word, jnp.bitwise_and(lane, 31)), 1)
    return jnp.where(g < live, bit, 0)


def masked_rows(features, words, live, g):
    bit = mask_row(words, live, g)
    values = jnp.where(bit > 0, features[g].astype(F32), 0.0)
    marks = jnp.broadcast_to(bit.astype(F32), (L - C, V))
    return jnp.transpose(jnp.concatenate([values, marks], axis=0)).astype(BF16)


def remote(source, target, sent, arrived, peer):
    return pltpu.make_async_remote_copy(
        src_ref=source, dst_ref=target, send_sem=sent, recv_sem=arrived,
        device_id={"space": peer}, device_id_type=pl.DeviceIdType.MESH,
    )


def greet_all(me):
    barrier = pltpu.get_barrier_semaphore()

    def tell(i, carry):
        pl.semaphore_signal(
            barrier, inc=1, device_id={"space": lax.rem(me + i, PEERS)},
            device_id_type=pl.DeviceIdType.MESH,
        )
        return carry

    lax.fori_loop(1, PEERS, tell, 0)


def greeted():
    pl.semaphore_wait(pltpu.get_barrier_semaphore(), PEERS - 1)


def swap(me, outbox, inbox, sent, arrived):
    def box(i):
        peer = lax.rem(me + i, PEERS)
        return pl.ds(pl.multiple_of(peer * 8, 8), 8), peer

    def start(i, carry):
        at, peer = box(i)
        mine = pl.ds(pl.multiple_of(me * 8, 8), 8)
        remote(outbox.at[at], inbox.at[mine], sent.at[peer], arrived.at[me], peer).start()
        return carry

    def finish(i, carry):
        at, peer = box(i)
        remote(outbox.at[at], inbox.at[at], sent.at[peer], arrived.at[peer], peer).wait()
        return carry

    return (
        lambda: lax.fori_loop(1, PEERS, start, 0),
        lambda: lax.fori_loop(1, PEERS, finish, 0),
    )


def section_kernel(
    table, live_ref, occupancy_ref, features_hbm, cotangent_hbm, w_subm_hbm, w_down_hbm,
    coarse_in, grad_features, total,
    features, cotangent, w_subm, w_down,
    own, lower, upper, outbox, inbox, coarse_box,
    source, pad, cols, wf, wb, wd, perm, spread, pre, dpre3, u, gpad, gsource,
    sums32, sums16, pair_in, chip32, chip16, y_in, y32, y16, z_in,
    part_lower, part_upper, from_lower, from_upper,
    load_sem, box_sent, box_arrived, back_sent, back_arrived, halo_sent, halo_arrived,
    rim_sent, rim_arrived, pair_sent, pair_arrived, ysent, yarrived, zsent, zarrived,
    gzsent, gzarrived, gysent, gyarrived, copy_sent, copy_arrived,
):
    me = lax.axis_index("space")
    y, z, core = me // 16, lax.rem(me // 2, 8), lax.rem(me, 2)
    partner = me + 1 - 2 * core
    has_up, has_down = me < PEERS - 1, me > 0
    loads = [
        pltpu.make_async_copy(hbm, ref, load_sem.at[n])
        for n, (hbm, ref) in enumerate(
            ((features_hbm, features), (cotangent_hbm, cotangent), (w_subm_hbm, w_subm), (w_down_hbm, w_down))
        )
    ]
    for load in loads:
        load.start()
    greet_all(me)

    i = lax.broadcasted_iota(jnp.int32, (V, V), 0)
    v = lax.broadcasted_iota(jnp.int32, (V, V), 1)
    j, t = i // 64, i % 64
    vx, vy, vz = 2 * (t // 16) + j // 4, 2 * (t // 4 % 4) + j // 2 % 2, 2 * (t % 4) + j % 2
    perm[...] = jnp.where(vx * 64 + vy * 8 + vz == v, 1.0, 0.0).astype(BF16)
    spread[...] = jnp.where(
        lax.broadcasted_iota(jnp.int32, (L, 6 * L), 1) // 8
        == lax.broadcasted_iota(jnp.int32, (L, 6 * L), 0),
        1.0, 0.0,
    ).astype(BF16)
    wf[...] = jnp.zeros_like(wf)
    wb[...] = jnp.zeros_like(wb)
    wd[...] = jnp.zeros_like(wd)
    dpre3[...] = jnp.zeros_like(dpre3)
    coarse_box[...] = jnp.zeros_like(coarse_box)
    source[6 * V :, :] = jnp.zeros((V, L), F32)

    loads[0].wait()
    for g in range(2):
        own[g] = masked_rows(features, occupancy_ref, live_ref[0], g)
    loads[1].wait()
    for n in range(6):
        outbox[pl.ds(n, PEERS, stride=8), :] = cotangent[:, n * L : (n + 1) * L].astype(F32)
    counts = jnp.broadcast_to(live_ref[0].astype(F32), (PEERS, L))
    for n in (6, 7):
        outbox[pl.ds(n, PEERS, stride=8), :] = counts

    greeted()
    up = remote(own, lower, halo_sent.at[0], halo_arrived.at[0], lax.min(me + 1, PEERS - 1))
    down = remote(own, upper, halo_sent.at[1], halo_arrived.at[1], lax.max(me - 1, 0))

    @pl.when(has_up)
    def _():
        up.start()

    @pl.when(has_down)
    def _():
        down.start()

    box_start, box_finish = swap(me, outbox, inbox, box_sent, box_arrived)
    box_start()
    mine = pl.ds(pl.multiple_of(me * 8, 8), 8)
    inbox[mine, :] = outbox[mine, :]

    loads[2].wait()
    loads[3].wait()
    for k in range(27):
        a, bc = divmod(k, 9)
        w = w_subm[k]
        wf[k * L : k * L + C, :C] = w
        wb[bc * L : bc * L + C, a * L : a * L + C] = w
    for j in range(8):
        wd[j * L : j * L + C, :C] = w_down[j]

    for g in range(2):
        source[(2 + g) * V : (3 + g) * V, :] = own[g].astype(F32)

    @pl.when(has_down)
    def _():
        up.wait_recv()

    @pl.when(jnp.logical_not(has_down))
    def _():
        lower[...] = jnp.zeros_like(lower)

    @pl.when(has_up)
    def _():
        down.wait_recv()

    @pl.when(jnp.logical_not(has_up))
    def _():
        upper[...] = jnp.zeros_like(upper)

    for g in range(2):
        source[g * V : (g + 1) * V, :] = lower[g].astype(F32)
        source[(4 + g) * V : (5 + g) * V, :] = upper[g].astype(F32)

    for g in range(2):
        for k, offset in enumerate(OFFSETS):
            base = (2 + g) * V if k == 13 else table[g, k] * V
            for s0, ss, p0, ps, count in segments(*offset):
                pad[rows(g * 1000 + p0, count, ps), :] = source[rows(base + s0, count, ss), :]

    def columns(gx, carry):
        for b in range(3):
            for c in range(3):
                piece = jnp.concatenate(
                    [pad[pl.ds(gx * 100 + (yy + b) * 10 + c, 8), :] for yy in range(8)], axis=0
                )
                bc = 3 * b + c
                cols[pl.ds(pl.multiple_of(gx * 64, 64), 64), bc * L : (bc + 1) * L] = piece.astype(BF16)
        return carry

    lax.fori_loop(0, 20, columns, 0)

    for g in range(2):
        acc = jnp.zeros((V, L), F32)
        for a in range(3):
            acc += jnp.dot(
                cols[g * 640 + a * 64 : g * 640 + a * 64 + V, :],
                wf[a * 9 * L : (a + 1) * 9 * L, :],
                preferred_element_type=F32,
            )
        pre[g * V : (g + 1) * V, :] = acc

    box_finish()
    boxes = jnp.concatenate(
        [inbox[pl.ds(n, PEERS, stride=8), :] for n in range(6)], axis=1
    ).astype(BF16)
    below = jnp.where(
        lax.broadcasted_iota(jnp.int32, (PEERS, L), 0) < me, inbox[pl.ds(6, PEERS, stride=8), :], 0.0
    )
    first = jnp.sum(below, axis=0, keepdims=True).astype(jnp.int32)[:, :64]
    pick = (
        lax.broadcasted_iota(jnp.int32, (64, 6 * L), 1) % 8
        == lax.broadcasted_iota(jnp.int32, (64, 6 * L), 0) % 8
    )
    peer = lax.broadcasted_iota(jnp.int32, (64, 64), 1)
    piece = lax.broadcasted_iota(jnp.int32, (64, 64), 0) // 8
    live = live_ref[0]
    s, q = 0.7978845608028654, 0.044715
    down_sums = jnp.zeros((L, 8 * L), F32)
    dealt = jnp.zeros((PEERS, 6 * L), F32)
    for g in range(2):
        mask = jnp.broadcast_to(own[g, :, C : C + 1].astype(F32), (V, L))
        tt = pre[g * V : (g + 1) * V, :]
        th = jnp.tanh(s * (tt + q * tt * tt * tt))
        hidden = (0.5 * tt * (1.0 + th) * mask).astype(BF16)
        slope = (0.5 * (1.0 + th) + 0.5 * tt * (1.0 - th * th) * (s * (1.0 + 3.0 * q * tt * tt))) * mask
        both = jnp.dot(
            perm[...], jnp.concatenate([hidden, mask.astype(BF16)], axis=1),
            preferred_element_type=F32,
        )
        kids = both[:, :L].astype(BF16)
        cmask = both[:64, L:]
        coarse = jnp.dot(kids[:64], wd[:L, :], preferred_element_type=F32)
        for j in range(1, 8):
            cmask = jnp.maximum(cmask, both[j * 64 : (j + 1) * 64, L:])
            coarse += jnp.dot(
                kids[j * 64 : (j + 1) * 64], wd[j * L : (j + 1) * L, :], preferred_element_type=F32
            )
        coarse = (coarse * cmask).astype(BF16)
        holder = jnp.bitwise_and(jnp.broadcast_to(first, (64, 64)) + g, 7) * 8 + piece
        chosen = jnp.where((holder == peer) & (g < live), 1.0, 0.0).astype(BF16)
        flat = jnp.dot(coarse, spread[...], preferred_element_type=F32)
        flat = jnp.where(pick, flat, 0.0).astype(BF16)
        dealt += lax.dot_general(chosen, flat, (((0,), (0,)), ((), ())), preferred_element_type=F32)
        dz = jnp.dot(chosen, boxes, preferred_element_type=F32)
        dz = jnp.where(pick, dz, 0.0).astype(BF16)
        dz = lax.dot_general(dz, spread[...], NT, preferred_element_type=F32)
        dz = jnp.where(cmask > 0, dz, 0.0)
        dzt = jnp.transpose(dz).astype(BF16)
        dz = dz.astype(BF16)
        down_sums += jnp.dot(
            dzt, jnp.concatenate([kids[j * 64 : (j + 1) * 64] for j in range(8)], axis=1),
            preferred_element_type=F32,
        )
        dh = jnp.concatenate(
            [
                lax.dot_general(dz, wd[j * L : (j + 1) * L, :], NT, preferred_element_type=F32)
                for j in range(8)
            ],
            axis=0,
        )
        high = dh.astype(BF16)
        low = (dh - high.astype(F32)).astype(BF16)
        dh = lax.dot_general(
            perm[...], jnp.concatenate([high, low], axis=1), (((0,), (0,)), ((), ())),
            preferred_element_type=F32,
        )
        dpre = slope * (dh[:, :L] + dh[:, L:])
        dpre16 = dpre.astype(BF16)
        for a in range(3):
            dpre3[g * 640 + a * 64 : g * 640 + a * 64 + V, a * L : (a + 1) * L] = dpre16
        pre[g * V : (g + 1) * V, :] = dpre
    for n in range(6):
        coarse_box[pl.ds(n, PEERS, stride=8), :] = dealt[:, n * L : (n + 1) * L]

    lane = lax.broadcasted_iota(jnp.int32, (C, L), 1)
    held = {}

    def keep(k, product):
        held[k % 4] = jnp.transpose(product)[:C]
        if k % 4 == 3 or k == 34:
            last = held.get(3)
            for n in range(3):
                slab = held[n]
                if last is not None:
                    slab = jnp.where(lane < C, slab, pltpu.roll(last, C - 32 * n, 1))
                at = (3 * (k // 4) + n) * C
                sums32[at : at + C, :] = slab
                sums16[at : at + C, :] = slab.astype(BF16)
            held.clear()

    dt = jnp.transpose(pre[...]).astype(BF16)
    for a in range(3):
        for bc in range(0, 9, 2):
            lanes = slice(bc * L, min(bc + 2, 9) * L)
            value = jnp.dot(
                dt[:, :V], cols[a * 64 : a * 64 + V, lanes], preferred_element_type=F32
            ) + jnp.dot(
                dt[:, V:], cols[640 + a * 64 : 640 + a * 64 + V, lanes], preferred_element_type=F32
            )
            for n in range(min(2, 9 - bc)):
                keep(a * 9 + bc + n, value[:, n * L : (n + 1) * L])
    for j in range(8):
        keep(27 + j, down_sums[:, j * L : (j + 1) * L])
    sums32[27 * C :, :] = jnp.zeros((C, L), F32)
    sums16[27 * C :, :] = jnp.zeros((C, L), BF16)

    def span(at, count):
        return pl.ds(pl.multiple_of(at, 16), count)

    def device(yy, zz):
        return yy * 16 + zz * 2 + core

    pair = remote(sums16.at[span((1 - core) * HALF, HALF)], pair_in, pair_sent, pair_arrived, partner)
    pair.start()
    back_start, back_finish = swap(me, coarse_box, coarse_in, back_sent, back_arrived)
    back_start()
    coarse_in[mine, :] = coarse_box[mine, :]
    pair.wait_recv()
    value = sums32[span(core * HALF, HALF), :] + pair_in[...].astype(F32)
    chip32[...] = value
    chip16[...] = value.astype(BF16)
    ysteps = []
    for n in range(3):
        yy = jnp.bitwise_and(y + n + 1, 3)
        ysteps.append(
            remote(chip16.at[span(yy * YPART, YPART)], y_in.at[n], ysent.at[n], yarrived.at[n], device(yy, z))
        )
        ysteps[n].start()

    gpad[...] = jnp.zeros_like(gpad)
    for bc in range(0, 9, 2):
        width = min(2, 9 - bc)
        u[:, : width * L] = lax.dot_general(
            dpre3[...], wb[bc * L : (bc + width) * L, :], NT, preferred_element_type=F32
        )

        def add(gx, carry):
            for n in range(width):
                b, c = divmod(bc + n, 3)
                for yy in range(8):
                    at = pl.ds(gx * 100 + (yy + b) * 10 + c, 8)
                    gpad[at, :] += u[pl.ds(pl.multiple_of(gx * 64 + yy * 8, 8), 8), n * L : (n + 1) * L]
            return carry

        lax.fori_loop(0, 20, add, 0)

    value = chip32[span(y * YPART, YPART), :]
    for n in range(3):
        ysteps[n].wait_recv()
        value = value + y_in[n].astype(F32)
    y32[...] = value
    y16[...] = value.astype(BF16)

    def zstep(n):
        zz = jnp.bitwise_and(z + n + 1, 7)
        at = span(lax.min(zz, 6) * ZPART, ZPART)
        return zz < 7, remote(y16.at[at], z_in.at[n], zsent.at[n], zarrived.at[n], device(y, zz))

    for n in range(7):
        wanted, copy = zstep(n)

        @pl.when(wanted)
        def _():
            copy.start()

    gsource[...] = jnp.zeros_like(gsource)
    for g in range(2):
        for s0, ss, p0, ps, count in segments(0, 0, 0):
            gsource[rows((2 + g) * V + s0, count, ss), :] = gpad[rows(g * 1000 + p0, count, ps), :]

    def give(n, carry):
        for g in range(2):
            for k, offset in enumerate(OFFSETS):
                if k != 13:
                    here = jnp.where(table[g, k] == n, 1.0, 0.0)
                    for s0, ss, p0, ps, count in segments(*offset):
                        at = rows(n * V + s0, count, ss)
                        gsource[at, :] += gpad[rows(g * 1000 + p0, count, ps), :] * here
        return carry

    lax.fori_loop(0, 6, give, 0)
    for g in range(2):
        part_lower[g] = gsource[g * V : (g + 1) * V, :].astype(BF16)
        part_upper[g] = gsource[(4 + g) * V : (5 + g) * V, :].astype(BF16)
    rim_up = remote(part_upper, from_lower, rim_sent.at[0], rim_arrived.at[0], lax.min(me + 1, PEERS - 1))
    rim_down = remote(part_lower, from_upper, rim_sent.at[1], rim_arrived.at[1], lax.max(me - 1, 0))

    @pl.when(has_up)
    def _():
        rim_up.start()

    @pl.when(has_down)
    def _():
        rim_down.start()

    def gzstep(n, owner, to):
        at = span(core * HALF + y * YPART + owner * ZPART, ZPART)
        return remote(total.at[at], total.at[at], gzsent.at[n], gzarrived.at[n], device(y, to))

    @pl.when(z < 7)
    def _():
        value = y32[span(z * ZPART, ZPART), :]
        for n in range(7):
            zstep(n)[1].wait_recv()
            value = value + z_in[n].astype(F32)
        total[span(core * HALF + y * YPART + z * ZPART, ZPART), :] = value.astype(BF16)
        for n in range(7):
            gzstep(n, z, jnp.bitwise_and(z + n + 1, 7)).start()

    @pl.when(has_down)
    def _():
        rim_up.wait_recv()

    @pl.when(jnp.logical_not(has_down))
    def _():
        from_lower[...] = jnp.zeros_like(from_lower)

    @pl.when(has_up)
    def _():
        rim_down.wait_recv()

    @pl.when(jnp.logical_not(has_up))
    def _():
        from_upper[...] = jnp.zeros_like(from_upper)

    for g in range(2):
        value = gsource[(2 + g) * V : (3 + g) * V, :] + from_lower[g].astype(F32) + from_upper[g].astype(F32)
        value = value * jnp.broadcast_to(own[g, :, C : C + 1].astype(F32), (V, L))
        grad_features[g] = jnp.transpose(value)[:C, :].astype(BF16)

    for n in range(7):
        owner = jnp.bitwise_and(z + 7 - n, 7)

        @pl.when(owner < 7)
        def _():
            gzstep(n, lax.min(owner, 6), owner).wait_recv()

    def gystep(n, owner, to):
        at = span(core * HALF + owner * YPART, YPART)
        return remote(total.at[at], total.at[at], gysent.at[n], gyarrived.at[n], device(to, z))

    def across(n, which, owner):
        at = span(which * HALF + owner * YPART, YPART)
        return remote(total.at[at], total.at[at], copy_sent.at[n], copy_arrived.at[n], partner)

    owners = [jnp.bitwise_and(y + 4 - n, 3) for n in range(4)]
    for n in range(3):
        gystep(n, y, jnp.bitwise_and(y + n + 1, 3)).start()
    across(0, core, y).start()
    for n in range(3):
        gystep(n, owners[n + 1], owners[n + 1]).wait_recv()
        across(n + 1, core, owners[n + 1]).start()
    back_finish()
    for n in range(4):
        across(n, 1 - core, owners[n]).wait_recv()

    @pl.when(has_up)
    def _():
        up.wait_send()
        rim_up.wait_send()

    @pl.when(has_down)
    def _():
        down.wait_send()
        rim_down.wait_send()

    pair.wait_send()
    for n in range(3):
        ysteps[n].wait_send()
        gystep(n, y, jnp.bitwise_and(y + n + 1, 3)).wait_send()
    for n in range(7):
        wanted, copy = zstep(n)

        @pl.when(wanted)
        def _():
            copy.wait_send()

    @pl.when(z < 7)
    def _():
        for n in range(7):
            gzstep(n, z, jnp.bitwise_and(z + n + 1, 7)).wait_send()

    for n in range(4):
        across(n, core, owners[n]).wait_send()


def smem():
    return pl.BlockSpec(memory_space=pltpu.SMEM)


def vmem(n):
    return [pl.BlockSpec(memory_space=pltpu.VMEM)] * n


def hbm(n):
    return [pl.BlockSpec(memory_space=pl.ANY)] * n


def run_section(neighbours, live_count, occupancy, features, grad_coarse, w_subm, w_down):
    dma = pltpu.SemaphoreType.DMA
    block = pltpu.VMEM((2, V, L), BF16)
    boxes = pltpu.VMEM((8 * PEERS, L), F32)
    return pl.pallas_call(
        section_kernel,
        out_shape=(
            jax.ShapeDtypeStruct((8 * PEERS, L), F32),
            jax.ShapeDtypeStruct((2, C, V), BF16),
            jax.ShapeDtypeStruct((2 * HALF, L), BF16),
        ),
        in_specs=[smem(), smem(), smem()] + hbm(4),
        out_specs=tuple(vmem(3)),
        scratch_shapes=[
            pltpu.VMEM((2, C, V), BF16),
            pltpu.VMEM((PEERS, 6 * L), BF16),
            pltpu.VMEM((27, C, C), BF16),
            pltpu.VMEM((8, C, C), BF16),
            block, block, block, boxes, boxes, boxes,
            pltpu.VMEM((7 * V, L), F32),
            pltpu.VMEM((2000, L), F32),
            pltpu.VMEM((1280, 9 * L), BF16),
            pltpu.VMEM((27 * L, L), BF16),
            pltpu.VMEM((9 * L, 3 * L), BF16),
            pltpu.VMEM((8 * L, L), BF16),
            pltpu.VMEM((V, V), BF16),
            pltpu.VMEM((L, 6 * L), BF16),
            pltpu.VMEM((2 * V, L), F32),
            pltpu.VMEM((1280, 3 * L), BF16),
            pltpu.VMEM((1280, 2 * L), F32),
            pltpu.VMEM((2000, L), F32),
            pltpu.VMEM((6 * V, L), F32),
            pltpu.VMEM((2 * HALF, L), F32),
            pltpu.VMEM((2 * HALF, L), BF16),
            pltpu.VMEM((HALF, L), BF16),
            pltpu.VMEM((HALF, L), F32),
            pltpu.VMEM((HALF, L), BF16),
            pltpu.VMEM((3, YPART, L), BF16),
            pltpu.VMEM((YPART, L), F32),
            pltpu.VMEM((YPART, L), BF16),
            pltpu.VMEM((7, ZPART, L), BF16),
            block, block, block, block,
            dma((4,)), dma((PEERS,)), dma((PEERS,)), dma((PEERS,)), dma((PEERS,)),
            dma((2,)), dma((2,)), dma((2,)), dma((2,)), dma(()), dma(()),
            dma((3,)), dma((3,)), dma((7,)), dma((7,)), dma((7,)), dma((7,)),
            dma((3,)), dma((3,)), dma((4,)), dma((4,)),
        ],
        compiler_params=pltpu.CompilerParams(
            vmem_limit_bytes=VMEM_LIMIT, collective_id=0, has_side_effects=True
        ),
    )(neighbours, live_count, occupancy, features, grad_coarse, w_subm, w_down)


def final_kernel(
    coarse_in, features_in, total, coarse_out, grad_features, grad_subm, grad_down,
    coarse, subm, down, sem,
):
    copies = [pltpu.make_async_copy(features_in, grad_features, sem.at[0])]
    copies[0].start()
    for n in range(6):
        coarse[:, n * L : (n + 1) * L] = coarse_in[pl.ds(n, PEERS, stride=8), :].astype(BF16)
    copies.append(pltpu.make_async_copy(coarse, coarse_out, sem.at[1]))
    copies[1].start()
    lane = lax.broadcasted_iota(jnp.int32, (C, L), 1)
    for k in range(35):
        quad, n = divmod(k, 4)
        if n < 3:
            at = (3 * quad + n) * C
            value = total[at : at + C, :].astype(F32)[:, :C]
        else:
            value = jnp.zeros((C, L), F32)
            for m in range(3):
                at = (3 * quad + m) * C
                piece = pltpu.roll(total[at : at + C, :].astype(F32), 32 + 32 * m, 1)
                value = jnp.where(lane // 32 == m, piece, value)
            value = value[:, :C]
        if k < 27:
            subm[k] = value
        else:
            down[k - 27] = value
        if k in (8, 17, 26):
            part = pl.ds(k - 8, 9)
            copies.append(pltpu.make_async_copy(subm.at[part], grad_subm.at[part], sem.at[2 + k // 9]))
            copies[-1].start()
    copies.append(pltpu.make_async_copy(down, grad_down, sem.at[5]))
    copies[-1].start()
    for copy in copies:
        copy.wait()


def run_final(coarse_in, grad_features, total):
    return pl.pallas_call(
        final_kernel,
        out_shape=(
            jax.ShapeDtypeStruct((PEERS, 6 * L), BF16),
            jax.ShapeDtypeStruct((2, C, V), BF16),
            jax.ShapeDtypeStruct((27, C, C), F32),
            jax.ShapeDtypeStruct((8, C, C), F32),
        ),
        in_specs=vmem(3),
        out_specs=tuple(hbm(4)),
        scratch_shapes=[
            pltpu.VMEM((PEERS, 6 * L), BF16),
            pltpu.VMEM((27, C, C), F32),
            pltpu.VMEM((8, C, C), F32),
            pltpu.SemaphoreType.DMA((6,)),
        ],
        compiler_params=pltpu.CompilerParams(vmem_limit_bytes=VMEM_LIMIT),
    )(coarse_in, grad_features, total)


def per_device(features, occupancy, neighbours, live_count, w_subm, w_down, grad_coarse):
    return run_final(
        *run_section(neighbours, live_count, occupancy, features, grad_coarse, w_subm, w_down)
    )


def solution(mesh):
    blocks = P(("rep", "space"), None)
    return jax.shard_map(
        per_device,
        mesh=mesh,
        in_specs=(
            P(("rep", "space"), None, None), blocks, blocks, P(("rep", "space")), P(), P(), blocks,
        ),
        out_specs=(
            blocks, P(("rep", "space"), None, None), P("rep", None, None), P("rep", None, None),
        ),
        check_vma=False,
    )
```

```python
import functools

import jax
import jax.numpy as jnp
from jax import lax
from jax.experimental import pallas as pl
from jax.experimental.pallas import tpu as pltpu
from jax.sharding import PartitionSpec as P

C, L, V = 96, 128, 512
OFFSETS = [(a, b, c) for a in (-1, 0, 1) for b in (-1, 0, 1) for c in (-1, 0, 1)]
PEERS = 64
HALF, YPART, ZPART = 1344, 336, 48
VMEM_LIMIT = 63 * 2**20 + 2**19
F32, BF16 = jnp.float32, jnp.bfloat16
NT = (((1,), (1,)), ((), ()))


def segments(a, b, c):
    span = {-1: [(7, 0)], 0: [(i, i + 1) for i in range(8)], 1: [(0, 9)]}
    xs, ys, zs = span[a], span[b], span[c]
    if c == 0:
        return [(x * 64 + y * 8, 1, tx * 100 + ty * 10 + 1, 1, 8) for x, tx in xs for y, ty in ys]
    z, tz = zs[0]
    if b == 0:
        return [(x * 64 + z, 8, tx * 100 + 10 + tz, 10, 8) for x, tx in xs]
    y, ty = ys[0]
    if a == 0:
        return [(y * 8 + z, 64, 100 + ty * 10 + tz, 100, 8)]
    x, tx = xs[0]
    return [(x * 64 + y * 8 + z, 1, tx * 100 + ty * 10 + tz, 1, 1)]


def rows(start, count, stride):
    return pl.ds(start, count) if stride == 1 else pl.ds(start, count, stride=stride)


def mask_row(words, live, g):
    lane = lax.broadcasted_iota(jnp.int32, (1, V), 1)
    word = jnp.zeros((1, V), jnp.int32)
    for w in range(16):
        word = jnp.where(lane // 32 == w, words[g, w], word)
    bit = jnp.bitwise_and(jnp.right_shift(word, jnp.bitwise_and(lane, 31)), 1)
    return jnp.where(g < live, bit, 0)


def masked_rows(features, words, live, g):
    bit = mask_row(words, live, g)
    values = jnp.where(bit > 0, features[g].astype(F32), 0.0)
    marks = jnp.broadcast_to(bit.astype(F32), (L - C, V))
    return jnp.transpose(jnp.concatenate([values, marks], axis=0)).astype(BF16)


def remote(source, target, sent, arrived, peer):
    return pltpu.make_async_remote_copy(
        src_ref=source, dst_ref=target, send_sem=sent, recv_sem=arrived,
        device_id={"space": peer}, device_id_type=pl.DeviceIdType.MESH,
    )


def greet_all(me):
    barrier = pltpu.get_barrier_semaphore()

    def tell(i, carry):
        pl.semaphore_signal(
            barrier, inc=1, device_id={"space": lax.rem(me + i, PEERS)},
            device_id_type=pl.DeviceIdType.MESH,
        )
        return carry

    lax.fori_loop(1, PEERS, tell, 0)


def greeted():
    pl.semaphore_wait(pltpu.get_barrier_semaphore(), PEERS - 1)


def swap(me, outbox, inbox, sent, arrived):
    def box(i):
        peer = lax.rem(me + i, PEERS)
        return pl.ds(pl.multiple_of(peer * 8, 8), 8), peer

    def start(i, carry):
        at, peer = box(i)
        mine = pl.ds(pl.multiple_of(me * 8, 8), 8)
        remote(outbox.at[at], inbox.at[mine], sent.at[peer], arrived.at[me], peer).start()
        return carry

    def finish(i, carry):
        at, peer = box(i)
        remote(outbox.at[at], inbox.at[at], sent.at[peer], arrived.at[peer], peer).wait()
        return carry

    return (
        lambda: lax.fori_loop(1, PEERS, start, 0),
        lambda: lax.fori_loop(1, PEERS, finish, 0),
    )


def section_kernel(
    table, live_ref, occupancy_ref, features_hbm, cotangent_hbm, w_subm_hbm, w_down_hbm,
    coarse_in, grad_features, total,
    features, cotangent, w_subm, w_down,
    own, lower, upper, outbox, inbox, coarse_box,
    source, pad, cols, wf, wb, wd, perm, spread, pre, dpre3, u, gpad, gsource,
    sums32, sums16, pair_in, chip32, chip16, y_in, y32, y16, z_in,
    part_lower, part_upper, from_lower, from_upper,
    load_sem, box_sent, box_arrived, back_sent, back_arrived, halo_sent, halo_arrived,
    rim_sent, rim_arrived, pair_sent, pair_arrived, ysent, yarrived, zsent, zarrived,
    gzsent, gzarrived, gysent, gyarrived, copy_sent, copy_arrived,
):
    me = lax.axis_index("space")
    y, z, core = me // 16, lax.rem(me // 2, 8), lax.rem(me, 2)
    partner = me + 1 - 2 * core
    has_up, has_down = me < PEERS - 1, me > 0
    loads = [
        pltpu.make_async_copy(hbm, ref, load_sem.at[n])
        for n, (hbm, ref) in enumerate(
            ((features_hbm, features), (cotangent_hbm, cotangent), (w_subm_hbm, w_subm), (w_down_hbm, w_down))
        )
    ]
    for load in loads:
        load.start()
    greet_all(me)

    i = lax.broadcasted_iota(jnp.int32, (V, V), 0)
    v = lax.broadcasted_iota(jnp.int32, (V, V), 1)
    j, t = i // 64, i % 64
    vx, vy, vz = 2 * (t // 16) + j // 4, 2 * (t // 4 % 4) + j // 2 % 2, 2 * (t % 4) + j % 2
    perm[...] = jnp.where(vx * 64 + vy * 8 + vz == v, 1.0, 0.0).astype(BF16)
    spread[...] = jnp.where(
        lax.broadcasted_iota(jnp.int32, (L, 6 * L), 1) // 8
        == lax.broadcasted_iota(jnp.int32, (L, 6 * L), 0),
        1.0, 0.0,
    ).astype(BF16)
    wf[...] = jnp.zeros_like(wf)
    wb[...] = jnp.zeros_like(wb)
    wd[...] = jnp.zeros_like(wd)
    dpre3[...] = jnp.zeros_like(dpre3)
    coarse_box[...] = jnp.zeros_like(coarse_box)
    source[6 * V :, :] = jnp.zeros((V, L), F32)

    loads[0].wait()
    for g in range(2):
        own[g] = masked_rows(features, occupancy_ref, live_ref[0], g)
    loads[1].wait()
    for n in range(6):
        outbox[pl.ds(n, PEERS, stride=8), :] = cotangent[:, n * L : (n + 1) * L].astype(F32)
    counts = jnp.broadcast_to(live_ref[0].astype(F32), (PEERS, L))
    for n in (6, 7):
        outbox[pl.ds(n, PEERS, stride=8), :] = counts

    greeted()
    up = remote(own, lower, halo_sent.at[0], halo_arrived.at[0], lax.min(me + 1, PEERS - 1))
    down = remote(own, upper, halo_sent.at[1], halo_arrived.at[1], lax.max(me - 1, 0))

    @pl.when(has_up)
    def _():
        up.start()

    @pl.when(has_down)
    def _():
        down.start()

    box_start, box_finish = swap(me, outbox, inbox, box_sent, box_arrived)
    box_start()
    mine = pl.ds(pl.multiple_of(me * 8, 8), 8)
    inbox[mine, :] = outbox[mine, :]

    loads[2].wait()
    loads[3].wait()
    for k in range(27):
        a, bc = divmod(k, 9)
        w = w_subm[k]
        wf[k * L : k * L + C, :C] = w
        wb[bc * L : bc * L + C, a * L : a * L + C] = w
    for j in range(8):
        wd[j * L : j * L + C, :C] = w_down[j]

    for g in range(2):
        source[(2 + g) * V : (3 + g) * V, :] = own[g].astype(F32)

    @pl.when(has_down)
    def _():
        up.wait_recv()

    @pl.when(jnp.logical_not(has_down))
    def _():
        lower[...] = jnp.zeros_like(lower)

    @pl.when(has_up)
    def _():
        down.wait_recv()

    @pl.when(jnp.logical_not(has_up))
    def _():
        upper[...] = jnp.zeros_like(upper)

    for g in range(2):
        source[g * V : (g + 1) * V, :] = lower[g].astype(F32)
        source[(4 + g) * V : (5 + g) * V, :] = upper[g].astype(F32)

    for g in range(2):
        for k, offset in enumerate(OFFSETS):
            base = (2 + g) * V if k == 13 else table[g, k] * V
            for s0, ss, p0, ps, count in segments(*offset):
                pad[rows(g * 1000 + p0, count, ps), :] = source[rows(base + s0, count, ss), :]

    def columns(gx, carry):
        for b in range(3):
            for c in range(3):
                piece = jnp.concatenate(
                    [pad[pl.ds(gx * 100 + (yy + b) * 10 + c, 8), :] for yy in range(8)], axis=0
                )
                bc = 3 * b + c
                cols[pl.ds(pl.multiple_of(gx * 64, 64), 64), bc * L : (bc + 1) * L] = piece.astype(BF16)
        return carry

    lax.fori_loop(0, 20, columns, 0)

    for g in range(2):
        acc = jnp.zeros((V, L), F32)
        for a in range(3):
            acc += jnp.dot(
                cols[g * 640 + a * 64 : g * 640 + a * 64 + V, :],
                wf[a * 9 * L : (a + 1) * 9 * L, :],
                preferred_element_type=F32,
            )
        pre[g * V : (g + 1) * V, :] = acc

    pick = (
        lax.broadcasted_iota(jnp.int32, (64, 6 * L), 1) % 8
        == lax.broadcasted_iota(jnp.int32, (64, 6 * L), 0) % 8
    )
    peer = lax.broadcasted_iota(jnp.int32, (64, 64), 1)
    piece = lax.broadcasted_iota(jnp.int32, (64, 64), 0) // 8
    live = live_ref[0]
    s, q = 0.7978845608028654, 0.044715
    down_sums = jnp.zeros((L, 8 * L), F32)
    dealt = jnp.zeros((PEERS, 6 * L), F32)
    halves = []
    for g in range(2):
        mask = jnp.broadcast_to(own[g, :, C : C + 1].astype(F32), (V, L))
        tt = pre[g * V : (g + 1) * V, :]
        th = jnp.tanh(s * (tt + q * tt * tt * tt))
        hidden = (0.5 * tt * (1.0 + th) * mask).astype(BF16)
        slope = (0.5 * (1.0 + th) + 0.5 * tt * (1.0 - th * th) * (s * (1.0 + 3.0 * q * tt * tt))) * mask
        both = jnp.dot(
            perm[...], jnp.concatenate([hidden, mask.astype(BF16)], axis=1),
            preferred_element_type=F32,
        )
        kids = both[:, :L].astype(BF16)
        cmask = both[:64, L:]
        coarse = jnp.dot(kids[:64], wd[:L, :], preferred_element_type=F32)
        for j in range(1, 8):
            cmask = jnp.maximum(cmask, both[j * 64 : (j + 1) * 64, L:])
            coarse += jnp.dot(
                kids[j * 64 : (j + 1) * 64], wd[j * L : (j + 1) * L, :], preferred_element_type=F32
            )
        coarse = (coarse * cmask).astype(BF16)
        flat = jnp.dot(coarse, spread[...], preferred_element_type=F32)
        halves.append((slope, kids, cmask, jnp.where(pick, flat, 0.0).astype(BF16)))

    box_finish()
    boxes = jnp.concatenate(
        [inbox[pl.ds(n, PEERS, stride=8), :] for n in range(6)], axis=1
    ).astype(BF16)
    below = jnp.where(
        lax.broadcasted_iota(jnp.int32, (PEERS, L), 0) < me, inbox[pl.ds(6, PEERS, stride=8), :], 0.0
    )
    first = jnp.sum(below, axis=0, keepdims=True).astype(jnp.int32)[:, :64]
    for g in range(2):
        slope, kids, cmask, flat = halves[g]
        holder = jnp.bitwise_and(jnp.broadcast_to(first, (64, 64)) + g, 7) * 8 + piece
        chosen = jnp.where((holder == peer) & (g < live), 1.0, 0.0).astype(BF16)
        dealt += lax.dot_general(chosen, flat, (((0,), (0,)), ((), ())), preferred_element_type=F32)
        dz = jnp.dot(chosen, boxes, preferred_element_type=F32)
        dz = jnp.where(pick, dz, 0.0).astype(BF16)
        dz = lax.dot_general(dz, spread[...], NT, preferred_element_type=F32)
        dz = jnp.where(cmask > 0, dz, 0.0)
        dzt = jnp.transpose(dz).astype(BF16)
        dz = dz.astype(BF16)
        down_sums += jnp.dot(
            dzt, jnp.concatenate([kids[j * 64 : (j + 1) * 64] for j in range(8)], axis=1),
            preferred_element_type=F32,
        )
        dh = jnp.concatenate(
            [
                lax.dot_general(dz, wd[j * L : (j + 1) * L, :], NT, preferred_element_type=F32)
                for j in range(8)
            ],
            axis=0,
        )
        high = dh.astype(BF16)
        low = (dh - high.astype(F32)).astype(BF16)
        dh = lax.dot_general(
            perm[...], jnp.concatenate([high, low], axis=1), (((0,), (0,)), ((), ())),
            preferred_element_type=F32,
        )
        dpre = slope * (dh[:, :L] + dh[:, L:])
        dpre16 = dpre.astype(BF16)
        for a in range(3):
            dpre3[g * 640 + a * 64 : g * 640 + a * 64 + V, a * L : (a + 1) * L] = dpre16
        pre[g * V : (g + 1) * V, :] = dpre
    for n in range(6):
        coarse_box[pl.ds(n, PEERS, stride=8), :] = dealt[:, n * L : (n + 1) * L]

    lane = lax.broadcasted_iota(jnp.int32, (C, L), 1)
    held = {}

    def keep(k, product):
        held[k % 4] = jnp.transpose(product)[:C]
        if k % 4 == 3 or k == 34:
            last = held.get(3)
            for n in range(3):
                slab = held[n]
                if last is not None:
                    slab = jnp.where(lane < C, slab, pltpu.roll(last, C - 32 * n, 1))
                at = (3 * (k // 4) + n) * C
                sums32[at : at + C, :] = slab
                sums16[at : at + C, :] = slab.astype(BF16)
            held.clear()

    dt = jnp.transpose(pre[...]).astype(BF16)
    for a in range(3):
        for bc in range(0, 9, 2):
            lanes = slice(bc * L, min(bc + 2, 9) * L)
            value = jnp.dot(
                dt[:, :V], cols[a * 64 : a * 64 + V, lanes], preferred_element_type=F32
            ) + jnp.dot(
                dt[:, V:], cols[640 + a * 64 : 640 + a * 64 + V, lanes], preferred_element_type=F32
            )
            for n in range(min(2, 9 - bc)):
                keep(a * 9 + bc + n, value[:, n * L : (n + 1) * L])
    for j in range(8):
        keep(27 + j, down_sums[:, j * L : (j + 1) * L])
    sums32[27 * C :, :] = jnp.zeros((C, L), F32)
    sums16[27 * C :, :] = jnp.zeros((C, L), BF16)

    def span(at, count):
        return pl.ds(pl.multiple_of(at, 16), count)

    def device(yy, zz):
        return yy * 16 + zz * 2 + core

    pair = remote(sums16.at[span((1 - core) * HALF, HALF)], pair_in, pair_sent, pair_arrived, partner)
    pair.start()
    pair.wait_recv()
    value = sums32[span(core * HALF, HALF), :] + pair_in[...].astype(F32)
    chip32[...] = value
    chip16[...] = value.astype(BF16)
    ysteps = []
    for n in range(3):
        yy = jnp.bitwise_and(y + n + 1, 3)
        ysteps.append(
            remote(chip16.at[span(yy * YPART, YPART)], y_in.at[n], ysent.at[n], yarrived.at[n], device(yy, z))
        )
        ysteps[n].start()

    gpad[...] = jnp.zeros_like(gpad)
    for bc in range(0, 9, 2):
        width = min(2, 9 - bc)
        u[:, : width * L] = lax.dot_general(
            dpre3[...], wb[bc * L : (bc + width) * L, :], NT, preferred_element_type=F32
        )

        def add(gx, carry):
            for n in range(width):
                b, c = divmod(bc + n, 3)
                for yy in range(8):
                    at = pl.ds(gx * 100 + (yy + b) * 10 + c, 8)
                    gpad[at, :] += u[pl.ds(pl.multiple_of(gx * 64 + yy * 8, 8), 8), n * L : (n + 1) * L]
            return carry

        lax.fori_loop(0, 20, add, 0)

    value = chip32[span(y * YPART, YPART), :]
    for n in range(3):
        ysteps[n].wait_recv()
        value = value + y_in[n].astype(F32)
    y32[...] = value
    y16[...] = value.astype(BF16)

    def zstep(n):
        zz = jnp.bitwise_and(z + n + 1, 7)
        at = span(lax.min(zz, 6) * ZPART, ZPART)
        return zz < 7, remote(y16.at[at], z_in.at[n], zsent.at[n], zarrived.at[n], device(y, zz))

    for n in range(7):
        wanted, copy = zstep(n)

        @pl.when(wanted)
        def _():
            copy.start()

    back_start, back_finish = swap(me, coarse_box, coarse_in, back_sent, back_arrived)
    back_start()
    coarse_in[mine, :] = coarse_box[mine, :]

    gsource[...] = jnp.zeros_like(gsource)
    for g in range(2):
        for s0, ss, p0, ps, count in segments(0, 0, 0):
            gsource[rows((2 + g) * V + s0, count, ss), :] = gpad[rows(g * 1000 + p0, count, ps), :]

    def give(n, carry):
        for g in range(2):
            for k, offset in enumerate(OFFSETS):
                if k != 13:
                    here = jnp.where(table[g, k] == n, 1.0, 0.0)
                    for s0, ss, p0, ps, count in segments(*offset):
                        at = rows(n * V + s0, count, ss)
                        gsource[at, :] += gpad[rows(g * 1000 + p0, count, ps), :] * here
        return carry

    lax.fori_loop(0, 6, give, 0)
    for g in range(2):
        part_lower[g] = gsource[g * V : (g + 1) * V, :].astype(BF16)
        part_upper[g] = gsource[(4 + g) * V : (5 + g) * V, :].astype(BF16)
    rim_up = remote(part_upper, from_lower, rim_sent.at[0], rim_arrived.at[0], lax.min(me + 1, PEERS - 1))
    rim_down = remote(part_lower, from_upper, rim_sent.at[1], rim_arrived.at[1], lax.max(me - 1, 0))

    @pl.when(has_up)
    def _():
        rim_up.start()

    @pl.when(has_down)
    def _():
        rim_down.start()

    def gzstep(n, owner, to):
        at = span(core * HALF + y * YPART + owner * ZPART, ZPART)
        return remote(total.at[at], total.at[at], gzsent.at[n], gzarrived.at[n], device(y, to))

    @pl.when(z < 7)
    def _():
        value = y32[span(z * ZPART, ZPART), :]
        for n in range(7):
            zstep(n)[1].wait_recv()
            value = value + z_in[n].astype(F32)
        total[span(core * HALF + y * YPART + z * ZPART, ZPART), :] = value.astype(BF16)
        for n in range(7):
            gzstep(n, z, jnp.bitwise_and(z + n + 1, 7)).start()

    for n in range(7):
        owner = jnp.bitwise_and(z + 7 - n, 7)

        @pl.when(owner < 7)
        def _():
            gzstep(n, lax.min(owner, 6), owner).wait_recv()

    def gystep(n, owner, to):
        at = span(core * HALF + owner * YPART, YPART)
        return remote(total.at[at], total.at[at], gysent.at[n], gyarrived.at[n], device(to, z))

    def across(n, which, owner):
        at = span(which * HALF + owner * YPART, YPART)
        return remote(total.at[at], total.at[at], copy_sent.at[n], copy_arrived.at[n], partner)

    owners = [jnp.bitwise_and(y + 4 - n, 3) for n in range(4)]
    for n in range(3):
        gystep(n, y, jnp.bitwise_and(y + n + 1, 3)).start()
    across(0, core, y).start()

    @pl.when(has_down)
    def _():
        rim_up.wait_recv()

    @pl.when(jnp.logical_not(has_down))
    def _():
        from_lower[...] = jnp.zeros_like(from_lower)

    @pl.when(has_up)
    def _():
        rim_down.wait_recv()

    @pl.when(jnp.logical_not(has_up))
    def _():
        from_upper[...] = jnp.zeros_like(from_upper)

    for g in range(2):
        value = gsource[(2 + g) * V : (3 + g) * V, :] + from_lower[g].astype(F32) + from_upper[g].astype(F32)
        value = value * jnp.broadcast_to(own[g, :, C : C + 1].astype(F32), (V, L))
        grad_features[g] = jnp.transpose(value)[:C, :].astype(BF16)

    for n in range(3):
        gystep(n, owners[n + 1], owners[n + 1]).wait_recv()
        across(n + 1, core, owners[n + 1]).start()
    back_finish()
    for n in range(4):
        across(n, 1 - core, owners[n]).wait_recv()

    @pl.when(has_up)
    def _():
        up.wait_send()
        rim_up.wait_send()

    @pl.when(has_down)
    def _():
        down.wait_send()
        rim_down.wait_send()

    pair.wait_send()
    for n in range(3):
        ysteps[n].wait_send()
        gystep(n, y, jnp.bitwise_and(y + n + 1, 3)).wait_send()
    for n in range(7):
        wanted, copy = zstep(n)

        @pl.when(wanted)
        def _():
            copy.wait_send()

    @pl.when(z < 7)
    def _():
        for n in range(7):
            gzstep(n, z, jnp.bitwise_and(z + n + 1, 7)).wait_send()

    for n in range(4):
        across(n, core, owners[n]).wait_send()


def smem():
    return pl.BlockSpec(memory_space=pltpu.SMEM)


def vmem(n):
    return [pl.BlockSpec(memory_space=pltpu.VMEM)] * n


def hbm(n):
    return [pl.BlockSpec(memory_space=pltpu.HBM)] * n


def run_section(neighbours, live_count, occupancy, features, grad_coarse, w_subm, w_down):
    dma = pltpu.SemaphoreType.DMA
    block = pltpu.VMEM((2, V, L), BF16)
    boxes = pltpu.VMEM((8 * PEERS, L), F32)
    return pl.pallas_call(
        section_kernel,
        out_shape=(
            jax.ShapeDtypeStruct((8 * PEERS, L), F32),
            jax.ShapeDtypeStruct((2, C, V), BF16),
            jax.ShapeDtypeStruct((2 * HALF, L), BF16),
        ),
        in_specs=[smem(), smem(), smem()] + hbm(4),
        out_specs=tuple(vmem(3)),
        scratch_shapes=[
            pltpu.VMEM((2, C, V), BF16),
            pltpu.VMEM((PEERS, 6 * L), BF16),
            pltpu.VMEM((27, C, C), BF16),
            pltpu.VMEM((8, C, C), BF16),
            block, block, block, boxes, boxes, boxes,
            pltpu.VMEM((7 * V, L), F32),
            pltpu.VMEM((2000, L), F32),
            pltpu.VMEM((1280, 9 * L), BF16),
            pltpu.VMEM((27 * L, L), BF16),
            pltpu.VMEM((9 * L, 3 * L), BF16),
            pltpu.VMEM((8 * L, L), BF16),
            pltpu.VMEM((V, V), BF16),
            pltpu.VMEM((L, 6 * L), BF16),
            pltpu.VMEM((2 * V, L), F32),
            pltpu.VMEM((1280, 3 * L), BF16),
            pltpu.VMEM((1280, 2 * L), F32),
            pltpu.VMEM((2000, L), F32),
            pltpu.VMEM((6 * V, L), F32),
            pltpu.VMEM((2 * HALF, L), F32),
            pltpu.VMEM((2 * HALF, L), BF16),
            pltpu.VMEM((HALF, L), BF16),
            pltpu.VMEM((HALF, L), F32),
            pltpu.VMEM((HALF, L), BF16),
            pltpu.VMEM((3, YPART, L), BF16),
            pltpu.VMEM((YPART, L), F32),
            pltpu.VMEM((YPART, L), BF16),
            pltpu.VMEM((7, ZPART, L), BF16),
            block, block, block, block,
            dma((4,)), dma((PEERS,)), dma((PEERS,)), dma((PEERS,)), dma((PEERS,)),
            dma((2,)), dma((2,)), dma((2,)), dma((2,)), dma(()), dma(()),
            dma((3,)), dma((3,)), dma((7,)), dma((7,)), dma((7,)), dma((7,)),
            dma((3,)), dma((3,)), dma((4,)), dma((4,)),
        ],
        compiler_params=pltpu.CompilerParams(
            vmem_limit_bytes=VMEM_LIMIT, collective_id=0, has_side_effects=True
        ),
    )(neighbours, live_count, occupancy, features, grad_coarse, w_subm, w_down)


def final_kernel(
    coarse_in, features_in, total, coarse_out, grad_features, grad_subm, grad_down,
    coarse, subm, down, sem,
):
    copies = [pltpu.make_async_copy(features_in, grad_features, sem.at[0])]
    copies[0].start()
    for n in range(6):
        coarse[:, n * L : (n + 1) * L] = coarse_in[pl.ds(n, PEERS, stride=8), :].astype(BF16)
    copies.append(pltpu.make_async_copy(coarse, coarse_out, sem.at[1]))
    copies[1].start()
    lane = lax.broadcasted_iota(jnp.int32, (C, L), 1)
    for k in range(35):
        quad, n = divmod(k, 4)
        if n < 3:
            at = (3 * quad + n) * C
            value = total[at : at + C, :].astype(F32)[:, :C]
        else:
            value = jnp.zeros((C, L), F32)
            for m in range(3):
                at = (3 * quad + m) * C
                piece = pltpu.roll(total[at : at + C, :].astype(F32), 32 + 32 * m, 1)
                value = jnp.where(lane // 32 == m, piece, value)
            value = value[:, :C]
        if k < 27:
            subm[k] = value
        else:
            down[k - 27] = value
        if k in (8, 17, 26):
            part = pl.ds(k - 8, 9)
            copies.append(pltpu.make_async_copy(subm.at[part], grad_subm.at[part], sem.at[2 + k // 9]))
            copies[-1].start()
    copies.append(pltpu.make_async_copy(down, grad_down, sem.at[5]))
    copies[-1].start()
    for copy in copies:
        copy.wait()


def run_final(coarse_in, grad_features, total):
    return pl.pallas_call(
        final_kernel,
        out_shape=(
            jax.ShapeDtypeStruct((PEERS, 6 * L), BF16),
            jax.ShapeDtypeStruct((2, C, V), BF16),
            jax.ShapeDtypeStruct((27, C, C), F32),
            jax.ShapeDtypeStruct((8, C, C), F32),
        ),
        in_specs=vmem(3),
        out_specs=tuple(hbm(4)),
        scratch_shapes=[
            pltpu.VMEM((PEERS, 6 * L), BF16),
            pltpu.VMEM((27, C, C), F32),
            pltpu.VMEM((8, C, C), F32),
            pltpu.SemaphoreType.DMA((6,)),
        ],
        compiler_params=pltpu.CompilerParams(vmem_limit_bytes=VMEM_LIMIT),
    )(coarse_in, grad_features, total)


def per_device(features, occupancy, neighbours, live_count, w_subm, w_down, grad_coarse):
    return run_final(
        *run_section(neighbours, live_count, occupancy, features, grad_coarse, w_subm, w_down)
    )


def solution(mesh):
    blocks = P(("rep", "space"), None)
    return jax.shard_map(
        per_device,
        mesh=mesh,
        in_specs=(
            P(("rep", "space"), None, None), blocks, blocks, P(("rep", "space")), P(), P(), blocks,
        ),
        out_specs=(
            blocks, P(("rep", "space"), None, None), P("rep", None, None), P("rep", None, None),
        ),
        check_vma=False,
    )
```

```python
import functools

import jax
import jax.numpy as jnp
from jax import lax
from jax.experimental import pallas as pl
from jax.experimental.pallas import tpu as pltpu
from jax.sharding import PartitionSpec as P

C, L, V = 96, 128, 512
OFFSETS = [(a, b, c) for a in (-1, 0, 1) for b in (-1, 0, 1) for c in (-1, 0, 1)]
PEERS, CHIPS = 64, 32
HALF, YPART, ZPART = 1344, 336, 48
VMEM_LIMIT = 63 * 2**20 + 2**19
F32, BF16 = jnp.float32, jnp.bfloat16
NT = (((1,), (1,)), ((), ()))


def segments(a, b, c):
    span = {-1: [(7, 0)], 0: [(i, i + 1) for i in range(8)], 1: [(0, 9)]}
    xs, ys, zs = span[a], span[b], span[c]
    if c == 0:
        return [(x * 64 + y * 8, 1, tx * 100 + ty * 10 + 1, 1, 8) for x, tx in xs for y, ty in ys]
    z, tz = zs[0]
    if b == 0:
        return [(x * 64 + z, 8, tx * 100 + 10 + tz, 10, 8) for x, tx in xs]
    y, ty = ys[0]
    if a == 0:
        return [(y * 8 + z, 64, 100 + ty * 10 + tz, 100, 8)]
    x, tx = xs[0]
    return [(x * 64 + y * 8 + z, 1, tx * 100 + ty * 10 + tz, 1, 1)]


def rows(start, count, stride):
    return pl.ds(start, count) if stride == 1 else pl.ds(start, count, stride=stride)


def mask_row(words, live, g):
    lane = lax.broadcasted_iota(jnp.int32, (1, V), 1)
    word = jnp.zeros((1, V), jnp.int32)
    for w in range(16):
        word = jnp.where(lane // 32 == w, words[g, w], word)
    bit = jnp.bitwise_and(jnp.right_shift(word, jnp.bitwise_and(lane, 31)), 1)
    return jnp.where(g < live, bit, 0)


def masked_rows(features, words, live, g):
    bit = mask_row(words, live, g)
    values = jnp.where(bit > 0, features[g].astype(F32), 0.0)
    marks = jnp.broadcast_to(bit.astype(F32), (L - C, V))
    return jnp.transpose(jnp.concatenate([values, marks], axis=0)).astype(BF16)


def remote(source, target, sent, arrived, peer):
    return pltpu.make_async_remote_copy(
        src_ref=source, dst_ref=target, send_sem=sent, recv_sem=arrived,
        device_id={"space": peer}, device_id_type=pl.DeviceIdType.MESH,
    )


def greet(me):
    barrier = pltpu.get_barrier_semaphore()
    here, core = me // 2, lax.rem(me, 2)

    def tell(peer):
        pl.semaphore_signal(
            barrier, inc=1, device_id={"space": peer}, device_id_type=pl.DeviceIdType.MESH
        )

    tell(lax.rem(me + 2 * core - 1 + PEERS, PEERS))
    tell(me + 1 - 2 * core)

    def tell_chip(i, carry):
        tell(jnp.bitwise_and(here + i, CHIPS - 1) * 2 + core)
        return carry

    lax.fori_loop(1, CHIPS, tell_chip, 0)


def greeted():
    pl.semaphore_wait(pltpu.get_barrier_semaphore(), CHIPS + 1)


class Deal:
    def __init__(self, me, outbox, near, far, sent, arrived, far_sent, far_arrived):
        self.here, self.core = me // 2, lax.rem(me, 2)
        self.outbox, self.near = outbox, near
        self.sems = sent, arrived
        self.across = remote(near, far, far_sent, far_arrived, me + 1 - 2 * self.core)
        every = pl.ds(0, 16 * (CHIPS - 1))
        self.every = remote(outbox.at[every], near.at[every], sent, arrived, me + 1 - 2 * self.core)

    def tile(self, chip):
        return pl.ds(pl.multiple_of(chip * 16, 16), 16)

    def start(self):
        def send(i, carry):
            there = jnp.bitwise_and(self.here + i, CHIPS - 1)
            remote(
                self.outbox.at[self.tile(there)], self.near.at[self.tile(self.here)],
                *self.sems, there * 2 + self.core,
            ).start()
            return carry

        lax.fori_loop(1, CHIPS, send, 0)
        self.near[self.tile(self.here), :] = self.outbox[self.tile(self.here), :]

    def forward(self):
        self.every.wait_recv()
        self.across.start()

    def finish(self):
        self.across.wait_recv()

    def close(self):
        self.every.wait_send()
        self.across.wait_send()


def box_rows(core, n):
    return pl.ds(core * 8 + n, CHIPS, stride=16)


def section_kernel(
    table, live_ref, occupancy_ref, features_hbm, cotangent_hbm, w_subm_hbm, w_down_hbm,
    coarse_out, grad_features, total,
    features, cotangent, w_subm, w_down,
    own, lower, upper, box32, near32, far32, out32, outbox, near, far, back, back_near, back_far,
    source, pad, cols, wf, wb, wd, perm, permt, spread, pre, dpre3, u, gpad, gsource,
    sums32, sums16, pair_in, chip32, chip16, y_in, y32, y16, z_in,
    part_lower, part_upper, from_lower, from_upper,
    load_sem, box_sem, back_sem, halo_sent, halo_arrived,
    rim_sent, rim_arrived, pair_sent, pair_arrived, ysent, yarrived, zsent, zarrived,
    gzsent, gzarrived, gysent, gyarrived, copy_sent, copy_arrived,
):
    me = lax.axis_index("space")
    y, z, core = me // 16, lax.rem(me // 2, 8), lax.rem(me, 2)
    partner = me + 1 - 2 * core
    has_up, has_down = me < PEERS - 1, me > 0
    loads = [
        pltpu.make_async_copy(hbm, ref, load_sem.at[n])
        for n, (hbm, ref) in enumerate(
            ((features_hbm, features), (cotangent_hbm, cotangent), (w_subm_hbm, w_subm), (w_down_hbm, w_down))
        )
    ]
    for load in loads:
        load.start()
    greet(me)

    i = lax.broadcasted_iota(jnp.int32, (V, V), 0)
    v = lax.broadcasted_iota(jnp.int32, (V, V), 1)

    def placed(index, parts):
        return sum(((index >> a) & b) << c for a, b, c in parts)

    to_voxel = ((8, 1, 6), (7, 1, 3), (6, 1, 0), (4, 3, 7), (2, 3, 4), (0, 3, 1))
    to_child = tuple((c, b, a) for a, b, c in to_voxel)
    perm[...] = jnp.where(placed(i[:, :1], to_voxel) == v, 1.0, 0.0).astype(BF16)
    permt[...] = jnp.where(placed(i[:, :1], to_child) == v, 1.0, 0.0).astype(BF16)
    spread[...] = jnp.where(
        lax.broadcasted_iota(jnp.int32, (L, 6 * L), 1) // 8
        == lax.broadcasted_iota(jnp.int32, (L, 6 * L), 0),
        1.0, 0.0,
    ).astype(BF16)
    wf[...] = jnp.zeros_like(wf)
    wb[...] = jnp.zeros_like(wb)
    wd[...] = jnp.zeros_like(wd)
    dpre3[...] = jnp.zeros_like(dpre3)
    source[6 * V :, :] = jnp.zeros((V, L), F32)

    loads[0].wait()
    for g in range(2):
        own[g] = masked_rows(features, occupancy_ref, live_ref[0], g)
    loads[1].wait()
    for n in range(6):
        box32[pl.ds(n, PEERS, stride=8), :] = cotangent[:, n * L : (n + 1) * L].astype(F32)
    counts = jnp.broadcast_to(live_ref[0].astype(F32), (PEERS, L))
    for n in (6, 7):
        box32[pl.ds(n, PEERS, stride=8), :] = counts
    outbox[...] = box32[...].astype(BF16)

    greeted()
    up = remote(own, lower, halo_sent.at[0], halo_arrived.at[0], lax.min(me + 1, PEERS - 1))
    down = remote(own, upper, halo_sent.at[1], halo_arrived.at[1], lax.max(me - 1, 0))

    @pl.when(has_up)
    def _():
        up.start()

    @pl.when(has_down)
    def _():
        down.start()

    deal = Deal(me, outbox, near, far, *(box_sem.at[n] for n in range(4)))
    deal.start()

    loads[2].wait()
    loads[3].wait()
    for k in range(27):
        a, bc = divmod(k, 9)
        w = w_subm[k]
        wf[k * L : k * L + C, :C] = w
        wb[bc * L : bc * L + C, a * L : a * L + C] = w
    for j in range(8):
        wd[j * L : j * L + C, :C] = w_down[j]

    for g in range(2):
        source[(2 + g) * V : (3 + g) * V, :] = own[g].astype(F32)

    @pl.when(has_down)
    def _():
        up.wait_recv()

    @pl.when(jnp.logical_not(has_down))
    def _():
        lower[...] = jnp.zeros_like(lower)

    @pl.when(has_up)
    def _():
        down.wait_recv()

    @pl.when(jnp.logical_not(has_up))
    def _():
        upper[...] = jnp.zeros_like(upper)

    for g in range(2):
        source[g * V : (g + 1) * V, :] = lower[g].astype(F32)
        source[(4 + g) * V : (5 + g) * V, :] = upper[g].astype(F32)

    for g in range(2):
        for k, offset in enumerate(OFFSETS):
            base = (2 + g) * V if k == 13 else table[g, k] * V
            for s0, ss, p0, ps, count in segments(*offset):
                pad[rows(g * 1000 + p0, count, ps), :] = source[rows(base + s0, count, ss), :]

    def columns(gx, carry):
        for b in range(3):
            for c in range(3):
                piece = jnp.concatenate(
                    [pad[pl.ds(gx * 100 + (yy + b) * 10 + c, 8), :] for yy in range(8)], axis=0
                )
                bc = 3 * b + c
                cols[pl.ds(pl.multiple_of(gx * 64, 64), 64), bc * L : (bc + 1) * L] = piece.astype(BF16)
        return carry

    lax.fori_loop(0, 20, columns, 0)
    deal.forward()

    for g in range(2):
        acc = jnp.zeros((V, L), F32)
        for a in range(3):
            acc += jnp.dot(
                cols[g * 640 + a * 64 : g * 640 + a * 64 + V, :],
                wf[a * 9 * L : (a + 1) * 9 * L, :],
                preferred_element_type=F32,
            )
        pre[g * V : (g + 1) * V, :] = acc

    pick = (
        lax.broadcasted_iota(jnp.int32, (64, 6 * L), 1) % 8
        == lax.broadcasted_iota(jnp.int32, (64, 6 * L), 0) % 8
    )
    piece = lax.broadcasted_iota(jnp.int32, (64, 64), 0) // 8
    live = live_ref[0]
    s, q = 0.7978845608028654, 0.044715
    down_sums = jnp.zeros((L, 8 * L), F32)
    dealt = jnp.zeros((PEERS, 6 * L), F32)
    halves = []
    for g in range(2):
        mask = jnp.broadcast_to(own[g, :, C : C + 1].astype(F32), (V, L))
        tt = pre[g * V : (g + 1) * V, :]
        th = jnp.tanh(s * (tt + q * tt * tt * tt))
        hidden = (0.5 * tt * (1.0 + th) * mask).astype(BF16)
        slope = (0.5 * (1.0 + th) + 0.5 * tt * (1.0 - th * th) * (s * (1.0 + 3.0 * q * tt * tt))) * mask
        both = jnp.dot(
            perm[...], jnp.concatenate([hidden, mask.astype(BF16)], axis=1),
            preferred_element_type=F32,
        )
        kids = both[:, :L].astype(BF16)
        cmask = both[:64, L:]
        coarse = jnp.dot(kids[:64], wd[:L, :], preferred_element_type=F32)
        for j in range(1, 8):
            cmask = jnp.maximum(cmask, both[j * 64 : (j + 1) * 64, L:])
            coarse += jnp.dot(
                kids[j * 64 : (j + 1) * 64], wd[j * L : (j + 1) * L, :], preferred_element_type=F32
            )
        coarse = (coarse * cmask).astype(BF16)
        flat = jnp.dot(coarse, spread[...], preferred_element_type=F32)
        halves.append((slope, kids, cmask, jnp.where(pick, flat, 0.0).astype(BF16)))

    deal.finish()
    near32[...] = near[...].astype(F32)
    far32[...] = far[...].astype(F32)

    def lines(n):
        return jnp.concatenate([near32[box_rows(core, n), :], far32[box_rows(core, n), :]], axis=0)

    def peers(dim, shape):
        order = lax.broadcasted_iota(jnp.int32, shape, dim)
        return jnp.where(order < CHIPS, 2 * order + core, 2 * (order - CHIPS) + 1 - core)

    boxes = jnp.concatenate([lines(n) for n in range(6)], axis=1).astype(BF16)
    below = jnp.where(peers(0, (PEERS, L)) < me, lines(6), 0.0)
    first = jnp.sum(below, axis=0, keepdims=True).astype(jnp.int32)[:, :64]
    for g in range(2):
        slope, kids, cmask, flat = halves[g]
        holder = jnp.bitwise_and(jnp.broadcast_to(first, (64, 64)) + g, 7) * 8 + piece
        chosen = jnp.where((holder == peers(1, (64, 64))) & (g < live), 1.0, 0.0).astype(BF16)
        dealt += lax.dot_general(chosen, flat, (((0,), (0,)), ((), ())), preferred_element_type=F32)
        dz = jnp.dot(chosen, boxes, preferred_element_type=F32)
        dz = jnp.where(pick, dz, 0.0).astype(BF16)
        dz = lax.dot_general(dz, spread[...], NT, preferred_element_type=F32)
        dz = jnp.where(cmask > 0, dz, 0.0)
        dzt = jnp.transpose(dz).astype(BF16)
        dz = dz.astype(BF16)
        down_sums += jnp.dot(
            dzt, jnp.concatenate([kids[j * 64 : (j + 1) * 64] for j in range(8)], axis=1),
            preferred_element_type=F32,
        )
        dh = jnp.concatenate(
            [
                lax.dot_general(dz, wd[j * L : (j + 1) * L, :], NT, preferred_element_type=F32)
                for j in range(8)
            ],
            axis=0,
        )
        high = dh.astype(BF16)
        low = (dh - high.astype(F32)).astype(BF16)
        dh = lax.dot_general(
            permt[...], jnp.concatenate([high, low], axis=1), (((1,), (0,)), ((), ())),
            preferred_element_type=F32,
        )
        dpre = slope * (dh[:, :L] + dh[:, L:])
        dpre16 = dpre.astype(BF16)
        for a in range(3):
            dpre3[g * 640 + a * 64 : g * 640 + a * 64 + V, a * L : (a + 1) * L] = dpre16
        pre[g * V : (g + 1) * V, :] = dpre
    for n in range(6):
        box32[box_rows(core, n), :] = dealt[:CHIPS, n * L : (n + 1) * L]
        box32[box_rows(1 - core, n), :] = dealt[CHIPS:, n * L : (n + 1) * L]
    back[...] = box32[...].astype(BF16)

    lane = lax.broadcasted_iota(jnp.int32, (C, L), 1)
    held = {}

    def keep(k, product):
        held[k % 4] = jnp.transpose(product)[:C]
        if k % 4 == 3 or k == 34:
            last = held.get(3)
            for n in range(3):
                slab = held[n]
                if last is not None:
                    slab = jnp.where(lane < C, slab, pltpu.roll(last, C - 32 * n, 1))
                at = (3 * (k // 4) + n) * C
                sums32[at : at + C, :] = slab
                sums16[at : at + C, :] = slab.astype(BF16)
            held.clear()

    dt = jnp.transpose(pre[...]).astype(BF16)
    for a in range(3):
        for bc in range(0, 9, 2):
            lanes = slice(bc * L, min(bc + 2, 9) * L)
            value = jnp.dot(
                dt[:, :V], cols[a * 64 : a * 64 + V, lanes], preferred_element_type=F32
            ) + jnp.dot(
                dt[:, V:], cols[640 + a * 64 : 640 + a * 64 + V, lanes], preferred_element_type=F32
            )
            for n in range(min(2, 9 - bc)):
                keep(a * 9 + bc + n, value[:, n * L : (n + 1) * L])
    for j in range(8):
        keep(27 + j, down_sums[:, j * L : (j + 1) * L])
    sums32[27 * C :, :] = jnp.zeros((C, L), F32)
    sums16[27 * C :, :] = jnp.zeros((C, L), BF16)

    def span(at, count):
        return pl.ds(pl.multiple_of(at, 16), count)

    def device(yy, zz):
        return yy * 16 + zz * 2 + core

    pair = remote(sums16.at[span((1 - core) * HALF, HALF)], pair_in, pair_sent, pair_arrived, partner)
    pair.start()
    pair.wait_recv()
    value = sums32[span(core * HALF, HALF), :] + pair_in[...].astype(F32)
    chip32[...] = value
    chip16[...] = value.astype(BF16)
    ysteps = []
    for n in range(3):
        yy = jnp.bitwise_and(y + n + 1, 3)
        ysteps.append(
            remote(chip16.at[span(yy * YPART, YPART)], y_in.at[n], ysent.at[n], yarrived.at[n], device(yy, z))
        )
        ysteps[n].start()

    gpad[...] = jnp.zeros_like(gpad)
    for bc in range(0, 9, 2):
        width = min(2, 9 - bc)
        u[:, : width * L] = lax.dot_general(
            dpre3[...], wb[bc * L : (bc + width) * L, :], NT, preferred_element_type=F32
        )

        def add(gx, carry):
            for n in range(width):
                b, c = divmod(bc + n, 3)
                for yy in range(8):
                    at = pl.ds(gx * 100 + (yy + b) * 10 + c, 8)
                    gpad[at, :] += u[pl.ds(pl.multiple_of(gx * 64 + yy * 8, 8), 8), n * L : (n + 1) * L]
            return carry

        lax.fori_loop(0, 20, add, 0)

    value = chip32[span(y * YPART, YPART), :]
    for n in range(3):
        ysteps[n].wait_recv()
        value = value + y_in[n].astype(F32)
    y32[...] = value
    y16[...] = value.astype(BF16)

    def zstep(n):
        zz = jnp.bitwise_and(z + n + 1, 7)
        at = span(lax.min(zz, 6) * ZPART, ZPART)
        return zz < 7, remote(y16.at[at], z_in.at[n], zsent.at[n], zarrived.at[n], device(y, zz))

    for n in range(7):
        wanted, copy = zstep(n)

        @pl.when(wanted)
        def _():
            copy.start()

    deal_back = Deal(me, back, back_near, back_far, *(back_sem.at[n] for n in range(4)))
    deal_back.start()

    gsource[...] = jnp.zeros_like(gsource)
    for g in range(2):
        for s0, ss, p0, ps, count in segments(0, 0, 0):
            gsource[rows((2 + g) * V + s0, count, ss), :] = gpad[rows(g * 1000 + p0, count, ps), :]

    def give(n, carry):
        for g in range(2):
            for k, offset in enumerate(OFFSETS):
                if k != 13:
                    here = jnp.where(table[g, k] == n, 1.0, 0.0)
                    for s0, ss, p0, ps, count in segments(*offset):
                        at = rows(n * V + s0, count, ss)
                        gsource[at, :] += gpad[rows(g * 1000 + p0, count, ps), :] * here
        return carry

    lax.fori_loop(0, 6, give, 0)
    for g in range(2):
        part_lower[g] = gsource[g * V : (g + 1) * V, :].astype(BF16)
        part_upper[g] = gsource[(4 + g) * V : (5 + g) * V, :].astype(BF16)
    rim_up = remote(part_upper, from_lower, rim_sent.at[0], rim_arrived.at[0], lax.min(me + 1, PEERS - 1))
    rim_down = remote(part_lower, from_upper, rim_sent.at[1], rim_arrived.at[1], lax.max(me - 1, 0))

    @pl.when(has_up)
    def _():
        rim_up.start()

    @pl.when(has_down)
    def _():
        rim_down.start()

    def gzstep(n, owner, to):
        at = span(core * HALF + y * YPART + owner * ZPART, ZPART)
        return remote(total.at[at], total.at[at], gzsent.at[n], gzarrived.at[n], device(y, to))

    @pl.when(z < 7)
    def _():
        value = y32[span(z * ZPART, ZPART), :]
        for n in range(7):
            zstep(n)[1].wait_recv()
            value = value + z_in[n].astype(F32)
        total[span(core * HALF + y * YPART + z * ZPART, ZPART), :] = value.astype(BF16)
        for n in range(7):
            gzstep(n, z, jnp.bitwise_and(z + n + 1, 7)).start()

    deal_back.forward()
    for n in range(7):
        owner = jnp.bitwise_and(z + 7 - n, 7)

        @pl.when(owner < 7)
        def _():
            gzstep(n, lax.min(owner, 6), owner).wait_recv()

    def gystep(n, owner, to):
        at = span(core * HALF + owner * YPART, YPART)
        return remote(total.at[at], total.at[at], gysent.at[n], gyarrived.at[n], device(to, z))

    def across(n, which, owner):
        at = span(which * HALF + owner * YPART, YPART)
        return remote(total.at[at], total.at[at], copy_sent.at[n], copy_arrived.at[n], partner)

    owners = [jnp.bitwise_and(y + 4 - n, 3) for n in range(4)]
    for n in range(3):
        gystep(n, y, jnp.bitwise_and(y + n + 1, 3)).start()
    across(0, core, y).start()

    @pl.when(has_down)
    def _():
        rim_up.wait_recv()

    @pl.when(jnp.logical_not(has_down))
    def _():
        from_lower[...] = jnp.zeros_like(from_lower)

    @pl.when(has_up)
    def _():
        rim_down.wait_recv()

    @pl.when(jnp.logical_not(has_up))
    def _():
        from_upper[...] = jnp.zeros_like(from_upper)

    for g in range(2):
        value = gsource[(2 + g) * V : (3 + g) * V, :] + from_lower[g].astype(F32) + from_upper[g].astype(F32)
        value = value * jnp.broadcast_to(own[g, :, C : C + 1].astype(F32), (V, L))
        grad_features[g] = jnp.transpose(value)[:C, :].astype(BF16)

    for n in range(3):
        gystep(n, owners[n + 1], owners[n + 1]).wait_recv()
        across(n + 1, core, owners[n + 1]).start()
    deal_back.finish()
    near32[...] = back_near[...].astype(F32)
    far32[...] = back_far[...].astype(F32)
    for n in range(6):
        out32[pl.ds(n * PEERS + core, CHIPS, stride=2), :] = near32[box_rows(core, n), :]
        out32[pl.ds(n * PEERS + 1 - core, CHIPS, stride=2), :] = far32[box_rows(core, n), :]
    for n in range(6):
        coarse_out[:, n * L : (n + 1) * L] = out32[n * PEERS : (n + 1) * PEERS, :].astype(BF16)
    for n in range(4):
        across(n, 1 - core, owners[n]).wait_recv()

    @pl.when(has_up)
    def _():
        up.wait_send()
        rim_up.wait_send()

    @pl.when(has_down)
    def _():
        down.wait_send()
        rim_down.wait_send()

    deal.close()
    deal_back.close()
    pair.wait_send()
    for n in range(3):
        ysteps[n].wait_send()
        gystep(n, y, jnp.bitwise_and(y + n + 1, 3)).wait_send()
    for n in range(7):
        wanted, copy = zstep(n)

        @pl.when(wanted)
        def _():
            copy.wait_send()

    @pl.when(z < 7)
    def _():
        for n in range(7):
            gzstep(n, z, jnp.bitwise_and(z + n + 1, 7)).wait_send()

    for n in range(4):
        across(n, core, owners[n]).wait_send()


def smem():
    return pl.BlockSpec(memory_space=pltpu.SMEM)


def vmem(n):
    return [pl.BlockSpec(memory_space=pltpu.VMEM)] * n


def hbm(n):
    return [pl.BlockSpec(memory_space=pltpu.HBM)] * n


def run_section(neighbours, live_count, occupancy, features, grad_coarse, w_subm, w_down):
    dma = pltpu.SemaphoreType.DMA
    block = pltpu.VMEM((2, V, L), BF16)
    boxes = pltpu.VMEM((8 * PEERS, L), F32)
    sent = pltpu.VMEM((8 * PEERS, L), BF16)
    return pl.pallas_call(
        section_kernel,
        out_shape=(
            jax.ShapeDtypeStruct((PEERS, 6 * L), BF16),
            jax.ShapeDtypeStruct((2, C, V), BF16),
            jax.ShapeDtypeStruct((2 * HALF, L), BF16),
        ),
        in_specs=[smem(), smem(), smem()] + hbm(4),
        out_specs=tuple(vmem(3)),
        scratch_shapes=[
            pltpu.VMEM((2, C, V), BF16),
            pltpu.VMEM((PEERS, 6 * L), BF16),
            pltpu.VMEM((27, C, C), BF16),
            pltpu.VMEM((8, C, C), BF16),
            block, block, block, boxes, boxes, boxes, pltpu.VMEM((6 * PEERS, L), F32),
            sent, sent, sent, sent, sent, sent,
            pltpu.VMEM((7 * V, L), F32),
            pltpu.VMEM((2000, L), F32),
            pltpu.VMEM((1280, 9 * L), BF16),
            pltpu.VMEM((27 * L, L), BF16),
            pltpu.VMEM((9 * L, 3 * L), BF16),
            pltpu.VMEM((8 * L, L), BF16),
            pltpu.VMEM((V, V), BF16),
            pltpu.VMEM((V, V), BF16),
            pltpu.VMEM((L, 6 * L), BF16),
            pltpu.VMEM((2 * V, L), F32),
            pltpu.VMEM((1280, 3 * L), BF16),
            pltpu.VMEM((1280, 2 * L), F32),
            pltpu.VMEM((2000, L), F32),
            pltpu.VMEM((6 * V, L), F32),
            pltpu.VMEM((2 * HALF, L), F32),
            pltpu.VMEM((2 * HALF, L), BF16),
            pltpu.VMEM((HALF, L), BF16),
            pltpu.VMEM((HALF, L), F32),
            pltpu.VMEM((HALF, L), BF16),
            pltpu.VMEM((3, YPART, L), BF16),
            pltpu.VMEM((YPART, L), F32),
            pltpu.VMEM((YPART, L), BF16),
            pltpu.VMEM((7, ZPART, L), BF16),
            block, block, block, block,
            dma((4,)), dma((4,)), dma((4,)),
            dma((2,)), dma((2,)), dma((2,)), dma((2,)), dma(()), dma(()),
            dma((3,)), dma((3,)), dma((7,)), dma((7,)), dma((7,)), dma((7,)),
            dma((3,)), dma((3,)), dma((4,)), dma((4,)),
        ],
        compiler_params=pltpu.CompilerParams(
            vmem_limit_bytes=VMEM_LIMIT, collective_id=0, has_side_effects=True
        ),
    )(neighbours, live_count, occupancy, features, grad_coarse, w_subm, w_down)


def final_kernel(
    coarse_in, features_in, total_in, coarse_out, grad_features, grad_subm, grad_down,
    total, subm, down, load_sem, sem,
):
    def chunk(n):
        return pl.ds(9 * C * n, 9 * C)

    loads = [
        pltpu.make_async_copy(total_in.at[chunk(n)], total.at[chunk(n)], load_sem.at[n]) for n in range(3)
    ]
    for load in loads:
        load.start()
    copies = [
        pltpu.make_async_copy(features_in, grad_features, sem.at[0]),
        pltpu.make_async_copy(coarse_in, coarse_out, sem.at[1]),
    ]
    copies[0].start()
    copies[1].start()
    lane = lax.broadcasted_iota(jnp.int32, (C, L), 1)
    for k in range(35):
        quad, n = divmod(k, 4)
        if k % 12 == 0:
            loads[k // 12].wait()
        if n < 3:
            at = (3 * quad + n) * C
            value = total[at : at + C, :].astype(F32)[:, :C]
        else:
            value = jnp.zeros((C, L), F32)
            for m in range(3):
                at = (3 * quad + m) * C
                piece = pltpu.roll(total[at : at + C, :].astype(F32), 32 + 32 * m, 1)
                value = jnp.where(lane // 32 == m, piece, value)
            value = value[:, :C]
        if k < 27:
            subm[k] = value
        else:
            down[k - 27] = value
        if k in (11, 23, 26):
            part = pl.ds(k // 12 * 12, 12 if k < 26 else 3)
            copies.append(pltpu.make_async_copy(subm.at[part], grad_subm.at[part], sem.at[2 + k // 12]))
            copies[-1].start()
    copies.append(pltpu.make_async_copy(down, grad_down, sem.at[5]))
    copies[-1].start()
    for copy in copies:
        copy.wait()


def run_final(coarse_in, grad_features, total):
    return pl.pallas_call(
        final_kernel,
        out_shape=(
            jax.ShapeDtypeStruct((PEERS, 6 * L), BF16),
            jax.ShapeDtypeStruct((2, C, V), BF16),
            jax.ShapeDtypeStruct((27, C, C), F32),
            jax.ShapeDtypeStruct((8, C, C), F32),
        ),
        in_specs=hbm(3),
        out_specs=tuple(hbm(4)),
        scratch_shapes=[
            pltpu.VMEM((27 * C, L), BF16),
            pltpu.VMEM((27, C, C), F32),
            pltpu.VMEM((8, C, C), F32),
            pltpu.SemaphoreType.DMA((3,)),
            pltpu.SemaphoreType.DMA((6,)),
        ],
        compiler_params=pltpu.CompilerParams(vmem_limit_bytes=VMEM_LIMIT),
    )(coarse_in, grad_features, total)


def per_device(features, occupancy, neighbours, live_count, w_subm, w_down, grad_coarse):
    return run_final(
        *run_section(neighbours, live_count, occupancy, features, grad_coarse, w_subm, w_down)
    )


def solution(mesh):
    blocks = P(("rep", "space"), None)
    return jax.shard_map(
        per_device,
        mesh=mesh,
        in_specs=(
            P(("rep", "space"), None, None), blocks, blocks, P(("rep", "space")), P(), P(), blocks,
        ),
        out_specs=(
            blocks, P(("rep", "space"), None, None), P("rep", None, None), P("rep", None, None),
        ),
        check_vma=False,
    )
```

```python
import functools

import jax
import jax.numpy as jnp
from jax import lax
from jax.experimental import pallas as pl
from jax.experimental.pallas import tpu as pltpu
from jax.sharding import PartitionSpec as P

C, L, V = 96, 128, 512
OFFSETS = [(a, b, c) for a in (-1, 0, 1) for b in (-1, 0, 1) for c in (-1, 0, 1)]
PEERS, CHIPS = 64, 32
HALF, YPART, ZPART = 1344, 336, 48
VMEM_LIMIT = 63 * 2**20 + 2**19
F32, BF16 = jnp.float32, jnp.bfloat16
NT = (((1,), (1,)), ((), ()))


def segments(a, b, c):
    span = {-1: [(7, 0)], 0: [(i, i + 1) for i in range(8)], 1: [(0, 9)]}
    xs, ys, zs = span[a], span[b], span[c]
    if c == 0:
        return [(x * 64 + y * 8, 1, tx * 100 + ty * 10 + 1, 1, 8) for x, tx in xs for y, ty in ys]
    z, tz = zs[0]
    if b == 0:
        return [(x * 64 + z, 8, tx * 100 + 10 + tz, 10, 8) for x, tx in xs]
    y, ty = ys[0]
    if a == 0:
        return [(y * 8 + z, 64, 100 + ty * 10 + tz, 100, 8)]
    x, tx = xs[0]
    return [(x * 64 + y * 8 + z, 1, tx * 100 + ty * 10 + tz, 1, 1)]


def rows(start, count, stride):
    return pl.ds(start, count) if stride == 1 else pl.ds(start, count, stride=stride)


def mask_row(words, live, g):
    lane = lax.broadcasted_iota(jnp.int32, (1, V), 1)
    word = jnp.zeros((1, V), jnp.int32)
    for w in range(16):
        word = jnp.where(lane // 32 == w, words[g, w], word)
    bit = jnp.bitwise_and(jnp.right_shift(word, jnp.bitwise_and(lane, 31)), 1)
    return jnp.where(g < live, bit, 0)


def masked_rows(features, words, live, g):
    bit = mask_row(words, live, g)
    values = jnp.where(bit > 0, features[g].astype(F32), 0.0)
    marks = jnp.broadcast_to(bit.astype(F32), (L - C, V))
    return jnp.transpose(jnp.concatenate([values, marks], axis=0)).astype(BF16)


def remote(source, target, sent, arrived, peer):
    return pltpu.make_async_remote_copy(
        src_ref=source, dst_ref=target, send_sem=sent, recv_sem=arrived,
        device_id={"space": peer}, device_id_type=pl.DeviceIdType.MESH,
    )


def greet(me):
    barrier = pltpu.get_barrier_semaphore()
    here, core = me // 2, lax.rem(me, 2)

    def tell(peer):
        pl.semaphore_signal(
            barrier, inc=1, device_id={"space": peer}, device_id_type=pl.DeviceIdType.MESH
        )

    tell(lax.rem(me + 2 * core - 1 + PEERS, PEERS))
    tell(me + 1 - 2 * core)

    def tell_chip(i, carry):
        tell(jnp.bitwise_and(here + i, CHIPS - 1) * 2 + core)
        return carry

    lax.fori_loop(1, CHIPS, tell_chip, 0)


def greeted():
    pl.semaphore_wait(pltpu.get_barrier_semaphore(), CHIPS + 1)


class Deal:
    def __init__(self, me, outbox, near, far, sent, arrived, far_sent, far_arrived):
        self.here, self.core = me // 2, lax.rem(me, 2)
        self.outbox, self.near = outbox, near
        self.sems = sent, arrived
        self.across = remote(near, far, far_sent, far_arrived, me + 1 - 2 * self.core)
        every = pl.ds(0, 16 * (CHIPS - 1))
        self.every = remote(outbox.at[every], near.at[every], sent, arrived, me + 1 - 2 * self.core)

    def tile(self, chip):
        return pl.ds(pl.multiple_of(chip * 16, 16), 16)

    def start(self):
        def send(i, carry):
            there = jnp.bitwise_and(self.here + i, CHIPS - 1)
            remote(
                self.outbox.at[self.tile(there)], self.near.at[self.tile(self.here)],
                *self.sems, there * 2 + self.core,
            ).start()
            return carry

        lax.fori_loop(1, CHIPS, send, 0)
        self.near[self.tile(self.here), :] = self.outbox[self.tile(self.here), :]

    def forward(self):
        self.every.wait_recv()
        self.across.start()

    def finish(self):
        self.across.wait_recv()

    def close(self):
        self.every.wait_send()
        self.across.wait_send()


def box_rows(core, n):
    return pl.ds(core * 8 + n, CHIPS, stride=16)


def section_kernel(
    table, live_ref, occupancy_ref, features_hbm, cotangent_hbm, w_subm_hbm, w_down_hbm,
    coarse_out, grad_features, total,
    features, cotangent, w_subm, w_down,
    own, lower, upper, box32, near32, far32, out32, outbox, near, far, back, back_near, back_far,
    source, pad, cols, wf, wb, wd, perm, permt, spread, pre, dpre3, u, gpad, gsource,
    sums32, sums16, pair_in, chip32, chip16, y_in, y32, y16, z_in,
    part_lower, part_upper, from_lower, from_upper,
    load_sem, box_sem, back_sem, halo_sent, halo_arrived,
    rim_sent, rim_arrived, pair_sent, pair_arrived, ysent, yarrived, zsent, zarrived,
    gzsent, gzarrived, gysent, gyarrived, copy_sent, copy_arrived,
):
    me = lax.axis_index("space")
    y, z, core = me // 16, lax.rem(me // 2, 8), lax.rem(me, 2)
    partner = me + 1 - 2 * core
    has_up, has_down = me < PEERS - 1, me > 0
    loads = [
        pltpu.make_async_copy(hbm, ref, load_sem.at[n])
        for n, (hbm, ref) in enumerate(
            ((features_hbm, features), (cotangent_hbm, cotangent), (w_subm_hbm, w_subm), (w_down_hbm, w_down))
        )
    ]
    for load in loads:
        load.start()
    greet(me)

    i = lax.broadcasted_iota(jnp.int32, (V, V), 0)
    v = lax.broadcasted_iota(jnp.int32, (V, V), 1)

    def placed(index, parts):
        return sum(((index >> a) & b) << c for a, b, c in parts)

    to_voxel = ((8, 1, 6), (7, 1, 3), (6, 1, 0), (4, 3, 7), (2, 3, 4), (0, 3, 1))
    to_child = tuple((c, b, a) for a, b, c in to_voxel)
    perm[...] = jnp.where(placed(i[:, :1], to_voxel) == v, 1.0, 0.0).astype(BF16)
    permt[...] = jnp.where(placed(i[:, :1], to_child) == v, 1.0, 0.0).astype(BF16)
    spread[...] = jnp.where(
        lax.broadcasted_iota(jnp.int32, (L, 6 * L), 1) // 8
        == lax.broadcasted_iota(jnp.int32, (L, 6 * L), 0),
        1.0, 0.0,
    ).astype(BF16)
    wf[...] = jnp.zeros_like(wf)
    wb[...] = jnp.zeros_like(wb)
    wd[...] = jnp.zeros_like(wd)
    dpre3[...] = jnp.zeros_like(dpre3)
    source[6 * V :, :] = jnp.zeros((V, L), F32)

    loads[0].wait()
    for g in range(2):
        own[g] = masked_rows(features, occupancy_ref, live_ref[0], g)
    loads[1].wait()
    for n in range(6):
        box32[pl.ds(n, PEERS, stride=8), :] = cotangent[:, n * L : (n + 1) * L].astype(F32)
    counts = jnp.broadcast_to(live_ref[0].astype(F32), (PEERS, L))
    for n in (6, 7):
        box32[pl.ds(n, PEERS, stride=8), :] = counts
    outbox[...] = box32[...].astype(BF16)

    greeted()
    up = remote(own, lower, halo_sent.at[0], halo_arrived.at[0], lax.min(me + 1, PEERS - 1))
    down = remote(own, upper, halo_sent.at[1], halo_arrived.at[1], lax.max(me - 1, 0))

    @pl.when(has_up)
    def _():
        up.start()

    @pl.when(has_down)
    def _():
        down.start()

    deal = Deal(me, outbox, near, far, *(box_sem.at[n] for n in range(4)))
    deal.start()

    loads[2].wait()
    loads[3].wait()
    for k in range(27):
        a, bc = divmod(k, 9)
        w = w_subm[k]
        wf[k * L : k * L + C, :C] = w
        wb[bc * L : bc * L + C, a * L : a * L + C] = w
    for j in range(8):
        wd[j * L : j * L + C, :C] = w_down[j]

    for g in range(2):
        source[(2 + g) * V : (3 + g) * V, :] = own[g].astype(F32)

    @pl.when(has_down)
    def _():
        up.wait_recv()

    @pl.when(jnp.logical_not(has_down))
    def _():
        lower[...] = jnp.zeros_like(lower)

    @pl.when(has_up)
    def _():
        down.wait_recv()

    @pl.when(jnp.logical_not(has_up))
    def _():
        upper[...] = jnp.zeros_like(upper)

    for g in range(2):
        source[g * V : (g + 1) * V, :] = lower[g].astype(F32)
        source[(4 + g) * V : (5 + g) * V, :] = upper[g].astype(F32)

    for g in range(2):
        for k, offset in enumerate(OFFSETS):
            base = (2 + g) * V if k == 13 else table[g, k] * V
            for s0, ss, p0, ps, count in segments(*offset):
                pad[rows(g * 1000 + p0, count, ps), :] = source[rows(base + s0, count, ss), :]

    def columns(gx, carry):
        for b in range(3):
            for c in range(3):
                piece = jnp.concatenate(
                    [pad[pl.ds(gx * 100 + (yy + b) * 10 + c, 8), :] for yy in range(8)], axis=0
                )
                bc = 3 * b + c
                cols[pl.ds(pl.multiple_of(gx * 64, 64), 64), bc * L : (bc + 1) * L] = piece.astype(BF16)
        return carry

    lax.fori_loop(0, 20, columns, 0)
    deal.forward()

    for g in range(2):
        acc = jnp.zeros((V, L), F32)
        for a in range(3):
            acc += jnp.dot(
                cols[g * 640 + a * 64 : g * 640 + a * 64 + V, :],
                wf[a * 9 * L : (a + 1) * 9 * L, :],
                preferred_element_type=F32,
            )
        pre[g * V : (g + 1) * V, :] = acc

    live = live_ref[0]
    s, q = 0.7978845608028654, 0.044715
    slopes, hiddens = [], []
    for g in range(2):
        mask = jnp.broadcast_to(own[g, :, C : C + 1].astype(F32), (V, L))
        tt = pre[g * V : (g + 1) * V, :]
        th = jnp.tanh(s * (tt + q * tt * tt * tt))
        hidden = 0.5 * tt * (1.0 + th) * mask
        slopes.append((0.5 * (1.0 + th) + 0.5 * tt * (1.0 - th * th) * (s * (1.0 + 3.0 * q * tt * tt))) * mask)
        hiddens.append(jnp.where(lax.broadcasted_iota(jnp.int32, (V, L), 1) < C, hidden, mask).astype(BF16))
    both = jnp.dot(perm[...], jnp.concatenate(hiddens, axis=1), preferred_element_type=F32)
    kids = []
    cmask = jnp.zeros((2 * 64, L), F32)
    coarse = jnp.zeros((2 * 64, L), F32)
    for j in range(8):
        kid = jnp.concatenate([both[j * 64 : (j + 1) * 64, :L], both[j * 64 : (j + 1) * 64, L:]], axis=0)
        cmask = jnp.maximum(cmask, kid)
        kids.append(kid.astype(BF16))
        coarse += jnp.dot(kids[j], wd[j * L : (j + 1) * L, :], preferred_element_type=F32)
    cmask = jnp.broadcast_to(cmask[:, C : C + 1], (2 * 64, L))

    deal.finish()
    near32[...] = near[...].astype(F32)
    far32[...] = far[...].astype(F32)

    def lines(n):
        return jnp.concatenate([near32[box_rows(core, n), :], far32[box_rows(core, n), :]], axis=0)

    def peers(dim, shape):
        order = lax.broadcasted_iota(jnp.int32, shape, dim)
        return jnp.where(order < CHIPS, 2 * order + core, 2 * (order - CHIPS) + 1 - core)

    boxes = jnp.concatenate([lines(n) for n in range(6)], axis=1).astype(BF16)
    below = jnp.where(peers(0, (PEERS, L)) < me, lines(6), 0.0)
    first = jnp.sum(below, axis=0, keepdims=True).astype(jnp.int32)[:, :64]
    row = lax.broadcasted_iota(jnp.int32, (128, 64), 0)
    block, piece = row >> 6, (row >> 3) & 7
    holder = jnp.bitwise_and(jnp.broadcast_to(first, (128, 64)) + block, 7) * 8 + piece
    chosen = jnp.where((holder == peers(1, (128, 64))) & (block < live), 1.0, 0.0).astype(BF16)
    pick = (
        lax.broadcasted_iota(jnp.int32, (128, 6 * L), 1) & 7
        == lax.broadcasted_iota(jnp.int32, (128, 6 * L), 0) & 7
    )
    dz = jnp.dot(chosen, boxes, preferred_element_type=F32)
    dz = jnp.where(pick, dz, 0.0).astype(BF16)
    dz = lax.dot_general(dz, spread[...], NT, preferred_element_type=F32)
    dz = jnp.where(cmask > 0, dz, 0.0)
    dzt = jnp.transpose(dz).astype(BF16)
    dz = dz.astype(BF16)
    dh = [
        lax.dot_general(dz, wd[j * L : (j + 1) * L, :], NT, preferred_element_type=F32) for j in range(8)
    ]
    parts = []
    for g in range(2):
        part = jnp.concatenate([piece[g * 64 : (g + 1) * 64] for piece in dh], axis=0)
        high = part.astype(BF16)
        parts += [high, (part - high.astype(F32)).astype(BF16)]
    dh = jnp.dot(permt[...], jnp.concatenate(parts, axis=1), preferred_element_type=F32)
    for g in range(2):
        dpre = slopes[g] * (dh[:, 2 * g * L : (2 * g + 1) * L] + dh[:, (2 * g + 1) * L : (2 * g + 2) * L])
        dpre16 = dpre.astype(BF16)
        for a in range(3):
            dpre3[g * 640 + a * 64 : g * 640 + a * 64 + V, a * L : (a + 1) * L] = dpre16
        pre[g * V : (g + 1) * V, :] = dpre
    down_sums = jnp.dot(dzt, jnp.concatenate(kids, axis=1), preferred_element_type=F32)

    lane = lax.broadcasted_iota(jnp.int32, (C, L), 1)
    held = {}

    def keep(k, product):
        held[k % 4] = jnp.transpose(product)[:C]
        if k % 4 == 3 or k == 34:
            last = held.get(3)
            for n in range(3):
                slab = held[n]
                if last is not None:
                    slab = jnp.where(lane < C, slab, pltpu.roll(last, C - 32 * n, 1))
                at = (3 * (k // 4) + n) * C
                sums32[at : at + C, :] = slab
                sums16[at : at + C, :] = slab.astype(BF16)
            held.clear()

    dt = jnp.transpose(pre[...]).astype(BF16)
    for a in range(3):
        for bc in range(0, 9, 2):
            lanes = slice(bc * L, min(bc + 2, 9) * L)
            value = jnp.dot(
                dt[:, :V], cols[a * 64 : a * 64 + V, lanes], preferred_element_type=F32
            ) + jnp.dot(
                dt[:, V:], cols[640 + a * 64 : 640 + a * 64 + V, lanes], preferred_element_type=F32
            )
            for n in range(min(2, 9 - bc)):
                keep(a * 9 + bc + n, value[:, n * L : (n + 1) * L])
    for j in range(8):
        keep(27 + j, down_sums[:, j * L : (j + 1) * L])
    sums32[27 * C :, :] = jnp.zeros((C, L), F32)
    sums16[27 * C :, :] = jnp.zeros((C, L), BF16)

    def span(at, count):
        return pl.ds(pl.multiple_of(at, 16), count)

    def device(yy, zz):
        return yy * 16 + zz * 2 + core

    pair = remote(sums16.at[span((1 - core) * HALF, HALF)], pair_in, pair_sent, pair_arrived, partner)
    pair.start()
    pair.wait_recv()
    value = sums32[span(core * HALF, HALF), :] + pair_in[...].astype(F32)
    chip32[...] = value
    chip16[...] = value.astype(BF16)
    ysteps = []
    for n in range(3):
        yy = jnp.bitwise_and(y + n + 1, 3)
        ysteps.append(
            remote(chip16.at[span(yy * YPART, YPART)], y_in.at[n], ysent.at[n], yarrived.at[n], device(yy, z))
        )
        ysteps[n].start()

    deal_back = Deal(me, back, back_near, back_far, *(back_sem.at[n] for n in range(4)))
    flat = jnp.dot((coarse * cmask).astype(BF16), spread[...], preferred_element_type=F32)
    flat = jnp.where(pick, flat, 0.0).astype(BF16)
    dealt = lax.dot_general(chosen, flat, (((0,), (0,)), ((), ())), preferred_element_type=F32)
    for n in range(6):
        box32[box_rows(core, n), :] = dealt[:CHIPS, n * L : (n + 1) * L]
        box32[box_rows(1 - core, n), :] = dealt[CHIPS:, n * L : (n + 1) * L]
    back[...] = box32[...].astype(BF16)

    gpad[...] = jnp.zeros_like(gpad)
    for bc in range(0, 9, 2):
        width = min(2, 9 - bc)
        u[:, : width * L] = lax.dot_general(
            dpre3[...], wb[bc * L : (bc + width) * L, :], NT, preferred_element_type=F32
        )

        def add(gx, carry):
            for n in range(width):
                b, c = divmod(bc + n, 3)
                for yy in range(8):
                    at = pl.ds(gx * 100 + (yy + b) * 10 + c, 8)
                    gpad[at, :] += u[pl.ds(pl.multiple_of(gx * 64 + yy * 8, 8), 8), n * L : (n + 1) * L]
            return carry

        lax.fori_loop(0, 20, add, 0)

    value = chip32[span(y * YPART, YPART), :]
    for n in range(3):
        ysteps[n].wait_recv()
        value = value + y_in[n].astype(F32)
    y32[...] = value
    y16[...] = value.astype(BF16)

    def zstep(n):
        zz = jnp.bitwise_and(z + n + 1, 7)
        at = span(lax.min(zz, 6) * ZPART, ZPART)
        return zz < 7, remote(y16.at[at], z_in.at[n], zsent.at[n], zarrived.at[n], device(y, zz))

    for n in range(7):
        wanted, copy = zstep(n)

        @pl.when(wanted)
        def _():
            copy.start()

    deal_back.start()

    gsource[...] = jnp.zeros_like(gsource)
    for g in range(2):
        for s0, ss, p0, ps, count in segments(0, 0, 0):
            gsource[rows((2 + g) * V + s0, count, ss), :] = gpad[rows(g * 1000 + p0, count, ps), :]

    def give(n, carry):
        for g in range(2):
            for k, offset in enumerate(OFFSETS):
                if k != 13:
                    here = jnp.where(table[g, k] == n, 1.0, 0.0)
                    for s0, ss, p0, ps, count in segments(*offset):
                        at = rows(n * V + s0, count, ss)
                        gsource[at, :] += gpad[rows(g * 1000 + p0, count, ps), :] * here
        return carry

    lax.fori_loop(0, 6, give, 0)
    for g in range(2):
        part_lower[g] = gsource[g * V : (g + 1) * V, :].astype(BF16)
        part_upper[g] = gsource[(4 + g) * V : (5 + g) * V, :].astype(BF16)
    rim_up = remote(part_upper, from_lower, rim_sent.at[0], rim_arrived.at[0], lax.min(me + 1, PEERS - 1))
    rim_down = remote(part_lower, from_upper, rim_sent.at[1], rim_arrived.at[1], lax.max(me - 1, 0))

    @pl.when(has_up)
    def _():
        rim_up.start()

    @pl.when(has_down)
    def _():
        rim_down.start()

    def gzstep(n, owner, to):
        at = span(core * HALF + y * YPART + owner * ZPART, ZPART)
        return remote(total.at[at], total.at[at], gzsent.at[n], gzarrived.at[n], device(y, to))

    @pl.when(z < 7)
    def _():
        value = y32[span(z * ZPART, ZPART), :]
        for n in range(7):
            zstep(n)[1].wait_recv()
            value = value + z_in[n].astype(F32)
        total[span(core * HALF + y * YPART + z * ZPART, ZPART), :] = value.astype(BF16)
        for n in range(7):
            gzstep(n, z, jnp.bitwise_and(z + n + 1, 7)).start()

    deal_back.forward()
    for n in range(7):
        owner = jnp.bitwise_and(z + 7 - n, 7)

        @pl.when(owner < 7)
        def _():
            gzstep(n, lax.min(owner, 6), owner).wait_recv()

    def gystep(n, owner, to):
        at = span(core * HALF + owner * YPART, YPART)
        return remote(total.at[at], total.at[at], gysent.at[n], gyarrived.at[n], device(to, z))

    def across(n, which, owner):
        at = span(which * HALF + owner * YPART, YPART)
        return remote(total.at[at], total.at[at], copy_sent.at[n], copy_arrived.at[n], partner)

    owners = [jnp.bitwise_and(y + 4 - n, 3) for n in range(4)]
    for n in range(3):
        gystep(n, y, jnp.bitwise_and(y + n + 1, 3)).start()
    across(0, core, y).start()

    @pl.when(has_down)
    def _():
        rim_up.wait_recv()

    @pl.when(jnp.logical_not(has_down))
    def _():
        from_lower[...] = jnp.zeros_like(from_lower)

    @pl.when(has_up)
    def _():
        rim_down.wait_recv()

    @pl.when(jnp.logical_not(has_up))
    def _():
        from_upper[...] = jnp.zeros_like(from_upper)

    for g in range(2):
        value = gsource[(2 + g) * V : (3 + g) * V, :] + from_lower[g].astype(F32) + from_upper[g].astype(F32)
        value = value * jnp.broadcast_to(own[g, :, C : C + 1].astype(F32), (V, L))
        grad_features[g] = jnp.transpose(value)[:C, :].astype(BF16)

    for n in range(3):
        gystep(n, owners[n + 1], owners[n + 1]).wait_recv()
        across(n + 1, core, owners[n + 1]).start()
    deal_back.finish()
    near32[...] = back_near[...].astype(F32)
    far32[...] = back_far[...].astype(F32)
    for n in range(6):
        out32[pl.ds(n * PEERS + core, CHIPS, stride=2), :] = near32[box_rows(core, n), :]
        out32[pl.ds(n * PEERS + 1 - core, CHIPS, stride=2), :] = far32[box_rows(core, n), :]
    for n in range(6):
        coarse_out[:, n * L : (n + 1) * L] = out32[n * PEERS : (n + 1) * PEERS, :].astype(BF16)
    for n in range(4):
        across(n, 1 - core, owners[n]).wait_recv()

    @pl.when(has_up)
    def _():
        up.wait_send()
        rim_up.wait_send()

    @pl.when(has_down)
    def _():
        down.wait_send()
        rim_down.wait_send()

    deal.close()
    deal_back.close()
    pair.wait_send()
    for n in range(3):
        ysteps[n].wait_send()
        gystep(n, y, jnp.bitwise_and(y + n + 1, 3)).wait_send()
    for n in range(7):
        wanted, copy = zstep(n)

        @pl.when(wanted)
        def _():
            copy.wait_send()

    @pl.when(z < 7)
    def _():
        for n in range(7):
            gzstep(n, z, jnp.bitwise_and(z + n + 1, 7)).wait_send()

    for n in range(4):
        across(n, core, owners[n]).wait_send()


def smem():
    return pl.BlockSpec(memory_space=pltpu.SMEM)


def vmem(n):
    return [pl.BlockSpec(memory_space=pltpu.VMEM)] * n


def hbm(n):
    return [pl.BlockSpec(memory_space=pltpu.HBM)] * n


def run_section(neighbours, live_count, occupancy, features, grad_coarse, w_subm, w_down):
    dma = pltpu.SemaphoreType.DMA
    block = pltpu.VMEM((2, V, L), BF16)
    boxes = pltpu.VMEM((8 * PEERS, L), F32)
    sent = pltpu.VMEM((8 * PEERS, L), BF16)
    return pl.pallas_call(
        section_kernel,
        out_shape=(
            jax.ShapeDtypeStruct((PEERS, 6 * L), BF16),
            jax.ShapeDtypeStruct((2, C, V), BF16),
            jax.ShapeDtypeStruct((2 * HALF, L), BF16),
        ),
        in_specs=[smem(), smem(), smem()] + hbm(4),
        out_specs=tuple(vmem(3)),
        scratch_shapes=[
            pltpu.VMEM((2, C, V), BF16),
            pltpu.VMEM((PEERS, 6 * L), BF16),
            pltpu.VMEM((27, C, C), BF16),
            pltpu.VMEM((8, C, C), BF16),
            block, block, block, boxes, boxes, boxes, pltpu.VMEM((6 * PEERS, L), F32),
            sent, sent, sent, sent, sent, sent,
            pltpu.VMEM((7 * V, L), F32),
            pltpu.VMEM((2000, L), F32),
            pltpu.VMEM((1280, 9 * L), BF16),
            pltpu.VMEM((27 * L, L), BF16),
            pltpu.VMEM((9 * L, 3 * L), BF16),
            pltpu.VMEM((8 * L, L), BF16),
            pltpu.VMEM((V, V), BF16),
            pltpu.VMEM((V, V), BF16),
            pltpu.VMEM((L, 6 * L), BF16),
            pltpu.VMEM((2 * V, L), F32),
            pltpu.VMEM((1280, 3 * L), BF16),
            pltpu.VMEM((1280, 2 * L), F32),
            pltpu.VMEM((2000, L), F32),
            pltpu.VMEM((6 * V, L), F32),
            pltpu.VMEM((2 * HALF, L), F32),
            pltpu.VMEM((2 * HALF, L), BF16),
            pltpu.VMEM((HALF, L), BF16),
            pltpu.VMEM((HALF, L), F32),
            pltpu.VMEM((HALF, L), BF16),
            pltpu.VMEM((3, YPART, L), BF16),
            pltpu.VMEM((YPART, L), F32),
            pltpu.VMEM((YPART, L), BF16),
            pltpu.VMEM((7, ZPART, L), BF16),
            block, block, block, block,
            dma((4,)), dma((4,)), dma((4,)),
            dma((2,)), dma((2,)), dma((2,)), dma((2,)), dma(()), dma(()),
            dma((3,)), dma((3,)), dma((7,)), dma((7,)), dma((7,)), dma((7,)),
            dma((3,)), dma((3,)), dma((4,)), dma((4,)),
        ],
        compiler_params=pltpu.CompilerParams(
            vmem_limit_bytes=VMEM_LIMIT, collective_id=0, has_side_effects=True
        ),
    )(neighbours, live_count, occupancy, features, grad_coarse, w_subm, w_down)


def final_kernel(
    coarse_in, features_in, total_in, coarse_out, grad_features, grad_subm, grad_down,
    total, subm, down, coarse, features, load_sem, sem,
):
    def chunk(n):
        return pl.ds(9 * C * n, 9 * C)

    loads = [
        pltpu.make_async_copy(total_in.at[chunk(n)], total.at[chunk(n)], load_sem.at[n]) for n in range(3)
    ]
    loads.append(pltpu.make_async_copy(features_in, features, load_sem.at[3]))
    loads.append(pltpu.make_async_copy(coarse_in, coarse, load_sem.at[4]))
    for load in loads:
        load.start()
    copies = [
        pltpu.make_async_copy(features, grad_features, sem.at[0]),
        pltpu.make_async_copy(coarse, coarse_out, sem.at[1]),
    ]
    lane = lax.broadcasted_iota(jnp.int32, (C, L), 1)
    for k in range(35):
        quad, n = divmod(k, 4)
        if k % 12 == 0:
            loads[k // 12].wait()
        if n < 3:
            at = (3 * quad + n) * C
            value = total[at : at + C, :].astype(F32)[:, :C]
        else:
            value = jnp.zeros((C, L), F32)
            for m in range(3):
                at = (3 * quad + m) * C
                piece = pltpu.roll(total[at : at + C, :].astype(F32), 32 + 32 * m, 1)
                value = jnp.where(lane // 32 == m, piece, value)
            value = value[:, :C]
        if k < 27:
            subm[k] = value
        else:
            down[k - 27] = value
        if k in (11, 23, 26):
            part = pl.ds(k // 12 * 12, 12 if k < 26 else 3)
            copies.append(pltpu.make_async_copy(subm.at[part], grad_subm.at[part], sem.at[2 + k // 12]))
            copies[-1].start()
        if k == 11:
            for n in range(2):
                loads[3 + n].wait()
                copies[n].start()
    copies.append(pltpu.make_async_copy(down, grad_down, sem.at[5]))
    copies[-1].start()
    for copy in copies:
        copy.wait()


def run_final(coarse_in, grad_features, total):
    return pl.pallas_call(
        final_kernel,
        out_shape=(
            jax.ShapeDtypeStruct((PEERS, 6 * L), BF16),
            jax.ShapeDtypeStruct((2, C, V), BF16),
            jax.ShapeDtypeStruct((27, C, C), F32),
            jax.ShapeDtypeStruct((8, C, C), F32),
        ),
        in_specs=hbm(3),
        out_specs=tuple(hbm(4)),
        scratch_shapes=[
            pltpu.VMEM((27 * C, L), BF16),
            pltpu.VMEM((27, C, C), F32),
            pltpu.VMEM((8, C, C), F32),
            pltpu.VMEM((PEERS, 6 * L), BF16),
            pltpu.VMEM((2, C, V), BF16),
            pltpu.SemaphoreType.DMA((5,)),
            pltpu.SemaphoreType.DMA((6,)),
        ],
        compiler_params=pltpu.CompilerParams(vmem_limit_bytes=VMEM_LIMIT),
    )(coarse_in, grad_features, total)


def per_device(features, occupancy, neighbours, live_count, w_subm, w_down, grad_coarse):
    return run_final(
        *run_section(neighbours, live_count, occupancy, features, grad_coarse, w_subm, w_down)
    )


def solution(mesh):
    blocks = P(("rep", "space"), None)
    return jax.shard_map(
        per_device,
        mesh=mesh,
        in_specs=(
            P(("rep", "space"), None, None), blocks, blocks, P(("rep", "space")), P(), P(), blocks,
        ),
        out_specs=(
            blocks, P(("rep", "space"), None, None), P("rep", None, None), P("rep", None, None),
        ),
        check_vma=False,
    )
```

```python
import functools

import jax
import jax.numpy as jnp
from jax import lax
from jax.experimental import pallas as pl
from jax.experimental.pallas import tpu as pltpu
from jax.sharding import PartitionSpec as P

C, L, V = 96, 128, 512
OFFSETS = [(a, b, c) for a in (-1, 0, 1) for b in (-1, 0, 1) for c in (-1, 0, 1)]
PEERS, CHIPS = 64, 32
HALF, YPART, ZPART = 1344, 336, 48
VMEM_LIMIT = 63 * 2**20 + 2**19
F32, BF16 = jnp.float32, jnp.bfloat16
NT = (((1,), (1,)), ((), ()))


def segments(a, b, c):
    span = {-1: [(7, 0)], 0: [(i, i + 1) for i in range(8)], 1: [(0, 9)]}
    xs, ys, zs = span[a], span[b], span[c]
    if c == 0:
        return [(x * 64 + y * 8, 1, tx * 100 + ty * 10 + 1, 1, 8) for x, tx in xs for y, ty in ys]
    z, tz = zs[0]
    if b == 0:
        return [(x * 64 + z, 8, tx * 100 + 10 + tz, 10, 8) for x, tx in xs]
    y, ty = ys[0]
    if a == 0:
        return [(y * 8 + z, 64, 100 + ty * 10 + tz, 100, 8)]
    x, tx = xs[0]
    return [(x * 64 + y * 8 + z, 1, tx * 100 + ty * 10 + tz, 1, 1)]


def rows(start, count, stride):
    return pl.ds(start, count) if stride == 1 else pl.ds(start, count, stride=stride)


def mask_row(words, live, g):
    lane = lax.broadcasted_iota(jnp.int32, (1, V), 1)
    word = jnp.zeros((1, V), jnp.int32)
    for w in range(16):
        word = jnp.where(lane // 32 == w, words[g, w], word)
    bit = jnp.bitwise_and(jnp.right_shift(word, jnp.bitwise_and(lane, 31)), 1)
    return jnp.where(g < live, bit, 0)


def masked_rows(features, words, live, g):
    bit = mask_row(words, live, g)
    values = jnp.where(bit > 0, features[g].astype(F32), 0.0)
    marks = jnp.broadcast_to(bit.astype(F32), (L - C, V))
    return jnp.transpose(jnp.concatenate([values, marks], axis=0)).astype(BF16)


def remote(source, target, sent, arrived, peer):
    return pltpu.make_async_remote_copy(
        src_ref=source, dst_ref=target, send_sem=sent, recv_sem=arrived,
        device_id={"space": peer}, device_id_type=pl.DeviceIdType.MESH,
    )


def greet(me):
    barrier = pltpu.get_barrier_semaphore()
    here, core = me // 2, lax.rem(me, 2)

    def tell(peer):
        pl.semaphore_signal(
            barrier, inc=1, device_id={"space": peer}, device_id_type=pl.DeviceIdType.MESH
        )

    tell(lax.rem(me + 2 * core - 1 + PEERS, PEERS))
    tell(me + 1 - 2 * core)

    def tell_chip(i, carry):
        tell(jnp.bitwise_and(here + i, CHIPS - 1) * 2 + core)
        return carry

    lax.fori_loop(1, CHIPS, tell_chip, 0)


def greeted():
    pl.semaphore_wait(pltpu.get_barrier_semaphore(), CHIPS + 1)


class Deal:
    def __init__(self, me, outbox, near, far, sent, arrived, far_sent, far_arrived):
        self.here, self.core = me // 2, lax.rem(me, 2)
        self.outbox, self.near = outbox, near
        self.sems = sent, arrived
        self.across = remote(near, far, far_sent, far_arrived, me + 1 - 2 * self.core)
        every = pl.ds(0, 16 * (CHIPS - 1))
        self.every = remote(outbox.at[every], near.at[every], sent, arrived, me + 1 - 2 * self.core)

    def tile(self, chip):
        return pl.ds(pl.multiple_of(chip * 16, 16), 16)

    def start(self):
        def send(i, carry):
            there = jnp.bitwise_and(self.here + i, CHIPS - 1)
            remote(
                self.outbox.at[self.tile(there)], self.near.at[self.tile(self.here)],
                *self.sems, there * 2 + self.core,
            ).start()
            return carry

        lax.fori_loop(1, CHIPS, send, 0)
        self.near[self.tile(self.here), :] = self.outbox[self.tile(self.here), :]

    def forward(self):
        self.every.wait_recv()
        self.across.start()

    def finish(self):
        self.across.wait_recv()

    def close(self):
        self.every.wait_send()
        self.across.wait_send()


def box_rows(core, n):
    return pl.ds(core * 8 + n, CHIPS, stride=16)


def section_kernel(
    table, live_ref, occupancy_ref, features_hbm, cotangent_hbm, w_subm_hbm, w_down_hbm,
    coarse_out, grad_features, total,
    features, cotangent, w_subm, w_down,
    own, lower, upper, box32, near32, far32, out32, outbox, near, far, back, back_near, back_far,
    source, pad, cols, wf, wb, wd, perm, permt, spread, pre, dpre3, u, gpad, gsource,
    sums32, sums16, pair_in, chip32, chip16, y_in, y32, y16, z_in,
    part_lower, part_upper, from_lower, from_upper,
    load_sem, box_sem, back_sem, halo_sent, halo_arrived,
    rim_sent, rim_arrived, pair_sent, pair_arrived, ysent, yarrived, zsent, zarrived,
    gzsent, gzarrived, gysent, gyarrived, copy_sent, copy_arrived,
):
    me = lax.axis_index("space")
    y, z, core = me // 16, lax.rem(me // 2, 8), lax.rem(me, 2)
    partner = me + 1 - 2 * core
    has_up, has_down = me < PEERS - 1, me > 0
    loads = [
        pltpu.make_async_copy(hbm, ref, load_sem.at[n])
        for n, (hbm, ref) in enumerate(
            ((features_hbm, features), (cotangent_hbm, cotangent), (w_subm_hbm, w_subm), (w_down_hbm, w_down))
        )
    ]
    for load in loads:
        load.start()
    greet(me)

    i = lax.broadcasted_iota(jnp.int32, (V, V), 0)
    v = lax.broadcasted_iota(jnp.int32, (V, V), 1)

    def placed(index, parts):
        return sum(((index >> a) & b) << c for a, b, c in parts)

    to_voxel = ((8, 1, 6), (7, 1, 3), (6, 1, 0), (4, 3, 7), (2, 3, 4), (0, 3, 1))
    to_child = tuple((c, b, a) for a, b, c in to_voxel)
    perm[...] = jnp.where(placed(i[:, :1], to_voxel) == v, 1.0, 0.0).astype(BF16)
    permt[...] = jnp.where(placed(i[:, :1], to_child) == v, 1.0, 0.0).astype(BF16)
    spread[...] = jnp.where(
        lax.broadcasted_iota(jnp.int32, (L, 6 * L), 1) // 8
        == lax.broadcasted_iota(jnp.int32, (L, 6 * L), 0),
        1.0, 0.0,
    ).astype(BF16)
    wf[...] = jnp.zeros_like(wf)
    wb[...] = jnp.zeros_like(wb)
    wd[...] = jnp.zeros_like(wd)
    dpre3[...] = jnp.zeros_like(dpre3)
    source[6 * V :, :] = jnp.zeros((V, L), F32)

    loads[0].wait()
    for g in range(2):
        own[g] = masked_rows(features, occupancy_ref, live_ref[0], g)
    loads[1].wait()
    for n in range(6):
        box32[pl.ds(n, PEERS, stride=8), :] = cotangent[:, n * L : (n + 1) * L].astype(F32)
    counts = jnp.broadcast_to(live_ref[0].astype(F32), (PEERS, L))
    for n in (6, 7):
        box32[pl.ds(n, PEERS, stride=8), :] = counts
    outbox[...] = box32[...].astype(BF16)

    greeted()
    up = remote(own, lower, halo_sent.at[0], halo_arrived.at[0], lax.min(me + 1, PEERS - 1))
    down = remote(own, upper, halo_sent.at[1], halo_arrived.at[1], lax.max(me - 1, 0))

    @pl.when(has_up)
    def _():
        up.start()

    @pl.when(has_down)
    def _():
        down.start()

    deal = Deal(me, outbox, near, far, *(box_sem.at[n] for n in range(4)))
    deal.start()

    loads[2].wait()
    loads[3].wait()
    for k in range(27):
        a, bc = divmod(k, 9)
        w = w_subm[k]
        wf[k * L : k * L + C, :C] = w
        wb[bc * L : bc * L + C, a * L : a * L + C] = w
    for j in range(8):
        wd[j * L : j * L + C, :C] = w_down[j]

    for g in range(2):
        source[(2 + g) * V : (3 + g) * V, :] = own[g].astype(F32)

    @pl.when(has_down)
    def _():
        up.wait_recv()

    @pl.when(jnp.logical_not(has_down))
    def _():
        lower[...] = jnp.zeros_like(lower)

    @pl.when(has_up)
    def _():
        down.wait_recv()

    @pl.when(jnp.logical_not(has_up))
    def _():
        upper[...] = jnp.zeros_like(upper)

    for g in range(2):
        source[g * V : (g + 1) * V, :] = lower[g].astype(F32)
        source[(4 + g) * V : (5 + g) * V, :] = upper[g].astype(F32)

    for g in range(2):
        for k, offset in enumerate(OFFSETS):
            base = (2 + g) * V if k == 13 else table[g, k] * V
            for s0, ss, p0, ps, count in segments(*offset):
                pad[rows(g * 1000 + p0, count, ps), :] = source[rows(base + s0, count, ss), :]

    def columns(gx, carry):
        for b in range(3):
            for c in range(3):
                piece = jnp.concatenate(
                    [pad[pl.ds(gx * 100 + (yy + b) * 10 + c, 8), :] for yy in range(8)], axis=0
                )
                bc = 3 * b + c
                cols[pl.ds(pl.multiple_of(gx * 64, 64), 64), bc * L : (bc + 1) * L] = piece.astype(BF16)
        return carry

    lax.fori_loop(0, 20, columns, 0)

    for g in range(2):
        acc = jnp.zeros((V, L), F32)
        for a in range(3):
            acc += jnp.dot(
                cols[g * 640 + a * 64 : g * 640 + a * 64 + V, :],
                wf[a * 9 * L : (a + 1) * 9 * L, :],
                preferred_element_type=F32,
            )
        pre[g * V : (g + 1) * V, :] = acc

    deal.forward()
    live = live_ref[0]
    s, q = 0.7978845608028654, 0.044715
    slopes, hiddens = [], []
    for g in range(2):
        mask = jnp.broadcast_to(own[g, :, C : C + 1].astype(F32), (V, L))
        tt = pre[g * V : (g + 1) * V, :]
        th = jnp.tanh(s * (tt + q * tt * tt * tt))
        hidden = 0.5 * tt * (1.0 + th) * mask
        slopes.append((0.5 * (1.0 + th) + 0.5 * tt * (1.0 - th * th) * (s * (1.0 + 3.0 * q * tt * tt))) * mask)
        hiddens.append(jnp.where(lax.broadcasted_iota(jnp.int32, (V, L), 1) < C, hidden, mask).astype(BF16))
    both = jnp.dot(perm[...], jnp.concatenate(hiddens, axis=1), preferred_element_type=F32)
    kids = []
    cmask = jnp.zeros((2 * 64, L), F32)
    coarse = jnp.zeros((2 * 64, L), F32)
    for j in range(8):
        kid = jnp.concatenate([both[j * 64 : (j + 1) * 64, :L], both[j * 64 : (j + 1) * 64, L:]], axis=0)
        cmask = jnp.maximum(cmask, kid)
        kids.append(kid.astype(BF16))
        coarse += jnp.dot(kids[j], wd[j * L : (j + 1) * L, :], preferred_element_type=F32)
    cmask = jnp.broadcast_to(cmask[:, C : C + 1], (2 * 64, L))

    deal.finish()
    near32[...] = near[...].astype(F32)
    far32[...] = far[...].astype(F32)

    def lines(n):
        return jnp.concatenate([near32[box_rows(core, n), :], far32[box_rows(core, n), :]], axis=0)

    def peers(dim, shape):
        order = lax.broadcasted_iota(jnp.int32, shape, dim)
        return jnp.where(order < CHIPS, 2 * order + core, 2 * (order - CHIPS) + 1 - core)

    boxes = jnp.concatenate([lines(n) for n in range(6)], axis=1).astype(BF16)
    below = jnp.where(peers(0, (PEERS, L)) < me, lines(6), 0.0)
    first = jnp.sum(below, axis=0, keepdims=True).astype(jnp.int32)[:, :64]
    row = lax.broadcasted_iota(jnp.int32, (128, 64), 0)
    block, piece = row >> 6, (row >> 3) & 7
    holder = jnp.bitwise_and(jnp.broadcast_to(first, (128, 64)) + block, 7) * 8 + piece
    chosen = jnp.where((holder == peers(1, (128, 64))) & (block < live), 1.0, 0.0).astype(BF16)
    pick = (
        lax.broadcasted_iota(jnp.int32, (128, 6 * L), 1) & 7
        == lax.broadcasted_iota(jnp.int32, (128, 6 * L), 0) & 7
    )
    dz = jnp.dot(chosen, boxes, preferred_element_type=F32)
    dz = jnp.where(pick, dz, 0.0).astype(BF16)
    dz = lax.dot_general(dz, spread[...], NT, preferred_element_type=F32)
    dz = jnp.where(cmask > 0, dz, 0.0)
    dzt = jnp.transpose(dz).astype(BF16)
    dz = dz.astype(BF16)
    dh = [
        lax.dot_general(dz, wd[j * L : (j + 1) * L, :], NT, preferred_element_type=F32) for j in range(8)
    ]
    parts = []
    for g in range(2):
        part = jnp.concatenate([piece[g * 64 : (g + 1) * 64] for piece in dh], axis=0)
        high = part.astype(BF16)
        parts += [high, (part - high.astype(F32)).astype(BF16)]
    dh = jnp.dot(permt[...], jnp.concatenate(parts, axis=1), preferred_element_type=F32)
    for g in range(2):
        dpre = slopes[g] * (dh[:, 2 * g * L : (2 * g + 1) * L] + dh[:, (2 * g + 1) * L : (2 * g + 2) * L])
        dpre16 = dpre.astype(BF16)
        for a in range(3):
            dpre3[g * 640 + a * 64 : g * 640 + a * 64 + V, a * L : (a + 1) * L] = dpre16
        pre[g * V : (g + 1) * V, :] = dpre
    down_sums = jnp.dot(dzt, jnp.concatenate(kids, axis=1), preferred_element_type=F32)

    lane = lax.broadcasted_iota(jnp.int32, (C, L), 1)
    held = {}

    def keep(k, product):
        held[k % 4] = jnp.transpose(product)[:C]
        if k % 4 == 3 or k == 34:
            last = held.get(3)
            for n in range(3):
                slab = held[n]
                if last is not None:
                    slab = jnp.where(lane < C, slab, pltpu.roll(last, C - 32 * n, 1))
                at = (3 * (k // 4) + n) * C
                sums32[at : at + C, :] = slab
                sums16[at : at + C, :] = slab.astype(BF16)
            held.clear()

    dt = jnp.transpose(pre[...]).astype(BF16)
    for a in range(3):
        for bc in range(0, 9, 2):
            lanes = slice(bc * L, min(bc + 2, 9) * L)
            value = jnp.dot(
                dt[:, :V], cols[a * 64 : a * 64 + V, lanes], preferred_element_type=F32
            ) + jnp.dot(
                dt[:, V:], cols[640 + a * 64 : 640 + a * 64 + V, lanes], preferred_element_type=F32
            )
            for n in range(min(2, 9 - bc)):
                keep(a * 9 + bc + n, value[:, n * L : (n + 1) * L])
    for j in range(8):
        keep(27 + j, down_sums[:, j * L : (j + 1) * L])
    sums32[27 * C :, :] = jnp.zeros((C, L), F32)
    sums16[27 * C :, :] = jnp.zeros((C, L), BF16)

    def span(at, count):
        return pl.ds(pl.multiple_of(at, 16), count)

    def device(yy, zz):
        return yy * 16 + zz * 2 + core

    pair = remote(sums16.at[span((1 - core) * HALF, HALF)], pair_in, pair_sent, pair_arrived, partner)
    pair.start()
    deal_back = Deal(me, back, back_near, back_far, *(back_sem.at[n] for n in range(4)))
    flat = jnp.dot((coarse * cmask).astype(BF16), spread[...], preferred_element_type=F32)
    flat = jnp.where(pick, flat, 0.0).astype(BF16)
    dealt = lax.dot_general(chosen, flat, (((0,), (0,)), ((), ())), preferred_element_type=F32)
    for n in range(6):
        box32[box_rows(core, n), :] = dealt[:CHIPS, n * L : (n + 1) * L]
        box32[box_rows(1 - core, n), :] = dealt[CHIPS:, n * L : (n + 1) * L]
    back[...] = box32[...].astype(BF16)
    deal_back.start()
    pair.wait_recv()
    value = sums32[span(core * HALF, HALF), :] + pair_in[...].astype(F32)
    chip32[...] = value
    chip16[...] = value.astype(BF16)
    ysteps = []
    for n in range(3):
        yy = jnp.bitwise_and(y + n + 1, 3)
        ysteps.append(
            remote(chip16.at[span(yy * YPART, YPART)], y_in.at[n], ysent.at[n], yarrived.at[n], device(yy, z))
        )
        ysteps[n].start()

    gpad[...] = jnp.zeros_like(gpad)
    for bc in range(0, 9, 2):
        width = min(2, 9 - bc)
        u[:, : width * L] = lax.dot_general(
            dpre3[...], wb[bc * L : (bc + width) * L, :], NT, preferred_element_type=F32
        )

        def add(gx, carry):
            for n in range(width):
                b, c = divmod(bc + n, 3)
                for yy in range(8):
                    at = pl.ds(gx * 100 + (yy + b) * 10 + c, 8)
                    gpad[at, :] += u[pl.ds(pl.multiple_of(gx * 64 + yy * 8, 8), 8), n * L : (n + 1) * L]
            return carry

        lax.fori_loop(0, 20, add, 0)

    value = chip32[span(y * YPART, YPART), :]
    for n in range(3):
        ysteps[n].wait_recv()
        value = value + y_in[n].astype(F32)
    y32[...] = value
    y16[...] = value.astype(BF16)

    def zstep(n):
        zz = jnp.bitwise_and(z + n + 1, 7)
        at = span(lax.min(zz, 6) * ZPART, ZPART)
        return zz < 7, remote(y16.at[at], z_in.at[n], zsent.at[n], zarrived.at[n], device(y, zz))

    for n in range(7):
        wanted, copy = zstep(n)

        @pl.when(wanted)
        def _():
            copy.start()

    gsource[...] = jnp.zeros_like(gsource)
    for g in range(2):
        for s0, ss, p0, ps, count in segments(0, 0, 0):
            gsource[rows((2 + g) * V + s0, count, ss), :] = gpad[rows(g * 1000 + p0, count, ps), :]

    def give(n, carry):
        for g in range(2):
            for k, offset in enumerate(OFFSETS):
                if k != 13:
                    here = jnp.where(table[g, k] == n, 1.0, 0.0)
                    for s0, ss, p0, ps, count in segments(*offset):
                        at = rows(n * V + s0, count, ss)
                        gsource[at, :] += gpad[rows(g * 1000 + p0, count, ps), :] * here
        return carry

    lax.fori_loop(0, 6, give, 0)
    for g in range(2):
        part_lower[g] = gsource[g * V : (g + 1) * V, :].astype(BF16)
        part_upper[g] = gsource[(4 + g) * V : (5 + g) * V, :].astype(BF16)
    def gzstep(n, owner, to):
        at = span(core * HALF + y * YPART + owner * ZPART, ZPART)
        return remote(total.at[at], total.at[at], gzsent.at[n], gzarrived.at[n], device(y, to))

    @pl.when(z < 7)
    def _():
        value = y32[span(z * ZPART, ZPART), :]
        for n in range(7):
            zstep(n)[1].wait_recv()
            value = value + z_in[n].astype(F32)
        total[span(core * HALF + y * YPART + z * ZPART, ZPART), :] = value.astype(BF16)
        for n in range(7):
            gzstep(n, z, jnp.bitwise_and(z + n + 1, 7)).start()

    deal_back.forward()
    for n in range(7):
        owner = jnp.bitwise_and(z + 7 - n, 7)

        @pl.when(owner < 7)
        def _():
            gzstep(n, lax.min(owner, 6), owner).wait_recv()

    def gystep(n, owner, to):
        at = span(core * HALF + owner * YPART, YPART)
        return remote(total.at[at], total.at[at], gysent.at[n], gyarrived.at[n], device(to, z))

    def across(n, which, owner):
        at = span(which * HALF + owner * YPART, YPART)
        return remote(total.at[at], total.at[at], copy_sent.at[n], copy_arrived.at[n], partner)

    owners = [jnp.bitwise_and(y + 4 - n, 3) for n in range(4)]
    for n in range(3):
        gystep(n, y, jnp.bitwise_and(y + n + 1, 3)).start()
    across(0, core, y).start()
    rim_up = remote(part_upper, from_lower, rim_sent.at[0], rim_arrived.at[0], lax.min(me + 1, PEERS - 1))
    rim_down = remote(part_lower, from_upper, rim_sent.at[1], rim_arrived.at[1], lax.max(me - 1, 0))

    @pl.when(has_up)
    def _():
        rim_up.start()

    @pl.when(has_down)
    def _():
        rim_down.start()

    deal_back.finish()
    near32[...] = back_near[...].astype(F32)
    far32[...] = back_far[...].astype(F32)
    for n in range(6):
        out32[pl.ds(n * PEERS + core, CHIPS, stride=2), :] = near32[box_rows(core, n), :]
        out32[pl.ds(n * PEERS + 1 - core, CHIPS, stride=2), :] = far32[box_rows(core, n), :]
    for n in range(6):
        coarse_out[:, n * L : (n + 1) * L] = out32[n * PEERS : (n + 1) * PEERS, :].astype(BF16)

    def pass_on(n):
        gystep(n, owners[n + 1], owners[n + 1]).wait_recv()
        across(n + 1, core, owners[n + 1]).start()

    pass_on(0)
    pass_on(2)

    @pl.when(has_down)
    def _():
        rim_up.wait_recv()

    @pl.when(jnp.logical_not(has_down))
    def _():
        from_lower[...] = jnp.zeros_like(from_lower)

    @pl.when(has_up)
    def _():
        rim_down.wait_recv()

    @pl.when(jnp.logical_not(has_up))
    def _():
        from_upper[...] = jnp.zeros_like(from_upper)

    for g in range(2):
        value = gsource[(2 + g) * V : (3 + g) * V, :] + from_lower[g].astype(F32) + from_upper[g].astype(F32)
        value = value * jnp.broadcast_to(own[g, :, C : C + 1].astype(F32), (V, L))
        grad_features[g] = jnp.transpose(value)[:C, :].astype(BF16)

    pass_on(1)
    for n in range(4):
        across(n, 1 - core, owners[n]).wait_recv()

    @pl.when(has_up)
    def _():
        up.wait_send()
        rim_up.wait_send()

    @pl.when(has_down)
    def _():
        down.wait_send()
        rim_down.wait_send()

    deal.close()
    deal_back.close()
    pair.wait_send()
    for n in range(3):
        ysteps[n].wait_send()
        gystep(n, y, jnp.bitwise_and(y + n + 1, 3)).wait_send()
    for n in range(7):
        wanted, copy = zstep(n)

        @pl.when(wanted)
        def _():
            copy.wait_send()

    @pl.when(z < 7)
    def _():
        for n in range(7):
            gzstep(n, z, jnp.bitwise_and(z + n + 1, 7)).wait_send()

    for n in range(4):
        across(n, core, owners[n]).wait_send()


def smem():
    return pl.BlockSpec(memory_space=pltpu.SMEM)


def vmem(n):
    return [pl.BlockSpec(memory_space=pltpu.VMEM)] * n


def hbm(n):
    return [pl.BlockSpec(memory_space=pltpu.HBM)] * n


def run_section(neighbours, live_count, occupancy, features, grad_coarse, w_subm, w_down):
    dma = pltpu.SemaphoreType.DMA
    block = pltpu.VMEM((2, V, L), BF16)
    boxes = pltpu.VMEM((8 * PEERS, L), F32)
    sent = pltpu.VMEM((8 * PEERS, L), BF16)
    return pl.pallas_call(
        section_kernel,
        out_shape=(
            jax.ShapeDtypeStruct((PEERS, 6 * L), BF16),
            jax.ShapeDtypeStruct((2, C, V), BF16),
            jax.ShapeDtypeStruct((2 * HALF, L), BF16),
        ),
        in_specs=[smem(), smem(), smem()] + hbm(4),
        out_specs=tuple(vmem(3)),
        scratch_shapes=[
            pltpu.VMEM((2, C, V), BF16),
            pltpu.VMEM((PEERS, 6 * L), BF16),
            pltpu.VMEM((27, C, C), BF16),
            pltpu.VMEM((8, C, C), BF16),
            block, block, block, boxes, boxes, boxes, pltpu.VMEM((6 * PEERS, L), F32),
            sent, sent, sent, sent, sent, sent,
            pltpu.VMEM((7 * V, L), F32),
            pltpu.VMEM((2000, L), F32),
            pltpu.VMEM((1280, 9 * L), BF16),
            pltpu.VMEM((27 * L, L), BF16),
            pltpu.VMEM((9 * L, 3 * L), BF16),
            pltpu.VMEM((8 * L, L), BF16),
            pltpu.VMEM((V, V), BF16),
            pltpu.VMEM((V, V), BF16),
            pltpu.VMEM((L, 6 * L), BF16),
            pltpu.VMEM((2 * V, L), F32),
            pltpu.VMEM((1280, 3 * L), BF16),
            pltpu.VMEM((1280, 2 * L), F32),
            pltpu.VMEM((2000, L), F32),
            pltpu.VMEM((6 * V, L), F32),
            pltpu.VMEM((2 * HALF, L), F32),
            pltpu.VMEM((2 * HALF, L), BF16),
            pltpu.VMEM((HALF, L), BF16),
            pltpu.VMEM((HALF, L), F32),
            pltpu.VMEM((HALF, L), BF16),
            pltpu.VMEM((3, YPART, L), BF16),
            pltpu.VMEM((YPART, L), F32),
            pltpu.VMEM((YPART, L), BF16),
            pltpu.VMEM((7, ZPART, L), BF16),
            block, block, block, block,
            dma((4,)), dma((4,)), dma((4,)),
            dma((2,)), dma((2,)), dma((2,)), dma((2,)), dma(()), dma(()),
            dma((3,)), dma((3,)), dma((7,)), dma((7,)), dma((7,)), dma((7,)),
            dma((3,)), dma((3,)), dma((4,)), dma((4,)),
        ],
        compiler_params=pltpu.CompilerParams(
            vmem_limit_bytes=VMEM_LIMIT, collective_id=0, has_side_effects=True
        ),
    )(neighbours, live_count, occupancy, features, grad_coarse, w_subm, w_down)


def final_kernel(
    coarse_in, features_in, total_in, coarse_out, grad_features, grad_subm, grad_down,
    total, subm, down, coarse, features, load_sem, sem,
):
    def chunk(n):
        return pl.ds(9 * C * n, 9 * C)

    loads = [
        pltpu.make_async_copy(total_in.at[chunk(n)], total.at[chunk(n)], load_sem.at[n]) for n in range(3)
    ]
    loads.append(pltpu.make_async_copy(features_in, features, load_sem.at[3]))
    loads.append(pltpu.make_async_copy(coarse_in, coarse, load_sem.at[4]))
    for load in loads:
        load.start()
    copies = [
        pltpu.make_async_copy(features, grad_features, sem.at[0]),
        pltpu.make_async_copy(coarse, coarse_out, sem.at[1]),
    ]
    lane = lax.broadcasted_iota(jnp.int32, (C, L), 1)
    for k in range(35):
        quad, n = divmod(k, 4)
        if k % 12 == 0:
            loads[k // 12].wait()
        if n < 3:
            at = (3 * quad + n) * C
            value = total[at : at + C, :].astype(F32)[:, :C]
        else:
            value = jnp.zeros((C, L), F32)
            for m in range(3):
                at = (3 * quad + m) * C
                piece = pltpu.roll(total[at : at + C, :].astype(F32), 32 + 32 * m, 1)
                value = jnp.where(lane // 32 == m, piece, value)
            value = value[:, :C]
        if k < 27:
            subm[k] = value
        else:
            down[k - 27] = value
        if k in (11, 23, 26):
            part = pl.ds(k // 12 * 12, 12 if k < 26 else 3)
            copies.append(pltpu.make_async_copy(subm.at[part], grad_subm.at[part], sem.at[2 + k // 12]))
            copies[-1].start()
        if k == 11:
            for n in range(2):
                loads[3 + n].wait()
                copies[n].start()
    copies.append(pltpu.make_async_copy(down, grad_down, sem.at[5]))
    copies[-1].start()
    for copy in copies:
        copy.wait()


def run_final(coarse_in, grad_features, total):
    return pl.pallas_call(
        final_kernel,
        out_shape=(
            jax.ShapeDtypeStruct((PEERS, 6 * L), BF16),
            jax.ShapeDtypeStruct((2, C, V), BF16),
            jax.ShapeDtypeStruct((27, C, C), F32),
            jax.ShapeDtypeStruct((8, C, C), F32),
        ),
        in_specs=hbm(3),
        out_specs=tuple(hbm(4)),
        scratch_shapes=[
            pltpu.VMEM((27 * C, L), BF16),
            pltpu.VMEM((27, C, C), F32),
            pltpu.VMEM((8, C, C), F32),
            pltpu.VMEM((PEERS, 6 * L), BF16),
            pltpu.VMEM((2, C, V), BF16),
            pltpu.SemaphoreType.DMA((5,)),
            pltpu.SemaphoreType.DMA((6,)),
        ],
        compiler_params=pltpu.CompilerParams(vmem_limit_bytes=VMEM_LIMIT),
    )(coarse_in, grad_features, total)


def per_device(features, occupancy, neighbours, live_count, w_subm, w_down, grad_coarse):
    return run_final(
        *run_section(neighbours, live_count, occupancy, features, grad_coarse, w_subm, w_down)
    )


def solution(mesh):
    blocks = P(("rep", "space"), None)
    return jax.shard_map(
        per_device,
        mesh=mesh,
        in_specs=(
            P(("rep", "space"), None, None), blocks, blocks, P(("rep", "space")), P(), P(), blocks,
        ),
        out_specs=(
            blocks, P(("rep", "space"), None, None), P("rep", None, None), P("rep", None, None),
        ),
        check_vma=False,
    )
```

```python
import functools

import jax
import jax.numpy as jnp
from jax import lax
from jax.experimental import pallas as pl
from jax.experimental.pallas import tpu as pltpu
from jax.sharding import PartitionSpec as P

C, L, V = 96, 128, 512
OFFSETS = [(a, b, c) for a in (-1, 0, 1) for b in (-1, 0, 1) for c in (-1, 0, 1)]
PEERS, CHIPS, SHELL = 64, 32, 320
HALF, YPART, ZPART = 1344, 336, 48
VMEM_LIMIT = 63 * 2**20 + 2**19
F32, BF16 = jnp.float32, jnp.bfloat16
NT = (((1,), (1,)), ((), ()))


def segments(a, b, c):
    span = {-1: [(7, 0)], 0: [(i, i + 1) for i in range(8)], 1: [(0, 9)]}
    xs, ys, zs = span[a], span[b], span[c]
    face = {0: 0, 7: 64}
    if c == 0:
        return [
            (face[x] + y * 8 if x in face else 112 + x * 16 + y // 7 * 8, 1, tx * 100 + ty * 10 + 1, 1, 8)
            for x, tx in xs
            for y, ty in ys
        ]
    z, tz = zs[0]
    if b == 0:
        return [
            (face[x] + z, 8, tx * 100 + 10 + tz, 10, 8)
            if x in face
            else (208 + x * 16 + z // 7 * 8, 1, tx * 100 + 10 + tz, 10, 8)
            for x, tx in xs
        ]
    y, ty = ys[0]
    if a == 0:
        at = ty * 10 + tz
        return [
            (y * 8 + z, 1, 100 + at, 1, 1),
            (128 + y // 7 * 8 + z, 16, 200 + at, 100, 6),
            (64 + y * 8 + z, 1, 800 + at, 1, 1),
        ]
    x, tx = xs[0]
    return [(face[x] + y * 8 + z, 1, tx * 100 + ty * 10 + tz, 1, 1)]


def shell_pieces():
    pieces = [(0, 0, 1, 64), (64, 448, 1, 64)]
    for x in range(1, 7):
        pieces += [(112 + x * 16, x * 64, 1, 8), (120 + x * 16, x * 64 + 56, 1, 8)]
        pieces += [(208 + x * 16, x * 64, 8, 8), (216 + x * 16, x * 64 + 7, 8, 8)]
    return pieces


def rows(start, count, stride):
    return pl.ds(start, count) if stride == 1 else pl.ds(start, count, stride=stride)


def mask_row(words, live, g):
    lane = lax.broadcasted_iota(jnp.int32, (1, V), 1)
    word = jnp.zeros((1, V), jnp.int32)
    for w in range(16):
        word = jnp.where(lane // 32 == w, words[g, w], word)
    bit = jnp.bitwise_and(jnp.right_shift(word, jnp.bitwise_and(lane, 31)), 1)
    return jnp.where(g < live, bit, 0)


def masked_rows(features, words, live, g):
    bit = mask_row(words, live, g)
    values = jnp.where(bit > 0, features[g].astype(F32), 0.0)
    marks = jnp.broadcast_to(bit.astype(F32), (L - C, V))
    return jnp.transpose(jnp.concatenate([values, marks], axis=0))


def remote(source, target, sent, arrived, peer):
    return pltpu.make_async_remote_copy(
        src_ref=source, dst_ref=target, send_sem=sent, recv_sem=arrived,
        device_id={"space": peer}, device_id_type=pl.DeviceIdType.MESH,
    )


def greet(me):
    barrier = pltpu.get_barrier_semaphore()
    here, core = me // 2, lax.rem(me, 2)

    def tell(peer):
        pl.semaphore_signal(
            barrier, inc=1, device_id={"space": peer}, device_id_type=pl.DeviceIdType.MESH
        )

    tell(lax.rem(me + 2 * core - 1 + PEERS, PEERS))
    tell(me + 1 - 2 * core)

    def tell_chip(i, carry):
        tell(jnp.bitwise_and(here + i, CHIPS - 1) * 2 + core)
        return carry

    lax.fori_loop(1, CHIPS, tell_chip, 0)


def greeted():
    pl.semaphore_wait(pltpu.get_barrier_semaphore(), CHIPS + 1)


class Deal:
    def __init__(self, me, outbox, near, far, sent, arrived, far_sent, far_arrived):
        self.here, self.core = me // 2, lax.rem(me, 2)
        self.outbox, self.near = outbox, near
        self.sems = sent, arrived
        self.across = remote(near, far, far_sent, far_arrived, me + 1 - 2 * self.core)
        every = pl.ds(0, 16 * (CHIPS - 1))
        self.every = remote(outbox.at[every], near.at[every], sent, arrived, me + 1 - 2 * self.core)

    def tile(self, chip):
        return pl.ds(pl.multiple_of(chip * 16, 16), 16)

    def start(self):
        def send(i, carry):
            there = jnp.bitwise_and(self.here + i, CHIPS - 1)
            remote(
                self.outbox.at[self.tile(there)], self.near.at[self.tile(self.here)],
                *self.sems, there * 2 + self.core,
            ).start()
            return carry

        lax.fori_loop(1, CHIPS, send, 0)
        self.near[self.tile(self.here), :] = self.outbox[self.tile(self.here), :]

    def forward(self):
        self.every.wait_recv()
        self.across.start()

    def finish(self):
        self.across.wait_recv()

    def close(self):
        self.every.wait_send()
        self.across.wait_send()


def box_rows(core, n):
    return pl.ds(core * 8 + n, CHIPS, stride=16)


def section_kernel(
    table_hbm, live_hbm, occupancy_hbm, features_hbm, cotangent_hbm, w_subm_hbm, w_down_hbm,
    coarse_out, grad_features, total,
    table, live_ref, occupancy_ref, features, cotangent, w_subm, w_down,
    own32, own, lower, upper, box32, near32, far32, out32, outbox, near, far, back, back_near, back_far,
    source, pad, cols, wf, wb, wd, perm, permt, spread, pre, dpre3, u, gpad, gsource,
    sums32, sums16, pair_in, chip32, chip16, y_in, y32, y16, z_in,
    part_lower, part_upper, from_lower, from_upper,
    load_sem, box_sem, back_sem, halo_sent, halo_arrived,
    rim_sent, rim_arrived, pair_sent, pair_arrived, ysent, yarrived, zsent, zarrived,
    gzsent, gzarrived, gysent, gyarrived, copy_sent, copy_arrived,
):
    me = lax.axis_index("space")
    y, z, core = me // 16, lax.rem(me // 2, 8), lax.rem(me, 2)
    partner = me + 1 - 2 * core
    has_up, has_down = me < PEERS - 1, me > 0
    loads = [
        pltpu.make_async_copy(hbm, ref, load_sem.at[n])
        for n, (hbm, ref) in enumerate(
            (
                (features_hbm, features), (cotangent_hbm, cotangent), (w_subm_hbm, w_subm), (w_down_hbm, w_down),
                (table_hbm, table), (live_hbm, live_ref), (occupancy_hbm, occupancy_ref),
            )
        )
    ]
    for load in loads:
        load.start()
    greet(me)

    i = lax.broadcasted_iota(jnp.int32, (V, V), 0)
    v = lax.broadcasted_iota(jnp.int32, (V, V), 1)

    def placed(index, parts):
        return sum(((index >> a) & b) << c for a, b, c in parts)

    to_voxel = ((8, 1, 6), (7, 1, 3), (6, 1, 0), (4, 3, 7), (2, 3, 4), (0, 3, 1))
    to_child = tuple((c, b, a) for a, b, c in to_voxel)
    perm[...] = jnp.where(placed(i[:, :1], to_voxel) == v, 1.0, 0.0).astype(BF16)
    permt[...] = jnp.where(placed(i[:, :1], to_child) == v, 1.0, 0.0).astype(BF16)
    spread[...] = jnp.where(
        lax.broadcasted_iota(jnp.int32, (L, 6 * L), 1) // 8
        == lax.broadcasted_iota(jnp.int32, (L, 6 * L), 0),
        1.0, 0.0,
    ).astype(BF16)
    wf[...] = jnp.zeros_like(wf)
    wb[...] = jnp.zeros_like(wb)
    wd[...] = jnp.zeros_like(wd)
    dpre3[...] = jnp.zeros_like(dpre3)
    source[6 * SHELL :, :] = jnp.zeros((SHELL, L), F32)

    for n in (0, 4, 5, 6):
        loads[n].wait()
    for g in range(2):
        own32[g * V : (g + 1) * V, :] = masked_rows(features, occupancy_ref, live_ref[0], g)
        for s0, v0, vs, count in shell_pieces():
            source[(2 + g) * SHELL + s0 : (2 + g) * SHELL + s0 + count, :] = own32[rows(g * V + v0, count, vs), :]
        own[g] = source[(2 + g) * SHELL : (3 + g) * SHELL, :].astype(BF16)
    loads[1].wait()
    for n in range(6):
        box32[pl.ds(n, PEERS, stride=8), :] = cotangent[:, n * L : (n + 1) * L].astype(F32)
    counts = jnp.broadcast_to(live_ref[0].astype(F32), (PEERS, L))
    for n in (6, 7):
        box32[pl.ds(n, PEERS, stride=8), :] = counts
    outbox[...] = box32[...].astype(BF16)

    greeted()
    up = remote(own, lower, halo_sent.at[0], halo_arrived.at[0], lax.min(me + 1, PEERS - 1))
    down = remote(own, upper, halo_sent.at[1], halo_arrived.at[1], lax.max(me - 1, 0))

    @pl.when(has_up)
    def _():
        up.start()

    @pl.when(has_down)
    def _():
        down.start()

    deal = Deal(me, outbox, near, far, *(box_sem.at[n] for n in range(4)))
    deal.start()

    loads[2].wait()
    loads[3].wait()
    for k in range(27):
        a, bc = divmod(k, 9)
        w = w_subm[k]
        wf[k * L : k * L + C, :C] = w
        wb[bc * L : bc * L + C, a * L : a * L + C] = w
    for j in range(8):
        wd[j * L : j * L + C, :C] = w_down[j]


    @pl.when(has_down)
    def _():
        up.wait_recv()

    @pl.when(jnp.logical_not(has_down))
    def _():
        lower[...] = jnp.zeros_like(lower)

    @pl.when(has_up)
    def _():
        down.wait_recv()

    @pl.when(jnp.logical_not(has_up))
    def _():
        upper[...] = jnp.zeros_like(upper)

    for g in range(2):
        source[g * SHELL : (g + 1) * SHELL, :] = lower[g].astype(F32)
        source[(4 + g) * SHELL : (5 + g) * SHELL, :] = upper[g].astype(F32)

    for g in range(2):
        for k, offset in enumerate(OFFSETS):
            if k == 13:
                continue
            base = table[g, k] * SHELL
            for s0, ss, p0, ps, count in segments(*offset):
                pad[rows(g * 1000 + p0, count, ps), :] = source[rows(base + s0, count, ss), :]

        for x in range(8):
            for yy in range(8):
                pad[pl.ds(g * 1000 + x * 100 + yy * 10 + 111, 8), :] = own32[pl.ds(g * V + x * 64 + yy * 8, 8), :]

    def columns(gx, carry):
        for b in range(3):
            for c in range(3):
                piece = jnp.concatenate(
                    [pad[pl.ds(gx * 100 + (yy + b) * 10 + c, 8), :] for yy in range(8)], axis=0
                )
                bc = 3 * b + c
                cols[pl.ds(pl.multiple_of(gx * 64, 64), 64), bc * L : (bc + 1) * L] = piece.astype(BF16)
        return carry

    lax.fori_loop(0, 20, columns, 0)

    for g in range(2):
        acc = jnp.zeros((V, L), F32)
        for a in range(3):
            acc += jnp.dot(
                cols[g * 640 + a * 64 : g * 640 + a * 64 + V, :],
                wf[a * 9 * L : (a + 1) * 9 * L, :],
                preferred_element_type=F32,
            )
        pre[g * V : (g + 1) * V, :] = acc

    deal.forward()
    live = live_ref[0]
    s, q = 0.7978845608028654, 0.044715
    slopes, hiddens = [], []
    for g in range(2):
        mask = jnp.broadcast_to(own32[g * V : (g + 1) * V, C : C + 1], (V, L))
        tt = pre[g * V : (g + 1) * V, :]
        th = jnp.tanh(s * (tt + q * tt * tt * tt))
        hidden = 0.5 * tt * (1.0 + th) * mask
        slopes.append((0.5 * (1.0 + th) + 0.5 * tt * (1.0 - th * th) * (s * (1.0 + 3.0 * q * tt * tt))) * mask)
        hiddens.append(jnp.where(lax.broadcasted_iota(jnp.int32, (V, L), 1) < C, hidden, mask).astype(BF16))
    both = jnp.dot(perm[...], jnp.concatenate(hiddens, axis=1), preferred_element_type=F32)
    kids = []
    cmask = jnp.zeros((2 * 64, L), F32)
    coarse = jnp.zeros((2 * 64, L), F32)
    for j in range(8):
        kid = jnp.concatenate([both[j * 64 : (j + 1) * 64, :L], both[j * 64 : (j + 1) * 64, L:]], axis=0)
        cmask = jnp.maximum(cmask, kid)
        kids.append(kid.astype(BF16))
        coarse += jnp.dot(kids[j], wd[j * L : (j + 1) * L, :], preferred_element_type=F32)
    cmask = jnp.broadcast_to(cmask[:, C : C + 1], (2 * 64, L))

    deal.finish()
    near32[...] = near[...].astype(F32)
    far32[...] = far[...].astype(F32)

    def lines(n):
        return jnp.concatenate([near32[box_rows(core, n), :], far32[box_rows(core, n), :]], axis=0)

    def peers(dim, shape):
        order = lax.broadcasted_iota(jnp.int32, shape, dim)
        return jnp.where(order < CHIPS, 2 * order + core, 2 * (order - CHIPS) + 1 - core)

    boxes = jnp.concatenate([lines(n) for n in range(6)], axis=1).astype(BF16)
    below = jnp.where(peers(0, (PEERS, L)) < me, lines(6), 0.0)
    first = jnp.sum(below, axis=0, keepdims=True).astype(jnp.int32)[:, :64]
    row = lax.broadcasted_iota(jnp.int32, (128, 64), 0)
    block, piece = row >> 6, (row >> 3) & 7
    holder = jnp.bitwise_and(jnp.broadcast_to(first, (128, 64)) + block, 7) * 8 + piece
    chosen = jnp.where((holder == peers(1, (128, 64))) & (block < live), 1.0, 0.0).astype(BF16)
    pick = (
        lax.broadcasted_iota(jnp.int32, (128, 6 * L), 1) & 7
        == lax.broadcasted_iota(jnp.int32, (128, 6 * L), 0) & 7
    )
    dz = jnp.dot(chosen, boxes, preferred_element_type=F32)
    dz = jnp.where(pick, dz, 0.0).astype(BF16)
    dz = lax.dot_general(dz, spread[...], NT, preferred_element_type=F32)
    dz = jnp.where(cmask > 0, dz, 0.0)
    dzt = jnp.transpose(dz).astype(BF16)
    dz = dz.astype(BF16)
    dh = [
        lax.dot_general(dz, wd[j * L : (j + 1) * L, :], NT, preferred_element_type=F32) for j in range(8)
    ]
    parts = []
    for g in range(2):
        part = jnp.concatenate([piece[g * 64 : (g + 1) * 64] for piece in dh], axis=0)
        high = part.astype(BF16)
        parts += [high, (part - high.astype(F32)).astype(BF16)]
    dh = jnp.dot(permt[...], jnp.concatenate(parts, axis=1), preferred_element_type=F32)
    for g in range(2):
        dpre = slopes[g] * (dh[:, 2 * g * L : (2 * g + 1) * L] + dh[:, (2 * g + 1) * L : (2 * g + 2) * L])
        dpre16 = dpre.astype(BF16)
        for a in range(3):
            dpre3[g * 640 + a * 64 : g * 640 + a * 64 + V, a * L : (a + 1) * L] = dpre16
        pre[g * V : (g + 1) * V, :] = dpre
    down_sums = jnp.dot(dzt, jnp.concatenate(kids, axis=1), preferred_element_type=F32)

    lane = lax.broadcasted_iota(jnp.int32, (C, L), 1)
    held = {}

    def keep(k, product):
        held[k % 4] = jnp.transpose(product)[:C]
        if k % 4 == 3 or k == 34:
            last = held.get(3)
            for n in range(3):
                slab = held[n]
                if last is not None:
                    slab = jnp.where(lane < C, slab, pltpu.roll(last, C - 32 * n, 1))
                at = (3 * (k // 4) + n) * C
                sums32[at : at + C, :] = slab
                sums16[at : at + C, :] = slab.astype(BF16)
            held.clear()

    dt = jnp.transpose(pre[...]).astype(BF16)
    for a in range(3):
        for bc in range(0, 9, 2):
            lanes = slice(bc * L, min(bc + 2, 9) * L)
            value = jnp.dot(
                dt[:, :V], cols[a * 64 : a * 64 + V, lanes], preferred_element_type=F32
            ) + jnp.dot(
                dt[:, V:], cols[640 + a * 64 : 640 + a * 64 + V, lanes], preferred_element_type=F32
            )
            for n in range(min(2, 9 - bc)):
                keep(a * 9 + bc + n, value[:, n * L : (n + 1) * L])
    for j in range(8):
        keep(27 + j, down_sums[:, j * L : (j + 1) * L])
    sums32[27 * C :, :] = jnp.zeros((C, L), F32)
    sums16[27 * C :, :] = jnp.zeros((C, L), BF16)

    def span(at, count):
        return pl.ds(pl.multiple_of(at, 16), count)

    def device(yy, zz):
        return yy * 16 + zz * 2 + core

    pair = remote(sums16.at[span((1 - core) * HALF, HALF)], pair_in, pair_sent, pair_arrived, partner)
    pair.start()
    deal_back = Deal(me, back, back_near, back_far, *(back_sem.at[n] for n in range(4)))
    flat = jnp.dot((coarse * cmask).astype(BF16), spread[...], preferred_element_type=F32)
    flat = jnp.where(pick, flat, 0.0).astype(BF16)
    dealt = lax.dot_general(chosen, flat, (((0,), (0,)), ((), ())), preferred_element_type=F32)
    for n in range(6):
        box32[box_rows(core, n), :] = dealt[:CHIPS, n * L : (n + 1) * L]
        box32[box_rows(1 - core, n), :] = dealt[CHIPS:, n * L : (n + 1) * L]
    back[...] = box32[...].astype(BF16)
    deal_back.start()
    pair.wait_recv()
    value = sums32[span(core * HALF, HALF), :] + pair_in[...].astype(F32)
    chip32[...] = value
    chip16[...] = value.astype(BF16)
    ysteps = []
    for n in range(3):
        yy = jnp.bitwise_and(y + n + 1, 3)
        ysteps.append(
            remote(chip16.at[span(yy * YPART, YPART)], y_in.at[n], ysent.at[n], yarrived.at[n], device(yy, z))
        )
        ysteps[n].start()

    gpad[...] = jnp.zeros_like(gpad)
    def pad_gradient(bc):
        width = min(2, 9 - bc)
        u[:, : width * L] = lax.dot_general(
            dpre3[...], wb[bc * L : (bc + width) * L, :], NT, preferred_element_type=F32
        )

        def add(gx, carry):
            for n in range(width):
                b, c = divmod(bc + n, 3)
                for yy in range(8):
                    at = pl.ds(gx * 100 + (yy + b) * 10 + c, 8)
                    gpad[at, :] += u[pl.ds(pl.multiple_of(gx * 64 + yy * 8, 8), 8), n * L : (n + 1) * L]
            return carry

        lax.fori_loop(0, 20, add, 0)

    for bc in (0, 2, 4):
        pad_gradient(bc)

    value = chip32[span(y * YPART, YPART), :]
    for n in range(3):
        ysteps[n].wait_recv()
        value = value + y_in[n].astype(F32)
    y32[...] = value
    y16[...] = value.astype(BF16)

    def zstep(n):
        zz = jnp.bitwise_and(z + n + 1, 7)
        at = span(lax.min(zz, 6) * ZPART, ZPART)
        return zz < 7, remote(y16.at[at], z_in.at[n], zsent.at[n], zarrived.at[n], device(y, zz))

    for n in range(7):
        wanted, copy = zstep(n)

        @pl.when(wanted)
        def _():
            copy.start()

    for bc in (6, 8):
        pad_gradient(bc)

    gsource[...] = jnp.zeros_like(gsource)

    def give(n, carry):
        for g in range(2):
            for k, offset in enumerate(OFFSETS):
                if k != 13:
                    here = jnp.where(table[g, k] == n, 1.0, 0.0)
                    for s0, ss, p0, ps, count in segments(*offset):
                        at = rows(n * SHELL + s0, count, ss)
                        gsource[at, :] += gpad[rows(g * 1000 + p0, count, ps), :] * here
        return carry

    lax.fori_loop(0, 6, give, 0)
    for g in range(2):
        part_lower[g] = gsource[g * SHELL : (g + 1) * SHELL, :].astype(BF16)
        part_upper[g] = gsource[(4 + g) * SHELL : (5 + g) * SHELL, :].astype(BF16)
    def gzstep(n, owner, to):
        at = span(core * HALF + y * YPART + owner * ZPART, ZPART)
        return remote(total.at[at], total.at[at], gzsent.at[n], gzarrived.at[n], device(y, to))

    @pl.when(z < 7)
    def _():
        value = y32[span(z * ZPART, ZPART), :]
        for n in range(7):
            zstep(n)[1].wait_recv()
            value = value + z_in[n].astype(F32)
        total[span(core * HALF + y * YPART + z * ZPART, ZPART), :] = value.astype(BF16)
        for n in range(7):
            gzstep(n, z, jnp.bitwise_and(z + n + 1, 7)).start()

    deal_back.forward()
    for n in range(7):
        owner = jnp.bitwise_and(z + 7 - n, 7)

        @pl.when(owner < 7)
        def _():
            gzstep(n, lax.min(owner, 6), owner).wait_recv()

    def gystep(n, owner, to):
        at = span(core * HALF + owner * YPART, YPART)
        return remote(total.at[at], total.at[at], gysent.at[n], gyarrived.at[n], device(to, z))

    def across(n, which, owner):
        at = span(which * HALF + owner * YPART, YPART)
        return remote(total.at[at], total.at[at], copy_sent.at[n], copy_arrived.at[n], partner)

    owners = [jnp.bitwise_and(y + 4 - n, 3) for n in range(4)]
    for n in range(3):
        gystep(n, y, jnp.bitwise_and(y + n + 1, 3)).start()
    across(0, core, y).start()
    rim_up = remote(part_upper, from_lower, rim_sent.at[0], rim_arrived.at[0], lax.min(me + 1, PEERS - 1))
    rim_down = remote(part_lower, from_upper, rim_sent.at[1], rim_arrived.at[1], lax.max(me - 1, 0))

    @pl.when(has_up)
    def _():
        rim_up.start()

    @pl.when(has_down)
    def _():
        rim_down.start()

    deal_back.finish()
    near32[...] = back_near[...].astype(F32)
    far32[...] = back_far[...].astype(F32)
    for n in range(6):
        out32[pl.ds(n * PEERS + core, CHIPS, stride=2), :] = near32[box_rows(core, n), :]
        out32[pl.ds(n * PEERS + 1 - core, CHIPS, stride=2), :] = far32[box_rows(core, n), :]
    for n in range(6):
        coarse_out[:, n * L : (n + 1) * L] = out32[n * PEERS : (n + 1) * PEERS, :].astype(BF16)

    def pass_on(n):
        gystep(n, owners[n + 1], owners[n + 1]).wait_recv()
        across(n + 1, core, owners[n + 1]).start()

    pass_on(0)
    pass_on(2)

    @pl.when(has_down)
    def _():
        rim_up.wait_recv()

    @pl.when(jnp.logical_not(has_down))
    def _():
        from_lower[...] = jnp.zeros_like(from_lower)

    @pl.when(has_up)
    def _():
        rim_down.wait_recv()

    @pl.when(jnp.logical_not(has_up))
    def _():
        from_upper[...] = jnp.zeros_like(from_upper)

    for g in range(2):
        shell = gsource[(2 + g) * SHELL : (3 + g) * SHELL, :]
        shell = shell + from_lower[g].astype(F32) + from_upper[g].astype(F32)
        for x in range(8):
            for yy in range(8):
                pre[pl.ds(g * V + x * 64 + yy * 8, 8), :] = gpad[pl.ds(g * 1000 + x * 100 + yy * 10 + 111, 8), :]
        for s0, v0, vs, count in shell_pieces():
            pre[rows(g * V + v0, count, vs), :] += shell[s0 : s0 + count]
        value = pre[g * V : (g + 1) * V, :]
        value = value * jnp.broadcast_to(own32[g * V : (g + 1) * V, C : C + 1], (V, L))
        grad_features[g] = jnp.transpose(value)[:C, :].astype(BF16)

    pass_on(1)
    for n in range(4):
        across(n, 1 - core, owners[n]).wait_recv()

    @pl.when(has_up)
    def _():
        up.wait_send()
        rim_up.wait_send()

    @pl.when(has_down)
    def _():
        down.wait_send()
        rim_down.wait_send()

    deal.close()
    deal_back.close()
    pair.wait_send()
    for n in range(3):
        ysteps[n].wait_send()
        gystep(n, y, jnp.bitwise_and(y + n + 1, 3)).wait_send()
    for n in range(7):
        wanted, copy = zstep(n)

        @pl.when(wanted)
        def _():
            copy.wait_send()

    @pl.when(z < 7)
    def _():
        for n in range(7):
            gzstep(n, z, jnp.bitwise_and(z + n + 1, 7)).wait_send()

    for n in range(4):
        across(n, core, owners[n]).wait_send()


def vmem(n):
    return [pl.BlockSpec(memory_space=pltpu.VMEM)] * n


def hbm(n):
    return [pl.BlockSpec(memory_space=pltpu.HBM)] * n


def run_section(neighbours, live_count, occupancy, features, grad_coarse, w_subm, w_down):
    dma = pltpu.SemaphoreType.DMA
    block = pltpu.VMEM((2, SHELL, L), BF16)
    boxes = pltpu.VMEM((8 * PEERS, L), F32)
    sent = pltpu.VMEM((8 * PEERS, L), BF16)
    return pl.pallas_call(
        section_kernel,
        out_shape=(
            jax.ShapeDtypeStruct((PEERS, 6 * L), BF16),
            jax.ShapeDtypeStruct((2, C, V), BF16),
            jax.ShapeDtypeStruct((2 * HALF, L), BF16),
        ),
        in_specs=hbm(7),
        out_specs=tuple(vmem(3)),
        scratch_shapes=[
            pltpu.SMEM((2, 27), jnp.int32),
            pltpu.SMEM((1,), jnp.int32),
            pltpu.SMEM((2, 16), jnp.int32),
            pltpu.VMEM((2, C, V), BF16),
            pltpu.VMEM((PEERS, 6 * L), BF16),
            pltpu.VMEM((27, C, C), BF16),
            pltpu.VMEM((8, C, C), BF16),
            pltpu.VMEM((2 * V, L), F32),
            block, block, block, boxes, boxes, boxes, pltpu.VMEM((6 * PEERS, L), F32),
            sent, sent, sent, sent, sent, sent,
            pltpu.VMEM((7 * SHELL, L), F32),
            pltpu.VMEM((2000, L), F32),
            pltpu.VMEM((1280, 9 * L), BF16),
            pltpu.VMEM((27 * L, L), BF16),
            pltpu.VMEM((9 * L, 3 * L), BF16),
            pltpu.VMEM((8 * L, L), BF16),
            pltpu.VMEM((V, V), BF16),
            pltpu.VMEM((V, V), BF16),
            pltpu.VMEM((L, 6 * L), BF16),
            pltpu.VMEM((2 * V, L), F32),
            pltpu.VMEM((1280, 3 * L), BF16),
            pltpu.VMEM((1280, 2 * L), F32),
            pltpu.VMEM((2000, L), F32),
            pltpu.VMEM((6 * SHELL, L), F32),
            pltpu.VMEM((2 * HALF, L), F32),
            pltpu.VMEM((2 * HALF, L), BF16),
            pltpu.VMEM((HALF, L), BF16),
            pltpu.VMEM((HALF, L), F32),
            pltpu.VMEM((HALF, L), BF16),
            pltpu.VMEM((3, YPART, L), BF16),
            pltpu.VMEM((YPART, L), F32),
            pltpu.VMEM((YPART, L), BF16),
            pltpu.VMEM((7, ZPART, L), BF16),
            block, block, block, block,
            dma((7,)), dma((4,)), dma((4,)),
            dma((2,)), dma((2,)), dma((2,)), dma((2,)), dma(()), dma(()),
            dma((3,)), dma((3,)), dma((7,)), dma((7,)), dma((7,)), dma((7,)),
            dma((3,)), dma((3,)), dma((4,)), dma((4,)),
        ],
        compiler_params=pltpu.CompilerParams(
            vmem_limit_bytes=VMEM_LIMIT, collective_id=0, has_side_effects=True
        ),
    )(neighbours, live_count, occupancy, features, grad_coarse, w_subm, w_down)


def final_kernel(
    coarse_in, features_in, total_in, coarse_out, grad_features, grad_subm, grad_down,
    total, subm, down, coarse, features, load_sem, sem,
):
    def chunk(n):
        return pl.ds(9 * C * n, 9 * C)

    loads = [
        pltpu.make_async_copy(total_in.at[chunk(n)], total.at[chunk(n)], load_sem.at[n]) for n in range(3)
    ]
    loads.append(pltpu.make_async_copy(features_in, features, load_sem.at[3]))
    loads.append(pltpu.make_async_copy(coarse_in, coarse, load_sem.at[4]))
    for load in loads:
        load.start()
    copies = [
        pltpu.make_async_copy(features, grad_features, sem.at[0]),
        pltpu.make_async_copy(coarse, coarse_out, sem.at[1]),
    ]
    lane = lax.broadcasted_iota(jnp.int32, (C, L), 1)
    for k in range(35):
        quad, n = divmod(k, 4)
        if k % 12 == 0:
            loads[k // 12].wait()
        if n < 3:
            at = (3 * quad + n) * C
            value = total[at : at + C, :].astype(F32)[:, :C]
        else:
            value = jnp.zeros((C, L), F32)
            for m in range(3):
                at = (3 * quad + m) * C
                piece = pltpu.roll(total[at : at + C, :].astype(F32), 32 + 32 * m, 1)
                value = jnp.where(lane // 32 == m, piece, value)
            value = value[:, :C]
        if k < 27:
            subm[k] = value
        else:
            down[k - 27] = value
        if k in (11, 23, 26):
            part = pl.ds(k // 12 * 12, 12 if k < 26 else 3)
            copies.append(pltpu.make_async_copy(subm.at[part], grad_subm.at[part], sem.at[2 + k // 12]))
            copies[-1].start()
        if k == 11:
            for n in range(2):
                loads[3 + n].wait()
                copies[n].start()
    copies.append(pltpu.make_async_copy(down, grad_down, sem.at[5]))
    copies[-1].start()
    for copy in copies:
        copy.wait()


def run_final(coarse_in, grad_features, total):
    return pl.pallas_call(
        final_kernel,
        out_shape=(
            jax.ShapeDtypeStruct((PEERS, 6 * L), BF16),
            jax.ShapeDtypeStruct((2, C, V), BF16),
            jax.ShapeDtypeStruct((27, C, C), F32),
            jax.ShapeDtypeStruct((8, C, C), F32),
        ),
        in_specs=hbm(3),
        out_specs=tuple(hbm(4)),
        scratch_shapes=[
            pltpu.VMEM((27 * C, L), BF16),
            pltpu.VMEM((27, C, C), F32),
            pltpu.VMEM((8, C, C), F32),
            pltpu.VMEM((PEERS, 6 * L), BF16),
            pltpu.VMEM((2, C, V), BF16),
            pltpu.SemaphoreType.DMA((5,)),
            pltpu.SemaphoreType.DMA((6,)),
        ],
        compiler_params=pltpu.CompilerParams(vmem_limit_bytes=VMEM_LIMIT),
    )(coarse_in, grad_features, total)


def per_device(features, occupancy, neighbours, live_count, w_subm, w_down, grad_coarse):
    return run_final(
        *run_section(neighbours, live_count, occupancy, features, grad_coarse, w_subm, w_down)
    )


def solution(mesh):
    blocks = P(("rep", "space"), None)
    return jax.shard_map(
        per_device,
        mesh=mesh,
        in_specs=(
            P(("rep", "space"), None, None), blocks, blocks, P(("rep", "space")), P(), P(), blocks,
        ),
        out_specs=(
            blocks, P(("rep", "space"), None, None), P("rep", None, None), P("rep", None, None),
        ),
        check_vma=False,
    )
```

```python
import functools

import jax
import jax.numpy as jnp
from jax import lax
from jax.experimental import pallas as pl
from jax.experimental.pallas import tpu as pltpu
from jax.sharding import PartitionSpec as P

C, L, V = 96, 128, 512
OFFSETS = [(a, b, c) for a in (-1, 0, 1) for b in (-1, 0, 1) for c in (-1, 0, 1)]
PEERS, CHIPS, SHELL = 64, 32, 320
YORDER, ZORDER = (1, 0, 2), (3, 2, 4, 1, 5, 0, 6)
HALF, YPART, ZPART = 1344, 336, 48
VMEM_LIMIT = 63 * 2**20 + 2**19
F32, BF16 = jnp.float32, jnp.bfloat16
NT = (((1,), (1,)), ((), ()))


def segments(a, b, c):
    span = {-1: [(7, 0)], 0: [(i, i + 1) for i in range(8)], 1: [(0, 9)]}
    xs, ys, zs = span[a], span[b], span[c]
    face = {0: 0, 7: 64}
    if c == 0:
        return [
            (face[x] + y * 8 if x in face else 112 + x * 16 + y // 7 * 8, 1, tx * 100 + ty * 10 + 1, 1, 8)
            for x, tx in xs
            for y, ty in ys
        ]
    z, tz = zs[0]
    if b == 0:
        return [
            (face[x] + z, 8, tx * 100 + 10 + tz, 10, 8)
            if x in face
            else (208 + x * 16 + z // 7 * 8, 1, tx * 100 + 10 + tz, 10, 8)
            for x, tx in xs
        ]
    y, ty = ys[0]
    if a == 0:
        at = ty * 10 + tz
        return [
            (y * 8 + z, 1, 100 + at, 1, 1),
            (128 + y // 7 * 8 + z, 16, 200 + at, 100, 6),
            (64 + y * 8 + z, 1, 800 + at, 1, 1),
        ]
    x, tx = xs[0]
    return [(face[x] + y * 8 + z, 1, tx * 100 + ty * 10 + tz, 1, 1)]


def shell_pieces():
    pieces = [(0, 0, 1, 64), (64, 448, 1, 64)]
    for x in range(1, 7):
        pieces += [(112 + x * 16, x * 64, 1, 8), (120 + x * 16, x * 64 + 56, 1, 8)]
        pieces += [(208 + x * 16, x * 64, 8, 8), (216 + x * 16, x * 64 + 7, 8, 8)]
    return pieces


def rows(start, count, stride):
    return pl.ds(start, count) if stride == 1 else pl.ds(start, count, stride=stride)


def mask_row(words, live, g):
    lane = lax.broadcasted_iota(jnp.int32, (1, V), 1)
    word = jnp.zeros((1, V), jnp.int32)
    for w in range(16):
        word = jnp.where(lane // 32 == w, words[g, w], word)
    bit = jnp.bitwise_and(jnp.right_shift(word, jnp.bitwise_and(lane, 31)), 1)
    return jnp.where(g < live, bit, 0)


def masked_rows(features, words, live, g):
    bit = mask_row(words, live, g)
    values = jnp.where(bit > 0, features[g].astype(F32), 0.0)
    marks = jnp.broadcast_to(bit.astype(F32), (L - C, V))
    return jnp.transpose(jnp.concatenate([values, marks], axis=0))


def remote(source, target, sent, arrived, peer):
    return pltpu.make_async_remote_copy(
        src_ref=source, dst_ref=target, send_sem=sent, recv_sem=arrived,
        device_id={"space": peer}, device_id_type=pl.DeviceIdType.MESH,
    )


def far_first():
    offsets = [(dy, dz) for dy in range(4) for dz in range(8) if dy or dz]
    return sorted(offsets, key=lambda at: -min(at[0], 4 - at[0]) - min(at[1], 8 - at[1]))


def chip_at(here, offset):
    dy, dz = offset
    return jnp.bitwise_and(here + 8 * dy, CHIPS - 8) + jnp.bitwise_and(here + dz, 7)


def greet(me):
    barrier = pltpu.get_barrier_semaphore()
    here, core = me // 2, lax.rem(me, 2)

    def tell(peer):
        pl.semaphore_signal(
            barrier, inc=1, device_id={"space": peer}, device_id_type=pl.DeviceIdType.MESH
        )

    for offset in far_first():
        tell(chip_at(here, offset) * 2 + core)
    tell(lax.rem(me + 2 * core - 1 + PEERS, PEERS))
    tell(me + 1 - 2 * core)


def greeted():
    pl.semaphore_wait(pltpu.get_barrier_semaphore(), CHIPS + 1)


class Deal:
    def __init__(self, me, outbox, near, far, sent, arrived, far_sent, far_arrived):
        self.here, self.core = me // 2, lax.rem(me, 2)
        self.outbox, self.near = outbox, near
        self.sems = sent, arrived
        self.across = remote(near, far, far_sent, far_arrived, me + 1 - 2 * self.core)
        every = pl.ds(0, 16 * (CHIPS - 1))
        self.every = remote(outbox.at[every], near.at[every], sent, arrived, me + 1 - 2 * self.core)

    def tile(self, chip):
        return pl.ds(pl.multiple_of(chip * 16, 16), 16)

    def start(self):
        for offset in far_first():
            there = chip_at(self.here, offset)
            remote(
                self.outbox.at[self.tile(there)], self.near.at[self.tile(self.here)],
                *self.sems, there * 2 + self.core,
            ).start()
        self.near[self.tile(self.here), :] = self.outbox[self.tile(self.here), :]

    def forward(self):
        self.every.wait_recv()
        self.across.start()

    def finish(self):
        self.across.wait_recv()

    def close(self):
        self.every.wait_send()
        self.across.wait_send()


def box_rows(core, n):
    return pl.ds(core * 8 + n, CHIPS, stride=16)


def section_kernel(
    table_hbm, live_hbm, occupancy_hbm, features_hbm, cotangent_hbm, w_subm_hbm, w_down_hbm,
    coarse_out, grad_features, total,
    table, live_ref, occupancy_ref, features, cotangent, w_subm, w_down,
    own32, own, lower, upper, box32, near32, far32, out32, outbox, near, far, back, back_near, back_far,
    source, pad, cols, wf, wb, wd, perm, permt, spread, pre, dpre3, u, gpad, gsource,
    sums32, sums16, pair_in, chip32, chip16, y_in, y32, y16, z_in,
    part_lower, part_upper, from_lower, from_upper,
    load_sem, box_sem, back_sem, halo_sent, halo_arrived,
    rim_sent, rim_arrived, pair_sent, pair_arrived, ysent, yarrived, zsent, zarrived,
    gzsent, gzarrived, gysent, gyarrived, copy_sent, copy_arrived,
):
    me = lax.axis_index("space")
    y, z, core = me // 16, lax.rem(me // 2, 8), lax.rem(me, 2)
    partner = me + 1 - 2 * core
    has_up, has_down = me < PEERS - 1, me > 0
    loads = [
        pltpu.make_async_copy(hbm, ref, load_sem.at[n])
        for n, (hbm, ref) in enumerate(
            (
                (features_hbm, features), (cotangent_hbm, cotangent), (w_subm_hbm, w_subm), (w_down_hbm, w_down),
                (table_hbm, table), (live_hbm, live_ref), (occupancy_hbm, occupancy_ref),
            )
        )
    ]
    for load in loads:
        load.start()
    greet(me)

    i = lax.broadcasted_iota(jnp.int32, (V, V), 0)
    v = lax.broadcasted_iota(jnp.int32, (V, V), 1)

    def placed(index, parts):
        return sum(((index >> a) & b) << c for a, b, c in parts)

    to_voxel = ((8, 1, 6), (7, 1, 3), (6, 1, 0), (4, 3, 7), (2, 3, 4), (0, 3, 1))
    to_child = tuple((c, b, a) for a, b, c in to_voxel)
    perm[...] = jnp.where(placed(i[:, :1], to_voxel) == v, 1.0, 0.0).astype(BF16)
    permt[...] = jnp.where(placed(i[:, :1], to_child) == v, 1.0, 0.0).astype(BF16)
    spread[...] = jnp.where(
        lax.broadcasted_iota(jnp.int32, (L, 6 * L), 1) // 8
        == lax.broadcasted_iota(jnp.int32, (L, 6 * L), 0),
        1.0, 0.0,
    ).astype(BF16)
    wf[...] = jnp.zeros_like(wf)
    wb[...] = jnp.zeros_like(wb)
    wd[...] = jnp.zeros_like(wd)
    dpre3[...] = jnp.zeros_like(dpre3)
    source[6 * SHELL :, :] = jnp.zeros((SHELL, L), F32)

    for n in (0, 4, 5, 6):
        loads[n].wait()
    for g in range(2):
        own32[g * V : (g + 1) * V, :] = masked_rows(features, occupancy_ref, live_ref[0], g)
        for s0, v0, vs, count in shell_pieces():
            source[(2 + g) * SHELL + s0 : (2 + g) * SHELL + s0 + count, :] = own32[rows(g * V + v0, count, vs), :]
        own[g] = source[(2 + g) * SHELL : (3 + g) * SHELL, :].astype(BF16)
    loads[1].wait()
    for n in range(6):
        box32[pl.ds(n, PEERS, stride=8), :] = cotangent[:, n * L : (n + 1) * L].astype(F32)
    counts = jnp.broadcast_to(live_ref[0].astype(F32), (PEERS, L))
    for n in (6, 7):
        box32[pl.ds(n, PEERS, stride=8), :] = counts
    outbox[...] = box32[...].astype(BF16)

    greeted()
    up = remote(own, lower, halo_sent.at[0], halo_arrived.at[0], lax.min(me + 1, PEERS - 1))
    down = remote(own, upper, halo_sent.at[1], halo_arrived.at[1], lax.max(me - 1, 0))

    @pl.when(has_up)
    def _():
        up.start()

    @pl.when(has_down)
    def _():
        down.start()

    deal = Deal(me, outbox, near, far, *(box_sem.at[n] for n in range(4)))
    deal.start()

    loads[2].wait()
    loads[3].wait()
    for k in range(27):
        a, bc = divmod(k, 9)
        w = w_subm[k]
        wf[k * L : k * L + C, :C] = w
        wb[bc * L : bc * L + C, a * L : a * L + C] = w
    for j in range(8):
        wd[j * L : j * L + C, :C] = w_down[j]


    @pl.when(has_down)
    def _():
        up.wait_recv()

    @pl.when(jnp.logical_not(has_down))
    def _():
        lower[...] = jnp.zeros_like(lower)

    @pl.when(has_up)
    def _():
        down.wait_recv()

    @pl.when(jnp.logical_not(has_up))
    def _():
        upper[...] = jnp.zeros_like(upper)

    for g in range(2):
        source[g * SHELL : (g + 1) * SHELL, :] = lower[g].astype(F32)
        source[(4 + g) * SHELL : (5 + g) * SHELL, :] = upper[g].astype(F32)

    for g in range(2):
        for k, offset in enumerate(OFFSETS):
            if k == 13:
                continue
            base = table[g, k] * SHELL
            for s0, ss, p0, ps, count in segments(*offset):
                pad[rows(g * 1000 + p0, count, ps), :] = source[rows(base + s0, count, ss), :]

        for x in range(8):
            for yy in range(8):
                pad[pl.ds(g * 1000 + x * 100 + yy * 10 + 111, 8), :] = own32[pl.ds(g * V + x * 64 + yy * 8, 8), :]

    def columns(gx, carry):
        for b in range(3):
            for c in range(3):
                piece = jnp.concatenate(
                    [pad[pl.ds(gx * 100 + (yy + b) * 10 + c, 8), :] for yy in range(8)], axis=0
                )
                bc = 3 * b + c
                cols[pl.ds(pl.multiple_of(gx * 64, 64), 64), bc * L : (bc + 1) * L] = piece.astype(BF16)
        return carry

    lax.fori_loop(0, 20, columns, 0)

    for g in range(2):
        acc = jnp.zeros((V, L), F32)
        for a in range(3):
            acc += jnp.dot(
                cols[g * 640 + a * 64 : g * 640 + a * 64 + V, :],
                wf[a * 9 * L : (a + 1) * 9 * L, :],
                preferred_element_type=F32,
            )
        pre[g * V : (g + 1) * V, :] = acc

    deal.forward()
    live = live_ref[0]
    s, q = 0.7978845608028654, 0.044715
    slopes, hiddens = [], []
    for g in range(2):
        mask = jnp.broadcast_to(own32[g * V : (g + 1) * V, C : C + 1], (V, L))
        tt = pre[g * V : (g + 1) * V, :]
        th = jnp.tanh(s * (tt + q * tt * tt * tt))
        hidden = 0.5 * tt * (1.0 + th) * mask
        slopes.append((0.5 * (1.0 + th) + 0.5 * tt * (1.0 - th * th) * (s * (1.0 + 3.0 * q * tt * tt))) * mask)
        hiddens.append(jnp.where(lax.broadcasted_iota(jnp.int32, (V, L), 1) < C, hidden, mask).astype(BF16))
    both = jnp.dot(perm[...], jnp.concatenate(hiddens, axis=1), preferred_element_type=F32)
    kids = []
    cmask = jnp.zeros((2 * 64, L), F32)
    coarse = jnp.zeros((2 * 64, L), F32)
    for j in range(8):
        kid = jnp.concatenate([both[j * 64 : (j + 1) * 64, :L], both[j * 64 : (j + 1) * 64, L:]], axis=0)
        cmask = jnp.maximum(cmask, kid)
        kids.append(kid.astype(BF16))
        coarse += jnp.dot(kids[j], wd[j * L : (j + 1) * L, :], preferred_element_type=F32)
    cmask = jnp.broadcast_to(cmask[:, C : C + 1], (2 * 64, L))

    deal.finish()
    near32[...] = near[...].astype(F32)
    far32[...] = far[...].astype(F32)

    def lines(n):
        return jnp.concatenate([near32[box_rows(core, n), :], far32[box_rows(core, n), :]], axis=0)

    def peers(dim, shape):
        order = lax.broadcasted_iota(jnp.int32, shape, dim)
        return jnp.where(order < CHIPS, 2 * order + core, 2 * (order - CHIPS) + 1 - core)

    boxes = jnp.concatenate([lines(n) for n in range(6)], axis=1).astype(BF16)
    below = jnp.where(peers(0, (PEERS, L)) < me, lines(6), 0.0)
    first = jnp.sum(below, axis=0, keepdims=True).astype(jnp.int32)[:, :64]
    row = lax.broadcasted_iota(jnp.int32, (128, 64), 0)
    block, piece = row >> 6, (row >> 3) & 7
    holder = jnp.bitwise_and(jnp.broadcast_to(first, (128, 64)) + block, 7) * 8 + piece
    chosen = jnp.where((holder == peers(1, (128, 64))) & (block < live), 1.0, 0.0).astype(BF16)
    pick = (
        lax.broadcasted_iota(jnp.int32, (128, 6 * L), 1) & 7
        == lax.broadcasted_iota(jnp.int32, (128, 6 * L), 0) & 7
    )
    dz = jnp.dot(chosen, boxes, preferred_element_type=F32)
    dz = jnp.where(pick, dz, 0.0).astype(BF16)
    dz = lax.dot_general(dz, spread[...], NT, preferred_element_type=F32)
    dz = jnp.where(cmask > 0, dz, 0.0)
    dzt = jnp.transpose(dz).astype(BF16)
    dz = dz.astype(BF16)
    dh = [
        lax.dot_general(dz, wd[j * L : (j + 1) * L, :], NT, preferred_element_type=F32) for j in range(8)
    ]
    parts = []
    for g in range(2):
        part = jnp.concatenate([piece[g * 64 : (g + 1) * 64] for piece in dh], axis=0)
        high = part.astype(BF16)
        parts += [high, (part - high.astype(F32)).astype(BF16)]
    dh = jnp.dot(permt[...], jnp.concatenate(parts, axis=1), preferred_element_type=F32)
    for g in range(2):
        dpre = slopes[g] * (dh[:, 2 * g * L : (2 * g + 1) * L] + dh[:, (2 * g + 1) * L : (2 * g + 2) * L])
        dpre16 = dpre.astype(BF16)
        for a in range(3):
            dpre3[g * 640 + a * 64 : g * 640 + a * 64 + V, a * L : (a + 1) * L] = dpre16
        pre[g * V : (g + 1) * V, :] = dpre
    down_sums = jnp.dot(dzt, jnp.concatenate(kids, axis=1), preferred_element_type=F32)

    lane = lax.broadcasted_iota(jnp.int32, (C, L), 1)
    held = {}

    def keep(k, product):
        held[k % 4] = jnp.transpose(product)[:C]
        if k % 4 == 3 or k == 34:
            last = held.get(3)
            for n in range(3):
                slab = held[n]
                if last is not None:
                    slab = jnp.where(lane < C, slab, pltpu.roll(last, C - 32 * n, 1))
                at = (3 * (k // 4) + n) * C
                sums32[at : at + C, :] = slab
                sums16[at : at + C, :] = slab.astype(BF16)
            held.clear()

    dt = jnp.transpose(pre[...]).astype(BF16)
    for a in range(3):
        for bc in range(0, 9, 2):
            lanes = slice(bc * L, min(bc + 2, 9) * L)
            value = jnp.dot(
                dt[:, :V], cols[a * 64 : a * 64 + V, lanes], preferred_element_type=F32
            ) + jnp.dot(
                dt[:, V:], cols[640 + a * 64 : 640 + a * 64 + V, lanes], preferred_element_type=F32
            )
            for n in range(min(2, 9 - bc)):
                keep(a * 9 + bc + n, value[:, n * L : (n + 1) * L])
    for j in range(8):
        keep(27 + j, down_sums[:, j * L : (j + 1) * L])
    sums32[27 * C :, :] = jnp.zeros((C, L), F32)
    sums16[27 * C :, :] = jnp.zeros((C, L), BF16)

    def span(at, count):
        return pl.ds(pl.multiple_of(at, 16), count)

    def device(yy, zz):
        return yy * 16 + zz * 2 + core

    pair = remote(sums16.at[span((1 - core) * HALF, HALF)], pair_in, pair_sent, pair_arrived, partner)
    pair.start()
    deal_back = Deal(me, back, back_near, back_far, *(back_sem.at[n] for n in range(4)))
    flat = jnp.dot((coarse * cmask).astype(BF16), spread[...], preferred_element_type=F32)
    flat = jnp.where(pick, flat, 0.0).astype(BF16)
    dealt = lax.dot_general(chosen, flat, (((0,), (0,)), ((), ())), preferred_element_type=F32)
    for n in range(6):
        box32[box_rows(core, n), :] = dealt[:CHIPS, n * L : (n + 1) * L]
        box32[box_rows(1 - core, n), :] = dealt[CHIPS:, n * L : (n + 1) * L]
    back[...] = box32[...].astype(BF16)
    deal_back.start()
    pair.wait_recv()
    value = sums32[span(core * HALF, HALF), :] + pair_in[...].astype(F32)
    chip32[...] = value
    chip16[...] = value.astype(BF16)
    ysteps = []
    for n in range(3):
        yy = jnp.bitwise_and(y + n + 1, 3)
        ysteps.append(
            remote(chip16.at[span(yy * YPART, YPART)], y_in.at[n], ysent.at[n], yarrived.at[n], device(yy, z))
        )

    for n in YORDER:
        ysteps[n].start()

    gpad[...] = jnp.zeros_like(gpad)
    def pad_gradient(bc):
        width = min(2, 9 - bc)
        u[:, : width * L] = lax.dot_general(
            dpre3[...], wb[bc * L : (bc + width) * L, :], NT, preferred_element_type=F32
        )

        def add(gx, carry):
            for n in range(width):
                b, c = divmod(bc + n, 3)
                for yy in range(8):
                    at = pl.ds(gx * 100 + (yy + b) * 10 + c, 8)
                    gpad[at, :] += u[pl.ds(pl.multiple_of(gx * 64 + yy * 8, 8), 8), n * L : (n + 1) * L]
            return carry

        lax.fori_loop(0, 20, add, 0)

    for bc in (0, 2, 4):
        pad_gradient(bc)

    value = chip32[span(y * YPART, YPART), :]
    for n in range(3):
        ysteps[n].wait_recv()
        value = value + y_in[n].astype(F32)
    y32[...] = value
    y16[...] = value.astype(BF16)

    def zstep(n):
        zz = jnp.bitwise_and(z + n + 1, 7)
        at = span(lax.min(zz, 6) * ZPART, ZPART)
        return zz < 7, remote(y16.at[at], z_in.at[n], zsent.at[n], zarrived.at[n], device(y, zz))

    for n in ZORDER:
        wanted, copy = zstep(n)

        @pl.when(wanted)
        def _():
            copy.start()

    for bc in (6, 8):
        pad_gradient(bc)

    gsource[...] = jnp.zeros_like(gsource)

    def give(n, carry):
        for g in range(2):
            for k, offset in enumerate(OFFSETS):
                if k != 13:
                    here = jnp.where(table[g, k] == n, 1.0, 0.0)
                    for s0, ss, p0, ps, count in segments(*offset):
                        at = rows(n * SHELL + s0, count, ss)
                        gsource[at, :] += gpad[rows(g * 1000 + p0, count, ps), :] * here
        return carry

    lax.fori_loop(0, 6, give, 0)
    for g in range(2):
        part_lower[g] = gsource[g * SHELL : (g + 1) * SHELL, :].astype(BF16)
        part_upper[g] = gsource[(4 + g) * SHELL : (5 + g) * SHELL, :].astype(BF16)
    def gzstep(n, owner, to):
        at = span(core * HALF + y * YPART + owner * ZPART, ZPART)
        return remote(total.at[at], total.at[at], gzsent.at[n], gzarrived.at[n], device(y, to))

    @pl.when(z < 7)
    def _():
        value = y32[span(z * ZPART, ZPART), :]
        for n in range(7):
            zstep(n)[1].wait_recv()
            value = value + z_in[n].astype(F32)
        total[span(core * HALF + y * YPART + z * ZPART, ZPART), :] = value.astype(BF16)
        for n in ZORDER:
            gzstep(n, z, jnp.bitwise_and(z + n + 1, 7)).start()

    deal_back.forward()
    for n in range(7):
        owner = jnp.bitwise_and(z + 7 - n, 7)

        @pl.when(owner < 7)
        def _():
            gzstep(n, lax.min(owner, 6), owner).wait_recv()

    def gystep(n, owner, to):
        at = span(core * HALF + owner * YPART, YPART)
        return remote(total.at[at], total.at[at], gysent.at[n], gyarrived.at[n], device(to, z))

    def across(n, which, owner):
        at = span(which * HALF + owner * YPART, YPART)
        return remote(total.at[at], total.at[at], copy_sent.at[n], copy_arrived.at[n], partner)

    owners = [jnp.bitwise_and(y + 4 - n, 3) for n in range(4)]
    for n in YORDER:
        gystep(n, y, jnp.bitwise_and(y + n + 1, 3)).start()
    across(0, core, y).start()
    rim_up = remote(part_upper, from_lower, rim_sent.at[0], rim_arrived.at[0], lax.min(me + 1, PEERS - 1))
    rim_down = remote(part_lower, from_upper, rim_sent.at[1], rim_arrived.at[1], lax.max(me - 1, 0))

    @pl.when(has_up)
    def _():
        rim_up.start()

    @pl.when(has_down)
    def _():
        rim_down.start()

    deal_back.finish()
    near32[...] = back_near[...].astype(F32)
    far32[...] = back_far[...].astype(F32)
    for n in range(6):
        out32[pl.ds(n * PEERS + core, CHIPS, stride=2), :] = near32[box_rows(core, n), :]
        out32[pl.ds(n * PEERS + 1 - core, CHIPS, stride=2), :] = far32[box_rows(core, n), :]
    for n in range(6):
        coarse_out[:, n * L : (n + 1) * L] = out32[n * PEERS : (n + 1) * PEERS, :].astype(BF16)

    def pass_on(n):
        gystep(n, owners[n + 1], owners[n + 1]).wait_recv()
        across(n + 1, core, owners[n + 1]).start()

    pass_on(0)
    pass_on(2)

    @pl.when(has_down)
    def _():
        rim_up.wait_recv()

    @pl.when(jnp.logical_not(has_down))
    def _():
        from_lower[...] = jnp.zeros_like(from_lower)

    @pl.when(has_up)
    def _():
        rim_down.wait_recv()

    @pl.when(jnp.logical_not(has_up))
    def _():
        from_upper[...] = jnp.zeros_like(from_upper)

    for g in range(2):
        shell = gsource[(2 + g) * SHELL : (3 + g) * SHELL, :]
        shell = shell + from_lower[g].astype(F32) + from_upper[g].astype(F32)
        for x in range(8):
            for yy in range(8):
                pre[pl.ds(g * V + x * 64 + yy * 8, 8), :] = gpad[pl.ds(g * 1000 + x * 100 + yy * 10 + 111, 8), :]
        for s0, v0, vs, count in shell_pieces():
            pre[rows(g * V + v0, count, vs), :] += shell[s0 : s0 + count]
        value = pre[g * V : (g + 1) * V, :]
        value = value * jnp.broadcast_to(own32[g * V : (g + 1) * V, C : C + 1], (V, L))
        grad_features[g] = jnp.transpose(value)[:C, :].astype(BF16)

    pass_on(1)
    for n in range(4):
        across(n, 1 - core, owners[n]).wait_recv()

    @pl.when(has_up)
    def _():
        up.wait_send()
        rim_up.wait_send()

    @pl.when(has_down)
    def _():
        down.wait_send()
        rim_down.wait_send()

    deal.close()
    deal_back.close()
    pair.wait_send()
    for n in range(3):
        ysteps[n].wait_send()
        gystep(n, y, jnp.bitwise_and(y + n + 1, 3)).wait_send()
    for n in range(7):
        wanted, copy = zstep(n)

        @pl.when(wanted)
        def _():
            copy.wait_send()

    @pl.when(z < 7)
    def _():
        for n in range(7):
            gzstep(n, z, jnp.bitwise_and(z + n + 1, 7)).wait_send()

    for n in range(4):
        across(n, core, owners[n]).wait_send()


def vmem(n):
    return [pl.BlockSpec(memory_space=pltpu.VMEM)] * n


def hbm(n):
    return [pl.BlockSpec(memory_space=pltpu.HBM)] * n


def run_section(neighbours, live_count, occupancy, features, grad_coarse, w_subm, w_down):
    dma = pltpu.SemaphoreType.DMA
    block = pltpu.VMEM((2, SHELL, L), BF16)
    boxes = pltpu.VMEM((8 * PEERS, L), F32)
    sent = pltpu.VMEM((8 * PEERS, L), BF16)
    return pl.pallas_call(
        section_kernel,
        out_shape=(
            jax.ShapeDtypeStruct((PEERS, 6 * L), BF16),
            jax.ShapeDtypeStruct((2, C, V), BF16),
            jax.ShapeDtypeStruct((2 * HALF, L), BF16),
        ),
        in_specs=hbm(7),
        out_specs=tuple(vmem(3)),
        scratch_shapes=[
            pltpu.SMEM((2, 27), jnp.int32),
            pltpu.SMEM((1,), jnp.int32),
            pltpu.SMEM((2, 16), jnp.int32),
            pltpu.VMEM((2, C, V), BF16),
            pltpu.VMEM((PEERS, 6 * L), BF16),
            pltpu.VMEM((27, C, C), BF16),
            pltpu.VMEM((8, C, C), BF16),
            pltpu.VMEM((2 * V, L), F32),
            block, block, block, boxes, boxes, boxes, pltpu.VMEM((6 * PEERS, L), F32),
            sent, sent, sent, sent, sent, sent,
            pltpu.VMEM((7 * SHELL, L), F32),
            pltpu.VMEM((2000, L), F32),
            pltpu.VMEM((1280, 9 * L), BF16),
            pltpu.VMEM((27 * L, L), BF16),
            pltpu.VMEM((9 * L, 3 * L), BF16),
            pltpu.VMEM((8 * L, L), BF16),
            pltpu.VMEM((V, V), BF16),
            pltpu.VMEM((V, V), BF16),
            pltpu.VMEM((L, 6 * L), BF16),
            pltpu.VMEM((2 * V, L), F32),
            pltpu.VMEM((1280, 3 * L), BF16),
            pltpu.VMEM((1280, 2 * L), F32),
            pltpu.VMEM((2000, L), F32),
            pltpu.VMEM((6 * SHELL, L), F32),
            pltpu.VMEM((2 * HALF, L), F32),
            pltpu.VMEM((2 * HALF, L), BF16),
            pltpu.VMEM((HALF, L), BF16),
            pltpu.VMEM((HALF, L), F32),
            pltpu.VMEM((HALF, L), BF16),
            pltpu.VMEM((3, YPART, L), BF16),
            pltpu.VMEM((YPART, L), F32),
            pltpu.VMEM((YPART, L), BF16),
            pltpu.VMEM((7, ZPART, L), BF16),
            block, block, block, block,
            dma((7,)), dma((4,)), dma((4,)),
            dma((2,)), dma((2,)), dma((2,)), dma((2,)), dma(()), dma(()),
            dma((3,)), dma((3,)), dma((7,)), dma((7,)), dma((7,)), dma((7,)),
            dma((3,)), dma((3,)), dma((4,)), dma((4,)),
        ],
        compiler_params=pltpu.CompilerParams(
            vmem_limit_bytes=VMEM_LIMIT, collective_id=0, has_side_effects=True
        ),
    )(neighbours, live_count, occupancy, features, grad_coarse, w_subm, w_down)


def final_kernel(
    coarse_in, features_in, total_in, coarse_out, grad_features, grad_subm, grad_down,
    total, subm, down, coarse, features, load_sem, sem,
):
    def chunk(n):
        return pl.ds(9 * C * n, 9 * C)

    loads = [
        pltpu.make_async_copy(total_in.at[chunk(n)], total.at[chunk(n)], load_sem.at[n]) for n in range(3)
    ]
    loads.append(pltpu.make_async_copy(features_in, features, load_sem.at[3]))
    loads.append(pltpu.make_async_copy(coarse_in, coarse, load_sem.at[4]))
    for load in loads:
        load.start()
    copies = [
        pltpu.make_async_copy(features, grad_features, sem.at[0]),
        pltpu.make_async_copy(coarse, coarse_out, sem.at[1]),
    ]
    lane = lax.broadcasted_iota(jnp.int32, (C, L), 1)
    for k in range(35):
        quad, n = divmod(k, 4)
        if k % 12 == 0:
            loads[k // 12].wait()
        if n < 3:
            at = (3 * quad + n) * C
            value = total[at : at + C, :].astype(F32)[:, :C]
        else:
            value = jnp.zeros((C, L), F32)
            for m in range(3):
                at = (3 * quad + m) * C
                piece = pltpu.roll(total[at : at + C, :].astype(F32), 32 + 32 * m, 1)
                value = jnp.where(lane // 32 == m, piece, value)
            value = value[:, :C]
        if k < 27:
            subm[k] = value
        else:
            down[k - 27] = value
        if k in (11, 23, 26):
            part = pl.ds(k // 12 * 12, 12 if k < 26 else 3)
            copies.append(pltpu.make_async_copy(subm.at[part], grad_subm.at[part], sem.at[2 + k // 12]))
            copies[-1].start()
        if k == 11:
            for n in range(2):
                loads[3 + n].wait()
                copies[n].start()
    copies.append(pltpu.make_async_copy(down, grad_down, sem.at[5]))
    copies[-1].start()
    for copy in copies:
        copy.wait()


def run_final(coarse_in, grad_features, total):
    return pl.pallas_call(
        final_kernel,
        out_shape=(
            jax.ShapeDtypeStruct((PEERS, 6 * L), BF16),
            jax.ShapeDtypeStruct((2, C, V), BF16),
            jax.ShapeDtypeStruct((27, C, C), F32),
            jax.ShapeDtypeStruct((8, C, C), F32),
        ),
        in_specs=hbm(3),
        out_specs=tuple(hbm(4)),
        scratch_shapes=[
            pltpu.VMEM((27 * C, L), BF16),
            pltpu.VMEM((27, C, C), F32),
            pltpu.VMEM((8, C, C), F32),
            pltpu.VMEM((PEERS, 6 * L), BF16),
            pltpu.VMEM((2, C, V), BF16),
            pltpu.SemaphoreType.DMA((5,)),
            pltpu.SemaphoreType.DMA((6,)),
        ],
        compiler_params=pltpu.CompilerParams(vmem_limit_bytes=VMEM_LIMIT),
    )(coarse_in, grad_features, total)


def per_device(features, occupancy, neighbours, live_count, w_subm, w_down, grad_coarse):
    return run_final(
        *run_section(neighbours, live_count, occupancy, features, grad_coarse, w_subm, w_down)
    )


def solution(mesh):
    blocks = P(("rep", "space"), None)
    return jax.shard_map(
        per_device,
        mesh=mesh,
        in_specs=(
            P(("rep", "space"), None, None), blocks, blocks, P(("rep", "space")), P(), P(), blocks,
        ),
        out_specs=(
            blocks, P(("rep", "space"), None, None), P("rep", None, None), P("rep", None, None),
        ),
        check_vma=False,
    )
```

```python
import functools

import jax
import jax.numpy as jnp
from jax import lax
from jax.experimental import pallas as pl
from jax.experimental.pallas import tpu as pltpu
from jax.sharding import PartitionSpec as P

C, L, V = 96, 128, 512
OFFSETS = [(a, b, c) for a in (-1, 0, 1) for b in (-1, 0, 1) for c in (-1, 0, 1)]
PEERS, CHIPS, SHELL = 64, 32, 320
YORDER, ZORDER = (1, 0, 2), (3, 2, 4, 1, 5, 0, 6)
HALF, YPART, ZPART, OWNED = 1344, 336, 192, 48
VMEM_LIMIT = 63 * 2**20 + 2**19
F32, BF16 = jnp.float32, jnp.bfloat16
NT = (((1,), (1,)), ((), ()))


def segments(a, b, c):
    span = {-1: [(7, 0)], 0: [(i, i + 1) for i in range(8)], 1: [(0, 9)]}
    xs, ys, zs = span[a], span[b], span[c]
    face = {0: 0, 7: 64}
    if c == 0:
        return [
            (face[x] + y * 8 if x in face else 112 + x * 16 + y // 7 * 8, 1, tx * 100 + ty * 10 + 1, 1, 8)
            for x, tx in xs
            for y, ty in ys
        ]
    z, tz = zs[0]
    if b == 0:
        return [
            (face[x] + z, 8, tx * 100 + 10 + tz, 10, 8)
            if x in face
            else (208 + x * 16 + z // 7 * 8, 1, tx * 100 + 10 + tz, 10, 8)
            for x, tx in xs
        ]
    y, ty = ys[0]
    if a == 0:
        at = ty * 10 + tz
        return [
            (y * 8 + z, 1, 100 + at, 1, 1),
            (128 + y // 7 * 8 + z, 16, 200 + at, 100, 6),
            (64 + y * 8 + z, 1, 800 + at, 1, 1),
        ]
    x, tx = xs[0]
    return [(face[x] + y * 8 + z, 1, tx * 100 + ty * 10 + tz, 1, 1)]


def shell_pieces():
    pieces = [(0, 0, 1, 64), (64, 448, 1, 64)]
    for x in range(1, 7):
        pieces += [(112 + x * 16, x * 64, 1, 8), (120 + x * 16, x * 64 + 56, 1, 8)]
        pieces += [(208 + x * 16, x * 64, 8, 8), (216 + x * 16, x * 64 + 7, 8, 8)]
    return pieces


def rows(start, count, stride):
    return pl.ds(start, count) if stride == 1 else pl.ds(start, count, stride=stride)


def mask_row(words, live, g):
    lane = lax.broadcasted_iota(jnp.int32, (1, V), 1)
    word = jnp.zeros((1, V), jnp.int32)
    for w in range(16):
        word = jnp.where(lane // 32 == w, words[g, w], word)
    bit = jnp.bitwise_and(jnp.right_shift(word, jnp.bitwise_and(lane, 31)), 1)
    return jnp.where(g < live, bit, 0)


def masked_rows(features, words, live, g):
    bit = mask_row(words, live, g)
    values = jnp.where(bit > 0, features[g].astype(F32), 0.0)
    marks = jnp.broadcast_to(bit.astype(F32), (L - C, V))
    return jnp.transpose(jnp.concatenate([values, marks], axis=0))


def remote(source, target, sent, arrived, peer):
    return pltpu.make_async_remote_copy(
        src_ref=source, dst_ref=target, send_sem=sent, recv_sem=arrived,
        device_id={"space": peer}, device_id_type=pl.DeviceIdType.MESH,
    )


def far_first():
    offsets = [(dy, dz) for dy in range(4) for dz in range(8) if dy or dz]
    return sorted(offsets, key=lambda at: -min(at[0], 4 - at[0]) - min(at[1], 8 - at[1]))


def chip_at(here, offset):
    dy, dz = offset
    return jnp.bitwise_and(here + 8 * dy, CHIPS - 8) + jnp.bitwise_and(here + dz, 7)


def greet(me):
    barrier = pltpu.get_barrier_semaphore()
    here, core = me // 2, lax.rem(me, 2)

    def tell(peer):
        pl.semaphore_signal(
            barrier, inc=1, device_id={"space": peer}, device_id_type=pl.DeviceIdType.MESH
        )

    for offset in far_first():
        tell(chip_at(here, offset) * 2 + core)
    tell(lax.rem(me + 2 * core - 1 + PEERS, PEERS))
    tell(me + 1 - 2 * core)


def greeted():
    pl.semaphore_wait(pltpu.get_barrier_semaphore(), CHIPS + 1)


class Deal:
    def __init__(self, me, outbox, near, far, sent, arrived, far_sent, far_arrived):
        self.here, self.core = me // 2, lax.rem(me, 2)
        self.outbox, self.near = outbox, near
        self.sems = sent, arrived
        self.across = remote(near, far, far_sent, far_arrived, me + 1 - 2 * self.core)
        every = pl.ds(0, 16 * (CHIPS - 1))
        self.every = remote(outbox.at[every], near.at[every], sent, arrived, me + 1 - 2 * self.core)

    def tile(self, chip):
        return pl.ds(pl.multiple_of(chip * 16, 16), 16)

    def start(self):
        for offset in far_first():
            there = chip_at(self.here, offset)
            remote(
                self.outbox.at[self.tile(there)], self.near.at[self.tile(self.here)],
                *self.sems, there * 2 + self.core,
            ).start()
        self.near[self.tile(self.here), :] = self.outbox[self.tile(self.here), :]

    def forward(self):
        self.every.wait_recv()
        self.across.start()

    def finish(self):
        self.across.wait_recv()

    def close(self):
        self.every.wait_send()
        self.across.wait_send()


def box_rows(core, n):
    return pl.ds(core * 8 + n, CHIPS, stride=16)


def section_kernel(
    table_hbm, live_hbm, occupancy_hbm, features_hbm, cotangent_hbm, w_subm_hbm, w_down_hbm,
    coarse_out, grad_features, total,
    table, live_ref, occupancy_ref, features, cotangent, w_subm, w_down,
    own32, own, lower, upper, box32, near32, far32, out32, outbox, near, far, back, back_near, back_far,
    source, pad, cols, wf, wb, wd, perm, permt, spread, pre, dpre3, u, gpad, gsource,
    sums32, sums16, pair_in, chip32, chip16, y_in, y32, y16, z_own, z_in, z32, z16, y_own,
    part_lower, part_upper, from_lower, from_upper,
    load_sem, box_sem, back_sem, halo_sent, halo_arrived,
    rim_sent, rim_arrived, pair_sent, pair_arrived, ysent, yarrived, zsent, zarrived,
    gzsent, gzarrived, gysent, gyarrived, copy_sent, copy_arrived,
):
    me = lax.axis_index("space")
    y, z, core = me // 16, lax.rem(me // 2, 8), lax.rem(me, 2)
    partner = me + 1 - 2 * core
    has_up, has_down = me < PEERS - 1, me > 0
    loads = [
        pltpu.make_async_copy(hbm, ref, load_sem.at[n])
        for n, (hbm, ref) in enumerate(
            (
                (features_hbm, features), (cotangent_hbm, cotangent), (w_subm_hbm, w_subm), (w_down_hbm, w_down),
                (table_hbm, table), (live_hbm, live_ref), (occupancy_hbm, occupancy_ref),
            )
        )
    ]
    for load in loads:
        load.start()
    greet(me)

    i = lax.broadcasted_iota(jnp.int32, (V, V), 0)
    v = lax.broadcasted_iota(jnp.int32, (V, V), 1)

    def placed(index, parts):
        return sum(((index >> a) & b) << c for a, b, c in parts)

    to_voxel = ((8, 1, 6), (7, 1, 3), (6, 1, 0), (4, 3, 7), (2, 3, 4), (0, 3, 1))
    to_child = tuple((c, b, a) for a, b, c in to_voxel)
    perm[...] = jnp.where(placed(i[:, :1], to_voxel) == v, 1.0, 0.0).astype(BF16)
    permt[...] = jnp.where(placed(i[:, :1], to_child) == v, 1.0, 0.0).astype(BF16)
    spread[...] = jnp.where(
        lax.broadcasted_iota(jnp.int32, (L, 6 * L), 1) // 8
        == lax.broadcasted_iota(jnp.int32, (L, 6 * L), 0),
        1.0, 0.0,
    ).astype(BF16)
    wf[...] = jnp.zeros_like(wf)
    wb[...] = jnp.zeros_like(wb)
    wd[...] = jnp.zeros_like(wd)
    dpre3[...] = jnp.zeros_like(dpre3)
    source[6 * SHELL :, :] = jnp.zeros((SHELL, L), F32)

    for n in (0, 4, 5, 6):
        loads[n].wait()
    for g in range(2):
        own32[g * V : (g + 1) * V, :] = masked_rows(features, occupancy_ref, live_ref[0], g)
        for s0, v0, vs, count in shell_pieces():
            source[(2 + g) * SHELL + s0 : (2 + g) * SHELL + s0 + count, :] = own32[rows(g * V + v0, count, vs), :]
        own[g] = source[(2 + g) * SHELL : (3 + g) * SHELL, :].astype(BF16)
    loads[1].wait()
    for n in range(6):
        box32[pl.ds(n, PEERS, stride=8), :] = cotangent[:, n * L : (n + 1) * L].astype(F32)
    counts = jnp.broadcast_to(live_ref[0].astype(F32), (PEERS, L))
    for n in (6, 7):
        box32[pl.ds(n, PEERS, stride=8), :] = counts
    outbox[...] = box32[...].astype(BF16)

    greeted()
    up = remote(own, lower, halo_sent.at[0], halo_arrived.at[0], lax.min(me + 1, PEERS - 1))
    down = remote(own, upper, halo_sent.at[1], halo_arrived.at[1], lax.max(me - 1, 0))

    @pl.when(has_up)
    def _():
        up.start()

    @pl.when(has_down)
    def _():
        down.start()

    deal = Deal(me, outbox, near, far, *(box_sem.at[n] for n in range(4)))
    deal.start()

    loads[2].wait()
    loads[3].wait()
    for k in range(27):
        a, bc = divmod(k, 9)
        w = w_subm[k]
        wf[k * L : k * L + C, :C] = w
        wb[bc * L : bc * L + C, a * L : a * L + C] = w
    for j in range(8):
        wd[j * L : j * L + C, :C] = w_down[j]


    @pl.when(has_down)
    def _():
        up.wait_recv()

    @pl.when(jnp.logical_not(has_down))
    def _():
        lower[...] = jnp.zeros_like(lower)

    @pl.when(has_up)
    def _():
        down.wait_recv()

    @pl.when(jnp.logical_not(has_up))
    def _():
        upper[...] = jnp.zeros_like(upper)

    for g in range(2):
        source[g * SHELL : (g + 1) * SHELL, :] = lower[g].astype(F32)
        source[(4 + g) * SHELL : (5 + g) * SHELL, :] = upper[g].astype(F32)

    for g in range(2):
        for k, offset in enumerate(OFFSETS):
            if k == 13:
                continue
            base = table[g, k] * SHELL
            for s0, ss, p0, ps, count in segments(*offset):
                pad[rows(g * 1000 + p0, count, ps), :] = source[rows(base + s0, count, ss), :]

        for x in range(8):
            for yy in range(8):
                pad[pl.ds(g * 1000 + x * 100 + yy * 10 + 111, 8), :] = own32[pl.ds(g * V + x * 64 + yy * 8, 8), :]

    def columns(gx, carry):
        for b in range(3):
            for c in range(3):
                piece = jnp.concatenate(
                    [pad[pl.ds(gx * 100 + (yy + b) * 10 + c, 8), :] for yy in range(8)], axis=0
                )
                bc = 3 * b + c
                cols[pl.ds(pl.multiple_of(gx * 64, 64), 64), bc * L : (bc + 1) * L] = piece.astype(BF16)
        return carry

    lax.fori_loop(0, 20, columns, 0)

    for g in range(2):
        acc = jnp.zeros((V, L), F32)
        for a in range(3):
            acc += jnp.dot(
                cols[g * 640 + a * 64 : g * 640 + a * 64 + V, :],
                wf[a * 9 * L : (a + 1) * 9 * L, :],
                preferred_element_type=F32,
            )
        pre[g * V : (g + 1) * V, :] = acc

    deal.forward()
    live = live_ref[0]
    s, q = 0.7978845608028654, 0.044715
    slopes, hiddens = [], []
    for g in range(2):
        mask = jnp.broadcast_to(own32[g * V : (g + 1) * V, C : C + 1], (V, L))
        tt = pre[g * V : (g + 1) * V, :]
        th = jnp.tanh(s * (tt + q * tt * tt * tt))
        hidden = 0.5 * tt * (1.0 + th) * mask
        slopes.append((0.5 * (1.0 + th) + 0.5 * tt * (1.0 - th * th) * (s * (1.0 + 3.0 * q * tt * tt))) * mask)
        hiddens.append(jnp.where(lax.broadcasted_iota(jnp.int32, (V, L), 1) < C, hidden, mask).astype(BF16))
    both = jnp.dot(perm[...], jnp.concatenate(hiddens, axis=1), preferred_element_type=F32)
    kids = []
    cmask = jnp.zeros((2 * 64, L), F32)
    coarse = jnp.zeros((2 * 64, L), F32)
    for j in range(8):
        kid = jnp.concatenate([both[j * 64 : (j + 1) * 64, :L], both[j * 64 : (j + 1) * 64, L:]], axis=0)
        cmask = jnp.maximum(cmask, kid)
        kids.append(kid.astype(BF16))
        coarse += jnp.dot(kids[j], wd[j * L : (j + 1) * L, :], preferred_element_type=F32)
    cmask = jnp.broadcast_to(cmask[:, C : C + 1], (2 * 64, L))

    deal.finish()
    near32[...] = near[...].astype(F32)
    far32[...] = far[...].astype(F32)

    def lines(n):
        return jnp.concatenate([near32[box_rows(core, n), :], far32[box_rows(core, n), :]], axis=0)

    def peers(dim, shape):
        order = lax.broadcasted_iota(jnp.int32, shape, dim)
        return jnp.where(order < CHIPS, 2 * order + core, 2 * (order - CHIPS) + 1 - core)

    boxes = jnp.concatenate([lines(n) for n in range(6)], axis=1).astype(BF16)
    below = jnp.where(peers(0, (PEERS, L)) < me, lines(6), 0.0)
    first = jnp.sum(below, axis=0, keepdims=True).astype(jnp.int32)[:, :64]
    row = lax.broadcasted_iota(jnp.int32, (128, 64), 0)
    block, piece = row >> 6, (row >> 3) & 7
    holder = jnp.bitwise_and(jnp.broadcast_to(first, (128, 64)) + block, 7) * 8 + piece
    chosen = jnp.where((holder == peers(1, (128, 64))) & (block < live), 1.0, 0.0).astype(BF16)
    pick = (
        lax.broadcasted_iota(jnp.int32, (128, 6 * L), 1) & 7
        == lax.broadcasted_iota(jnp.int32, (128, 6 * L), 0) & 7
    )
    dz = jnp.dot(chosen, boxes, preferred_element_type=F32)
    dz = jnp.where(pick, dz, 0.0).astype(BF16)
    dz = lax.dot_general(dz, spread[...], NT, preferred_element_type=F32)
    dz = jnp.where(cmask > 0, dz, 0.0)
    dzt = jnp.transpose(dz).astype(BF16)
    dz = dz.astype(BF16)
    dh = [
        lax.dot_general(dz, wd[j * L : (j + 1) * L, :], NT, preferred_element_type=F32) for j in range(8)
    ]
    parts = []
    for g in range(2):
        part = jnp.concatenate([piece[g * 64 : (g + 1) * 64] for piece in dh], axis=0)
        high = part.astype(BF16)
        parts += [high, (part - high.astype(F32)).astype(BF16)]
    dh = jnp.dot(permt[...], jnp.concatenate(parts, axis=1), preferred_element_type=F32)
    for g in range(2):
        dpre = slopes[g] * (dh[:, 2 * g * L : (2 * g + 1) * L] + dh[:, (2 * g + 1) * L : (2 * g + 2) * L])
        dpre16 = dpre.astype(BF16)
        for a in range(3):
            dpre3[g * 640 + a * 64 : g * 640 + a * 64 + V, a * L : (a + 1) * L] = dpre16
        pre[g * V : (g + 1) * V, :] = dpre
    down_sums = jnp.dot(dzt, jnp.concatenate(kids, axis=1), preferred_element_type=F32)

    lane = lax.broadcasted_iota(jnp.int32, (C, L), 1)
    held = {}

    def keep(k, product):
        held[k % 4] = jnp.transpose(product)[:C]
        if k % 4 == 3 or k == 34:
            last = held.get(3)
            for n in range(3):
                slab = held[n]
                if last is not None:
                    slab = jnp.where(lane < C, slab, pltpu.roll(last, C - 32 * n, 1))
                at = (3 * (k // 4) + n) * C
                sums32[at : at + C, :] = slab
                sums16[at : at + C, :] = slab.astype(BF16)
            held.clear()

    dt = jnp.transpose(pre[...]).astype(BF16)
    for a in range(3):
        for bc in range(0, 9, 2):
            lanes = slice(bc * L, min(bc + 2, 9) * L)
            value = jnp.dot(
                dt[:, :V], cols[a * 64 : a * 64 + V, lanes], preferred_element_type=F32
            ) + jnp.dot(
                dt[:, V:], cols[640 + a * 64 : 640 + a * 64 + V, lanes], preferred_element_type=F32
            )
            for n in range(min(2, 9 - bc)):
                keep(a * 9 + bc + n, value[:, n * L : (n + 1) * L])
    for j in range(8):
        keep(27 + j, down_sums[:, j * L : (j + 1) * L])
    sums32[27 * C :, :] = jnp.zeros((C, L), F32)
    sums16[27 * C :, :] = jnp.zeros((C, L), BF16)

    def span(at, count):
        return pl.ds(pl.multiple_of(at, 16), count)

    pair = remote(sums16.at[span((1 - core) * HALF, HALF)], pair_in, pair_sent, pair_arrived, partner)
    pair.start()
    deal_back = Deal(me, back, back_near, back_far, *(back_sem.at[n] for n in range(4)))
    flat = jnp.dot((coarse * cmask).astype(BF16), spread[...], preferred_element_type=F32)
    flat = jnp.where(pick, flat, 0.0).astype(BF16)
    dealt = lax.dot_general(chosen, flat, (((0,), (0,)), ((), ())), preferred_element_type=F32)
    for n in range(6):
        box32[box_rows(core, n), :] = dealt[:CHIPS, n * L : (n + 1) * L]
        box32[box_rows(1 - core, n), :] = dealt[CHIPS:, n * L : (n + 1) * L]
    back[...] = box32[...].astype(BF16)
    deal_back.start()
    pair.wait_recv()
    value = sums32[span(core * HALF, HALF), :] + pair_in[...].astype(F32)
    chip32[...] = value
    chip16[...] = value.astype(BF16)

    on_y, on_z, owner = core == 0, core == 1, z < 7

    def copies(order, place, size, step, wanted=None):
        def act(what, back=False):
            for n in order:
                to = jnp.bitwise_and(place + (size - n - 1 if back else n + 1), size - 1)
                copy = step(n, to)
                if wanted is None:
                    what(copy)
                else:
                    pl.when(wanted(to))(functools.partial(what, copy))

        return act

    def start(copy):
        copy.start()

    def wait_recv(copy):
        copy.wait_recv()

    def wait_send(copy):
        copy.wait_send()

    def owns(zz):
        return zz < 7

    def low(zz):
        return lax.min(zz, 6)

    def y_first(n, yy):
        return remote(
            chip16.at[span(yy * YPART, YPART)], y_in.at[n], ysent.at[n], yarrived.at[n], yy * 16 + z * 2
        )

    def z_second(n, zz):
        return remote(
            y16.at[span(low(zz) * OWNED, OWNED)], z_own.at[n], zsent.at[n], zarrived.at[n], y * 16 + zz * 2
        )

    def z_first(n, zz):
        return remote(
            chip16.at[span(low(zz) * ZPART, ZPART)], z_in.at[n], zsent.at[n], zarrived.at[n],
            y * 16 + zz * 2 + 1,
        )

    def y_second(n, yy):
        return remote(
            z16.at[span(yy * OWNED, OWNED)], y_own.at[n], ysent.at[n], yarrived.at[n], yy * 16 + z * 2 + 1
        )

    def on_total(at, count, sent, arrived, peer):
        at = span(at, count)
        return remote(total.at[at], total.at[at], sent, arrived, peer)

    def back_z_first(n, to, source):
        return on_total(
            y * YPART + low(source) * OWNED, OWNED, gzsent.at[n], gzarrived.at[n], y * 16 + to * 2
        )

    def back_y_second(n, to, source):
        return on_total(source * YPART, YPART, gysent.at[n], gyarrived.at[n], to * 16 + z * 2)

    def back_y_first(n, to, source):
        return on_total(
            HALF + low(z) * ZPART + source * OWNED, OWNED, gysent.at[n], gyarrived.at[n], to * 16 + z * 2 + 1
        )

    def back_z_second(n, to, source):
        return on_total(
            HALF + low(source) * ZPART, ZPART, gzsent.at[n], gzarrived.at[n], y * 16 + to * 2 + 1
        )

    def sends(step, mine):
        return lambda n, to: step(n, to, mine)

    def comes(step):
        return lambda n, source: step(n, source, source)

    @pl.when(on_y)
    def _():
        copies(YORDER, y, 4, y_first)(start)

    @pl.when(on_z)
    def _():
        copies(ZORDER, z, 8, z_first, owns)(start)

    gpad[...] = jnp.zeros_like(gpad)
    def pad_gradient(bc):
        width = min(2, 9 - bc)
        u[:, : width * L] = lax.dot_general(
            dpre3[...], wb[bc * L : (bc + width) * L, :], NT, preferred_element_type=F32
        )

        def add(gx, carry):
            for n in range(width):
                b, c = divmod(bc + n, 3)
                for yy in range(8):
                    at = pl.ds(gx * 100 + (yy + b) * 10 + c, 8)
                    gpad[at, :] += u[pl.ds(pl.multiple_of(gx * 64 + yy * 8, 8), 8), n * L : (n + 1) * L]
            return carry

        lax.fori_loop(0, 20, add, 0)

    for bc in (0, 2, 4, 6):
        pad_gradient(bc)

    @pl.when(on_y)
    def _():
        copies(range(3), y, 4, y_first)(wait_recv)
        value = chip32[span(y * YPART, YPART), :]
        for n in range(3):
            value = value + y_in[n].astype(F32)
        y32[...] = value
        y16[...] = value.astype(BF16)
        copies(ZORDER, z, 8, z_second, owns)(start)

    @pl.when(on_z & owner)
    def _():
        copies(range(7), z, 8, z_first)(wait_recv)
        value = chip32[span(z * ZPART, ZPART), :]
        for n in range(7):
            value = value + z_in[n].astype(F32)
        z32[...] = value
        z16[...] = value.astype(BF16)
        copies(YORDER, y, 4, y_second)(start)

    pad_gradient(8)

    gsource[...] = jnp.zeros_like(gsource)

    def give(n, carry):
        for g in range(2):
            for k, offset in enumerate(OFFSETS):
                if k != 13:
                    here = jnp.where(table[g, k] == n, 1.0, 0.0)
                    for s0, ss, p0, ps, count in segments(*offset):
                        at = rows(n * SHELL + s0, count, ss)
                        gsource[at, :] += gpad[rows(g * 1000 + p0, count, ps), :] * here
        return carry

    lax.fori_loop(0, 6, give, 0)
    for g in range(2):
        part_lower[g] = gsource[g * SHELL : (g + 1) * SHELL, :].astype(BF16)
        part_upper[g] = gsource[(4 + g) * SHELL : (5 + g) * SHELL, :].astype(BF16)
    @pl.when(on_y & owner)
    def _():
        copies(range(7), z, 8, z_second)(wait_recv)
        value = y32[span(z * OWNED, OWNED), :]
        for n in range(7):
            value = value + z_own[n].astype(F32)
        total[span(y * YPART + z * OWNED, OWNED), :] = value.astype(BF16)
        copies(ZORDER, z, 8, sends(back_z_first, z))(start)

    @pl.when(on_z & owner)
    def _():
        copies(range(3), y, 4, y_second)(wait_recv)
        value = z32[span(y * OWNED, OWNED), :]
        for n in range(3):
            value = value + y_own[n].astype(F32)
        total[span(HALF + z * ZPART + y * OWNED, OWNED), :] = value.astype(BF16)
        copies(YORDER, y, 4, sends(back_y_first, y))(start)

    rim_up = remote(part_upper, from_lower, rim_sent.at[0], rim_arrived.at[0], lax.min(me + 1, PEERS - 1))
    rim_down = remote(part_lower, from_upper, rim_sent.at[1], rim_arrived.at[1], lax.max(me - 1, 0))

    @pl.when(has_up)
    def _():
        rim_up.start()

    @pl.when(has_down)
    def _():
        rim_down.start()

    deal_back.forward()

    def across(which, part):
        rows_at, count = (part * YPART, YPART) if which == 0 else (HALF + part * ZPART, ZPART)
        return on_total(rows_at, count, copy_sent.at[part], copy_arrived.at[part], partner)

    @pl.when(on_y)
    def _():
        copies(range(7), z, 8, comes(back_z_first), owns)(wait_recv, back=True)
        copies(YORDER, y, 4, sends(back_y_second, y))(start)
        across(0, y).start()

    @pl.when(on_z & owner)
    def _():
        copies(range(3), y, 4, comes(back_y_first))(wait_recv, back=True)
        copies(ZORDER, z, 8, sends(back_z_second, z))(start)
        across(1, z).start()

    deal_back.finish()
    near32[...] = back_near[...].astype(F32)
    far32[...] = back_far[...].astype(F32)
    for n in range(6):
        out32[pl.ds(n * PEERS + core, CHIPS, stride=2), :] = near32[box_rows(core, n), :]
        out32[pl.ds(n * PEERS + 1 - core, CHIPS, stride=2), :] = far32[box_rows(core, n), :]
    for n in range(6):
        coarse_out[:, n * L : (n + 1) * L] = out32[n * PEERS : (n + 1) * PEERS, :].astype(BF16)

    def pass_on_y(n):
        source = jnp.bitwise_and(y + 3 - n, 3)
        back_y_second(n, source, source).wait_recv()
        across(0, source).start()

    def pass_on_z(n):
        source = jnp.bitwise_and(z + 7 - n, 7)

        @pl.when(owns(source))
        def _():
            back_z_second(n, source, source).wait_recv()
            across(1, low(source)).start()

    @pl.when(on_y)
    def _():
        pass_on_y(0)
        pass_on_y(2)

    @pl.when(on_z)
    def _():
        for n in (0, 6, 1, 5):
            pass_on_z(n)

    @pl.when(has_down)
    def _():
        rim_up.wait_recv()

    @pl.when(jnp.logical_not(has_down))
    def _():
        from_lower[...] = jnp.zeros_like(from_lower)

    @pl.when(has_up)
    def _():
        rim_down.wait_recv()

    @pl.when(jnp.logical_not(has_up))
    def _():
        from_upper[...] = jnp.zeros_like(from_upper)

    for g in range(2):
        shell = gsource[(2 + g) * SHELL : (3 + g) * SHELL, :]
        shell = shell + from_lower[g].astype(F32) + from_upper[g].astype(F32)
        for x in range(8):
            for yy in range(8):
                pre[pl.ds(g * V + x * 64 + yy * 8, 8), :] = gpad[pl.ds(g * 1000 + x * 100 + yy * 10 + 111, 8), :]
        for s0, v0, vs, count in shell_pieces():
            pre[rows(g * V + v0, count, vs), :] += shell[s0 : s0 + count]
        value = pre[g * V : (g + 1) * V, :]
        value = value * jnp.broadcast_to(own32[g * V : (g + 1) * V, C : C + 1], (V, L))
        grad_features[g] = jnp.transpose(value)[:C, :].astype(BF16)

    @pl.when(on_y)
    def _():
        pass_on_y(1)
        for part in range(7):
            across(1, part).wait_recv()

    @pl.when(on_z)
    def _():
        for n in (2, 4, 3):
            pass_on_z(n)
        for part in range(4):
            across(0, part).wait_recv()

    @pl.when(has_up)
    def _():
        up.wait_send()
        rim_up.wait_send()

    @pl.when(has_down)
    def _():
        down.wait_send()
        rim_down.wait_send()

    deal.close()
    deal_back.close()
    pair.wait_send()

    @pl.when(on_y)
    def _():
        copies(range(3), y, 4, y_first)(wait_send)
        copies(range(7), z, 8, z_second, owns)(wait_send)
        copies(range(3), y, 4, sends(back_y_second, y))(wait_send)
        for part in range(4):
            across(0, part).wait_send()

    @pl.when(on_z)
    def _():
        copies(range(7), z, 8, z_first, owns)(wait_send)
        for part in range(7):
            across(1, part).wait_send()

    @pl.when(on_y & owner)
    def _():
        copies(range(7), z, 8, sends(back_z_first, z))(wait_send)

    @pl.when(on_z & owner)
    def _():
        copies(range(3), y, 4, y_second)(wait_send)
        copies(range(3), y, 4, sends(back_y_first, y))(wait_send)
        copies(range(7), z, 8, sends(back_z_second, z))(wait_send)


def vmem(n):
    return [pl.BlockSpec(memory_space=pltpu.VMEM)] * n


def hbm(n):
    return [pl.BlockSpec(memory_space=pltpu.HBM)] * n


def run_section(neighbours, live_count, occupancy, features, grad_coarse, w_subm, w_down):
    dma = pltpu.SemaphoreType.DMA
    block = pltpu.VMEM((2, SHELL, L), BF16)
    boxes = pltpu.VMEM((8 * PEERS, L), F32)
    sent = pltpu.VMEM((8 * PEERS, L), BF16)
    return pl.pallas_call(
        section_kernel,
        out_shape=(
            jax.ShapeDtypeStruct((PEERS, 6 * L), BF16),
            jax.ShapeDtypeStruct((2, C, V), BF16),
            jax.ShapeDtypeStruct((2 * HALF, L), BF16),
        ),
        in_specs=hbm(7),
        out_specs=tuple(vmem(3)),
        scratch_shapes=[
            pltpu.SMEM((2, 27), jnp.int32),
            pltpu.SMEM((1,), jnp.int32),
            pltpu.SMEM((2, 16), jnp.int32),
            pltpu.VMEM((2, C, V), BF16),
            pltpu.VMEM((PEERS, 6 * L), BF16),
            pltpu.VMEM((27, C, C), BF16),
            pltpu.VMEM((8, C, C), BF16),
            pltpu.VMEM((2 * V, L), F32),
            block, block, block, boxes, boxes, boxes, pltpu.VMEM((6 * PEERS, L), F32),
            sent, sent, sent, sent, sent, sent,
            pltpu.VMEM((7 * SHELL, L), F32),
            pltpu.VMEM((2000, L), F32),
            pltpu.VMEM((1280, 9 * L), BF16),
            pltpu.VMEM((27 * L, L), BF16),
            pltpu.VMEM((9 * L, 3 * L), BF16),
            pltpu.VMEM((8 * L, L), BF16),
            pltpu.VMEM((V, V), BF16),
            pltpu.VMEM((V, V), BF16),
            pltpu.VMEM((L, 6 * L), BF16),
            pltpu.VMEM((2 * V, L), F32),
            pltpu.VMEM((1280, 3 * L), BF16),
            pltpu.VMEM((1280, 2 * L), F32),
            pltpu.VMEM((2000, L), F32),
            pltpu.VMEM((6 * SHELL, L), F32),
            pltpu.VMEM((2 * HALF, L), F32),
            pltpu.VMEM((2 * HALF, L), BF16),
            pltpu.VMEM((HALF, L), BF16),
            pltpu.VMEM((HALF, L), F32),
            pltpu.VMEM((HALF, L), BF16),
            pltpu.VMEM((3, YPART, L), BF16),
            pltpu.VMEM((YPART, L), F32),
            pltpu.VMEM((YPART, L), BF16),
            pltpu.VMEM((7, OWNED, L), BF16),
            pltpu.VMEM((7, ZPART, L), BF16),
            pltpu.VMEM((ZPART, L), F32),
            pltpu.VMEM((ZPART, L), BF16),
            pltpu.VMEM((3, OWNED, L), BF16),
            block, block, block, block,
            dma((7,)), dma((4,)), dma((4,)),
            dma((2,)), dma((2,)), dma((2,)), dma((2,)), dma(()), dma(()),
            dma((3,)), dma((3,)), dma((7,)), dma((7,)), dma((7,)), dma((7,)),
            dma((3,)), dma((3,)), dma((7,)), dma((7,)),
        ],
        compiler_params=pltpu.CompilerParams(
            vmem_limit_bytes=VMEM_LIMIT, collective_id=0, has_side_effects=True
        ),
    )(neighbours, live_count, occupancy, features, grad_coarse, w_subm, w_down)


def final_kernel(
    coarse_in, features_in, total_in, coarse_out, grad_features, grad_subm, grad_down,
    total, subm, down, coarse, features, load_sem, sem,
):
    def chunk(n):
        return pl.ds(9 * C * n, 9 * C)

    loads = [
        pltpu.make_async_copy(total_in.at[chunk(n)], total.at[chunk(n)], load_sem.at[n]) for n in range(3)
    ]
    loads.append(pltpu.make_async_copy(features_in, features, load_sem.at[3]))
    loads.append(pltpu.make_async_copy(coarse_in, coarse, load_sem.at[4]))
    for load in loads:
        load.start()
    copies = [
        pltpu.make_async_copy(features, grad_features, sem.at[0]),
        pltpu.make_async_copy(coarse, coarse_out, sem.at[1]),
    ]
    lane = lax.broadcasted_iota(jnp.int32, (C, L), 1)
    for k in range(35):
        quad, n = divmod(k, 4)
        if k % 12 == 0:
            loads[k // 12].wait()
        if n < 3:
            at = (3 * quad + n) * C
            value = total[at : at + C, :].astype(F32)[:, :C]
        else:
            value = jnp.zeros((C, L), F32)
            for m in range(3):
                at = (3 * quad + m) * C
                piece = pltpu.roll(total[at : at + C, :].astype(F32), 32 + 32 * m, 1)
                value = jnp.where(lane // 32 == m, piece, value)
            value = value[:, :C]
        if k < 27:
            subm[k] = value
        else:
            down[k - 27] = value
        if k in (11, 23, 26):
            part = pl.ds(k // 12 * 12, 12 if k < 26 else 3)
            copies.append(pltpu.make_async_copy(subm.at[part], grad_subm.at[part], sem.at[2 + k // 12]))
            copies[-1].start()
        if k == 11:
            for n in range(2):
                loads[3 + n].wait()
                copies[n].start()
    copies.append(pltpu.make_async_copy(down, grad_down, sem.at[5]))
    copies[-1].start()
    for copy in copies:
        copy.wait()


def run_final(coarse_in, grad_features, total):
    return pl.pallas_call(
        final_kernel,
        out_shape=(
            jax.ShapeDtypeStruct((PEERS, 6 * L), BF16),
            jax.ShapeDtypeStruct((2, C, V), BF16),
            jax.ShapeDtypeStruct((27, C, C), F32),
            jax.ShapeDtypeStruct((8, C, C), F32),
        ),
        in_specs=hbm(3),
        out_specs=tuple(hbm(4)),
        scratch_shapes=[
            pltpu.VMEM((27 * C, L), BF16),
            pltpu.VMEM((27, C, C), F32),
            pltpu.VMEM((8, C, C), F32),
            pltpu.VMEM((PEERS, 6 * L), BF16),
            pltpu.VMEM((2, C, V), BF16),
            pltpu.SemaphoreType.DMA((5,)),
            pltpu.SemaphoreType.DMA((6,)),
        ],
        compiler_params=pltpu.CompilerParams(vmem_limit_bytes=VMEM_LIMIT),
    )(coarse_in, grad_features, total)


def per_device(features, occupancy, neighbours, live_count, w_subm, w_down, grad_coarse):
    return run_final(
        *run_section(neighbours, live_count, occupancy, features, grad_coarse, w_subm, w_down)
    )


def solution(mesh):
    blocks = P(("rep", "space"), None)
    return jax.shard_map(
        per_device,
        mesh=mesh,
        in_specs=(
            P(("rep", "space"), None, None), blocks, blocks, P(("rep", "space")), P(), P(), blocks,
        ),
        out_specs=(
            blocks, P(("rep", "space"), None, None), P("rep", None, None), P("rep", None, None),
        ),
        check_vma=False,
    )
```

```python
import functools

import jax
import jax.numpy as jnp
from jax import lax
from jax.experimental import pallas as pl
from jax.experimental.pallas import tpu as pltpu
from jax.sharding import PartitionSpec as P

C, L, V = 96, 128, 512
OFFSETS = [(a, b, c) for a in (-1, 0, 1) for b in (-1, 0, 1) for c in (-1, 0, 1)]
PEERS, CHIPS, SHELL = 64, 32, 320
YORDER, ZORDER = (1, 0, 2), (3, 2, 4, 1, 5, 0, 6)
SUMS, SPLIT, YPART, ZPART, YOWNED, ZOWNED = 2688, 1792, 448, 128, 64, 32
VMEM_LIMIT = 63 * 2**20 + 2**19
F32, BF16 = jnp.float32, jnp.bfloat16
NT = (((1,), (1,)), ((), ()))


def segments(a, b, c):
    span = {-1: [(7, 0)], 0: [(i, i + 1) for i in range(8)], 1: [(0, 9)]}
    xs, ys, zs = span[a], span[b], span[c]
    face = {0: 0, 7: 64}
    if c == 0:
        return [
            (face[x] + y * 8 if x in face else 112 + x * 16 + y // 7 * 8, 1, tx * 100 + ty * 10 + 1, 1, 8)
            for x, tx in xs
            for y, ty in ys
        ]
    z, tz = zs[0]
    if b == 0:
        return [
            (face[x] + z, 8, tx * 100 + 10 + tz, 10, 8)
            if x in face
            else (208 + x * 16 + z // 7 * 8, 1, tx * 100 + 10 + tz, 10, 8)
            for x, tx in xs
        ]
    y, ty = ys[0]
    if a == 0:
        at = ty * 10 + tz
        return [
            (y * 8 + z, 1, 100 + at, 1, 1),
            (128 + y // 7 * 8 + z, 16, 200 + at, 100, 6),
            (64 + y * 8 + z, 1, 800 + at, 1, 1),
        ]
    x, tx = xs[0]
    return [(face[x] + y * 8 + z, 1, tx * 100 + ty * 10 + tz, 1, 1)]


def shell_pieces():
    pieces = [(0, 0, 1, 64), (64, 448, 1, 64)]
    for x in range(1, 7):
        pieces += [(112 + x * 16, x * 64, 1, 8), (120 + x * 16, x * 64 + 56, 1, 8)]
        pieces += [(208 + x * 16, x * 64, 8, 8), (216 + x * 16, x * 64 + 7, 8, 8)]
    return pieces


def rows(start, count, stride):
    return pl.ds(start, count) if stride == 1 else pl.ds(start, count, stride=stride)


def mask_row(words, live, g):
    lane = lax.broadcasted_iota(jnp.int32, (1, V), 1)
    word = jnp.zeros((1, V), jnp.int32)
    for w in range(16):
        word = jnp.where(lane // 32 == w, words[g, w], word)
    bit = jnp.bitwise_and(jnp.right_shift(word, jnp.bitwise_and(lane, 31)), 1)
    return jnp.where(g < live, bit, 0)


def masked_rows(features, words, live, g):
    bit = mask_row(words, live, g)
    values = jnp.where(bit > 0, features[g].astype(F32), 0.0)
    marks = jnp.broadcast_to(bit.astype(F32), (L - C, V))
    return jnp.transpose(jnp.concatenate([values, marks], axis=0))


def remote(source, target, sent, arrived, peer):
    return pltpu.make_async_remote_copy(
        src_ref=source, dst_ref=target, send_sem=sent, recv_sem=arrived,
        device_id={"space": peer}, device_id_type=pl.DeviceIdType.MESH,
    )


def far_first():
    offsets = [(dy, dz) for dy in range(4) for dz in range(8) if dy or dz]
    return sorted(offsets, key=lambda at: -min(at[0], 4 - at[0]) - min(at[1], 8 - at[1]))


def chip_at(here, offset):
    dy, dz = offset
    return jnp.bitwise_and(here + 8 * dy, CHIPS - 8) + jnp.bitwise_and(here + dz, 7)


def greet(me):
    barrier = pltpu.get_barrier_semaphore()
    here, core = me // 2, lax.rem(me, 2)

    def tell(peer):
        pl.semaphore_signal(
            barrier, inc=1, device_id={"space": peer}, device_id_type=pl.DeviceIdType.MESH
        )

    for offset in far_first():
        tell(chip_at(here, offset) * 2 + core)
    tell(lax.rem(me + 2 * core - 1 + PEERS, PEERS))
    tell(me + 1 - 2 * core)


def greeted():
    pl.semaphore_wait(pltpu.get_barrier_semaphore(), CHIPS + 1)


class Deal:
    def __init__(self, me, outbox, near, far, sent, arrived, far_sent, far_arrived):
        self.here, self.core = me // 2, lax.rem(me, 2)
        self.outbox, self.near = outbox, near
        self.sems = sent, arrived
        self.across = remote(near, far, far_sent, far_arrived, me + 1 - 2 * self.core)
        every = pl.ds(0, 16 * (CHIPS - 1))
        self.every = remote(outbox.at[every], near.at[every], sent, arrived, me + 1 - 2 * self.core)

    def tile(self, chip):
        return pl.ds(pl.multiple_of(chip * 16, 16), 16)

    def start(self):
        for offset in far_first():
            there = chip_at(self.here, offset)
            remote(
                self.outbox.at[self.tile(there)], self.near.at[self.tile(self.here)],
                *self.sems, there * 2 + self.core,
            ).start()
        self.near[self.tile(self.here), :] = self.outbox[self.tile(self.here), :]

    def forward(self):
        self.every.wait_recv()
        self.across.start()

    def finish(self):
        self.across.wait_recv()

    def close(self):
        self.every.wait_send()
        self.across.wait_send()


def box_rows(core, n):
    return pl.ds(core * 8 + n, CHIPS, stride=16)


def section_kernel(
    table_hbm, live_hbm, occupancy_hbm, features_hbm, cotangent_hbm, w_subm_hbm, w_down_hbm,
    coarse_out, grad_features, total,
    table, live_ref, occupancy_ref, features, cotangent, w_subm, w_down,
    own32, own, lower, upper, box32, near32, far32, out32, outbox, near, far, back, back_near, back_far,
    source, pad, cols, wf, wb, wd, perm, permt, spread, pre, dpre3, u, gpad, gsource,
    sums32, sums16, pair_in, chip32, chip16, y_in, y32, y16, z_own, z_in, z32, z16, y_own,
    part_lower, part_upper, from_lower, from_upper,
    load_sem, box_sem, back_sem, halo_sent, halo_arrived,
    rim_sent, rim_arrived, pair_sent, pair_arrived, ysent, yarrived, zsent, zarrived,
    gzsent, gzarrived, gysent, gyarrived, copy_sent, copy_arrived,
):
    me = lax.axis_index("space")
    y, z, core = me // 16, lax.rem(me // 2, 8), lax.rem(me, 2)
    partner = me + 1 - 2 * core
    has_up, has_down = me < PEERS - 1, me > 0
    loads = [
        pltpu.make_async_copy(hbm, ref, load_sem.at[n])
        for n, (hbm, ref) in enumerate(
            (
                (features_hbm, features), (cotangent_hbm, cotangent), (w_subm_hbm, w_subm), (w_down_hbm, w_down),
                (table_hbm, table), (live_hbm, live_ref), (occupancy_hbm, occupancy_ref),
            )
        )
    ]
    for load in loads:
        load.start()
    greet(me)

    i = lax.broadcasted_iota(jnp.int32, (V, V), 0)
    v = lax.broadcasted_iota(jnp.int32, (V, V), 1)

    def placed(index, parts):
        return sum(((index >> a) & b) << c for a, b, c in parts)

    to_voxel = ((8, 1, 6), (7, 1, 3), (6, 1, 0), (4, 3, 7), (2, 3, 4), (0, 3, 1))
    to_child = tuple((c, b, a) for a, b, c in to_voxel)
    perm[...] = jnp.where(placed(i[:, :1], to_voxel) == v, 1.0, 0.0).astype(BF16)
    permt[...] = jnp.where(placed(i[:, :1], to_child) == v, 1.0, 0.0).astype(BF16)
    spread[...] = jnp.where(
        lax.broadcasted_iota(jnp.int32, (L, 6 * L), 1) // 8
        == lax.broadcasted_iota(jnp.int32, (L, 6 * L), 0),
        1.0, 0.0,
    ).astype(BF16)
    wf[...] = jnp.zeros_like(wf)
    wb[...] = jnp.zeros_like(wb)
    wd[...] = jnp.zeros_like(wd)
    dpre3[...] = jnp.zeros_like(dpre3)
    source[6 * SHELL :, :] = jnp.zeros((SHELL, L), F32)

    for n in (0, 4, 5, 6):
        loads[n].wait()
    for g in range(2):
        own32[g * V : (g + 1) * V, :] = masked_rows(features, occupancy_ref, live_ref[0], g)
        for s0, v0, vs, count in shell_pieces():
            source[(2 + g) * SHELL + s0 : (2 + g) * SHELL + s0 + count, :] = own32[rows(g * V + v0, count, vs), :]
        own[g] = source[(2 + g) * SHELL : (3 + g) * SHELL, :].astype(BF16)
    loads[1].wait()
    for n in range(6):
        box32[pl.ds(n, PEERS, stride=8), :] = cotangent[:, n * L : (n + 1) * L].astype(F32)
    counts = jnp.broadcast_to(live_ref[0].astype(F32), (PEERS, L))
    for n in (6, 7):
        box32[pl.ds(n, PEERS, stride=8), :] = counts
    outbox[...] = box32[...].astype(BF16)

    greeted()
    up = remote(own, lower, halo_sent.at[0], halo_arrived.at[0], lax.min(me + 1, PEERS - 1))
    down = remote(own, upper, halo_sent.at[1], halo_arrived.at[1], lax.max(me - 1, 0))

    @pl.when(has_up)
    def _():
        up.start()

    @pl.when(has_down)
    def _():
        down.start()

    deal = Deal(me, outbox, near, far, *(box_sem.at[n] for n in range(4)))
    deal.start()

    loads[2].wait()
    loads[3].wait()
    for k in range(27):
        a, bc = divmod(k, 9)
        w = w_subm[k]
        wf[k * L : k * L + C, :C] = w
        wb[bc * L : bc * L + C, a * L : a * L + C] = w
    for j in range(8):
        wd[j * L : j * L + C, :C] = w_down[j]


    @pl.when(has_down)
    def _():
        up.wait_recv()

    @pl.when(jnp.logical_not(has_down))
    def _():
        lower[...] = jnp.zeros_like(lower)

    @pl.when(has_up)
    def _():
        down.wait_recv()

    @pl.when(jnp.logical_not(has_up))
    def _():
        upper[...] = jnp.zeros_like(upper)

    for g in range(2):
        source[g * SHELL : (g + 1) * SHELL, :] = lower[g].astype(F32)
        source[(4 + g) * SHELL : (5 + g) * SHELL, :] = upper[g].astype(F32)

    for g in range(2):
        for k, offset in enumerate(OFFSETS):
            if k == 13:
                continue
            base = table[g, k] * SHELL
            for s0, ss, p0, ps, count in segments(*offset):
                pad[rows(g * 1000 + p0, count, ps), :] = source[rows(base + s0, count, ss), :]

        for x in range(8):
            for yy in range(8):
                pad[pl.ds(g * 1000 + x * 100 + yy * 10 + 111, 8), :] = own32[pl.ds(g * V + x * 64 + yy * 8, 8), :]

    def columns(gx, carry):
        for b in range(3):
            for c in range(3):
                piece = jnp.concatenate(
                    [pad[pl.ds(gx * 100 + (yy + b) * 10 + c, 8), :] for yy in range(8)], axis=0
                )
                bc = 3 * b + c
                cols[pl.ds(pl.multiple_of(gx * 64, 64), 64), bc * L : (bc + 1) * L] = piece.astype(BF16)
        return carry

    lax.fori_loop(0, 20, columns, 0)

    for g in range(2):
        acc = jnp.zeros((V, L), F32)
        for a in range(3):
            acc += jnp.dot(
                cols[g * 640 + a * 64 : g * 640 + a * 64 + V, :],
                wf[a * 9 * L : (a + 1) * 9 * L, :],
                preferred_element_type=F32,
            )
        pre[g * V : (g + 1) * V, :] = acc

    deal.forward()
    live = live_ref[0]
    s, q = 0.7978845608028654, 0.044715
    slopes, hiddens = [], []
    for g in range(2):
        mask = jnp.broadcast_to(own32[g * V : (g + 1) * V, C : C + 1], (V, L))
        tt = pre[g * V : (g + 1) * V, :]
        th = jnp.tanh(s * (tt + q * tt * tt * tt))
        hidden = 0.5 * tt * (1.0 + th) * mask
        slopes.append((0.5 * (1.0 + th) + 0.5 * tt * (1.0 - th * th) * (s * (1.0 + 3.0 * q * tt * tt))) * mask)
        hiddens.append(jnp.where(lax.broadcasted_iota(jnp.int32, (V, L), 1) < C, hidden, mask).astype(BF16))
    both = jnp.dot(perm[...], jnp.concatenate(hiddens, axis=1), preferred_element_type=F32)
    kids = []
    cmask = jnp.zeros((2 * 64, L), F32)
    coarse = jnp.zeros((2 * 64, L), F32)
    for j in range(8):
        kid = jnp.concatenate([both[j * 64 : (j + 1) * 64, :L], both[j * 64 : (j + 1) * 64, L:]], axis=0)
        cmask = jnp.maximum(cmask, kid)
        kids.append(kid.astype(BF16))
        coarse += jnp.dot(kids[j], wd[j * L : (j + 1) * L, :], preferred_element_type=F32)
    cmask = jnp.broadcast_to(cmask[:, C : C + 1], (2 * 64, L))

    deal.finish()
    near32[...] = near[...].astype(F32)
    far32[...] = far[...].astype(F32)

    def lines(n):
        return jnp.concatenate([near32[box_rows(core, n), :], far32[box_rows(core, n), :]], axis=0)

    def peers(dim, shape):
        order = lax.broadcasted_iota(jnp.int32, shape, dim)
        return jnp.where(order < CHIPS, 2 * order + core, 2 * (order - CHIPS) + 1 - core)

    boxes = jnp.concatenate([lines(n) for n in range(6)], axis=1).astype(BF16)
    below = jnp.where(peers(0, (PEERS, L)) < me, lines(6), 0.0)
    first = jnp.sum(below, axis=0, keepdims=True).astype(jnp.int32)[:, :64]
    row = lax.broadcasted_iota(jnp.int32, (128, 64), 0)
    block, piece = row >> 6, (row >> 3) & 7
    holder = jnp.bitwise_and(jnp.broadcast_to(first, (128, 64)) + block, 7) * 8 + piece
    chosen = jnp.where((holder == peers(1, (128, 64))) & (block < live), 1.0, 0.0).astype(BF16)
    pick = (
        lax.broadcasted_iota(jnp.int32, (128, 6 * L), 1) & 7
        == lax.broadcasted_iota(jnp.int32, (128, 6 * L), 0) & 7
    )
    dz = jnp.dot(chosen, boxes, preferred_element_type=F32)
    dz = jnp.where(pick, dz, 0.0).astype(BF16)
    dz = lax.dot_general(dz, spread[...], NT, preferred_element_type=F32)
    dz = jnp.where(cmask > 0, dz, 0.0)
    dzt = jnp.transpose(dz).astype(BF16)
    dz = dz.astype(BF16)
    dh = [
        lax.dot_general(dz, wd[j * L : (j + 1) * L, :], NT, preferred_element_type=F32) for j in range(8)
    ]
    parts = []
    for g in range(2):
        part = jnp.concatenate([piece[g * 64 : (g + 1) * 64] for piece in dh], axis=0)
        high = part.astype(BF16)
        parts += [high, (part - high.astype(F32)).astype(BF16)]
    dh = jnp.dot(permt[...], jnp.concatenate(parts, axis=1), preferred_element_type=F32)
    for g in range(2):
        dpre = slopes[g] * (dh[:, 2 * g * L : (2 * g + 1) * L] + dh[:, (2 * g + 1) * L : (2 * g + 2) * L])
        dpre16 = dpre.astype(BF16)
        for a in range(3):
            dpre3[g * 640 + a * 64 : g * 640 + a * 64 + V, a * L : (a + 1) * L] = dpre16
        pre[g * V : (g + 1) * V, :] = dpre
    down_sums = jnp.dot(dzt, jnp.concatenate(kids, axis=1), preferred_element_type=F32)

    lane = lax.broadcasted_iota(jnp.int32, (C, L), 1)
    held = {}

    def keep(k, product):
        held[k % 4] = jnp.transpose(product)[:C]
        if k % 4 == 3 or k == 34:
            last = held.get(3)
            for n in range(3):
                slab = held[n]
                if last is not None:
                    slab = jnp.where(lane < C, slab, pltpu.roll(last, C - 32 * n, 1))
                at = (3 * (k // 4) + n) * C
                sums32[at : at + C, :] = slab
                sums16[at : at + C, :] = slab.astype(BF16)
            held.clear()

    dt = jnp.transpose(pre[...]).astype(BF16)
    for a in range(3):
        for bc in range(0, 9, 2):
            lanes = slice(bc * L, min(bc + 2, 9) * L)
            value = jnp.dot(
                dt[:, :V], cols[a * 64 : a * 64 + V, lanes], preferred_element_type=F32
            ) + jnp.dot(
                dt[:, V:], cols[640 + a * 64 : 640 + a * 64 + V, lanes], preferred_element_type=F32
            )
            for n in range(min(2, 9 - bc)):
                keep(a * 9 + bc + n, value[:, n * L : (n + 1) * L])
    for j in range(8):
        keep(27 + j, down_sums[:, j * L : (j + 1) * L])
    sums32[27 * C :, :] = jnp.zeros((C, L), F32)
    sums16[27 * C :, :] = jnp.zeros((C, L), BF16)

    def span(at, count):
        return pl.ds(pl.multiple_of(at, 16), count)

    on_y, on_z, owner = core == 0, core == 1, z < 7
    pair_y = remote(
        sums16.at[pl.ds(0, SPLIT)], pair_in, pair_sent, pair_arrived, partner
    )
    pair_z = remote(
        sums16.at[pl.ds(SPLIT, SUMS - SPLIT)], pair_in.at[pl.ds(0, SUMS - SPLIT)], pair_sent, pair_arrived,
        partner,
    )

    @pl.when(on_y)
    def _():
        pair_z.start()

    @pl.when(on_z)
    def _():
        pair_y.start()

    deal_back = Deal(me, back, back_near, back_far, *(back_sem.at[n] for n in range(4)))
    flat = jnp.dot((coarse * cmask).astype(BF16), spread[...], preferred_element_type=F32)
    flat = jnp.where(pick, flat, 0.0).astype(BF16)
    dealt = lax.dot_general(chosen, flat, (((0,), (0,)), ((), ())), preferred_element_type=F32)
    for n in range(6):
        box32[box_rows(core, n), :] = dealt[:CHIPS, n * L : (n + 1) * L]
        box32[box_rows(1 - core, n), :] = dealt[CHIPS:, n * L : (n + 1) * L]
    back[...] = box32[...].astype(BF16)
    deal_back.start()
    def add_pair(copy, at, count):
        copy.wait_recv()
        value = sums32[at : at + count, :] + pair_in[:count].astype(F32)
        chip32[:count] = value
        chip16[:count] = value.astype(BF16)

    @pl.when(on_y)
    def _():
        add_pair(pair_y, 0, SPLIT)

    @pl.when(on_z)
    def _():
        add_pair(pair_z, SPLIT, SUMS - SPLIT)


    def copies(order, place, size, step, wanted=None):
        def act(what, back=False):
            for n in order:
                to = jnp.bitwise_and(place + (size - n - 1 if back else n + 1), size - 1)
                copy = step(n, to)
                if wanted is None:
                    what(copy)
                else:
                    pl.when(wanted(to))(functools.partial(what, copy))

        return act

    def start(copy):
        copy.start()

    def wait_recv(copy):
        copy.wait_recv()

    def wait_send(copy):
        copy.wait_send()

    def owns(zz):
        return zz < 7

    def low(zz):
        return lax.min(zz, 6)

    def y_first(n, yy):
        return remote(
            chip16.at[span(yy * YPART, YPART)], y_in.at[n], ysent.at[n], yarrived.at[n], yy * 16 + z * 2
        )

    def z_second(n, zz):
        return remote(
            y16.at[span(low(zz) * YOWNED, YOWNED)], z_own.at[n], zsent.at[n], zarrived.at[n], y * 16 + zz * 2
        )

    def z_first(n, zz):
        return remote(
            chip16.at[span(low(zz) * ZPART, ZPART)], z_in.at[n], zsent.at[n], zarrived.at[n],
            y * 16 + zz * 2 + 1,
        )

    def y_second(n, yy):
        return remote(
            z16.at[span(yy * ZOWNED, ZOWNED)], y_own.at[n], ysent.at[n], yarrived.at[n], yy * 16 + z * 2 + 1
        )

    def on_total(at, count, sent, arrived, peer):
        at = span(at, count)
        return remote(total.at[at], total.at[at], sent, arrived, peer)

    def back_z_first(n, to, source):
        return on_total(
            y * YPART + low(source) * YOWNED, YOWNED, gzsent.at[n], gzarrived.at[n], y * 16 + to * 2
        )

    def back_y_second(n, to, source):
        return on_total(source * YPART, YPART, gysent.at[n], gyarrived.at[n], to * 16 + z * 2)

    def back_y_first(n, to, source):
        return on_total(
            SPLIT + low(z) * ZPART + source * ZOWNED, ZOWNED, gysent.at[n], gyarrived.at[n], to * 16 + z * 2 + 1
        )

    def back_z_second(n, to, source):
        return on_total(
            SPLIT + low(source) * ZPART, ZPART, gzsent.at[n], gzarrived.at[n], y * 16 + to * 2 + 1
        )

    def sends(step, mine):
        return lambda n, to: step(n, to, mine)

    def comes(step):
        return lambda n, source: step(n, source, source)

    @pl.when(on_y)
    def _():
        copies(YORDER, y, 4, y_first)(start)

    @pl.when(on_z)
    def _():
        copies(ZORDER, z, 8, z_first, owns)(start)

    gpad[...] = jnp.zeros_like(gpad)
    def pad_gradient(bc):
        width = min(2, 9 - bc)
        u[:, : width * L] = lax.dot_general(
            dpre3[...], wb[bc * L : (bc + width) * L, :], NT, preferred_element_type=F32
        )

        def add(gx, carry):
            for n in range(width):
                b, c = divmod(bc + n, 3)
                for yy in range(8):
                    at = pl.ds(gx * 100 + (yy + b) * 10 + c, 8)
                    gpad[at, :] += u[pl.ds(pl.multiple_of(gx * 64 + yy * 8, 8), 8), n * L : (n + 1) * L]
            return carry

        lax.fori_loop(0, 20, add, 0)

    for bc in (0, 2, 4, 6):
        pad_gradient(bc)

    @pl.when(on_y)
    def _():
        copies(range(3), y, 4, y_first)(wait_recv)
        value = chip32[span(y * YPART, YPART), :]
        for n in range(3):
            value = value + y_in[n].astype(F32)
        y32[...] = value
        y16[...] = value.astype(BF16)
        copies(ZORDER, z, 8, z_second, owns)(start)

    @pl.when(on_z & owner)
    def _():
        copies(range(7), z, 8, z_first)(wait_recv)
        value = chip32[span(z * ZPART, ZPART), :]
        for n in range(7):
            value = value + z_in[n].astype(F32)
        z32[...] = value
        z16[...] = value.astype(BF16)
        copies(YORDER, y, 4, y_second)(start)

    pad_gradient(8)

    gsource[...] = jnp.zeros_like(gsource)

    def give(n, carry):
        for g in range(2):
            for k, offset in enumerate(OFFSETS):
                if k != 13:
                    here = jnp.where(table[g, k] == n, 1.0, 0.0)
                    for s0, ss, p0, ps, count in segments(*offset):
                        at = rows(n * SHELL + s0, count, ss)
                        gsource[at, :] += gpad[rows(g * 1000 + p0, count, ps), :] * here
        return carry

    lax.fori_loop(0, 6, give, 0)
    for g in range(2):
        part_lower[g] = gsource[g * SHELL : (g + 1) * SHELL, :].astype(BF16)
        part_upper[g] = gsource[(4 + g) * SHELL : (5 + g) * SHELL, :].astype(BF16)
    @pl.when(on_y & owner)
    def _():
        copies(range(7), z, 8, z_second)(wait_recv)
        value = y32[span(z * YOWNED, YOWNED), :]
        for n in range(7):
            value = value + z_own[n].astype(F32)
        total[span(y * YPART + z * YOWNED, YOWNED), :] = value.astype(BF16)
        copies(ZORDER, z, 8, sends(back_z_first, z))(start)

    @pl.when(on_z & owner)
    def _():
        copies(range(3), y, 4, y_second)(wait_recv)
        value = z32[span(y * ZOWNED, ZOWNED), :]
        for n in range(3):
            value = value + y_own[n].astype(F32)
        total[span(SPLIT + z * ZPART + y * ZOWNED, ZOWNED), :] = value.astype(BF16)
        copies(YORDER, y, 4, sends(back_y_first, y))(start)

    rim_up = remote(part_upper, from_lower, rim_sent.at[0], rim_arrived.at[0], lax.min(me + 1, PEERS - 1))
    rim_down = remote(part_lower, from_upper, rim_sent.at[1], rim_arrived.at[1], lax.max(me - 1, 0))

    @pl.when(has_up)
    def _():
        rim_up.start()

    @pl.when(has_down)
    def _():
        rim_down.start()

    deal_back.forward()

    def across(which, part):
        rows_at, count = (part * YPART, YPART) if which == 0 else (SPLIT + part * ZPART, ZPART)
        return on_total(rows_at, count, copy_sent.at[part], copy_arrived.at[part], partner)

    @pl.when(on_y)
    def _():
        copies(range(7), z, 8, comes(back_z_first), owns)(wait_recv, back=True)
        copies(YORDER, y, 4, sends(back_y_second, y))(start)
        across(0, y).start()

    @pl.when(on_z & owner)
    def _():
        copies(range(3), y, 4, comes(back_y_first))(wait_recv, back=True)
        copies(ZORDER, z, 8, sends(back_z_second, z))(start)
        across(1, z).start()

    deal_back.finish()
    near32[...] = back_near[...].astype(F32)
    far32[...] = back_far[...].astype(F32)
    for n in range(6):
        out32[pl.ds(n * PEERS + core, CHIPS, stride=2), :] = near32[box_rows(core, n), :]
        out32[pl.ds(n * PEERS + 1 - core, CHIPS, stride=2), :] = far32[box_rows(core, n), :]
    for n in range(6):
        coarse_out[:, n * L : (n + 1) * L] = out32[n * PEERS : (n + 1) * PEERS, :].astype(BF16)

    def pass_on_y(n):
        source = jnp.bitwise_and(y + 3 - n, 3)
        back_y_second(n, source, source).wait_recv()
        across(0, source).start()

    def pass_on_z(n):
        source = jnp.bitwise_and(z + 7 - n, 7)

        @pl.when(owns(source))
        def _():
            back_z_second(n, source, source).wait_recv()
            across(1, low(source)).start()

    @pl.when(on_y)
    def _():
        pass_on_y(0)
        pass_on_y(2)

    @pl.when(on_z)
    def _():
        for n in (0, 6, 1, 5):
            pass_on_z(n)

    @pl.when(has_down)
    def _():
        rim_up.wait_recv()

    @pl.when(jnp.logical_not(has_down))
    def _():
        from_lower[...] = jnp.zeros_like(from_lower)

    @pl.when(has_up)
    def _():
        rim_down.wait_recv()

    @pl.when(jnp.logical_not(has_up))
    def _():
        from_upper[...] = jnp.zeros_like(from_upper)

    for g in range(2):
        shell = gsource[(2 + g) * SHELL : (3 + g) * SHELL, :]
        shell = shell + from_lower[g].astype(F32) + from_upper[g].astype(F32)
        for x in range(8):
            for yy in range(8):
                pre[pl.ds(g * V + x * 64 + yy * 8, 8), :] = gpad[pl.ds(g * 1000 + x * 100 + yy * 10 + 111, 8), :]
        for s0, v0, vs, count in shell_pieces():
            pre[rows(g * V + v0, count, vs), :] += shell[s0 : s0 + count]
        value = pre[g * V : (g + 1) * V, :]
        value = value * jnp.broadcast_to(own32[g * V : (g + 1) * V, C : C + 1], (V, L))
        grad_features[g] = jnp.transpose(value)[:C, :].astype(BF16)

    @pl.when(on_y)
    def _():
        pass_on_y(1)
        for part in range(7):
            across(1, part).wait_recv()

    @pl.when(on_z)
    def _():
        for n in (2, 4, 3):
            pass_on_z(n)
        for part in range(4):
            across(0, part).wait_recv()

    @pl.when(has_up)
    def _():
        up.wait_send()
        rim_up.wait_send()

    @pl.when(has_down)
    def _():
        down.wait_send()
        rim_down.wait_send()

    deal.close()
    deal_back.close()
    @pl.when(on_y)
    def _():
        pair_z.wait_send()
        copies(range(3), y, 4, y_first)(wait_send)
        copies(range(7), z, 8, z_second, owns)(wait_send)
        copies(range(3), y, 4, sends(back_y_second, y))(wait_send)
        for part in range(4):
            across(0, part).wait_send()

    @pl.when(on_z)
    def _():
        pair_y.wait_send()
        copies(range(7), z, 8, z_first, owns)(wait_send)
        for part in range(7):
            across(1, part).wait_send()

    @pl.when(on_y & owner)
    def _():
        copies(range(7), z, 8, sends(back_z_first, z))(wait_send)

    @pl.when(on_z & owner)
    def _():
        copies(range(3), y, 4, y_second)(wait_send)
        copies(range(3), y, 4, sends(back_y_first, y))(wait_send)
        copies(range(7), z, 8, sends(back_z_second, z))(wait_send)


def vmem(n):
    return [pl.BlockSpec(memory_space=pltpu.VMEM)] * n


def hbm(n):
    return [pl.BlockSpec(memory_space=pltpu.HBM)] * n


def run_section(neighbours, live_count, occupancy, features, grad_coarse, w_subm, w_down):
    dma = pltpu.SemaphoreType.DMA
    block = pltpu.VMEM((2, SHELL, L), BF16)
    boxes = pltpu.VMEM((8 * PEERS, L), F32)
    sent = pltpu.VMEM((8 * PEERS, L), BF16)
    return pl.pallas_call(
        section_kernel,
        out_shape=(
            jax.ShapeDtypeStruct((PEERS, 6 * L), BF16),
            jax.ShapeDtypeStruct((2, C, V), BF16),
            jax.ShapeDtypeStruct((SUMS, L), BF16),
        ),
        in_specs=hbm(7),
        out_specs=tuple(vmem(3)),
        scratch_shapes=[
            pltpu.SMEM((2, 27), jnp.int32),
            pltpu.SMEM((1,), jnp.int32),
            pltpu.SMEM((2, 16), jnp.int32),
            pltpu.VMEM((2, C, V), BF16),
            pltpu.VMEM((PEERS, 6 * L), BF16),
            pltpu.VMEM((27, C, C), BF16),
            pltpu.VMEM((8, C, C), BF16),
            pltpu.VMEM((2 * V, L), F32),
            block, block, block, boxes, boxes, boxes, pltpu.VMEM((6 * PEERS, L), F32),
            sent, sent, sent, sent, sent, sent,
            pltpu.VMEM((7 * SHELL, L), F32),
            pltpu.VMEM((2000, L), F32),
            pltpu.VMEM((1280, 9 * L), BF16),
            pltpu.VMEM((27 * L, L), BF16),
            pltpu.VMEM((9 * L, 3 * L), BF16),
            pltpu.VMEM((8 * L, L), BF16),
            pltpu.VMEM((V, V), BF16),
            pltpu.VMEM((V, V), BF16),
            pltpu.VMEM((L, 6 * L), BF16),
            pltpu.VMEM((2 * V, L), F32),
            pltpu.VMEM((1280, 3 * L), BF16),
            pltpu.VMEM((1280, 2 * L), F32),
            pltpu.VMEM((2000, L), F32),
            pltpu.VMEM((6 * SHELL, L), F32),
            pltpu.VMEM((SUMS, L), F32),
            pltpu.VMEM((SUMS, L), BF16),
            pltpu.VMEM((SPLIT, L), BF16),
            pltpu.VMEM((SPLIT, L), F32),
            pltpu.VMEM((SPLIT, L), BF16),
            pltpu.VMEM((3, YPART, L), BF16),
            pltpu.VMEM((YPART, L), F32),
            pltpu.VMEM((YPART, L), BF16),
            pltpu.VMEM((7, YOWNED, L), BF16),
            pltpu.VMEM((7, ZPART, L), BF16),
            pltpu.VMEM((ZPART, L), F32),
            pltpu.VMEM((ZPART, L), BF16),
            pltpu.VMEM((3, ZOWNED, L), BF16),
            block, block, block, block,
            dma((7,)), dma((4,)), dma((4,)),
            dma((2,)), dma((2,)), dma((2,)), dma((2,)), dma(()), dma(()),
            dma((3,)), dma((3,)), dma((7,)), dma((7,)), dma((7,)), dma((7,)),
            dma((3,)), dma((3,)), dma((7,)), dma((7,)),
        ],
        compiler_params=pltpu.CompilerParams(
            vmem_limit_bytes=VMEM_LIMIT, collective_id=0, has_side_effects=True
        ),
    )(neighbours, live_count, occupancy, features, grad_coarse, w_subm, w_down)


def final_kernel(
    coarse_in, features_in, total_in, coarse_out, grad_features, grad_subm, grad_down,
    total, subm, down, coarse, features, load_sem, sem,
):
    def chunk(n):
        return pl.ds(9 * C * n, 9 * C)

    loads = [
        pltpu.make_async_copy(total_in.at[chunk(n)], total.at[chunk(n)], load_sem.at[n]) for n in range(3)
    ]
    loads.append(pltpu.make_async_copy(features_in, features, load_sem.at[3]))
    loads.append(pltpu.make_async_copy(coarse_in, coarse, load_sem.at[4]))
    for load in loads:
        load.start()
    copies = [
        pltpu.make_async_copy(features, grad_features, sem.at[0]),
        pltpu.make_async_copy(coarse, coarse_out, sem.at[1]),
    ]
    lane = lax.broadcasted_iota(jnp.int32, (C, L), 1)
    for k in range(35):
        quad, n = divmod(k, 4)
        if k % 12 == 0:
            loads[k // 12].wait()
        if n < 3:
            at = (3 * quad + n) * C
            value = total[at : at + C, :].astype(F32)[:, :C]
        else:
            value = jnp.zeros((C, L), F32)
            for m in range(3):
                at = (3 * quad + m) * C
                piece = pltpu.roll(total[at : at + C, :].astype(F32), 32 + 32 * m, 1)
                value = jnp.where(lane // 32 == m, piece, value)
            value = value[:, :C]
        if k < 27:
            subm[k] = value
        else:
            down[k - 27] = value
        if k in (11, 23, 26):
            part = pl.ds(k // 12 * 12, 12 if k < 26 else 3)
            copies.append(pltpu.make_async_copy(subm.at[part], grad_subm.at[part], sem.at[2 + k // 12]))
            copies[-1].start()
        if k == 11:
            for n in range(2):
                loads[3 + n].wait()
                copies[n].start()
    copies.append(pltpu.make_async_copy(down, grad_down, sem.at[5]))
    copies[-1].start()
    for copy in copies:
        copy.wait()


def run_final(coarse_in, grad_features, total):
    return pl.pallas_call(
        final_kernel,
        out_shape=(
            jax.ShapeDtypeStruct((PEERS, 6 * L), BF16),
            jax.ShapeDtypeStruct((2, C, V), BF16),
            jax.ShapeDtypeStruct((27, C, C), F32),
            jax.ShapeDtypeStruct((8, C, C), F32),
        ),
        in_specs=hbm(3),
        out_specs=tuple(hbm(4)),
        scratch_shapes=[
            pltpu.VMEM((27 * C, L), BF16),
            pltpu.VMEM((27, C, C), F32),
            pltpu.VMEM((8, C, C), F32),
            pltpu.VMEM((PEERS, 6 * L), BF16),
            pltpu.VMEM((2, C, V), BF16),
            pltpu.SemaphoreType.DMA((5,)),
            pltpu.SemaphoreType.DMA((6,)),
        ],
        compiler_params=pltpu.CompilerParams(vmem_limit_bytes=VMEM_LIMIT),
    )(coarse_in, grad_features, total)


def per_device(features, occupancy, neighbours, live_count, w_subm, w_down, grad_coarse):
    return run_final(
        *run_section(neighbours, live_count, occupancy, features, grad_coarse, w_subm, w_down)
    )


def solution(mesh):
    blocks = P(("rep", "space"), None)
    return jax.shard_map(
        per_device,
        mesh=mesh,
        in_specs=(
            P(("rep", "space"), None, None), blocks, blocks, P(("rep", "space")), P(), P(), blocks,
        ),
        out_specs=(
            blocks, P(("rep", "space"), None, None), P("rep", None, None), P("rep", None, None),
        ),
        check_vma=False,
    )
```

```python
import functools

import jax
import jax.numpy as jnp
from jax import lax
from jax.experimental import pallas as pl
from jax.experimental.pallas import tpu as pltpu
from jax.sharding import PartitionSpec as P

C, L, V = 96, 128, 512
OFFSETS = [(a, b, c) for a in (-1, 0, 1) for b in (-1, 0, 1) for c in (-1, 0, 1)]
PEERS, CHIPS, SHELL = 64, 32, 320
YORDER, ZORDER = (1, 0, 2), (3, 2, 4, 1, 5, 0, 6)
HALF, YPART, ZPART, OWNED = 1344, 336, 192, 48
VMEM_LIMIT = 63 * 2**20 + 2**19
F32, BF16 = jnp.float32, jnp.bfloat16
NT = (((1,), (1,)), ((), ()))


def segments(a, b, c):
    span = {-1: [(7, 0)], 0: [(i, i + 1) for i in range(8)], 1: [(0, 9)]}
    xs, ys, zs = span[a], span[b], span[c]
    face = {0: 0, 7: 64}
    if c == 0:
        return [
            (face[x] + y * 8 if x in face else 112 + x * 16 + y // 7 * 8, 1, tx * 100 + ty * 10 + 1, 1, 8)
            for x, tx in xs
            for y, ty in ys
        ]
    z, tz = zs[0]
    if b == 0:
        return [
            (face[x] + z, 8, tx * 100 + 10 + tz, 10, 8)
            if x in face
            else (208 + x * 16 + z // 7 * 8, 1, tx * 100 + 10 + tz, 10, 8)
            for x, tx in xs
        ]
    y, ty = ys[0]
    if a == 0:
        at = ty * 10 + tz
        return [
            (y * 8 + z, 1, 100 + at, 1, 1),
            (128 + y // 7 * 8 + z, 16, 200 + at, 100, 6),
            (64 + y * 8 + z, 1, 800 + at, 1, 1),
        ]
    x, tx = xs[0]
    return [(face[x] + y * 8 + z, 1, tx * 100 + ty * 10 + tz, 1, 1)]


def shell_pieces():
    pieces = [(0, 0, 1, 64), (64, 448, 1, 64)]
    for x in range(1, 7):
        pieces += [(112 + x * 16, x * 64, 1, 8), (120 + x * 16, x * 64 + 56, 1, 8)]
        pieces += [(208 + x * 16, x * 64, 8, 8), (216 + x * 16, x * 64 + 7, 8, 8)]
    return pieces


def rows(start, count, stride):
    return pl.ds(start, count) if stride == 1 else pl.ds(start, count, stride=stride)


def mask_row(words, live, g):
    lane = lax.broadcasted_iota(jnp.int32, (1, V), 1)
    word = jnp.zeros((1, V), jnp.int32)
    for w in range(16):
        word = jnp.where(lane // 32 == w, words[g, w], word)
    bit = jnp.bitwise_and(jnp.right_shift(word, jnp.bitwise_and(lane, 31)), 1)
    return jnp.where(g < live, bit, 0)


def masked_rows(features, words, live, g):
    bit = mask_row(words, live, g)
    values = jnp.where(bit > 0, features[g].astype(F32), 0.0)
    marks = jnp.broadcast_to(bit.astype(F32), (L - C, V))
    return jnp.transpose(jnp.concatenate([values, marks], axis=0))


def remote(source, target, sent, arrived, peer):
    return pltpu.make_async_remote_copy(
        src_ref=source, dst_ref=target, send_sem=sent, recv_sem=arrived,
        device_id={"space": peer}, device_id_type=pl.DeviceIdType.MESH,
    )


def far_first():
    offsets = [(dy, dz) for dy in range(4) for dz in range(8) if dy or dz]
    return sorted(offsets, key=lambda at: -min(at[0], 4 - at[0]) - min(at[1], 8 - at[1]))


def chip_at(here, offset):
    dy, dz = offset
    return jnp.bitwise_and(here + 8 * dy, CHIPS - 8) + jnp.bitwise_and(here + dz, 7)


def greet(me):
    barrier = pltpu.get_barrier_semaphore()
    here, core = me // 2, lax.rem(me, 2)

    def tell(peer):
        pl.semaphore_signal(
            barrier, inc=1, device_id={"space": peer}, device_id_type=pl.DeviceIdType.MESH
        )

    for offset in far_first():
        tell(chip_at(here, offset) * 2 + core)
    tell(lax.rem(me + 2 * core - 1 + PEERS, PEERS))
    tell(me + 1 - 2 * core)


def greeted():
    pl.semaphore_wait(pltpu.get_barrier_semaphore(), CHIPS + 1)


class Deal:
    def __init__(self, me, outbox, near, far, sent, arrived, far_sent, far_arrived):
        self.here, self.core = me // 2, lax.rem(me, 2)
        self.outbox, self.near = outbox, near
        self.sems = sent, arrived
        self.across = remote(near, far, far_sent, far_arrived, me + 1 - 2 * self.core)
        every = pl.ds(0, 16 * (CHIPS - 1))
        self.every = remote(outbox.at[every], near.at[every], sent, arrived, me + 1 - 2 * self.core)

    def tile(self, chip):
        return pl.ds(pl.multiple_of(chip * 16, 16), 16)

    def start(self):
        for offset in far_first():
            there = chip_at(self.here, offset)
            remote(
                self.outbox.at[self.tile(there)], self.near.at[self.tile(self.here)],
                *self.sems, there * 2 + self.core,
            ).start()
        self.near[self.tile(self.here), :] = self.outbox[self.tile(self.here), :]

    def forward(self):
        self.every.wait_recv()
        self.across.start()

    def finish(self):
        self.across.wait_recv()

    def close(self):
        self.every.wait_send()
        self.across.wait_send()


def box_rows(core, n):
    return pl.ds(core * 8 + n, CHIPS, stride=16)


def section_kernel(
    table_hbm, live_hbm, occupancy_hbm, features_hbm, cotangent_hbm, w_subm_hbm, w_down_hbm,
    coarse_out, grad_features, total,
    table, live_ref, occupancy_ref, features, cotangent, w_subm, w_down,
    own32, own, lower, upper, box32, near32, far32, out32, outbox, near, far, back, back_near, back_far,
    source, pad, cols, wf, wb, wd, perm, permt, spread, pre, dpre3, u, gpad, gsource,
    sums32, sums16, pair_in, chip32, chip16, y_in, y32, y16, z_own, z_in, z32, z16, y_own,
    part_lower, part_upper, from_lower, from_upper,
    load_sem, box_sem, back_sem, halo_sent, halo_arrived,
    rim_sent, rim_arrived, pair_sent, pair_arrived, ysent, yarrived, zsent, zarrived,
    gzsent, gzarrived, gysent, gyarrived, copy_sent, copy_arrived,
):
    me = lax.axis_index("space")
    y, z, core = me // 16, lax.rem(me // 2, 8), lax.rem(me, 2)
    partner = me + 1 - 2 * core
    has_up, has_down = me < PEERS - 1, me > 0
    loads = [
        pltpu.make_async_copy(hbm, ref, load_sem.at[n])
        for n, (hbm, ref) in enumerate(
            (
                (features_hbm, features), (cotangent_hbm, cotangent), (w_subm_hbm, w_subm), (w_down_hbm, w_down),
                (table_hbm, table), (live_hbm, live_ref), (occupancy_hbm, occupancy_ref),
            )
        )
    ]
    for load in loads:
        load.start()
    greet(me)

    i = lax.broadcasted_iota(jnp.int32, (V, V), 0)
    v = lax.broadcasted_iota(jnp.int32, (V, V), 1)

    def placed(index, parts):
        return sum(((index >> a) & b) << c for a, b, c in parts)

    to_voxel = ((8, 1, 6), (7, 1, 3), (6, 1, 0), (4, 3, 7), (2, 3, 4), (0, 3, 1))
    to_child = tuple((c, b, a) for a, b, c in to_voxel)
    perm[...] = jnp.where(placed(i[:, :1], to_voxel) == v, 1.0, 0.0).astype(BF16)
    permt[...] = jnp.where(placed(i[:, :1], to_child) == v, 1.0, 0.0).astype(BF16)
    spread[...] = jnp.where(
        lax.broadcasted_iota(jnp.int32, (L, 6 * L), 1) // 8
        == lax.broadcasted_iota(jnp.int32, (L, 6 * L), 0),
        1.0, 0.0,
    ).astype(BF16)
    wf[...] = jnp.zeros_like(wf)
    wb[...] = jnp.zeros_like(wb)
    wd[...] = jnp.zeros_like(wd)
    dpre3[...] = jnp.zeros_like(dpre3)
    source[6 * SHELL :, :] = jnp.zeros((SHELL, L), F32)

    for n in (0, 4, 5, 6):
        loads[n].wait()
    for g in range(2):
        own32[g * V : (g + 1) * V, :] = masked_rows(features, occupancy_ref, live_ref[0], g)
        for s0, v0, vs, count in shell_pieces():
            source[(2 + g) * SHELL + s0 : (2 + g) * SHELL + s0 + count, :] = own32[rows(g * V + v0, count, vs), :]
        own[g] = source[(2 + g) * SHELL : (3 + g) * SHELL, :].astype(BF16)
    loads[1].wait()
    for n in range(6):
        box32[pl.ds(n, PEERS, stride=8), :] = cotangent[:, n * L : (n + 1) * L].astype(F32)
    counts = jnp.broadcast_to(live_ref[0].astype(F32), (PEERS, L))
    for n in (6, 7):
        box32[pl.ds(n, PEERS, stride=8), :] = counts
    outbox[...] = box32[...].astype(BF16)

    greeted()
    up = remote(own, lower, halo_sent.at[0], halo_arrived.at[0], lax.min(me + 1, PEERS - 1))
    down = remote(own, upper, halo_sent.at[1], halo_arrived.at[1], lax.max(me - 1, 0))

    @pl.when(has_up)
    def _():
        up.start()

    @pl.when(has_down)
    def _():
        down.start()

    deal = Deal(me, outbox, near, far, *(box_sem.at[n] for n in range(4)))
    deal.start()

    loads[2].wait()
    loads[3].wait()
    for k in range(27):
        a, bc = divmod(k, 9)
        w = w_subm[k]
        wf[k * L : k * L + C, :C] = w
        wb[bc * L : bc * L + C, a * L : a * L + C] = w
    for j in range(8):
        wd[j * L : j * L + C, :C] = w_down[j]


    @pl.when(has_down)
    def _():
        up.wait_recv()

    @pl.when(jnp.logical_not(has_down))
    def _():
        lower[...] = jnp.zeros_like(lower)

    @pl.when(has_up)
    def _():
        down.wait_recv()

    @pl.when(jnp.logical_not(has_up))
    def _():
        upper[...] = jnp.zeros_like(upper)

    for g in range(2):
        source[g * SHELL : (g + 1) * SHELL, :] = lower[g].astype(F32)
        source[(4 + g) * SHELL : (5 + g) * SHELL, :] = upper[g].astype(F32)

    for g in range(2):
        for k, offset in enumerate(OFFSETS):
            if k == 13:
                continue
            base = table[g, k] * SHELL
            for s0, ss, p0, ps, count in segments(*offset):
                pad[rows(g * 1000 + p0, count, ps), :] = source[rows(base + s0, count, ss), :]

        for x in range(8):
            for yy in range(8):
                pad[pl.ds(g * 1000 + x * 100 + yy * 10 + 111, 8), :] = own32[pl.ds(g * V + x * 64 + yy * 8, 8), :]

    def columns(gx, carry):
        for b in range(3):
            for c in range(3):
                piece = jnp.concatenate(
                    [pad[pl.ds(gx * 100 + (yy + b) * 10 + c, 8), :] for yy in range(8)], axis=0
                )
                bc = 3 * b + c
                cols[pl.ds(pl.multiple_of(gx * 64, 64), 64), bc * L : (bc + 1) * L] = piece.astype(BF16)
        return carry

    lax.fori_loop(0, 20, columns, 0)

    for g in range(2):
        acc = jnp.zeros((V, L), F32)
        for a in range(3):
            acc += jnp.dot(
                cols[g * 640 + a * 64 : g * 640 + a * 64 + V, :],
                wf[a * 9 * L : (a + 1) * 9 * L, :],
                preferred_element_type=F32,
            )
        pre[g * V : (g + 1) * V, :] = acc

    deal.forward()
    live = live_ref[0]
    s, q = 0.7978845608028654, 0.044715
    slopes, hiddens = [], []
    for g in range(2):
        mask = jnp.broadcast_to(own32[g * V : (g + 1) * V, C : C + 1], (V, L))
        tt = pre[g * V : (g + 1) * V, :]
        th = jnp.tanh(s * (tt + q * tt * tt * tt))
        hidden = 0.5 * tt * (1.0 + th) * mask
        slopes.append((0.5 * (1.0 + th) + 0.5 * tt * (1.0 - th * th) * (s * (1.0 + 3.0 * q * tt * tt))) * mask)
        hiddens.append(jnp.where(lax.broadcasted_iota(jnp.int32, (V, L), 1) < C, hidden, mask).astype(BF16))
    both = jnp.dot(perm[...], jnp.concatenate(hiddens, axis=1), preferred_element_type=F32)
    kids = []
    cmask = jnp.zeros((2 * 64, L), F32)
    coarse = jnp.zeros((2 * 64, L), F32)
    for j in range(8):
        kid = jnp.concatenate([both[j * 64 : (j + 1) * 64, :L], both[j * 64 : (j + 1) * 64, L:]], axis=0)
        cmask = jnp.maximum(cmask, kid)
        kids.append(kid.astype(BF16))
        coarse += jnp.dot(kids[j], wd[j * L : (j + 1) * L, :], preferred_element_type=F32)
    cmask = jnp.broadcast_to(cmask[:, C : C + 1], (2 * 64, L))

    deal.finish()
    near32[...] = near[...].astype(F32)
    far32[...] = far[...].astype(F32)

    def lines(n):
        return jnp.concatenate([near32[box_rows(core, n), :], far32[box_rows(core, n), :]], axis=0)

    def peers(dim, shape):
        order = lax.broadcasted_iota(jnp.int32, shape, dim)
        return jnp.where(order < CHIPS, 2 * order + core, 2 * (order - CHIPS) + 1 - core)

    boxes = jnp.concatenate([lines(n) for n in range(6)], axis=1).astype(BF16)
    below = jnp.where(peers(0, (PEERS, L)) < me, lines(6), 0.0)
    first = jnp.sum(below, axis=0, keepdims=True).astype(jnp.int32)[:, :64]
    row = lax.broadcasted_iota(jnp.int32, (128, 64), 0)
    block, piece = row >> 6, (row >> 3) & 7
    holder = jnp.bitwise_and(jnp.broadcast_to(first, (128, 64)) + block, 7) * 8 + piece
    chosen = jnp.where((holder == peers(1, (128, 64))) & (block < live), 1.0, 0.0).astype(BF16)
    pick = (
        lax.broadcasted_iota(jnp.int32, (128, 6 * L), 1) & 7
        == lax.broadcasted_iota(jnp.int32, (128, 6 * L), 0) & 7
    )
    dz = jnp.dot(chosen, boxes, preferred_element_type=F32)
    dz = jnp.where(pick, dz, 0.0).astype(BF16)
    dz = lax.dot_general(dz, spread[...], NT, preferred_element_type=F32)
    dz = jnp.where(cmask > 0, dz, 0.0)
    dzt = jnp.transpose(dz).astype(BF16)
    dz = dz.astype(BF16)
    dh = [
        lax.dot_general(dz, wd[j * L : (j + 1) * L, :], NT, preferred_element_type=F32) for j in range(8)
    ]
    parts = []
    for g in range(2):
        part = jnp.concatenate([piece[g * 64 : (g + 1) * 64] for piece in dh], axis=0)
        high = part.astype(BF16)
        parts += [high, (part - high.astype(F32)).astype(BF16)]
    dh = jnp.dot(permt[...], jnp.concatenate(parts, axis=1), preferred_element_type=F32)
    for g in range(2):
        dpre = slopes[g] * (dh[:, 2 * g * L : (2 * g + 1) * L] + dh[:, (2 * g + 1) * L : (2 * g + 2) * L])
        dpre16 = dpre.astype(BF16)
        for a in range(3):
            dpre3[g * 640 + a * 64 : g * 640 + a * 64 + V, a * L : (a + 1) * L] = dpre16
        pre[g * V : (g + 1) * V, :] = dpre
    down_sums = jnp.dot(dzt, jnp.concatenate(kids, axis=1), preferred_element_type=F32)

    lane = lax.broadcasted_iota(jnp.int32, (C, L), 1)
    held = {}

    def keep(k, product):
        held[k % 4] = jnp.transpose(product)[:C]
        if k % 4 == 3 or k == 34:
            last = held.get(3)
            for n in range(3):
                slab = held[n]
                if last is not None:
                    slab = jnp.where(lane < C, slab, pltpu.roll(last, C - 32 * n, 1))
                at = (3 * (k // 4) + n) * C
                sums32[at : at + C, :] = slab
                sums16[at : at + C, :] = slab.astype(BF16)
            held.clear()

    dt = jnp.transpose(pre[...]).astype(BF16)
    for a in range(3):
        for bc in range(0, 9, 2):
            lanes = slice(bc * L, min(bc + 2, 9) * L)
            value = jnp.dot(
                dt[:, :V], cols[a * 64 : a * 64 + V, lanes], preferred_element_type=F32
            ) + jnp.dot(
                dt[:, V:], cols[640 + a * 64 : 640 + a * 64 + V, lanes], preferred_element_type=F32
            )
            for n in range(min(2, 9 - bc)):
                keep(a * 9 + bc + n, value[:, n * L : (n + 1) * L])
    for j in range(8):
        keep(27 + j, down_sums[:, j * L : (j + 1) * L])
    sums32[27 * C :, :] = jnp.zeros((C, L), F32)
    sums16[27 * C :, :] = jnp.zeros((C, L), BF16)

    def span(at, count):
        return pl.ds(pl.multiple_of(at, 16), count)

    pair = remote(sums16.at[span((1 - core) * HALF, HALF)], pair_in, pair_sent, pair_arrived, partner)
    pair.start()
    pair.wait_recv()
    value = sums32[span(core * HALF, HALF), :] + pair_in[...].astype(F32)
    chip32[...] = value
    chip16[...] = value.astype(BF16)

    on_y, on_z, owner = core == 0, core == 1, z < 7

    def copies(order, place, size, step, wanted=None):
        def act(what, back=False):
            for n in order:
                to = jnp.bitwise_and(place + (size - n - 1 if back else n + 1), size - 1)
                copy = step(n, to)
                if wanted is None:
                    what(copy)
                else:
                    pl.when(wanted(to))(functools.partial(what, copy))

        return act

    def start(copy):
        copy.start()

    def wait_recv(copy):
        copy.wait_recv()

    def wait_send(copy):
        copy.wait_send()

    def owns(zz):
        return zz < 7

    def low(zz):
        return lax.min(zz, 6)

    def y_first(n, yy):
        return remote(
            chip16.at[span(yy * YPART, YPART)], y_in.at[n], ysent.at[n], yarrived.at[n], yy * 16 + z * 2
        )

    def z_second(n, zz):
        return remote(
            y16.at[span(low(zz) * OWNED, OWNED)], z_own.at[n], zsent.at[n], zarrived.at[n], y * 16 + zz * 2
        )

    def z_first(n, zz):
        return remote(
            chip16.at[span(low(zz) * ZPART, ZPART)], z_in.at[n], zsent.at[n], zarrived.at[n],
            y * 16 + zz * 2 + 1,
        )

    def y_second(n, yy):
        return remote(
            z16.at[span(yy * OWNED, OWNED)], y_own.at[n], ysent.at[n], yarrived.at[n], yy * 16 + z * 2 + 1
        )

    def on_total(at, count, sent, arrived, peer):
        at = span(at, count)
        return remote(total.at[at], total.at[at], sent, arrived, peer)

    def back_z_first(n, to, source):
        return on_total(
            y * YPART + low(source) * OWNED, OWNED, gzsent.at[n], gzarrived.at[n], y * 16 + to * 2
        )

    def back_y_second(n, to, source):
        return on_total(source * YPART, YPART, gysent.at[n], gyarrived.at[n], to * 16 + z * 2)

    def back_y_first(n, to, source):
        return on_total(
            HALF + low(z) * ZPART + source * OWNED, OWNED, gysent.at[n], gyarrived.at[n], to * 16 + z * 2 + 1
        )

    def back_z_second(n, to, source):
        return on_total(
            HALF + low(source) * ZPART, ZPART, gzsent.at[n], gzarrived.at[n], y * 16 + to * 2 + 1
        )

    def sends(step, mine):
        return lambda n, to: step(n, to, mine)

    def comes(step):
        return lambda n, source: step(n, source, source)

    @pl.when(on_y)
    def _():
        copies(YORDER, y, 4, y_first)(start)

    @pl.when(on_z)
    def _():
        copies(ZORDER, z, 8, z_first, owns)(start)

    gpad[...] = jnp.zeros_like(gpad)
    def pad_gradient(bc):
        width = min(2, 9 - bc)
        u[:, : width * L] = lax.dot_general(
            dpre3[...], wb[bc * L : (bc + width) * L, :], NT, preferred_element_type=F32
        )

        def add(gx, carry):
            for n in range(width):
                b, c = divmod(bc + n, 3)
                for yy in range(8):
                    at = pl.ds(gx * 100 + (yy + b) * 10 + c, 8)
                    gpad[at, :] += u[pl.ds(pl.multiple_of(gx * 64 + yy * 8, 8), 8), n * L : (n + 1) * L]
            return carry

        lax.fori_loop(0, 20, add, 0)

    for bc in (0, 2, 4, 6):
        pad_gradient(bc)

    @pl.when(on_y)
    def _():
        copies(range(3), y, 4, y_first)(wait_recv)
        value = chip32[span(y * YPART, YPART), :]
        for n in range(3):
            value = value + y_in[n].astype(F32)
        y32[...] = value
        y16[...] = value.astype(BF16)
        copies(ZORDER, z, 8, z_second, owns)(start)

    @pl.when(on_z & owner)
    def _():
        copies(range(7), z, 8, z_first)(wait_recv)
        value = chip32[span(z * ZPART, ZPART), :]
        for n in range(7):
            value = value + z_in[n].astype(F32)
        z32[...] = value
        z16[...] = value.astype(BF16)
        copies(YORDER, y, 4, y_second)(start)

    deal_back = Deal(me, back, back_near, back_far, *(back_sem.at[n] for n in range(4)))
    flat = jnp.dot((coarse * cmask).astype(BF16), spread[...], preferred_element_type=F32)
    flat = jnp.where(pick, flat, 0.0).astype(BF16)
    dealt = lax.dot_general(chosen, flat, (((0,), (0,)), ((), ())), preferred_element_type=F32)
    for n in range(6):
        box32[box_rows(core, n), :] = dealt[:CHIPS, n * L : (n + 1) * L]
        box32[box_rows(1 - core, n), :] = dealt[CHIPS:, n * L : (n + 1) * L]
    back[...] = box32[...].astype(BF16)
    deal_back.start()

    @pl.when(on_y & owner)
    def _():
        copies(range(7), z, 8, z_second)(wait_recv)
        value = y32[span(z * OWNED, OWNED), :]
        for n in range(7):
            value = value + z_own[n].astype(F32)
        total[span(y * YPART + z * OWNED, OWNED), :] = value.astype(BF16)
        copies(ZORDER, z, 8, sends(back_z_first, z))(start)

    @pl.when(on_z & owner)
    def _():
        copies(range(3), y, 4, y_second)(wait_recv)
        value = z32[span(y * OWNED, OWNED), :]
        for n in range(3):
            value = value + y_own[n].astype(F32)
        total[span(HALF + z * ZPART + y * OWNED, OWNED), :] = value.astype(BF16)
        copies(YORDER, y, 4, sends(back_y_first, y))(start)

    pad_gradient(8)

    gsource[...] = jnp.zeros_like(gsource)

    def give(n, carry):
        for g in range(2):
            for k, offset in enumerate(OFFSETS):
                if k != 13:
                    here = jnp.where(table[g, k] == n, 1.0, 0.0)
                    for s0, ss, p0, ps, count in segments(*offset):
                        at = rows(n * SHELL + s0, count, ss)
                        gsource[at, :] += gpad[rows(g * 1000 + p0, count, ps), :] * here
        return carry

    lax.fori_loop(0, 6, give, 0)
    for g in range(2):
        part_lower[g] = gsource[g * SHELL : (g + 1) * SHELL, :].astype(BF16)
        part_upper[g] = gsource[(4 + g) * SHELL : (5 + g) * SHELL, :].astype(BF16)

    rim_up = remote(part_upper, from_lower, rim_sent.at[0], rim_arrived.at[0], lax.min(me + 1, PEERS - 1))
    rim_down = remote(part_lower, from_upper, rim_sent.at[1], rim_arrived.at[1], lax.max(me - 1, 0))

    @pl.when(has_up)
    def _():
        rim_up.start()

    @pl.when(has_down)
    def _():
        rim_down.start()

    def across(which, part):
        rows_at, count = (part * YPART, YPART) if which == 0 else (HALF + part * ZPART, ZPART)
        return on_total(rows_at, count, copy_sent.at[part], copy_arrived.at[part], partner)

    @pl.when(on_y)
    def _():
        copies(range(7), z, 8, comes(back_z_first), owns)(wait_recv, back=True)
        copies(YORDER, y, 4, sends(back_y_second, y))(start)
        across(0, y).start()

    @pl.when(on_z & owner)
    def _():
        copies(range(3), y, 4, comes(back_y_first))(wait_recv, back=True)
        copies(ZORDER, z, 8, sends(back_z_second, z))(start)
        across(1, z).start()

    deal_back.forward()

    def pass_on_y(n):
        source = jnp.bitwise_and(y + 3 - n, 3)
        back_y_second(n, source, source).wait_recv()
        across(0, source).start()

    def pass_on_z(n):
        source = jnp.bitwise_and(z + 7 - n, 7)

        @pl.when(owns(source))
        def _():
            back_z_second(n, source, source).wait_recv()
            across(1, low(source)).start()

    @pl.when(on_y)
    def _():
        pass_on_y(0)
        pass_on_y(2)

    @pl.when(on_z)
    def _():
        for n in (0, 6, 1, 5):
            pass_on_z(n)

    @pl.when(has_down)
    def _():
        rim_up.wait_recv()

    @pl.when(jnp.logical_not(has_down))
    def _():
        from_lower[...] = jnp.zeros_like(from_lower)

    @pl.when(has_up)
    def _():
        rim_down.wait_recv()

    @pl.when(jnp.logical_not(has_up))
    def _():
        from_upper[...] = jnp.zeros_like(from_upper)

    for g in range(2):
        shell = gsource[(2 + g) * SHELL : (3 + g) * SHELL, :]
        shell = shell + from_lower[g].astype(F32) + from_upper[g].astype(F32)
        for x in range(8):
            for yy in range(8):
                pre[pl.ds(g * V + x * 64 + yy * 8, 8), :] = gpad[pl.ds(g * 1000 + x * 100 + yy * 10 + 111, 8), :]
        for s0, v0, vs, count in shell_pieces():
            pre[rows(g * V + v0, count, vs), :] += shell[s0 : s0 + count]
        value = pre[g * V : (g + 1) * V, :]
        value = value * jnp.broadcast_to(own32[g * V : (g + 1) * V, C : C + 1], (V, L))
        grad_features[g] = jnp.transpose(value)[:C, :].astype(BF16)

    deal_back.finish()
    near32[...] = back_near[...].astype(F32)
    far32[...] = back_far[...].astype(F32)
    for n in range(6):
        out32[pl.ds(n * PEERS + core, CHIPS, stride=2), :] = near32[box_rows(core, n), :]
        out32[pl.ds(n * PEERS + 1 - core, CHIPS, stride=2), :] = far32[box_rows(core, n), :]
    for n in range(6):
        coarse_out[:, n * L : (n + 1) * L] = out32[n * PEERS : (n + 1) * PEERS, :].astype(BF16)

    @pl.when(on_y)
    def _():
        pass_on_y(1)
        for part in range(7):
            across(1, part).wait_recv()

    @pl.when(on_z)
    def _():
        for n in (2, 4, 3):
            pass_on_z(n)
        for part in range(4):
            across(0, part).wait_recv()

    @pl.when(has_up)
    def _():
        up.wait_send()
        rim_up.wait_send()

    @pl.when(has_down)
    def _():
        down.wait_send()
        rim_down.wait_send()

    deal.close()
    deal_back.close()
    pair.wait_send()

    @pl.when(on_y)
    def _():
        copies(range(3), y, 4, y_first)(wait_send)
        copies(range(7), z, 8, z_second, owns)(wait_send)
        copies(range(3), y, 4, sends(back_y_second, y))(wait_send)
        for part in range(4):
            across(0, part).wait_send()

    @pl.when(on_z)
    def _():
        copies(range(7), z, 8, z_first, owns)(wait_send)
        for part in range(7):
            across(1, part).wait_send()

    @pl.when(on_y & owner)
    def _():
        copies(range(7), z, 8, sends(back_z_first, z))(wait_send)

    @pl.when(on_z & owner)
    def _():
        copies(range(3), y, 4, y_second)(wait_send)
        copies(range(3), y, 4, sends(back_y_first, y))(wait_send)
        copies(range(7), z, 8, sends(back_z_second, z))(wait_send)


def vmem(n):
    return [pl.BlockSpec(memory_space=pltpu.VMEM)] * n


def hbm(n):
    return [pl.BlockSpec(memory_space=pltpu.HBM)] * n


def run_section(neighbours, live_count, occupancy, features, grad_coarse, w_subm, w_down):
    dma = pltpu.SemaphoreType.DMA
    block = pltpu.VMEM((2, SHELL, L), BF16)
    boxes = pltpu.VMEM((8 * PEERS, L), F32)
    sent = pltpu.VMEM((8 * PEERS, L), BF16)
    return pl.pallas_call(
        section_kernel,
        out_shape=(
            jax.ShapeDtypeStruct((PEERS, 6 * L), BF16),
            jax.ShapeDtypeStruct((2, C, V), BF16),
            jax.ShapeDtypeStruct((2 * HALF, L), BF16),
        ),
        in_specs=hbm(7),
        out_specs=tuple(vmem(3)),
        scratch_shapes=[
            pltpu.SMEM((2, 27), jnp.int32),
            pltpu.SMEM((1,), jnp.int32),
            pltpu.SMEM((2, 16), jnp.int32),
            pltpu.VMEM((2, C, V), BF16),
            pltpu.VMEM((PEERS, 6 * L), BF16),
            pltpu.VMEM((27, C, C), BF16),
            pltpu.VMEM((8, C, C), BF16),
            pltpu.VMEM((2 * V, L), F32),
            block, block, block, boxes, boxes, boxes, pltpu.VMEM((6 * PEERS, L), F32),
            sent, sent, sent, sent, sent, sent,
            pltpu.VMEM((7 * SHELL, L), F32),
            pltpu.VMEM((2000, L), F32),
            pltpu.VMEM((1280, 9 * L), BF16),
            pltpu.VMEM((27 * L, L), BF16),
            pltpu.VMEM((9 * L, 3 * L), BF16),
            pltpu.VMEM((8 * L, L), BF16),
            pltpu.VMEM((V, V), BF16),
            pltpu.VMEM((V, V), BF16),
            pltpu.VMEM((L, 6 * L), BF16),
            pltpu.VMEM((2 * V, L), F32),
            pltpu.VMEM((1280, 3 * L), BF16),
            pltpu.VMEM((1280, 2 * L), F32),
            pltpu.VMEM((2000, L), F32),
            pltpu.VMEM((6 * SHELL, L), F32),
            pltpu.VMEM((2 * HALF, L), F32),
            pltpu.VMEM((2 * HALF, L), BF16),
            pltpu.VMEM((HALF, L), BF16),
            pltpu.VMEM((HALF, L), F32),
            pltpu.VMEM((HALF, L), BF16),
            pltpu.VMEM((3, YPART, L), BF16),
            pltpu.VMEM((YPART, L), F32),
            pltpu.VMEM((YPART, L), BF16),
            pltpu.VMEM((7, OWNED, L), BF16),
            pltpu.VMEM((7, ZPART, L), BF16),
            pltpu.VMEM((ZPART, L), F32),
            pltpu.VMEM((ZPART, L), BF16),
            pltpu.VMEM((3, OWNED, L), BF16),
            block, block, block, block,
            dma((7,)), dma((4,)), dma((4,)),
            dma((2,)), dma((2,)), dma((2,)), dma((2,)), dma(()), dma(()),
            dma((3,)), dma((3,)), dma((7,)), dma((7,)), dma((7,)), dma((7,)),
            dma((3,)), dma((3,)), dma((7,)), dma((7,)),
        ],
        compiler_params=pltpu.CompilerParams(
            vmem_limit_bytes=VMEM_LIMIT, collective_id=0, has_side_effects=True
        ),
    )(neighbours, live_count, occupancy, features, grad_coarse, w_subm, w_down)


def final_kernel(
    coarse_in, features_in, total_in, coarse_out, grad_features, grad_subm, grad_down,
    total, subm, down, coarse, features, load_sem, sem,
):
    def chunk(n):
        return pl.ds(9 * C * n, 9 * C)

    loads = [
        pltpu.make_async_copy(total_in.at[chunk(n)], total.at[chunk(n)], load_sem.at[n]) for n in range(3)
    ]
    loads.append(pltpu.make_async_copy(features_in, features, load_sem.at[3]))
    loads.append(pltpu.make_async_copy(coarse_in, coarse, load_sem.at[4]))
    for load in loads:
        load.start()
    copies = [
        pltpu.make_async_copy(features, grad_features, sem.at[0]),
        pltpu.make_async_copy(coarse, coarse_out, sem.at[1]),
    ]
    lane = lax.broadcasted_iota(jnp.int32, (C, L), 1)
    for k in range(35):
        quad, n = divmod(k, 4)
        if k % 12 == 0:
            loads[k // 12].wait()
        if n < 3:
            at = (3 * quad + n) * C
            value = total[at : at + C, :].astype(F32)[:, :C]
        else:
            value = jnp.zeros((C, L), F32)
            for m in range(3):
                at = (3 * quad + m) * C
                piece = pltpu.roll(total[at : at + C, :].astype(F32), 32 + 32 * m, 1)
                value = jnp.where(lane // 32 == m, piece, value)
            value = value[:, :C]
        if k < 27:
            subm[k] = value
        else:
            down[k - 27] = value
        if k in (11, 23, 26):
            part = pl.ds(k // 12 * 12, 12 if k < 26 else 3)
            copies.append(pltpu.make_async_copy(subm.at[part], grad_subm.at[part], sem.at[2 + k // 12]))
            copies[-1].start()
        if k == 11:
            for n in range(2):
                loads[3 + n].wait()
                copies[n].start()
    copies.append(pltpu.make_async_copy(down, grad_down, sem.at[5]))
    copies[-1].start()
    for copy in copies:
        copy.wait()


def run_final(coarse_in, grad_features, total):
    return pl.pallas_call(
        final_kernel,
        out_shape=(
            jax.ShapeDtypeStruct((PEERS, 6 * L), BF16),
            jax.ShapeDtypeStruct((2, C, V), BF16),
            jax.ShapeDtypeStruct((27, C, C), F32),
            jax.ShapeDtypeStruct((8, C, C), F32),
        ),
        in_specs=hbm(3),
        out_specs=tuple(hbm(4)),
        scratch_shapes=[
            pltpu.VMEM((27 * C, L), BF16),
            pltpu.VMEM((27, C, C), F32),
            pltpu.VMEM((8, C, C), F32),
            pltpu.VMEM((PEERS, 6 * L), BF16),
            pltpu.VMEM((2, C, V), BF16),
            pltpu.SemaphoreType.DMA((5,)),
            pltpu.SemaphoreType.DMA((6,)),
        ],
        compiler_params=pltpu.CompilerParams(vmem_limit_bytes=VMEM_LIMIT),
    )(coarse_in, grad_features, total)


def per_device(features, occupancy, neighbours, live_count, w_subm, w_down, grad_coarse):
    return run_final(
        *run_section(neighbours, live_count, occupancy, features, grad_coarse, w_subm, w_down)
    )


def solution(mesh):
    blocks = P(("rep", "space"), None)
    return jax.shard_map(
        per_device,
        mesh=mesh,
        in_specs=(
            P(("rep", "space"), None, None), blocks, blocks, P(("rep", "space")), P(), P(), blocks,
        ),
        out_specs=(
            blocks, P(("rep", "space"), None, None), P("rep", None, None), P("rep", None, None),
        ),
        check_vma=False,
    )
```

```python
import functools

import jax
import jax.numpy as jnp
from jax import lax
from jax.experimental import pallas as pl
from jax.experimental.pallas import tpu as pltpu
from jax.sharding import PartitionSpec as P

C, L, V = 96, 128, 512
OFFSETS = [(a, b, c) for a in (-1, 0, 1) for b in (-1, 0, 1) for c in (-1, 0, 1)]
PEERS, CHIPS, SHELL = 64, 32, 320
YORDER, ZORDER = (1, 0, 2), (3, 2, 4, 1, 5, 0, 6)
HALF, YPART, ZPART, OWNED = 1344, 336, 192, 48
VMEM_LIMIT = 63 * 2**20 + 2**19
F32, BF16 = jnp.float32, jnp.bfloat16
NT = (((1,), (1,)), ((), ()))


def segments(a, b, c):
    span = {-1: [(7, 0)], 0: [(i, i + 1) for i in range(8)], 1: [(0, 9)]}
    xs, ys, zs = span[a], span[b], span[c]
    face = {0: 0, 7: 64}
    if c == 0:
        return [
            (face[x] + y * 8 if x in face else 112 + x * 16 + y // 7 * 8, 1, tx * 100 + ty * 10 + 1, 1, 8)
            for x, tx in xs
            for y, ty in ys
        ]
    z, tz = zs[0]
    if b == 0:
        return [
            (face[x] + z, 8, tx * 100 + 10 + tz, 10, 8)
            if x in face
            else (208 + x * 16 + z // 7 * 8, 1, tx * 100 + 10 + tz, 10, 8)
            for x, tx in xs
        ]
    y, ty = ys[0]
    if a == 0:
        at = ty * 10 + tz
        return [
            (y * 8 + z, 1, 100 + at, 1, 1),
            (128 + y // 7 * 8 + z, 16, 200 + at, 100, 6),
            (64 + y * 8 + z, 1, 800 + at, 1, 1),
        ]
    x, tx = xs[0]
    return [(face[x] + y * 8 + z, 1, tx * 100 + ty * 10 + tz, 1, 1)]


def shell_pieces():
    pieces = [(0, 0, 1, 64), (64, 448, 1, 64)]
    for x in range(1, 7):
        pieces += [(112 + x * 16, x * 64, 1, 8), (120 + x * 16, x * 64 + 56, 1, 8)]
        pieces += [(208 + x * 16, x * 64, 8, 8), (216 + x * 16, x * 64 + 7, 8, 8)]
    return pieces


def rows(start, count, stride):
    return pl.ds(start, count) if stride == 1 else pl.ds(start, count, stride=stride)


def mask_row(words, live, g):
    lane = lax.broadcasted_iota(jnp.int32, (1, V), 1)
    word = jnp.zeros((1, V), jnp.int32)
    for w in range(16):
        word = jnp.where(lane // 32 == w, words[g, w], word)
    bit = jnp.bitwise_and(jnp.right_shift(word, jnp.bitwise_and(lane, 31)), 1)
    return jnp.where(g < live, bit, 0)


def masked_rows(features, words, live, g):
    bit = mask_row(words, live, g)
    values = jnp.where(bit > 0, features[g].astype(F32), 0.0)
    marks = jnp.broadcast_to(bit.astype(F32), (L - C, V))
    return jnp.transpose(jnp.concatenate([values, marks], axis=0))


def remote(source, target, sent, arrived, peer):
    return pltpu.make_async_remote_copy(
        src_ref=source, dst_ref=target, send_sem=sent, recv_sem=arrived,
        device_id={"space": peer}, device_id_type=pl.DeviceIdType.MESH,
    )


def far_first():
    offsets = [(dy, dz) for dy in range(4) for dz in range(8) if dy or dz]
    return sorted(offsets, key=lambda at: -min(at[0], 4 - at[0]) - min(at[1], 8 - at[1]))


def chip_at(here, offset):
    dy, dz = offset
    return jnp.bitwise_and(here + 8 * dy, CHIPS - 8) + jnp.bitwise_and(here + dz, 7)


def greet(me):
    barrier = pltpu.get_barrier_semaphore()
    here, core = me // 2, lax.rem(me, 2)

    def tell(peer):
        pl.semaphore_signal(
            barrier, inc=1, device_id={"space": peer}, device_id_type=pl.DeviceIdType.MESH
        )

    for offset in far_first():
        tell(chip_at(here, offset) * 2 + core)
    tell(lax.rem(me + 2 * core - 1 + PEERS, PEERS))
    tell(me + 1 - 2 * core)


def greeted():
    pl.semaphore_wait(pltpu.get_barrier_semaphore(), CHIPS + 1)


class Deal:
    def __init__(self, me, outbox, near, far, sent, arrived, far_sent, far_arrived):
        self.here, self.core = me // 2, lax.rem(me, 2)
        self.outbox, self.near = outbox, near
        self.sems = sent, arrived
        self.across = remote(near, far, far_sent, far_arrived, me + 1 - 2 * self.core)
        every = pl.ds(0, 16 * (CHIPS - 1))
        self.every = remote(outbox.at[every], near.at[every], sent, arrived, me + 1 - 2 * self.core)

    def tile(self, chip):
        return pl.ds(pl.multiple_of(chip * 16, 16), 16)

    def start(self):
        for offset in far_first():
            there = chip_at(self.here, offset)
            remote(
                self.outbox.at[self.tile(there)], self.near.at[self.tile(self.here)],
                *self.sems, there * 2 + self.core,
            ).start()
        self.near[self.tile(self.here), :] = self.outbox[self.tile(self.here), :]

    def forward(self):
        self.every.wait_recv()
        self.across.start()

    def finish(self):
        self.across.wait_recv()

    def close(self):
        self.every.wait_send()
        self.across.wait_send()


def box_rows(core, n):
    return pl.ds(core * 8 + n, CHIPS, stride=16)


def section_kernel(
    table_hbm, live_hbm, occupancy_hbm, features_hbm, cotangent_hbm, w_subm_hbm, w_down_hbm,
    coarse_out, grad_features, total,
    table, live_ref, occupancy_ref, features, cotangent, w_subm, w_down,
    own32, own, lower, upper, box32, near32, far32, out32, outbox, near, far, back, back_near, back_far,
    source, pad, cols, wf, wb, wd, perm, permt, spread, pre, dpre3, u, gpad, gsource,
    sums32, sums16, pair_in, chip32, chip16, y_in, y32, y16, z_own, z_in, z32, z16, y_own,
    part_lower, part_upper, from_lower, from_upper,
    load_sem, box_sem, back_sem, halo_sent, halo_arrived,
    rim_sent, rim_arrived, pair_sent, pair_arrived, ysent, yarrived, zsent, zarrived,
    gzsent, gzarrived, gysent, gyarrived, copy_sent, copy_arrived,
):
    me = lax.axis_index("space")
    y, z, core = me // 16, lax.rem(me // 2, 8), lax.rem(me, 2)
    partner = me + 1 - 2 * core
    has_up, has_down = me < PEERS - 1, me > 0
    loads = [
        pltpu.make_async_copy(hbm, ref, load_sem.at[n])
        for n, (hbm, ref) in enumerate(
            (
                (features_hbm, features), (cotangent_hbm, cotangent), (w_subm_hbm, w_subm), (w_down_hbm, w_down),
                (table_hbm, table), (live_hbm, live_ref), (occupancy_hbm, occupancy_ref),
            )
        )
    ]
    for load in loads:
        load.start()
    greet(me)

    i = lax.broadcasted_iota(jnp.int32, (V, V), 0)
    v = lax.broadcasted_iota(jnp.int32, (V, V), 1)

    def placed(index, parts):
        return sum(((index >> a) & b) << c for a, b, c in parts)

    to_voxel = ((8, 1, 6), (7, 1, 3), (6, 1, 0), (4, 3, 7), (2, 3, 4), (0, 3, 1))
    to_child = tuple((c, b, a) for a, b, c in to_voxel)
    perm[...] = jnp.where(placed(i[:, :1], to_voxel) == v, 1.0, 0.0).astype(BF16)
    permt[...] = jnp.where(placed(i[:, :1], to_child) == v, 1.0, 0.0).astype(BF16)
    spread[...] = jnp.where(
        lax.broadcasted_iota(jnp.int32, (L, 6 * L), 1) // 8
        == lax.broadcasted_iota(jnp.int32, (L, 6 * L), 0),
        1.0, 0.0,
    ).astype(BF16)
    wf[...] = jnp.zeros_like(wf)
    wb[...] = jnp.zeros_like(wb)
    wd[...] = jnp.zeros_like(wd)
    dpre3[...] = jnp.zeros_like(dpre3)
    source[6 * SHELL :, :] = jnp.zeros((SHELL, L), F32)

    for n in (0, 4, 5, 6):
        loads[n].wait()
    for g in range(2):
        own32[g * V : (g + 1) * V, :] = masked_rows(features, occupancy_ref, live_ref[0], g)
        for s0, v0, vs, count in shell_pieces():
            source[(2 + g) * SHELL + s0 : (2 + g) * SHELL + s0 + count, :] = own32[rows(g * V + v0, count, vs), :]
        own[g] = source[(2 + g) * SHELL : (3 + g) * SHELL, :].astype(BF16)
    loads[1].wait()
    for n in range(6):
        box32[pl.ds(n, PEERS, stride=8), :] = cotangent[:, n * L : (n + 1) * L].astype(F32)
    counts = jnp.broadcast_to(live_ref[0].astype(F32), (PEERS, L))
    for n in (6, 7):
        box32[pl.ds(n, PEERS, stride=8), :] = counts
    outbox[...] = box32[...].astype(BF16)

    greeted()
    up = remote(own, lower, halo_sent.at[0], halo_arrived.at[0], lax.min(me + 1, PEERS - 1))
    down = remote(own, upper, halo_sent.at[1], halo_arrived.at[1], lax.max(me - 1, 0))

    @pl.when(has_up)
    def _():
        up.start()

    @pl.when(has_down)
    def _():
        down.start()

    deal = Deal(me, outbox, near, far, *(box_sem.at[n] for n in range(4)))
    deal.start()

    loads[2].wait()
    loads[3].wait()
    for k in range(27):
        a, bc = divmod(k, 9)
        w = w_subm[k]
        wf[k * L : k * L + C, :C] = w
        wb[bc * L : bc * L + C, a * L : a * L + C] = w
    for j in range(8):
        wd[j * L : j * L + C, :C] = w_down[j]


    @pl.when(has_down)
    def _():
        up.wait_recv()

    @pl.when(jnp.logical_not(has_down))
    def _():
        lower[...] = jnp.zeros_like(lower)

    @pl.when(has_up)
    def _():
        down.wait_recv()

    @pl.when(jnp.logical_not(has_up))
    def _():
        upper[...] = jnp.zeros_like(upper)

    for g in range(2):
        source[g * SHELL : (g + 1) * SHELL, :] = lower[g].astype(F32)
        source[(4 + g) * SHELL : (5 + g) * SHELL, :] = upper[g].astype(F32)

    for g in range(2):
        for k, offset in enumerate(OFFSETS):
            if k == 13:
                continue
            base = table[g, k] * SHELL
            for s0, ss, p0, ps, count in segments(*offset):
                pad[rows(g * 1000 + p0, count, ps), :] = source[rows(base + s0, count, ss), :]

        for x in range(8):
            for yy in range(8):
                pad[pl.ds(g * 1000 + x * 100 + yy * 10 + 111, 8), :] = own32[pl.ds(g * V + x * 64 + yy * 8, 8), :]

    def columns(gx, carry):
        for b in range(3):
            for c in range(3):
                piece = jnp.concatenate(
                    [pad[pl.ds(gx * 100 + (yy + b) * 10 + c, 8), :] for yy in range(8)], axis=0
                )
                bc = 3 * b + c
                cols[pl.ds(pl.multiple_of(gx * 64, 64), 64), bc * L : (bc + 1) * L] = piece.astype(BF16)
        return carry

    lax.fori_loop(0, 20, columns, 0)

    for g in range(2):
        acc = jnp.zeros((V, L), F32)
        for a in range(3):
            acc += jnp.dot(
                cols[g * 640 + a * 64 : g * 640 + a * 64 + V, :],
                wf[a * 9 * L : (a + 1) * 9 * L, :],
                preferred_element_type=F32,
            )
        pre[g * V : (g + 1) * V, :] = acc

    deal.forward()
    live = live_ref[0]
    s, q = 0.7978845608028654, 0.044715
    slopes, hiddens = [], []
    for g in range(2):
        mask = jnp.broadcast_to(own32[g * V : (g + 1) * V, C : C + 1], (V, L))
        tt = pre[g * V : (g + 1) * V, :]
        th = jnp.tanh(s * (tt + q * tt * tt * tt))
        hidden = 0.5 * tt * (1.0 + th) * mask
        slopes.append((0.5 * (1.0 + th) + 0.5 * tt * (1.0 - th * th) * (s * (1.0 + 3.0 * q * tt * tt))) * mask)
        hiddens.append(jnp.where(lax.broadcasted_iota(jnp.int32, (V, L), 1) < C, hidden, mask).astype(BF16))
    both = jnp.dot(perm[...], jnp.concatenate(hiddens, axis=1), preferred_element_type=F32)
    kids = []
    cmask = jnp.zeros((2 * 64, L), F32)
    coarse = jnp.zeros((2 * 64, L), F32)
    for j in range(8):
        kid = jnp.concatenate([both[j * 64 : (j + 1) * 64, :L], both[j * 64 : (j + 1) * 64, L:]], axis=0)
        cmask = jnp.maximum(cmask, kid)
        kids.append(kid.astype(BF16))
        coarse += jnp.dot(kids[j], wd[j * L : (j + 1) * L, :], preferred_element_type=F32)
    cmask = jnp.broadcast_to(cmask[:, C : C + 1], (2 * 64, L))

    deal.finish()
    near32[...] = near[...].astype(F32)
    far32[...] = far[...].astype(F32)

    def lines(n):
        return jnp.concatenate([near32[box_rows(core, n), :], far32[box_rows(core, n), :]], axis=0)

    def peers(dim, shape):
        order = lax.broadcasted_iota(jnp.int32, shape, dim)
        return jnp.where(order < CHIPS, 2 * order + core, 2 * (order - CHIPS) + 1 - core)

    boxes = jnp.concatenate([lines(n) for n in range(6)], axis=1).astype(BF16)
    below = jnp.where(peers(0, (PEERS, L)) < me, lines(6), 0.0)
    first = jnp.sum(below, axis=0, keepdims=True).astype(jnp.int32)[:, :64]
    row = lax.broadcasted_iota(jnp.int32, (128, 64), 0)
    block, piece = row >> 6, (row >> 3) & 7
    holder = jnp.bitwise_and(jnp.broadcast_to(first, (128, 64)) + block, 7) * 8 + piece
    chosen = jnp.where((holder == peers(1, (128, 64))) & (block < live), 1.0, 0.0).astype(BF16)
    pick = (
        lax.broadcasted_iota(jnp.int32, (128, 6 * L), 1) & 7
        == lax.broadcasted_iota(jnp.int32, (128, 6 * L), 0) & 7
    )
    dz = jnp.dot(chosen, boxes, preferred_element_type=F32)
    dz = jnp.where(pick, dz, 0.0).astype(BF16)
    dz = lax.dot_general(dz, spread[...], NT, preferred_element_type=F32)
    dz = jnp.where(cmask > 0, dz, 0.0)
    dzt = jnp.transpose(dz).astype(BF16)
    dz = dz.astype(BF16)
    dh = lax.dot_general(dz, wd[...], NT, preferred_element_type=F32)
    dh = [dh[:, j * L : (j + 1) * L] for j in range(8)]
    parts = []
    for g in range(2):
        part = jnp.concatenate([piece[g * 64 : (g + 1) * 64] for piece in dh], axis=0)
        high = part.astype(BF16)
        parts += [high, (part - high.astype(F32)).astype(BF16)]
    dh = jnp.dot(permt[...], jnp.concatenate(parts, axis=1), preferred_element_type=F32)
    for g in range(2):
        dpre = slopes[g] * (dh[:, 2 * g * L : (2 * g + 1) * L] + dh[:, (2 * g + 1) * L : (2 * g + 2) * L])
        dpre16 = dpre.astype(BF16)
        for a in range(3):
            dpre3[g * 640 + a * 64 : g * 640 + a * 64 + V, a * L : (a + 1) * L] = dpre16
        pre[g * V : (g + 1) * V, :] = dpre
    down_sums = jnp.dot(dzt, jnp.concatenate(kids, axis=1), preferred_element_type=F32)

    lane = lax.broadcasted_iota(jnp.int32, (C, L), 1)
    held = {}

    def keep(k, product):
        held[k % 4] = jnp.transpose(product)[:C]
        if k % 4 == 3 or k == 34:
            last = held.get(3)
            for n in range(3):
                slab = held[n]
                if last is not None:
                    slab = jnp.where(lane < C, slab, pltpu.roll(last, C - 32 * n, 1))
                at = (3 * (k // 4) + n) * C
                sums32[at : at + C, :] = slab
                sums16[at : at + C, :] = slab.astype(BF16)
            held.clear()

    dt = jnp.transpose(pre[...]).astype(BF16)
    for a in range(3):
        for bc in range(0, 9, 2):
            lanes = slice(bc * L, min(bc + 2, 9) * L)
            value = jnp.dot(
                dt[:, :V], cols[a * 64 : a * 64 + V, lanes], preferred_element_type=F32
            ) + jnp.dot(
                dt[:, V:], cols[640 + a * 64 : 640 + a * 64 + V, lanes], preferred_element_type=F32
            )
            for n in range(min(2, 9 - bc)):
                keep(a * 9 + bc + n, value[:, n * L : (n + 1) * L])
    for j in range(8):
        keep(27 + j, down_sums[:, j * L : (j + 1) * L])
    sums32[27 * C :, :] = jnp.zeros((C, L), F32)
    sums16[27 * C :, :] = jnp.zeros((C, L), BF16)

    def span(at, count):
        return pl.ds(pl.multiple_of(at, 16), count)

    pair = remote(sums16.at[span((1 - core) * HALF, HALF)], pair_in, pair_sent, pair_arrived, partner)
    pair.start()
    pair.wait_recv()
    value = sums32[span(core * HALF, HALF), :] + pair_in[...].astype(F32)
    chip32[...] = value
    chip16[...] = value.astype(BF16)

    on_y, on_z, owner = core == 0, core == 1, z < 7

    def copies(order, place, size, step, wanted=None):
        def act(what, back=False):
            for n in order:
                to = jnp.bitwise_and(place + (size - n - 1 if back else n + 1), size - 1)
                copy = step(n, to)
                if wanted is None:
                    what(copy)
                else:
                    pl.when(wanted(to))(functools.partial(what, copy))

        return act

    def start(copy):
        copy.start()

    def wait_recv(copy):
        copy.wait_recv()

    def wait_send(copy):
        copy.wait_send()

    def owns(zz):
        return zz < 7

    def low(zz):
        return lax.min(zz, 6)

    def y_first(n, yy):
        return remote(
            chip16.at[span(yy * YPART, YPART)], y_in.at[n], ysent.at[n], yarrived.at[n], yy * 16 + z * 2
        )

    def z_second(n, zz):
        return remote(
            y16.at[span(low(zz) * OWNED, OWNED)], z_own.at[n], zsent.at[n], zarrived.at[n], y * 16 + zz * 2
        )

    def z_first(n, zz):
        return remote(
            chip16.at[span(low(zz) * ZPART, ZPART)], z_in.at[n], zsent.at[n], zarrived.at[n],
            y * 16 + zz * 2 + 1,
        )

    def y_second(n, yy):
        return remote(
            z16.at[span(yy * OWNED, OWNED)], y_own.at[n], ysent.at[n], yarrived.at[n], yy * 16 + z * 2 + 1
        )

    def on_total(at, count, sent, arrived, peer):
        at = span(at, count)
        return remote(total.at[at], total.at[at], sent, arrived, peer)

    def back_z_first(n, to, source):
        return on_total(
            y * YPART + low(source) * OWNED, OWNED, gzsent.at[n], gzarrived.at[n], y * 16 + to * 2
        )

    def back_y_second(n, to, source):
        return on_total(source * YPART, YPART, gysent.at[n], gyarrived.at[n], to * 16 + z * 2)

    def back_y_first(n, to, source):
        return on_total(
            HALF + low(z) * ZPART + source * OWNED, OWNED, gysent.at[n], gyarrived.at[n], to * 16 + z * 2 + 1
        )

    def back_z_second(n, to, source):
        return on_total(
            HALF + low(source) * ZPART, ZPART, gzsent.at[n], gzarrived.at[n], y * 16 + to * 2 + 1
        )

    def sends(step, mine):
        return lambda n, to: step(n, to, mine)

    def comes(step):
        return lambda n, source: step(n, source, source)

    @pl.when(on_y)
    def _():
        copies(YORDER, y, 4, y_first)(start)

    @pl.when(on_z)
    def _():
        copies(ZORDER, z, 8, z_first, owns)(start)

    deal_back = Deal(me, back, back_near, back_far, *(back_sem.at[n] for n in range(4)))
    flat = jnp.dot((coarse * cmask).astype(BF16), spread[...], preferred_element_type=F32)
    flat = jnp.where(pick, flat, 0.0).astype(BF16)
    dealt = lax.dot_general(chosen, flat, (((0,), (0,)), ((), ())), preferred_element_type=F32)
    for n in range(6):
        box32[box_rows(core, n), :] = dealt[:CHIPS, n * L : (n + 1) * L]
        box32[box_rows(1 - core, n), :] = dealt[CHIPS:, n * L : (n + 1) * L]
    back[...] = box32[...].astype(BF16)
    deal_back.start()

    gpad[...] = jnp.zeros_like(gpad)
    def pad_gradient(bc):
        width = min(2, 9 - bc)
        u[:, : width * L] = lax.dot_general(
            dpre3[...], wb[bc * L : (bc + width) * L, :], NT, preferred_element_type=F32
        )

        def add(gx, carry):
            for n in range(width):
                b, c = divmod(bc + n, 3)
                for yy in range(8):
                    at = pl.ds(gx * 100 + (yy + b) * 10 + c, 8)
                    gpad[at, :] += u[pl.ds(pl.multiple_of(gx * 64 + yy * 8, 8), 8), n * L : (n + 1) * L]
            return carry

        lax.fori_loop(0, 20, add, 0)

    for bc in (0, 2):
        pad_gradient(bc)

    @pl.when(on_y)
    def _():
        copies(range(3), y, 4, y_first)(wait_recv)
        value = chip32[span(y * YPART, YPART), :]
        for n in range(3):
            value = value + y_in[n].astype(F32)
        y32[...] = value
        y16[...] = value.astype(BF16)
        copies(ZORDER, z, 8, z_second, owns)(start)

    @pl.when(on_z & owner)
    def _():
        copies(range(7), z, 8, z_first)(wait_recv)
        value = chip32[span(z * ZPART, ZPART), :]
        for n in range(7):
            value = value + z_in[n].astype(F32)
        z32[...] = value
        z16[...] = value.astype(BF16)
        copies(YORDER, y, 4, y_second)(start)

    for bc in (4, 6):
        pad_gradient(bc)

    @pl.when(on_y & owner)
    def _():
        copies(range(7), z, 8, z_second)(wait_recv)
        value = y32[span(z * OWNED, OWNED), :]
        for n in range(7):
            value = value + z_own[n].astype(F32)
        total[span(y * YPART + z * OWNED, OWNED), :] = value.astype(BF16)
        copies(ZORDER, z, 8, sends(back_z_first, z))(start)

    @pl.when(on_z & owner)
    def _():
        copies(range(3), y, 4, y_second)(wait_recv)
        value = z32[span(y * OWNED, OWNED), :]
        for n in range(3):
            value = value + y_own[n].astype(F32)
        total[span(HALF + z * ZPART + y * OWNED, OWNED), :] = value.astype(BF16)
        copies(YORDER, y, 4, sends(back_y_first, y))(start)

    deal_back.forward()
    pad_gradient(8)

    gsource[...] = jnp.zeros_like(gsource)

    def give(n, carry):
        for g in range(2):
            for k, offset in enumerate(OFFSETS):
                if k != 13:
                    here = jnp.where(table[g, k] == n, 1.0, 0.0)
                    for s0, ss, p0, ps, count in segments(*offset):
                        at = rows(n * SHELL + s0, count, ss)
                        gsource[at, :] += gpad[rows(g * 1000 + p0, count, ps), :] * here
        return carry

    lax.fori_loop(0, 6, give, 0)
    for g in range(2):
        part_lower[g] = gsource[g * SHELL : (g + 1) * SHELL, :].astype(BF16)
        part_upper[g] = gsource[(4 + g) * SHELL : (5 + g) * SHELL, :].astype(BF16)
    rim_up = remote(part_upper, from_lower, rim_sent.at[0], rim_arrived.at[0], lax.min(me + 1, PEERS - 1))
    rim_down = remote(part_lower, from_upper, rim_sent.at[1], rim_arrived.at[1], lax.max(me - 1, 0))

    @pl.when(has_up)
    def _():
        rim_up.start()

    @pl.when(has_down)
    def _():
        rim_down.start()

    def across(which, part):
        rows_at, count = (part * YPART, YPART) if which == 0 else (HALF + part * ZPART, ZPART)
        return on_total(rows_at, count, copy_sent.at[part], copy_arrived.at[part], partner)

    @pl.when(on_y)
    def _():
        copies(range(7), z, 8, comes(back_z_first), owns)(wait_recv, back=True)
        copies(YORDER, y, 4, sends(back_y_second, y))(start)
        across(0, y).start()

    @pl.when(on_z & owner)
    def _():
        copies(range(3), y, 4, comes(back_y_first))(wait_recv, back=True)
        copies(ZORDER, z, 8, sends(back_z_second, z))(start)
        across(1, z).start()

    deal_back.finish()
    near32[...] = back_near[...].astype(F32)
    far32[...] = back_far[...].astype(F32)
    for n in range(6):
        out32[pl.ds(n * PEERS + core, CHIPS, stride=2), :] = near32[box_rows(core, n), :]
        out32[pl.ds(n * PEERS + 1 - core, CHIPS, stride=2), :] = far32[box_rows(core, n), :]
    for n in range(6):
        coarse_out[:, n * L : (n + 1) * L] = out32[n * PEERS : (n + 1) * PEERS, :].astype(BF16)

    def pass_on_y(n):
        source = jnp.bitwise_and(y + 3 - n, 3)
        back_y_second(n, source, source).wait_recv()
        across(0, source).start()

    def pass_on_z(n):
        source = jnp.bitwise_and(z + 7 - n, 7)

        @pl.when(owns(source))
        def _():
            back_z_second(n, source, source).wait_recv()
            across(1, low(source)).start()

    @pl.when(on_y)
    def _():
        pass_on_y(0)
        pass_on_y(2)

    @pl.when(on_z)
    def _():
        for n in (0, 6, 1, 5):
            pass_on_z(n)

    @pl.when(has_down)
    def _():
        rim_up.wait_recv()

    @pl.when(jnp.logical_not(has_down))
    def _():
        from_lower[...] = jnp.zeros_like(from_lower)

    @pl.when(has_up)
    def _():
        rim_down.wait_recv()

    @pl.when(jnp.logical_not(has_up))
    def _():
        from_upper[...] = jnp.zeros_like(from_upper)

    for g in range(2):
        shell = gsource[(2 + g) * SHELL : (3 + g) * SHELL, :]
        shell = shell + from_lower[g].astype(F32) + from_upper[g].astype(F32)
        for x in range(8):
            for yy in range(8):
                pre[pl.ds(g * V + x * 64 + yy * 8, 8), :] = gpad[pl.ds(g * 1000 + x * 100 + yy * 10 + 111, 8), :]
        for s0, v0, vs, count in shell_pieces():
            pre[rows(g * V + v0, count, vs), :] += shell[s0 : s0 + count]
        value = pre[g * V : (g + 1) * V, :]
        value = value * jnp.broadcast_to(own32[g * V : (g + 1) * V, C : C + 1], (V, L))
        grad_features[g] = jnp.transpose(value)[:C, :].astype(BF16)

    @pl.when(on_y)
    def _():
        pass_on_y(1)
        for part in range(7):
            across(1, part).wait_recv()

    @pl.when(on_z)
    def _():
        for n in (2, 4, 3):
            pass_on_z(n)
        for part in range(4):
            across(0, part).wait_recv()

    @pl.when(has_up)
    def _():
        up.wait_send()
        rim_up.wait_send()

    @pl.when(has_down)
    def _():
        down.wait_send()
        rim_down.wait_send()

    deal.close()
    deal_back.close()
    pair.wait_send()

    @pl.when(on_y)
    def _():
        copies(range(3), y, 4, y_first)(wait_send)
        copies(range(7), z, 8, z_second, owns)(wait_send)
        copies(range(3), y, 4, sends(back_y_second, y))(wait_send)
        for part in range(4):
            across(0, part).wait_send()

    @pl.when(on_z)
    def _():
        copies(range(7), z, 8, z_first, owns)(wait_send)
        for part in range(7):
            across(1, part).wait_send()

    @pl.when(on_y & owner)
    def _():
        copies(range(7), z, 8, sends(back_z_first, z))(wait_send)

    @pl.when(on_z & owner)
    def _():
        copies(range(3), y, 4, y_second)(wait_send)
        copies(range(3), y, 4, sends(back_y_first, y))(wait_send)
        copies(range(7), z, 8, sends(back_z_second, z))(wait_send)


def vmem(n):
    return [pl.BlockSpec(memory_space=pltpu.VMEM)] * n


def hbm(n):
    return [pl.BlockSpec(memory_space=pltpu.HBM)] * n


def run_section(neighbours, live_count, occupancy, features, grad_coarse, w_subm, w_down):
    dma = pltpu.SemaphoreType.DMA
    block = pltpu.VMEM((2, SHELL, L), BF16)
    boxes = pltpu.VMEM((8 * PEERS, L), F32)
    sent = pltpu.VMEM((8 * PEERS, L), BF16)
    return pl.pallas_call(
        section_kernel,
        out_shape=(
            jax.ShapeDtypeStruct((PEERS, 6 * L), BF16),
            jax.ShapeDtypeStruct((2, C, V), BF16),
            jax.ShapeDtypeStruct((2 * HALF, L), BF16),
        ),
        in_specs=hbm(7),
        out_specs=tuple(vmem(3)),
        scratch_shapes=[
            pltpu.SMEM((2, 27), jnp.int32),
            pltpu.SMEM((1,), jnp.int32),
            pltpu.SMEM((2, 16), jnp.int32),
            pltpu.VMEM((2, C, V), BF16),
            pltpu.VMEM((PEERS, 6 * L), BF16),
            pltpu.VMEM((27, C, C), BF16),
            pltpu.VMEM((8, C, C), BF16),
            pltpu.VMEM((2 * V, L), F32),
            block, block, block, boxes, boxes, boxes, pltpu.VMEM((6 * PEERS, L), F32),
            sent, sent, sent, sent, sent, sent,
            pltpu.VMEM((7 * SHELL, L), F32),
            pltpu.VMEM((2000, L), F32),
            pltpu.VMEM((1280, 9 * L), BF16),
            pltpu.VMEM((27 * L, L), BF16),
            pltpu.VMEM((9 * L, 3 * L), BF16),
            pltpu.VMEM((8 * L, L), BF16),
            pltpu.VMEM((V, V), BF16),
            pltpu.VMEM((V, V), BF16),
            pltpu.VMEM((L, 6 * L), BF16),
            pltpu.VMEM((2 * V, L), F32),
            pltpu.VMEM((1280, 3 * L), BF16),
            pltpu.VMEM((1280, 2 * L), F32),
            pltpu.VMEM((2000, L), F32),
            pltpu.VMEM((6 * SHELL, L), F32),
            pltpu.VMEM((2 * HALF, L), F32),
            pltpu.VMEM((2 * HALF, L), BF16),
            pltpu.VMEM((HALF, L), BF16),
            pltpu.VMEM((HALF, L), F32),
            pltpu.VMEM((HALF, L), BF16),
            pltpu.VMEM((3, YPART, L), BF16),
            pltpu.VMEM((YPART, L), F32),
            pltpu.VMEM((YPART, L), BF16),
            pltpu.VMEM((7, OWNED, L), BF16),
            pltpu.VMEM((7, ZPART, L), BF16),
            pltpu.VMEM((ZPART, L), F32),
            pltpu.VMEM((ZPART, L), BF16),
            pltpu.VMEM((3, OWNED, L), BF16),
            block, block, block, block,
            dma((7,)), dma((4,)), dma((4,)),
            dma((2,)), dma((2,)), dma((2,)), dma((2,)), dma(()), dma(()),
            dma((3,)), dma((3,)), dma((7,)), dma((7,)), dma((7,)), dma((7,)),
            dma((3,)), dma((3,)), dma((7,)), dma((7,)),
        ],
        compiler_params=pltpu.CompilerParams(
            vmem_limit_bytes=VMEM_LIMIT, collective_id=0, has_side_effects=True
        ),
    )(neighbours, live_count, occupancy, features, grad_coarse, w_subm, w_down)


def final_kernel(
    coarse_in, features_in, total_in, coarse_out, grad_features, grad_subm, grad_down,
    total, subm, down, coarse, features, load_sem, sem,
):
    def chunk(n):
        return pl.ds(9 * C * n, 9 * C)

    loads = [
        pltpu.make_async_copy(total_in.at[chunk(n)], total.at[chunk(n)], load_sem.at[n]) for n in range(3)
    ]
    loads.append(pltpu.make_async_copy(features_in, features, load_sem.at[3]))
    loads.append(pltpu.make_async_copy(coarse_in, coarse, load_sem.at[4]))
    for load in loads:
        load.start()
    copies = [
        pltpu.make_async_copy(features, grad_features, sem.at[0]),
        pltpu.make_async_copy(coarse, coarse_out, sem.at[1]),
    ]
    lane = lax.broadcasted_iota(jnp.int32, (C, L), 1)
    for k in range(35):
        quad, n = divmod(k, 4)
        if k % 12 == 0:
            loads[k // 12].wait()
        if n < 3:
            at = (3 * quad + n) * C
            value = total[at : at + C, :].astype(F32)[:, :C]
        else:
            value = jnp.zeros((C, L), F32)
            for m in range(3):
                at = (3 * quad + m) * C
                piece = pltpu.roll(total[at : at + C, :].astype(F32), 32 + 32 * m, 1)
                value = jnp.where(lane // 32 == m, piece, value)
            value = value[:, :C]
        if k < 27:
            subm[k] = value
        else:
            down[k - 27] = value
        if k in (11, 23, 26):
            part = pl.ds(k // 12 * 12, 12 if k < 26 else 3)
            copies.append(pltpu.make_async_copy(subm.at[part], grad_subm.at[part], sem.at[2 + k // 12]))
            copies[-1].start()
        if k == 11:
            for n in range(2):
                loads[3 + n].wait()
                copies[n].start()
    copies.append(pltpu.make_async_copy(down, grad_down, sem.at[5]))
    copies[-1].start()
    for copy in copies:
        copy.wait()


def run_final(coarse_in, grad_features, total):
    return pl.pallas_call(
        final_kernel,
        out_shape=(
            jax.ShapeDtypeStruct((PEERS, 6 * L), BF16),
            jax.ShapeDtypeStruct((2, C, V), BF16),
            jax.ShapeDtypeStruct((27, C, C), F32),
            jax.ShapeDtypeStruct((8, C, C), F32),
        ),
        in_specs=hbm(3),
        out_specs=tuple(hbm(4)),
        scratch_shapes=[
            pltpu.VMEM((27 * C, L), BF16),
            pltpu.VMEM((27, C, C), F32),
            pltpu.VMEM((8, C, C), F32),
            pltpu.VMEM((PEERS, 6 * L), BF16),
            pltpu.VMEM((2, C, V), BF16),
            pltpu.SemaphoreType.DMA((5,)),
            pltpu.SemaphoreType.DMA((6,)),
        ],
        compiler_params=pltpu.CompilerParams(vmem_limit_bytes=VMEM_LIMIT),
    )(coarse_in, grad_features, total)


def per_device(features, occupancy, neighbours, live_count, w_subm, w_down, grad_coarse):
    return run_final(
        *run_section(neighbours, live_count, occupancy, features, grad_coarse, w_subm, w_down)
    )


def solution(mesh):
    blocks = P(("rep", "space"), None)
    return jax.shard_map(
        per_device,
        mesh=mesh,
        in_specs=(
            P(("rep", "space"), None, None), blocks, blocks, P(("rep", "space")), P(), P(), blocks,
        ),
        out_specs=(
            blocks, P(("rep", "space"), None, None), P("rep", None, None), P("rep", None, None),
        ),
        check_vma=False,
    )
```

```python
import functools

import jax
import jax.numpy as jnp
from jax import lax
from jax.experimental import pallas as pl
from jax.experimental.pallas import tpu as pltpu
from jax.sharding import PartitionSpec as P

C, L, V = 96, 128, 512
OFFSETS = [(a, b, c) for a in (-1, 0, 1) for b in (-1, 0, 1) for c in (-1, 0, 1)]
PEERS, CHIPS, SHELL = 64, 32, 320
YORDER, ZORDER = (1, 0, 2), (3, 2, 4, 1, 5, 0, 6)
HALF, YPART, ZPART, OWNED = 1344, 336, 192, 48
VMEM_LIMIT = 63 * 2**20 + 2**19
F32, BF16 = jnp.float32, jnp.bfloat16
NT = (((1,), (1,)), ((), ()))


def segments(a, b, c):
    span = {-1: [(7, 0)], 0: [(i, i + 1) for i in range(8)], 1: [(0, 9)]}
    xs, ys, zs = span[a], span[b], span[c]
    face = {0: 0, 7: 64}
    if c == 0:
        return [
            (face[x] + y * 8 if x in face else 112 + x * 16 + y // 7 * 8, 1, tx * 100 + ty * 10 + 1, 1, 8)
            for x, tx in xs
            for y, ty in ys
        ]
    z, tz = zs[0]
    if b == 0:
        return [
            (face[x] + z, 8, tx * 100 + 10 + tz, 10, 8)
            if x in face
            else (208 + x * 16 + z // 7 * 8, 1, tx * 100 + 10 + tz, 10, 8)
            for x, tx in xs
        ]
    y, ty = ys[0]
    if a == 0:
        at = ty * 10 + tz
        return [
            (y * 8 + z, 1, 100 + at, 1, 1),
            (128 + y // 7 * 8 + z, 16, 200 + at, 100, 6),
            (64 + y * 8 + z, 1, 800 + at, 1, 1),
        ]
    x, tx = xs[0]
    return [(face[x] + y * 8 + z, 1, tx * 100 + ty * 10 + tz, 1, 1)]


def shell_pieces():
    pieces = [(0, 0, 1, 64), (64, 448, 1, 64)]
    for x in range(1, 7):
        pieces += [(112 + x * 16, x * 64, 1, 8), (120 + x * 16, x * 64 + 56, 1, 8)]
        pieces += [(208 + x * 16, x * 64, 8, 8), (216 + x * 16, x * 64 + 7, 8, 8)]
    return pieces


def rows(start, count, stride):
    return pl.ds(start, count) if stride == 1 else pl.ds(start, count, stride=stride)


def mask_row(words, live, g):
    lane = lax.broadcasted_iota(jnp.int32, (1, V), 1)
    word = jnp.zeros((1, V), jnp.int32)
    for w in range(16):
        word = jnp.where(lane // 32 == w, words[g, w], word)
    bit = jnp.bitwise_and(jnp.right_shift(word, jnp.bitwise_and(lane, 31)), 1)
    return jnp.where(g < live, bit, 0)


def masked_rows(features, words, live, g):
    bit = mask_row(words, live, g)
    values = jnp.where(bit > 0, features[g].astype(F32), 0.0)
    marks = jnp.broadcast_to(bit.astype(F32), (L - C, V))
    return jnp.transpose(jnp.concatenate([values, marks], axis=0))


def remote(source, target, sent, arrived, peer):
    return pltpu.make_async_remote_copy(
        src_ref=source, dst_ref=target, send_sem=sent, recv_sem=arrived,
        device_id={"space": peer}, device_id_type=pl.DeviceIdType.MESH,
    )


def far_first():
    offsets = [(dy, dz) for dy in range(4) for dz in range(8) if dy or dz]
    return sorted(offsets, key=lambda at: -min(at[0], 4 - at[0]) - min(at[1], 8 - at[1]))


def chip_at(here, offset):
    dy, dz = offset
    return jnp.bitwise_and(here + 8 * dy, CHIPS - 8) + jnp.bitwise_and(here + dz, 7)


def greet(me):
    barrier = pltpu.get_barrier_semaphore()
    here, core = me // 2, lax.rem(me, 2)

    def tell(peer):
        pl.semaphore_signal(
            barrier, inc=1, device_id={"space": peer}, device_id_type=pl.DeviceIdType.MESH
        )

    for offset in far_first():
        tell(chip_at(here, offset) * 2 + core)
    tell(lax.rem(me + 2 * core - 1 + PEERS, PEERS))
    tell(me + 1 - 2 * core)


def greeted():
    pl.semaphore_wait(pltpu.get_barrier_semaphore(), CHIPS + 1)


class Deal:
    def __init__(self, me, outbox, near, far, sent, arrived, far_sent, far_arrived):
        self.here, self.core = me // 2, lax.rem(me, 2)
        self.outbox, self.near = outbox, near
        self.sems = sent, arrived
        self.across = remote(near, far, far_sent, far_arrived, me + 1 - 2 * self.core)
        every = pl.ds(0, 16 * (CHIPS - 1))
        self.every = remote(outbox.at[every], near.at[every], sent, arrived, me + 1 - 2 * self.core)

    def tile(self, chip):
        return pl.ds(pl.multiple_of(chip * 16, 16), 16)

    def start(self, first=0, last=CHIPS - 1):
        for offset in far_first()[first:last]:
            there = chip_at(self.here, offset)
            remote(
                self.outbox.at[self.tile(there)], self.near.at[self.tile(self.here)],
                *self.sems, there * 2 + self.core,
            ).start()
        if last == CHIPS - 1:
            self.near[self.tile(self.here), :] = self.outbox[self.tile(self.here), :]

    def forward(self):
        self.every.wait_recv()
        self.across.start()

    def finish(self):
        self.across.wait_recv()

    def close(self):
        self.every.wait_send()
        self.across.wait_send()


def box_rows(core, n):
    return pl.ds(core * 8 + n, CHIPS, stride=16)


def section_kernel(
    table_hbm, live_hbm, occupancy_hbm, features_hbm, cotangent_hbm, w_subm_hbm, w_down_hbm,
    coarse_out, grad_features, total,
    table, live_ref, occupancy_ref, features, cotangent, w_subm, w_down,
    own32, own, lower, upper, box32, near32, far32, out32, outbox, near, far, back, back_near, back_far,
    source, pad, cols, wf, wb, wd, perm, permt, spread, pre, dpre3, u, gpad, gsource,
    sums32, sums16, pair_in, chip32, chip16, y_in, y32, y16, z_own, z_in, z32, z16, y_own,
    part_lower, part_upper, from_lower, from_upper,
    load_sem, box_sem, back_sem, halo_sent, halo_arrived,
    rim_sent, rim_arrived, pair_sent, pair_arrived, ysent, yarrived, zsent, zarrived,
    gzsent, gzarrived, gysent, gyarrived, copy_sent, copy_arrived,
):
    me = lax.axis_index("space")
    y, z, core = me // 16, lax.rem(me // 2, 8), lax.rem(me, 2)
    partner = me + 1 - 2 * core
    has_up, has_down = me < PEERS - 1, me > 0
    loads = [
        pltpu.make_async_copy(hbm, ref, load_sem.at[n])
        for n, (hbm, ref) in enumerate(
            (
                (features_hbm, features), (cotangent_hbm, cotangent), (w_subm_hbm, w_subm), (w_down_hbm, w_down),
                (table_hbm, table), (live_hbm, live_ref), (occupancy_hbm, occupancy_ref),
            )
        )
    ]
    for load in loads:
        load.start()
    greet(me)

    i = lax.broadcasted_iota(jnp.int32, (V, V), 0)
    v = lax.broadcasted_iota(jnp.int32, (V, V), 1)

    def placed(index, parts):
        return sum(((index >> a) & b) << c for a, b, c in parts)

    to_voxel = ((8, 1, 6), (7, 1, 3), (6, 1, 0), (4, 3, 7), (2, 3, 4), (0, 3, 1))
    to_child = tuple((c, b, a) for a, b, c in to_voxel)
    perm[...] = jnp.where(placed(i[:, :1], to_voxel) == v, 1.0, 0.0).astype(BF16)
    permt[...] = jnp.where(placed(i[:, :1], to_child) == v, 1.0, 0.0).astype(BF16)
    spread[...] = jnp.where(
        lax.broadcasted_iota(jnp.int32, (L, 6 * L), 1) // 8
        == lax.broadcasted_iota(jnp.int32, (L, 6 * L), 0),
        1.0, 0.0,
    ).astype(BF16)
    wf[...] = jnp.zeros_like(wf)
    wb[...] = jnp.zeros_like(wb)
    wd[...] = jnp.zeros_like(wd)
    dpre3[...] = jnp.zeros_like(dpre3)
    source[6 * SHELL :, :] = jnp.zeros((SHELL, L), F32)

    for n in (0, 4, 5, 6):
        loads[n].wait()
    for g in range(2):
        own32[g * V : (g + 1) * V, :] = masked_rows(features, occupancy_ref, live_ref[0], g)
        for s0, v0, vs, count in shell_pieces():
            source[(2 + g) * SHELL + s0 : (2 + g) * SHELL + s0 + count, :] = own32[rows(g * V + v0, count, vs), :]
        own[g] = source[(2 + g) * SHELL : (3 + g) * SHELL, :].astype(BF16)
    loads[1].wait()
    for n in range(6):
        box32[pl.ds(n, PEERS, stride=8), :] = cotangent[:, n * L : (n + 1) * L].astype(F32)
    counts = jnp.broadcast_to(live_ref[0].astype(F32), (PEERS, L))
    for n in (6, 7):
        box32[pl.ds(n, PEERS, stride=8), :] = counts
    outbox[...] = box32[...].astype(BF16)

    greeted()
    up = remote(own, lower, halo_sent.at[0], halo_arrived.at[0], lax.min(me + 1, PEERS - 1))
    down = remote(own, upper, halo_sent.at[1], halo_arrived.at[1], lax.max(me - 1, 0))

    @pl.when(has_up)
    def _():
        up.start()

    @pl.when(has_down)
    def _():
        down.start()

    deal = Deal(me, outbox, near, far, *(box_sem.at[n] for n in range(4)))
    deal.start()

    loads[2].wait()
    loads[3].wait()
    for k in range(27):
        a, bc = divmod(k, 9)
        w = w_subm[k]
        wf[k * L : k * L + C, :C] = w
        wb[bc * L : bc * L + C, a * L : a * L + C] = w
    for j in range(8):
        wd[j * L : j * L + C, :C] = w_down[j]


    @pl.when(has_down)
    def _():
        up.wait_recv()

    @pl.when(jnp.logical_not(has_down))
    def _():
        lower[...] = jnp.zeros_like(lower)

    @pl.when(has_up)
    def _():
        down.wait_recv()

    @pl.when(jnp.logical_not(has_up))
    def _():
        upper[...] = jnp.zeros_like(upper)

    for g in range(2):
        source[g * SHELL : (g + 1) * SHELL, :] = lower[g].astype(F32)
        source[(4 + g) * SHELL : (5 + g) * SHELL, :] = upper[g].astype(F32)

    for g in range(2):
        for k, offset in enumerate(OFFSETS):
            if k == 13:
                continue
            base = table[g, k] * SHELL
            for s0, ss, p0, ps, count in segments(*offset):
                pad[rows(g * 1000 + p0, count, ps), :] = source[rows(base + s0, count, ss), :]

        for x in range(8):
            for yy in range(8):
                pad[pl.ds(g * 1000 + x * 100 + yy * 10 + 111, 8), :] = own32[pl.ds(g * V + x * 64 + yy * 8, 8), :]

    def columns(gx, carry):
        for b in range(3):
            for c in range(3):
                piece = jnp.concatenate(
                    [pad[pl.ds(gx * 100 + (yy + b) * 10 + c, 8), :] for yy in range(8)], axis=0
                )
                bc = 3 * b + c
                cols[pl.ds(pl.multiple_of(gx * 64, 64), 64), bc * L : (bc + 1) * L] = piece.astype(BF16)
        return carry

    lax.fori_loop(0, 20, columns, 0)

    for g in range(2):
        acc = jnp.zeros((V, L), F32)
        for a in range(3):
            acc += jnp.dot(
                cols[g * 640 + a * 64 : g * 640 + a * 64 + V, :],
                wf[a * 9 * L : (a + 1) * 9 * L, :],
                preferred_element_type=F32,
            )
        pre[g * V : (g + 1) * V, :] = acc

    deal.forward()
    live = live_ref[0]
    s, q = 0.7978845608028654, 0.044715
    slopes, hiddens = [], []
    for g in range(2):
        mask = jnp.broadcast_to(own32[g * V : (g + 1) * V, C : C + 1], (V, L))
        tt = pre[g * V : (g + 1) * V, :]
        th = jnp.tanh(s * (tt + q * tt * tt * tt))
        hidden = 0.5 * tt * (1.0 + th) * mask
        slopes.append((0.5 * (1.0 + th) + 0.5 * tt * (1.0 - th * th) * (s * (1.0 + 3.0 * q * tt * tt))) * mask)
        hiddens.append(jnp.where(lax.broadcasted_iota(jnp.int32, (V, L), 1) < C, hidden, mask).astype(BF16))
    both = jnp.dot(perm[...], jnp.concatenate(hiddens, axis=1), preferred_element_type=F32)
    kids = []
    cmask = jnp.zeros((2 * 64, L), F32)
    coarse = jnp.zeros((2 * 64, L), F32)
    for j in range(8):
        kid = jnp.concatenate([both[j * 64 : (j + 1) * 64, :L], both[j * 64 : (j + 1) * 64, L:]], axis=0)
        cmask = jnp.maximum(cmask, kid)
        kids.append(kid.astype(BF16))
        coarse += jnp.dot(kids[j], wd[j * L : (j + 1) * L, :], preferred_element_type=F32)
    cmask = jnp.broadcast_to(cmask[:, C : C + 1], (2 * 64, L))

    deal.finish()
    near32[...] = near[...].astype(F32)
    far32[...] = far[...].astype(F32)

    def lines(n):
        return jnp.concatenate([near32[box_rows(core, n), :], far32[box_rows(core, n), :]], axis=0)

    def peers(dim, shape):
        order = lax.broadcasted_iota(jnp.int32, shape, dim)
        return jnp.where(order < CHIPS, 2 * order + core, 2 * (order - CHIPS) + 1 - core)

    boxes = jnp.concatenate([lines(n) for n in range(6)], axis=1).astype(BF16)
    below = jnp.where(peers(0, (PEERS, L)) < me, lines(6), 0.0)
    first = jnp.sum(below, axis=0, keepdims=True).astype(jnp.int32)[:, :64]
    row = lax.broadcasted_iota(jnp.int32, (128, 64), 0)
    block, piece = row >> 6, (row >> 3) & 7
    holder = jnp.bitwise_and(jnp.broadcast_to(first, (128, 64)) + block, 7) * 8 + piece
    chosen = jnp.where((holder == peers(1, (128, 64))) & (block < live), 1.0, 0.0).astype(BF16)
    pick = (
        lax.broadcasted_iota(jnp.int32, (128, 6 * L), 1) & 7
        == lax.broadcasted_iota(jnp.int32, (128, 6 * L), 0) & 7
    )
    dz = jnp.dot(chosen, boxes, preferred_element_type=F32)
    dz = jnp.where(pick, dz, 0.0).astype(BF16)
    dz = lax.dot_general(dz, spread[...], NT, preferred_element_type=F32)
    dz = jnp.where(cmask > 0, dz, 0.0)
    dzt = jnp.transpose(dz).astype(BF16)
    dz = dz.astype(BF16)
    dh = [
        lax.dot_general(dz, wd[j * L : (j + 1) * L, :], NT, preferred_element_type=F32) for j in range(8)
    ]
    parts = []
    for g in range(2):
        part = jnp.concatenate([piece[g * 64 : (g + 1) * 64] for piece in dh], axis=0)
        high = part.astype(BF16)
        parts += [high, (part - high.astype(F32)).astype(BF16)]
    dh = jnp.dot(permt[...], jnp.concatenate(parts, axis=1), preferred_element_type=F32)
    for g in range(2):
        dpre = slopes[g] * (dh[:, 2 * g * L : (2 * g + 1) * L] + dh[:, (2 * g + 1) * L : (2 * g + 2) * L])
        dpre16 = dpre.astype(BF16)
        for a in range(3):
            dpre3[g * 640 + a * 64 : g * 640 + a * 64 + V, a * L : (a + 1) * L] = dpre16
        pre[g * V : (g + 1) * V, :] = dpre
    down_sums = jnp.dot(dzt, jnp.concatenate(kids, axis=1), preferred_element_type=F32)

    lane = lax.broadcasted_iota(jnp.int32, (C, L), 1)
    held = {}

    def keep(k, product):
        held[k % 4] = jnp.transpose(product)[:C]
        if k % 4 == 3 or k == 34:
            last = held.get(3)
            for n in range(3):
                slab = held[n]
                if last is not None:
                    slab = jnp.where(lane < C, slab, pltpu.roll(last, C - 32 * n, 1))
                at = (3 * (k // 4) + n) * C
                sums32[at : at + C, :] = slab
                sums16[at : at + C, :] = slab.astype(BF16)
            held.clear()

    dt = jnp.transpose(pre[...]).astype(BF16)
    for a in range(3):
        for bc in range(0, 9, 2):
            lanes = slice(bc * L, min(bc + 2, 9) * L)
            value = jnp.dot(
                dt[:, :V], cols[a * 64 : a * 64 + V, lanes], preferred_element_type=F32
            ) + jnp.dot(
                dt[:, V:], cols[640 + a * 64 : 640 + a * 64 + V, lanes], preferred_element_type=F32
            )
            for n in range(min(2, 9 - bc)):
                keep(a * 9 + bc + n, value[:, n * L : (n + 1) * L])
    for j in range(8):
        keep(27 + j, down_sums[:, j * L : (j + 1) * L])
    sums32[27 * C :, :] = jnp.zeros((C, L), F32)
    sums16[27 * C :, :] = jnp.zeros((C, L), BF16)

    def span(at, count):
        return pl.ds(pl.multiple_of(at, 16), count)

    pair = remote(sums16.at[span((1 - core) * HALF, HALF)], pair_in, pair_sent, pair_arrived, partner)
    pair.start()
    deal_back = Deal(me, back, back_near, back_far, *(back_sem.at[n] for n in range(4)))
    flat = jnp.dot((coarse * cmask).astype(BF16), spread[...], preferred_element_type=F32)
    flat = jnp.where(pick, flat, 0.0).astype(BF16)
    dealt = lax.dot_general(chosen, flat, (((0,), (0,)), ((), ())), preferred_element_type=F32)
    for n in range(6):
        box32[box_rows(core, n), :] = dealt[:CHIPS, n * L : (n + 1) * L]
        box32[box_rows(1 - core, n), :] = dealt[CHIPS:, n * L : (n + 1) * L]
    back[...] = box32[...].astype(BF16)
    deal_back.start(0, 12)
    pair.wait_recv()
    value = sums32[span(core * HALF, HALF), :] + pair_in[...].astype(F32)
    chip32[...] = value
    chip16[...] = value.astype(BF16)

    on_y, on_z, owner = core == 0, core == 1, z < 7

    def copies(order, place, size, step, wanted=None):
        def act(what, back=False):
            for n in order:
                to = jnp.bitwise_and(place + (size - n - 1 if back else n + 1), size - 1)
                copy = step(n, to)
                if wanted is None:
                    what(copy)
                else:
                    pl.when(wanted(to))(functools.partial(what, copy))

        return act

    def start(copy):
        copy.start()

    def wait_recv(copy):
        copy.wait_recv()

    def wait_send(copy):
        copy.wait_send()

    def owns(zz):
        return zz < 7

    def low(zz):
        return lax.min(zz, 6)

    def y_first(n, yy):
        return remote(
            chip16.at[span(yy * YPART, YPART)], y_in.at[n], ysent.at[n], yarrived.at[n], yy * 16 + z * 2
        )

    def z_second(n, zz):
        return remote(
            y16.at[span(low(zz) * OWNED, OWNED)], z_own.at[n], zsent.at[n], zarrived.at[n], y * 16 + zz * 2
        )

    def z_first(n, zz):
        return remote(
            chip16.at[span(low(zz) * ZPART, ZPART)], z_in.at[n], zsent.at[n], zarrived.at[n],
            y * 16 + zz * 2 + 1,
        )

    def y_second(n, yy):
        return remote(
            z16.at[span(yy * OWNED, OWNED)], y_own.at[n], ysent.at[n], yarrived.at[n], yy * 16 + z * 2 + 1
        )

    def on_total(at, count, sent, arrived, peer):
        at = span(at, count)
        return remote(total.at[at], total.at[at], sent, arrived, peer)

    def back_z_first(n, to, source):
        return on_total(
            y * YPART + low(source) * OWNED, OWNED, gzsent.at[n], gzarrived.at[n], y * 16 + to * 2
        )

    def back_y_second(n, to, source):
        return on_total(source * YPART, YPART, gysent.at[n], gyarrived.at[n], to * 16 + z * 2)

    def back_y_first(n, to, source):
        return on_total(
            HALF + low(z) * ZPART + source * OWNED, OWNED, gysent.at[n], gyarrived.at[n], to * 16 + z * 2 + 1
        )

    def back_z_second(n, to, source):
        return on_total(
            HALF + low(source) * ZPART, ZPART, gzsent.at[n], gzarrived.at[n], y * 16 + to * 2 + 1
        )

    def sends(step, mine):
        return lambda n, to: step(n, to, mine)

    def comes(step):
        return lambda n, source: step(n, source, source)

    @pl.when(on_y)
    def _():
        copies(YORDER, y, 4, y_first)(start)

    @pl.when(on_z)
    def _():
        copies(ZORDER, z, 8, z_first, owns)(start)

    deal_back.start(12)

    gpad[...] = jnp.zeros_like(gpad)
    def pad_gradient(bc):
        width = min(2, 9 - bc)
        u[:, : width * L] = lax.dot_general(
            dpre3[...], wb[bc * L : (bc + width) * L, :], NT, preferred_element_type=F32
        )

        def add(gx, carry):
            for n in range(width):
                b, c = divmod(bc + n, 3)
                for yy in range(8):
                    at = pl.ds(gx * 100 + (yy + b) * 10 + c, 8)
                    gpad[at, :] += u[pl.ds(pl.multiple_of(gx * 64 + yy * 8, 8), 8), n * L : (n + 1) * L]
            return carry

        lax.fori_loop(0, 20, add, 0)

    for bc in (0, 2, 4, 6):
        pad_gradient(bc)

    @pl.when(on_y)
    def _():
        copies(range(3), y, 4, y_first)(wait_recv)
        value = chip32[span(y * YPART, YPART), :]
        for n in range(3):
            value = value + y_in[n].astype(F32)
        y32[...] = value
        y16[...] = value.astype(BF16)
        copies(ZORDER, z, 8, z_second, owns)(start)

    @pl.when(on_z & owner)
    def _():
        copies(range(7), z, 8, z_first)(wait_recv)
        value = chip32[span(z * ZPART, ZPART), :]
        for n in range(7):
            value = value + z_in[n].astype(F32)
        z32[...] = value
        z16[...] = value.astype(BF16)
        copies(YORDER, y, 4, y_second)(start)

    pad_gradient(8)

    gsource[...] = jnp.zeros_like(gsource)

    def give(n, carry):
        for g in range(2):
            for k, offset in enumerate(OFFSETS):
                if k != 13:
                    here = jnp.where(table[g, k] == n, 1.0, 0.0)
                    for s0, ss, p0, ps, count in segments(*offset):
                        at = rows(n * SHELL + s0, count, ss)
                        gsource[at, :] += gpad[rows(g * 1000 + p0, count, ps), :] * here
        return carry

    lax.fori_loop(0, 6, give, 0)
    for g in range(2):
        part_lower[g] = gsource[g * SHELL : (g + 1) * SHELL, :].astype(BF16)
        part_upper[g] = gsource[(4 + g) * SHELL : (5 + g) * SHELL, :].astype(BF16)
    @pl.when(on_y & owner)
    def _():
        copies(range(7), z, 8, z_second)(wait_recv)
        value = y32[span(z * OWNED, OWNED), :]
        for n in range(7):
            value = value + z_own[n].astype(F32)
        total[span(y * YPART + z * OWNED, OWNED), :] = value.astype(BF16)
        copies(ZORDER, z, 8, sends(back_z_first, z))(start)

    @pl.when(on_z & owner)
    def _():
        copies(range(3), y, 4, y_second)(wait_recv)
        value = z32[span(y * OWNED, OWNED), :]
        for n in range(3):
            value = value + y_own[n].astype(F32)
        total[span(HALF + z * ZPART + y * OWNED, OWNED), :] = value.astype(BF16)
        copies(YORDER, y, 4, sends(back_y_first, y))(start)

    rim_up = remote(part_upper, from_lower, rim_sent.at[0], rim_arrived.at[0], lax.min(me + 1, PEERS - 1))
    rim_down = remote(part_lower, from_upper, rim_sent.at[1], rim_arrived.at[1], lax.max(me - 1, 0))

    @pl.when(has_up)
    def _():
        rim_up.start()

    @pl.when(has_down)
    def _():
        rim_down.start()

    deal_back.forward()

    def across(which, part):
        rows_at, count = (part * YPART, YPART) if which == 0 else (HALF + part * ZPART, ZPART)
        return on_total(rows_at, count, copy_sent.at[part], copy_arrived.at[part], partner)

    @pl.when(on_y)
    def _():
        copies(range(7), z, 8, comes(back_z_first), owns)(wait_recv, back=True)
        copies(YORDER, y, 4, sends(back_y_second, y))(start)
        across(0, y).start()

    @pl.when(on_z & owner)
    def _():
        copies(range(3), y, 4, comes(back_y_first))(wait_recv, back=True)
        copies(ZORDER, z, 8, sends(back_z_second, z))(start)
        across(1, z).start()

    deal_back.finish()
    near32[...] = back_near[...].astype(F32)
    far32[...] = back_far[...].astype(F32)
    for n in range(6):
        out32[pl.ds(n * PEERS + core, CHIPS, stride=2), :] = near32[box_rows(core, n), :]
        out32[pl.ds(n * PEERS + 1 - core, CHIPS, stride=2), :] = far32[box_rows(core, n), :]
    for n in range(6):
        coarse_out[:, n * L : (n + 1) * L] = out32[n * PEERS : (n + 1) * PEERS, :].astype(BF16)

    def pass_on_y(n):
        source = jnp.bitwise_and(y + 3 - n, 3)
        back_y_second(n, source, source).wait_recv()
        across(0, source).start()

    def pass_on_z(n):
        source = jnp.bitwise_and(z + 7 - n, 7)

        @pl.when(owns(source))
        def _():
            back_z_second(n, source, source).wait_recv()
            across(1, low(source)).start()

    @pl.when(on_y)
    def _():
        pass_on_y(0)
        pass_on_y(2)

    @pl.when(on_z)
    def _():
        for n in (0, 6, 1, 5):
            pass_on_z(n)

    @pl.when(has_down)
    def _():
        rim_up.wait_recv()

    @pl.when(jnp.logical_not(has_down))
    def _():
        from_lower[...] = jnp.zeros_like(from_lower)

    @pl.when(has_up)
    def _():
        rim_down.wait_recv()

    @pl.when(jnp.logical_not(has_up))
    def _():
        from_upper[...] = jnp.zeros_like(from_upper)

    for g in range(2):
        shell = gsource[(2 + g) * SHELL : (3 + g) * SHELL, :]
        shell = shell + from_lower[g].astype(F32) + from_upper[g].astype(F32)
        for x in range(8):
            for yy in range(8):
                pre[pl.ds(g * V + x * 64 + yy * 8, 8), :] = gpad[pl.ds(g * 1000 + x * 100 + yy * 10 + 111, 8), :]
        for s0, v0, vs, count in shell_pieces():
            pre[rows(g * V + v0, count, vs), :] += shell[s0 : s0 + count]
        value = pre[g * V : (g + 1) * V, :]
        value = value * jnp.broadcast_to(own32[g * V : (g + 1) * V, C : C + 1], (V, L))
        grad_features[g] = jnp.transpose(value)[:C, :].astype(BF16)

    @pl.when(on_y)
    def _():
        pass_on_y(1)
        for part in range(7):
            across(1, part).wait_recv()

    @pl.when(on_z)
    def _():
        for n in (2, 4, 3):
            pass_on_z(n)
        for part in range(4):
            across(0, part).wait_recv()

    @pl.when(has_up)
    def _():
        up.wait_send()
        rim_up.wait_send()

    @pl.when(has_down)
    def _():
        down.wait_send()
        rim_down.wait_send()

    deal.close()
    deal_back.close()
    pair.wait_send()

    @pl.when(on_y)
    def _():
        copies(range(3), y, 4, y_first)(wait_send)
        copies(range(7), z, 8, z_second, owns)(wait_send)
        copies(range(3), y, 4, sends(back_y_second, y))(wait_send)
        for part in range(4):
            across(0, part).wait_send()

    @pl.when(on_z)
    def _():
        copies(range(7), z, 8, z_first, owns)(wait_send)
        for part in range(7):
            across(1, part).wait_send()

    @pl.when(on_y & owner)
    def _():
        copies(range(7), z, 8, sends(back_z_first, z))(wait_send)

    @pl.when(on_z & owner)
    def _():
        copies(range(3), y, 4, y_second)(wait_send)
        copies(range(3), y, 4, sends(back_y_first, y))(wait_send)
        copies(range(7), z, 8, sends(back_z_second, z))(wait_send)


def vmem(n):
    return [pl.BlockSpec(memory_space=pltpu.VMEM)] * n


def hbm(n):
    return [pl.BlockSpec(memory_space=pltpu.HBM)] * n


def run_section(neighbours, live_count, occupancy, features, grad_coarse, w_subm, w_down):
    dma = pltpu.SemaphoreType.DMA
    block = pltpu.VMEM((2, SHELL, L), BF16)
    boxes = pltpu.VMEM((8 * PEERS, L), F32)
    sent = pltpu.VMEM((8 * PEERS, L), BF16)
    return pl.pallas_call(
        section_kernel,
        out_shape=(
            jax.ShapeDtypeStruct((PEERS, 6 * L), BF16),
            jax.ShapeDtypeStruct((2, C, V), BF16),
            jax.ShapeDtypeStruct((2 * HALF, L), BF16),
        ),
        in_specs=hbm(7),
        out_specs=tuple(vmem(3)),
        scratch_shapes=[
            pltpu.SMEM((2, 27), jnp.int32),
            pltpu.SMEM((1,), jnp.int32),
            pltpu.SMEM((2, 16), jnp.int32),
            pltpu.VMEM((2, C, V), BF16),
            pltpu.VMEM((PEERS, 6 * L), BF16),
            pltpu.VMEM((27, C, C), BF16),
            pltpu.VMEM((8, C, C), BF16),
            pltpu.VMEM((2 * V, L), F32),
            block, block, block, boxes, boxes, boxes, pltpu.VMEM((6 * PEERS, L), F32),
            sent, sent, sent, sent, sent, sent,
            pltpu.VMEM((7 * SHELL, L), F32),
            pltpu.VMEM((2000, L), F32),
            pltpu.VMEM((1280, 9 * L), BF16),
            pltpu.VMEM((27 * L, L), BF16),
            pltpu.VMEM((9 * L, 3 * L), BF16),
            pltpu.VMEM((8 * L, L), BF16),
            pltpu.VMEM((V, V), BF16),
            pltpu.VMEM((V, V), BF16),
            pltpu.VMEM((L, 6 * L), BF16),
            pltpu.VMEM((2 * V, L), F32),
            pltpu.VMEM((1280, 3 * L), BF16),
            pltpu.VMEM((1280, 2 * L), F32),
            pltpu.VMEM((2000, L), F32),
            pltpu.VMEM((6 * SHELL, L), F32),
            pltpu.VMEM((2 * HALF, L), F32),
            pltpu.VMEM((2 * HALF, L), BF16),
            pltpu.VMEM((HALF, L), BF16),
            pltpu.VMEM((HALF, L), F32),
            pltpu.VMEM((HALF, L), BF16),
            pltpu.VMEM((3, YPART, L), BF16),
            pltpu.VMEM((YPART, L), F32),
            pltpu.VMEM((YPART, L), BF16),
            pltpu.VMEM((7, OWNED, L), BF16),
            pltpu.VMEM((7, ZPART, L), BF16),
            pltpu.VMEM((ZPART, L), F32),
            pltpu.VMEM((ZPART, L), BF16),
            pltpu.VMEM((3, OWNED, L), BF16),
            block, block, block, block,
            dma((7,)), dma((4,)), dma((4,)),
            dma((2,)), dma((2,)), dma((2,)), dma((2,)), dma(()), dma(()),
            dma((3,)), dma((3,)), dma((7,)), dma((7,)), dma((7,)), dma((7,)),
            dma((3,)), dma((3,)), dma((7,)), dma((7,)),
        ],
        compiler_params=pltpu.CompilerParams(
            vmem_limit_bytes=VMEM_LIMIT, collective_id=0, has_side_effects=True
        ),
    )(neighbours, live_count, occupancy, features, grad_coarse, w_subm, w_down)


def final_kernel(
    coarse_in, features_in, total_in, coarse_out, grad_features, grad_subm, grad_down,
    total, subm, down, coarse, features, load_sem, sem,
):
    def chunk(n):
        return pl.ds(9 * C * n, 9 * C)

    loads = [
        pltpu.make_async_copy(total_in.at[chunk(n)], total.at[chunk(n)], load_sem.at[n]) for n in range(3)
    ]
    loads.append(pltpu.make_async_copy(features_in, features, load_sem.at[3]))
    loads.append(pltpu.make_async_copy(coarse_in, coarse, load_sem.at[4]))
    for load in loads:
        load.start()
    copies = [
        pltpu.make_async_copy(features, grad_features, sem.at[0]),
        pltpu.make_async_copy(coarse, coarse_out, sem.at[1]),
    ]
    lane = lax.broadcasted_iota(jnp.int32, (C, L), 1)
    for k in range(35):
        quad, n = divmod(k, 4)
        if k % 12 == 0:
            loads[k // 12].wait()
        if n < 3:
            at = (3 * quad + n) * C
            value = total[at : at + C, :].astype(F32)[:, :C]
        else:
            value = jnp.zeros((C, L), F32)
            for m in range(3):
                at = (3 * quad + m) * C
                piece = pltpu.roll(total[at : at + C, :].astype(F32), 32 + 32 * m, 1)
                value = jnp.where(lane // 32 == m, piece, value)
            value = value[:, :C]
        if k < 27:
            subm[k] = value
        else:
            down[k - 27] = value
        if k in (11, 23, 26):
            part = pl.ds(k // 12 * 12, 12 if k < 26 else 3)
            copies.append(pltpu.make_async_copy(subm.at[part], grad_subm.at[part], sem.at[2 + k // 12]))
            copies[-1].start()
        if k == 11:
            for n in range(2):
                loads[3 + n].wait()
                copies[n].start()
    copies.append(pltpu.make_async_copy(down, grad_down, sem.at[5]))
    copies[-1].start()
    for copy in copies:
        copy.wait()


def run_final(coarse_in, grad_features, total):
    return pl.pallas_call(
        final_kernel,
        out_shape=(
            jax.ShapeDtypeStruct((PEERS, 6 * L), BF16),
            jax.ShapeDtypeStruct((2, C, V), BF16),
            jax.ShapeDtypeStruct((27, C, C), F32),
            jax.ShapeDtypeStruct((8, C, C), F32),
        ),
        in_specs=hbm(3),
        out_specs=tuple(hbm(4)),
        scratch_shapes=[
            pltpu.VMEM((27 * C, L), BF16),
            pltpu.VMEM((27, C, C), F32),
            pltpu.VMEM((8, C, C), F32),
            pltpu.VMEM((PEERS, 6 * L), BF16),
            pltpu.VMEM((2, C, V), BF16),
            pltpu.SemaphoreType.DMA((5,)),
            pltpu.SemaphoreType.DMA((6,)),
        ],
        compiler_params=pltpu.CompilerParams(vmem_limit_bytes=VMEM_LIMIT),
    )(coarse_in, grad_features, total)


def per_device(features, occupancy, neighbours, live_count, w_subm, w_down, grad_coarse):
    return run_final(
        *run_section(neighbours, live_count, occupancy, features, grad_coarse, w_subm, w_down)
    )


def solution(mesh):
    blocks = P(("rep", "space"), None)
    return jax.shard_map(
        per_device,
        mesh=mesh,
        in_specs=(
            P(("rep", "space"), None, None), blocks, blocks, P(("rep", "space")), P(), P(), blocks,
        ),
        out_specs=(
            blocks, P(("rep", "space"), None, None), P("rep", None, None), P("rep", None, None),
        ),
        check_vma=False,
    )
```

```python
import functools

import jax
import jax.numpy as jnp
from jax import lax
from jax.experimental import pallas as pl
from jax.experimental.pallas import tpu as pltpu
from jax.sharding import PartitionSpec as P

C, L, V = 96, 128, 512
OFFSETS = [(a, b, c) for a in (-1, 0, 1) for b in (-1, 0, 1) for c in (-1, 0, 1)]
PEERS, CHIPS, SHELL = 64, 32, 320
YORDER, ZORDER = (1, 0, 2), (3, 2, 4, 1, 5, 0, 6)
HALF, YPART, ZPART, OWNED = 1344, 336, 192, 48
VMEM_LIMIT = 63 * 2**20 + 2**19
F32, BF16 = jnp.float32, jnp.bfloat16
NT = (((1,), (1,)), ((), ()))


def segments(a, b, c):
    span = {-1: [(7, 0)], 0: [(i, i + 1) for i in range(8)], 1: [(0, 9)]}
    xs, ys, zs = span[a], span[b], span[c]
    face = {0: 0, 7: 64}
    if c == 0:
        return [
            (face[x] + y * 8 if x in face else 112 + x * 16 + y // 7 * 8, 1, tx * 100 + ty * 10 + 1, 1, 8)
            for x, tx in xs
            for y, ty in ys
        ]
    z, tz = zs[0]
    if b == 0:
        return [
            (face[x] + z, 8, tx * 100 + 10 + tz, 10, 8)
            if x in face
            else (208 + x * 16 + z // 7 * 8, 1, tx * 100 + 10 + tz, 10, 8)
            for x, tx in xs
        ]
    y, ty = ys[0]
    if a == 0:
        at = ty * 10 + tz
        return [
            (y * 8 + z, 1, 100 + at, 1, 1),
            (128 + y // 7 * 8 + z, 16, 200 + at, 100, 6),
            (64 + y * 8 + z, 1, 800 + at, 1, 1),
        ]
    x, tx = xs[0]
    return [(face[x] + y * 8 + z, 1, tx * 100 + ty * 10 + tz, 1, 1)]


def shell_pieces():
    pieces = [(0, 0, 1, 64), (64, 448, 1, 64)]
    for x in range(1, 7):
        pieces += [(112 + x * 16, x * 64, 1, 8), (120 + x * 16, x * 64 + 56, 1, 8)]
        pieces += [(208 + x * 16, x * 64, 8, 8), (216 + x * 16, x * 64 + 7, 8, 8)]
    return pieces


def rows(start, count, stride):
    return pl.ds(start, count) if stride == 1 else pl.ds(start, count, stride=stride)


def mask_row(words, live, g):
    lane = lax.broadcasted_iota(jnp.int32, (1, V), 1)
    word = jnp.zeros((1, V), jnp.int32)
    for w in range(16):
        word = jnp.where(lane // 32 == w, words[g, w], word)
    bit = jnp.bitwise_and(jnp.right_shift(word, jnp.bitwise_and(lane, 31)), 1)
    return jnp.where(g < live, bit, 0)


def masked_rows(features, words, live, g):
    bit = mask_row(words, live, g)
    values = jnp.where(bit > 0, features[g].astype(F32), 0.0)
    marks = jnp.broadcast_to(bit.astype(F32), (L - C, V))
    return jnp.transpose(jnp.concatenate([values, marks], axis=0))


def remote(source, target, sent, arrived, peer):
    return pltpu.make_async_remote_copy(
        src_ref=source, dst_ref=target, send_sem=sent, recv_sem=arrived,
        device_id={"space": peer}, device_id_type=pl.DeviceIdType.MESH,
    )


def far_first():
    offsets = [(dy, dz) for dy in range(4) for dz in range(8) if dy or dz]
    return sorted(offsets, key=lambda at: -min(at[0], 4 - at[0]) - min(at[1], 8 - at[1]))


def chip_at(here, offset):
    dy, dz = offset
    return jnp.bitwise_and(here + 8 * dy, CHIPS - 8) + jnp.bitwise_and(here + dz, 7)


def greet(me):
    barrier = pltpu.get_barrier_semaphore()
    here, core = me // 2, lax.rem(me, 2)

    def tell(peer):
        pl.semaphore_signal(
            barrier, inc=1, device_id={"space": peer}, device_id_type=pl.DeviceIdType.MESH
        )

    for offset in far_first():
        tell(chip_at(here, offset) * 2 + core)
    tell(lax.rem(me + 2 * core - 1 + PEERS, PEERS))
    tell(me + 1 - 2 * core)


def greeted():
    pl.semaphore_wait(pltpu.get_barrier_semaphore(), CHIPS + 1)


class Deal:
    def __init__(self, me, outbox, near, far, sent, arrived, far_sent, far_arrived):
        self.here, self.core = me // 2, lax.rem(me, 2)
        self.outbox, self.near = outbox, near
        self.sems = sent, arrived
        self.across = remote(near, far, far_sent, far_arrived, me + 1 - 2 * self.core)
        every = pl.ds(0, 16 * (CHIPS - 1))
        self.every = remote(outbox.at[every], near.at[every], sent, arrived, me + 1 - 2 * self.core)

    def tile(self, chip):
        return pl.ds(pl.multiple_of(chip * 16, 16), 16)

    def start(self, first=0, last=CHIPS - 1):
        for offset in far_first()[first:last]:
            there = chip_at(self.here, offset)
            remote(
                self.outbox.at[self.tile(there)], self.near.at[self.tile(self.here)],
                *self.sems, there * 2 + self.core,
            ).start()
        if last == CHIPS - 1:
            self.near[self.tile(self.here), :] = self.outbox[self.tile(self.here), :]

    def forward(self):
        self.every.wait_recv()
        self.across.start()

    def finish(self):
        self.across.wait_recv()

    def close(self):
        self.every.wait_send()
        self.across.wait_send()


def box_rows(core, n):
    return pl.ds(core * 8 + n, CHIPS, stride=16)


def section_kernel(
    table_hbm, live_hbm, occupancy_hbm, features_hbm, cotangent_hbm, w_subm_hbm, w_down_hbm,
    coarse_out, grad_features, total,
    table, live_ref, occupancy_ref, features, cotangent, w_subm, w_down,
    own32, own, lower, upper, box32, near32, far32, out32, outbox, near, far, back, back_near, back_far,
    source, pad, cols, wf, wb, wd, perm, permt, spread, pre, dpre3, u, gpad, gsource,
    sums32, sums16, pair_in, chip32, chip16, y_in, y32, y16, z_own, z_in, z32, z16, y_own,
    part_lower, part_upper, from_lower, from_upper,
    load_sem, box_sem, back_sem, halo_sent, halo_arrived,
    rim_sent, rim_arrived, pair_sent, pair_arrived, ysent, yarrived, zsent, zarrived,
    gzsent, gzarrived, gysent, gyarrived, copy_sent, copy_arrived,
):
    me = lax.axis_index("space")
    y, z, core = me // 16, lax.rem(me // 2, 8), lax.rem(me, 2)
    partner = me + 1 - 2 * core
    has_up, has_down = me < PEERS - 1, me > 0
    loads = [
        pltpu.make_async_copy(hbm, ref, load_sem.at[n])
        for n, (hbm, ref) in enumerate(
            (
                (features_hbm, features), (cotangent_hbm, cotangent), (w_subm_hbm, w_subm), (w_down_hbm, w_down),
                (table_hbm, table), (live_hbm, live_ref), (occupancy_hbm, occupancy_ref),
            )
        )
    ]
    for load in loads:
        load.start()
    greet(me)

    i = lax.broadcasted_iota(jnp.int32, (V, V), 0)
    v = lax.broadcasted_iota(jnp.int32, (V, V), 1)

    def placed(index, parts):
        return sum(((index >> a) & b) << c for a, b, c in parts)

    to_voxel = ((8, 1, 6), (7, 1, 3), (6, 1, 0), (4, 3, 7), (2, 3, 4), (0, 3, 1))
    to_child = tuple((c, b, a) for a, b, c in to_voxel)
    perm[...] = jnp.where(placed(i[:, :1], to_voxel) == v, 1.0, 0.0).astype(BF16)
    permt[...] = jnp.where(placed(i[:, :1], to_child) == v, 1.0, 0.0).astype(BF16)
    spread[...] = jnp.where(
        lax.broadcasted_iota(jnp.int32, (L, 6 * L), 1) // 8
        == lax.broadcasted_iota(jnp.int32, (L, 6 * L), 0),
        1.0, 0.0,
    ).astype(BF16)
    wf[...] = jnp.zeros_like(wf)
    wb[...] = jnp.zeros_like(wb)
    wd[...] = jnp.zeros_like(wd)
    dpre3[...] = jnp.zeros_like(dpre3)
    source[6 * SHELL :, :] = jnp.zeros((SHELL, L), F32)

    for n in (0, 4, 5, 6):
        loads[n].wait()
    for g in range(2):
        own32[g * V : (g + 1) * V, :] = masked_rows(features, occupancy_ref, live_ref[0], g)
        for s0, v0, vs, count in shell_pieces():
            source[(2 + g) * SHELL + s0 : (2 + g) * SHELL + s0 + count, :] = own32[rows(g * V + v0, count, vs), :]
        own[g] = source[(2 + g) * SHELL : (3 + g) * SHELL, :].astype(BF16)
    loads[1].wait()
    for n in range(6):
        box32[pl.ds(n, PEERS, stride=8), :] = cotangent[:, n * L : (n + 1) * L].astype(F32)
    counts = jnp.broadcast_to(live_ref[0].astype(F32), (PEERS, L))
    for n in (6, 7):
        box32[pl.ds(n, PEERS, stride=8), :] = counts
    outbox[...] = box32[...].astype(BF16)

    greeted()
    up = remote(own, lower, halo_sent.at[0], halo_arrived.at[0], lax.min(me + 1, PEERS - 1))
    down = remote(own, upper, halo_sent.at[1], halo_arrived.at[1], lax.max(me - 1, 0))

    @pl.when(has_up)
    def _():
        up.start()

    @pl.when(has_down)
    def _():
        down.start()

    deal = Deal(me, outbox, near, far, *(box_sem.at[n] for n in range(4)))
    deal.start()

    loads[2].wait()
    loads[3].wait()
    for k in range(27):
        a, bc = divmod(k, 9)
        w = w_subm[k]
        wf[k * L : k * L + C, :C] = w
        wb[bc * L : bc * L + C, a * L : a * L + C] = w
    for j in range(8):
        wd[j * L : j * L + C, :C] = w_down[j]


    @pl.when(has_down)
    def _():
        up.wait_recv()

    @pl.when(jnp.logical_not(has_down))
    def _():
        lower[...] = jnp.zeros_like(lower)

    @pl.when(has_up)
    def _():
        down.wait_recv()

    @pl.when(jnp.logical_not(has_up))
    def _():
        upper[...] = jnp.zeros_like(upper)

    for g in range(2):
        source[g * SHELL : (g + 1) * SHELL, :] = lower[g].astype(F32)
        source[(4 + g) * SHELL : (5 + g) * SHELL, :] = upper[g].astype(F32)

    for g in range(2):
        for k, offset in enumerate(OFFSETS):
            if k == 13:
                continue
            base = table[g, k] * SHELL
            for s0, ss, p0, ps, count in segments(*offset):
                pad[rows(g * 1000 + p0, count, ps), :] = source[rows(base + s0, count, ss), :]

        for x in range(8):
            for yy in range(8):
                pad[pl.ds(g * 1000 + x * 100 + yy * 10 + 111, 8), :] = own32[pl.ds(g * V + x * 64 + yy * 8, 8), :]

    def columns(gx, carry):
        for b in range(3):
            for c in range(3):
                piece = jnp.concatenate(
                    [pad[pl.ds(gx * 100 + (yy + b) * 10 + c, 8), :] for yy in range(8)], axis=0
                )
                bc = 3 * b + c
                cols[pl.ds(pl.multiple_of(gx * 64, 64), 64), bc * L : (bc + 1) * L] = piece.astype(BF16)
        return carry

    lax.fori_loop(0, 20, columns, 0)

    for g in range(2):
        acc = jnp.zeros((V, L), F32)
        for a in range(3):
            acc += jnp.dot(
                cols[g * 640 + a * 64 : g * 640 + a * 64 + V, :],
                wf[a * 9 * L : (a + 1) * 9 * L, :],
                preferred_element_type=F32,
            )
        pre[g * V : (g + 1) * V, :] = acc

    deal.forward()
    live = live_ref[0]
    s, q = 0.7978845608028654, 0.044715
    slopes, hiddens = [], []
    for g in range(2):
        mask = jnp.broadcast_to(own32[g * V : (g + 1) * V, C : C + 1], (V, L))
        tt = pre[g * V : (g + 1) * V, :]
        th = jnp.tanh(s * (tt + q * tt * tt * tt))
        hidden = 0.5 * tt * (1.0 + th) * mask
        slopes.append((0.5 * (1.0 + th) + 0.5 * tt * (1.0 - th * th) * (s * (1.0 + 3.0 * q * tt * tt))) * mask)
        hiddens.append(jnp.where(lax.broadcasted_iota(jnp.int32, (V, L), 1) < C, hidden, mask).astype(BF16))
    both = jnp.dot(perm[...], jnp.concatenate(hiddens, axis=1), preferred_element_type=F32)
    kids = []
    cmask = jnp.zeros((2 * 64, L), F32)
    coarse = jnp.zeros((2 * 64, L), F32)
    for j in range(8):
        kid = jnp.concatenate([both[j * 64 : (j + 1) * 64, :L], both[j * 64 : (j + 1) * 64, L:]], axis=0)
        cmask = jnp.maximum(cmask, kid)
        kids.append(kid.astype(BF16))
        coarse += jnp.dot(kids[j], wd[j * L : (j + 1) * L, :], preferred_element_type=F32)
    cmask = jnp.broadcast_to(cmask[:, C : C + 1], (2 * 64, L))

    deal.finish()
    near32[...] = near[...].astype(F32)
    far32[...] = far[...].astype(F32)

    def lines(n):
        return jnp.concatenate([near32[box_rows(core, n), :], far32[box_rows(core, n), :]], axis=0)

    def peers(dim, shape):
        order = lax.broadcasted_iota(jnp.int32, shape, dim)
        return jnp.where(order < CHIPS, 2 * order + core, 2 * (order - CHIPS) + 1 - core)

    boxes = jnp.concatenate([lines(n) for n in range(6)], axis=1).astype(BF16)
    below = jnp.where(peers(0, (PEERS, L)) < me, lines(6), 0.0)
    first = jnp.sum(below, axis=0, keepdims=True).astype(jnp.int32)[:, :64]
    row = lax.broadcasted_iota(jnp.int32, (128, 64), 0)
    block, piece = row >> 6, (row >> 3) & 7
    holder = jnp.bitwise_and(jnp.broadcast_to(first, (128, 64)) + block, 7) * 8 + piece
    chosen = jnp.where((holder == peers(1, (128, 64))) & (block < live), 1.0, 0.0).astype(BF16)
    pick = (
        lax.broadcasted_iota(jnp.int32, (128, 6 * L), 1) & 7
        == lax.broadcasted_iota(jnp.int32, (128, 6 * L), 0) & 7
    )
    dz = jnp.dot(chosen, boxes, preferred_element_type=F32)
    dz = jnp.where(pick, dz, 0.0).astype(BF16)
    dz = lax.dot_general(dz, spread[...], NT, preferred_element_type=F32)
    dz = jnp.where(cmask > 0, dz, 0.0)
    dzt = jnp.transpose(dz).astype(BF16)
    dz = dz.astype(BF16)
    dh = lax.dot_general(dz, wd[...], NT, preferred_element_type=F32)
    dh = [dh[:, j * L : (j + 1) * L] for j in range(8)]
    parts = []
    for g in range(2):
        part = jnp.concatenate([piece[g * 64 : (g + 1) * 64] for piece in dh], axis=0)
        high = part.astype(BF16)
        parts += [high, (part - high.astype(F32)).astype(BF16)]
    dh = jnp.dot(permt[...], jnp.concatenate(parts, axis=1), preferred_element_type=F32)
    for g in range(2):
        dpre = slopes[g] * (dh[:, 2 * g * L : (2 * g + 1) * L] + dh[:, (2 * g + 1) * L : (2 * g + 2) * L])
        dpre16 = dpre.astype(BF16)
        for a in range(3):
            dpre3[g * 640 + a * 64 : g * 640 + a * 64 + V, a * L : (a + 1) * L] = dpre16
        pre[g * V : (g + 1) * V, :] = dpre
    down_sums = jnp.dot(dzt, jnp.concatenate(kids, axis=1), preferred_element_type=F32)

    lane = lax.broadcasted_iota(jnp.int32, (C, L), 1)
    held = {}

    def keep(k, product):
        held[k % 4] = jnp.transpose(product)[:C]
        if k % 4 == 3 or k == 34:
            last = held.get(3)
            for n in range(3):
                slab = held[n]
                if last is not None:
                    slab = jnp.where(lane < C, slab, pltpu.roll(last, C - 32 * n, 1))
                at = (3 * (k // 4) + n) * C
                sums32[at : at + C, :] = slab
                sums16[at : at + C, :] = slab.astype(BF16)
            held.clear()

    dt = jnp.transpose(pre[...]).astype(BF16)
    for a in range(3):
        for bc in range(0, 9, 2):
            lanes = slice(bc * L, min(bc + 2, 9) * L)
            value = jnp.dot(
                dt[:, :V], cols[a * 64 : a * 64 + V, lanes], preferred_element_type=F32
            ) + jnp.dot(
                dt[:, V:], cols[640 + a * 64 : 640 + a * 64 + V, lanes], preferred_element_type=F32
            )
            for n in range(min(2, 9 - bc)):
                keep(a * 9 + bc + n, value[:, n * L : (n + 1) * L])
    for j in range(8):
        keep(27 + j, down_sums[:, j * L : (j + 1) * L])
    sums32[27 * C :, :] = jnp.zeros((C, L), F32)
    sums16[27 * C :, :] = jnp.zeros((C, L), BF16)

    def span(at, count):
        return pl.ds(pl.multiple_of(at, 16), count)

    pair = remote(sums16.at[span((1 - core) * HALF, HALF)], pair_in, pair_sent, pair_arrived, partner)
    pair.start()
    deal_back = Deal(me, back, back_near, back_far, *(back_sem.at[n] for n in range(4)))
    flat = jnp.dot((coarse * cmask).astype(BF16), spread[...], preferred_element_type=F32)
    flat = jnp.where(pick, flat, 0.0).astype(BF16)
    dealt = lax.dot_general(chosen, flat, (((0,), (0,)), ((), ())), preferred_element_type=F32)
    for n in range(6):
        box32[box_rows(core, n), :] = dealt[:CHIPS, n * L : (n + 1) * L]
        box32[box_rows(1 - core, n), :] = dealt[CHIPS:, n * L : (n + 1) * L]
    back[...] = box32[...].astype(BF16)
    deal_back.start(0, 12)
    pair.wait_recv()
    value = sums32[span(core * HALF, HALF), :] + pair_in[...].astype(F32)
    chip32[...] = value
    chip16[...] = value.astype(BF16)

    on_y, on_z, owner = core == 0, core == 1, z < 7

    def copies(order, place, size, step, wanted=None):
        def act(what, back=False):
            for n in order:
                to = jnp.bitwise_and(place + (size - n - 1 if back else n + 1), size - 1)
                copy = step(n, to)
                if wanted is None:
                    what(copy)
                else:
                    pl.when(wanted(to))(functools.partial(what, copy))

        return act

    def start(copy):
        copy.start()

    def wait_recv(copy):
        copy.wait_recv()

    def wait_send(copy):
        copy.wait_send()

    def owns(zz):
        return zz < 7

    def low(zz):
        return lax.min(zz, 6)

    def y_first(n, yy):
        return remote(
            chip16.at[span(yy * YPART, YPART)], y_in.at[n], ysent.at[n], yarrived.at[n], yy * 16 + z * 2
        )

    def z_second(n, zz):
        return remote(
            y16.at[span(low(zz) * OWNED, OWNED)], z_own.at[n], zsent.at[n], zarrived.at[n], y * 16 + zz * 2
        )

    def z_first(n, zz):
        return remote(
            chip16.at[span(low(zz) * ZPART, ZPART)], z_in.at[n], zsent.at[n], zarrived.at[n],
            y * 16 + zz * 2 + 1,
        )

    def y_second(n, yy):
        return remote(
            z16.at[span(yy * OWNED, OWNED)], y_own.at[n], ysent.at[n], yarrived.at[n], yy * 16 + z * 2 + 1
        )

    def on_total(at, count, sent, arrived, peer):
        at = span(at, count)
        return remote(total.at[at], total.at[at], sent, arrived, peer)

    def back_z_first(n, to, source):
        return on_total(
            y * YPART + low(source) * OWNED, OWNED, gzsent.at[n], gzarrived.at[n], y * 16 + to * 2
        )

    def back_y_second(n, to, source):
        return on_total(source * YPART, YPART, gysent.at[n], gyarrived.at[n], to * 16 + z * 2)

    def back_y_first(n, to, source):
        return on_total(
            HALF + low(z) * ZPART + source * OWNED, OWNED, gysent.at[n], gyarrived.at[n], to * 16 + z * 2 + 1
        )

    def back_z_second(n, to, source):
        return on_total(
            HALF + low(source) * ZPART, ZPART, gzsent.at[n], gzarrived.at[n], y * 16 + to * 2 + 1
        )

    def sends(step, mine):
        return lambda n, to: step(n, to, mine)

    def comes(step):
        return lambda n, source: step(n, source, source)

    @pl.when(on_y)
    def _():
        copies(YORDER, y, 4, y_first)(start)

    @pl.when(on_z)
    def _():
        copies(ZORDER, z, 8, z_first, owns)(start)

    deal_back.start(12)

    gpad[...] = jnp.zeros_like(gpad)
    def pad_gradient(bc):
        width = min(2, 9 - bc)
        u[:, : width * L] = lax.dot_general(
            dpre3[...], wb[bc * L : (bc + width) * L, :], NT, preferred_element_type=F32
        )

        def add(gx, carry):
            for n in range(width):
                b, c = divmod(bc + n, 3)
                for yy in range(8):
                    at = pl.ds(gx * 100 + (yy + b) * 10 + c, 8)
                    gpad[at, :] += u[pl.ds(pl.multiple_of(gx * 64 + yy * 8, 8), 8), n * L : (n + 1) * L]
            return carry

        lax.fori_loop(0, 20, add, 0)

    for bc in (0, 2):
        pad_gradient(bc)

    @pl.when(on_y)
    def _():
        copies(range(3), y, 4, y_first)(wait_recv)
        value = chip32[span(y * YPART, YPART), :]
        for n in range(3):
            value = value + y_in[n].astype(F32)
        y32[...] = value
        y16[...] = value.astype(BF16)
        copies(ZORDER, z, 8, z_second, owns)(start)

    @pl.when(on_z & owner)
    def _():
        copies(range(7), z, 8, z_first)(wait_recv)
        value = chip32[span(z * ZPART, ZPART), :]
        for n in range(7):
            value = value + z_in[n].astype(F32)
        z32[...] = value
        z16[...] = value.astype(BF16)
        copies(YORDER, y, 4, y_second)(start)

    for bc in (4, 6):
        pad_gradient(bc)

    @pl.when(on_y & owner)
    def _():
        copies(range(7), z, 8, z_second)(wait_recv)
        value = y32[span(z * OWNED, OWNED), :]
        for n in range(7):
            value = value + z_own[n].astype(F32)
        total[span(y * YPART + z * OWNED, OWNED), :] = value.astype(BF16)
        copies(ZORDER, z, 8, sends(back_z_first, z))(start)

    @pl.when(on_z & owner)
    def _():
        copies(range(3), y, 4, y_second)(wait_recv)
        value = z32[span(y * OWNED, OWNED), :]
        for n in range(3):
            value = value + y_own[n].astype(F32)
        total[span(HALF + z * ZPART + y * OWNED, OWNED), :] = value.astype(BF16)
        copies(YORDER, y, 4, sends(back_y_first, y))(start)

    pad_gradient(8)

    gsource[...] = jnp.zeros_like(gsource)

    def give(n, carry):
        for g in range(2):
            for k, offset in enumerate(OFFSETS):
                if k != 13:
                    here = jnp.where(table[g, k] == n, 1.0, 0.0)
                    for s0, ss, p0, ps, count in segments(*offset):
                        at = rows(n * SHELL + s0, count, ss)
                        gsource[at, :] += gpad[rows(g * 1000 + p0, count, ps), :] * here
        return carry

    lax.fori_loop(0, 6, give, 0)
    for g in range(2):
        part_lower[g] = gsource[g * SHELL : (g + 1) * SHELL, :].astype(BF16)
        part_upper[g] = gsource[(4 + g) * SHELL : (5 + g) * SHELL, :].astype(BF16)
    rim_up = remote(part_upper, from_lower, rim_sent.at[0], rim_arrived.at[0], lax.min(me + 1, PEERS - 1))
    rim_down = remote(part_lower, from_upper, rim_sent.at[1], rim_arrived.at[1], lax.max(me - 1, 0))

    @pl.when(has_up)
    def _():
        rim_up.start()

    @pl.when(has_down)
    def _():
        rim_down.start()

    deal_back.forward()

    def across(which, part):
        rows_at, count = (part * YPART, YPART) if which == 0 else (HALF + part * ZPART, ZPART)
        return on_total(rows_at, count, copy_sent.at[part], copy_arrived.at[part], partner)

    @pl.when(on_y)
    def _():
        copies(range(7), z, 8, comes(back_z_first), owns)(wait_recv, back=True)
        copies(YORDER, y, 4, sends(back_y_second, y))(start)
        across(0, y).start()

    @pl.when(on_z & owner)
    def _():
        copies(range(3), y, 4, comes(back_y_first))(wait_recv, back=True)
        copies(ZORDER, z, 8, sends(back_z_second, z))(start)
        across(1, z).start()

    deal_back.finish()
    near32[...] = back_near[...].astype(F32)
    far32[...] = back_far[...].astype(F32)
    for n in range(6):
        out32[pl.ds(n * PEERS + core, CHIPS, stride=2), :] = near32[box_rows(core, n), :]
        out32[pl.ds(n * PEERS + 1 - core, CHIPS, stride=2), :] = far32[box_rows(core, n), :]
    for n in range(6):
        coarse_out[:, n * L : (n + 1) * L] = out32[n * PEERS : (n + 1) * PEERS, :].astype(BF16)

    def pass_on_y(n):
        source = jnp.bitwise_and(y + 3 - n, 3)
        back_y_second(n, source, source).wait_recv()
        across(0, source).start()

    def pass_on_z(n):
        source = jnp.bitwise_and(z + 7 - n, 7)

        @pl.when(owns(source))
        def _():
            back_z_second(n, source, source).wait_recv()
            across(1, low(source)).start()

    @pl.when(on_y)
    def _():
        pass_on_y(0)
        pass_on_y(2)

    @pl.when(on_z)
    def _():
        for n in (0, 6, 1, 5):
            pass_on_z(n)

    @pl.when(has_down)
    def _():
        rim_up.wait_recv()

    @pl.when(jnp.logical_not(has_down))
    def _():
        from_lower[...] = jnp.zeros_like(from_lower)

    @pl.when(has_up)
    def _():
        rim_down.wait_recv()

    @pl.when(jnp.logical_not(has_up))
    def _():
        from_upper[...] = jnp.zeros_like(from_upper)

    for g in range(2):
        shell = gsource[(2 + g) * SHELL : (3 + g) * SHELL, :]
        shell = shell + from_lower[g].astype(F32) + from_upper[g].astype(F32)
        for x in range(8):
            for yy in range(8):
                pre[pl.ds(g * V + x * 64 + yy * 8, 8), :] = gpad[pl.ds(g * 1000 + x * 100 + yy * 10 + 111, 8), :]
        for s0, v0, vs, count in shell_pieces():
            pre[rows(g * V + v0, count, vs), :] += shell[s0 : s0 + count]
        value = pre[g * V : (g + 1) * V, :]
        value = value * jnp.broadcast_to(own32[g * V : (g + 1) * V, C : C + 1], (V, L))
        grad_features[g] = jnp.transpose(value)[:C, :].astype(BF16)

    @pl.when(on_y)
    def _():
        pass_on_y(1)
        for part in range(7):
            across(1, part).wait_recv()

    @pl.when(on_z)
    def _():
        for n in (2, 4, 3):
            pass_on_z(n)
        for part in range(4):
            across(0, part).wait_recv()

    @pl.when(has_up)
    def _():
        up.wait_send()
        rim_up.wait_send()

    @pl.when(has_down)
    def _():
        down.wait_send()
        rim_down.wait_send()

    deal.close()
    deal_back.close()
    pair.wait_send()

    @pl.when(on_y)
    def _():
        copies(range(3), y, 4, y_first)(wait_send)
        copies(range(7), z, 8, z_second, owns)(wait_send)
        copies(range(3), y, 4, sends(back_y_second, y))(wait_send)
        for part in range(4):
            across(0, part).wait_send()

    @pl.when(on_z)
    def _():
        copies(range(7), z, 8, z_first, owns)(wait_send)
        for part in range(7):
            across(1, part).wait_send()

    @pl.when(on_y & owner)
    def _():
        copies(range(7), z, 8, sends(back_z_first, z))(wait_send)

    @pl.when(on_z & owner)
    def _():
        copies(range(3), y, 4, y_second)(wait_send)
        copies(range(3), y, 4, sends(back_y_first, y))(wait_send)
        copies(range(7), z, 8, sends(back_z_second, z))(wait_send)


def vmem(n):
    return [pl.BlockSpec(memory_space=pltpu.VMEM)] * n


def hbm(n):
    return [pl.BlockSpec(memory_space=pltpu.HBM)] * n


def run_section(neighbours, live_count, occupancy, features, grad_coarse, w_subm, w_down):
    dma = pltpu.SemaphoreType.DMA
    block = pltpu.VMEM((2, SHELL, L), BF16)
    boxes = pltpu.VMEM((8 * PEERS, L), F32)
    sent = pltpu.VMEM((8 * PEERS, L), BF16)
    return pl.pallas_call(
        section_kernel,
        out_shape=(
            jax.ShapeDtypeStruct((PEERS, 6 * L), BF16),
            jax.ShapeDtypeStruct((2, C, V), BF16),
            jax.ShapeDtypeStruct((2 * HALF, L), BF16),
        ),
        in_specs=hbm(7),
        out_specs=tuple(vmem(3)),
        scratch_shapes=[
            pltpu.SMEM((2, 27), jnp.int32),
            pltpu.SMEM((1,), jnp.int32),
            pltpu.SMEM((2, 16), jnp.int32),
            pltpu.VMEM((2, C, V), BF16),
            pltpu.VMEM((PEERS, 6 * L), BF16),
            pltpu.VMEM((27, C, C), BF16),
            pltpu.VMEM((8, C, C), BF16),
            pltpu.VMEM((2 * V, L), F32),
            block, block, block, boxes, boxes, boxes, pltpu.VMEM((6 * PEERS, L), F32),
            sent, sent, sent, sent, sent, sent,
            pltpu.VMEM((7 * SHELL, L), F32),
            pltpu.VMEM((2000, L), F32),
            pltpu.VMEM((1280, 9 * L), BF16),
            pltpu.VMEM((27 * L, L), BF16),
            pltpu.VMEM((9 * L, 3 * L), BF16),
            pltpu.VMEM((8 * L, L), BF16),
            pltpu.VMEM((V, V), BF16),
            pltpu.VMEM((V, V), BF16),
            pltpu.VMEM((L, 6 * L), BF16),
            pltpu.VMEM((2 * V, L), F32),
            pltpu.VMEM((1280, 3 * L), BF16),
            pltpu.VMEM((1280, 2 * L), F32),
            pltpu.VMEM((2000, L), F32),
            pltpu.VMEM((6 * SHELL, L), F32),
            pltpu.VMEM((2 * HALF, L), F32),
            pltpu.VMEM((2 * HALF, L), BF16),
            pltpu.VMEM((HALF, L), BF16),
            pltpu.VMEM((HALF, L), F32),
            pltpu.VMEM((HALF, L), BF16),
            pltpu.VMEM((3, YPART, L), BF16),
            pltpu.VMEM((YPART, L), F32),
            pltpu.VMEM((YPART, L), BF16),
            pltpu.VMEM((7, OWNED, L), BF16),
            pltpu.VMEM((7, ZPART, L), BF16),
            pltpu.VMEM((ZPART, L), F32),
            pltpu.VMEM((ZPART, L), BF16),
            pltpu.VMEM((3, OWNED, L), BF16),
            block, block, block, block,
            dma((7,)), dma((4,)), dma((4,)),
            dma((2,)), dma((2,)), dma((2,)), dma((2,)), dma(()), dma(()),
            dma((3,)), dma((3,)), dma((7,)), dma((7,)), dma((7,)), dma((7,)),
            dma((3,)), dma((3,)), dma((7,)), dma((7,)),
        ],
        compiler_params=pltpu.CompilerParams(
            vmem_limit_bytes=VMEM_LIMIT, collective_id=0, has_side_effects=True
        ),
    )(neighbours, live_count, occupancy, features, grad_coarse, w_subm, w_down)


def final_kernel(
    coarse_in, features_in, total_in, coarse_out, grad_features, grad_subm, grad_down,
    total, subm, down, coarse, features, load_sem, sem,
):
    def chunk(n):
        return pl.ds(9 * C * n, 9 * C)

    loads = [
        pltpu.make_async_copy(total_in.at[chunk(n)], total.at[chunk(n)], load_sem.at[n]) for n in range(3)
    ]
    loads.append(pltpu.make_async_copy(features_in, features, load_sem.at[3]))
    loads.append(pltpu.make_async_copy(coarse_in, coarse, load_sem.at[4]))
    for load in loads:
        load.start()
    copies = [
        pltpu.make_async_copy(features, grad_features, sem.at[0]),
        pltpu.make_async_copy(coarse, coarse_out, sem.at[1]),
    ]
    lane = lax.broadcasted_iota(jnp.int32, (C, L), 1)
    for k in range(35):
        quad, n = divmod(k, 4)
        if k % 12 == 0:
            loads[k // 12].wait()
        if n < 3:
            at = (3 * quad + n) * C
            value = total[at : at + C, :].astype(F32)[:, :C]
        else:
            value = jnp.zeros((C, L), F32)
            for m in range(3):
                at = (3 * quad + m) * C
                piece = pltpu.roll(total[at : at + C, :].astype(F32), 32 + 32 * m, 1)
                value = jnp.where(lane // 32 == m, piece, value)
            value = value[:, :C]
        if k < 27:
            subm[k] = value
        else:
            down[k - 27] = value
        if k in (11, 23, 26):
            part = pl.ds(k // 12 * 12, 12 if k < 26 else 3)
            copies.append(pltpu.make_async_copy(subm.at[part], grad_subm.at[part], sem.at[2 + k // 12]))
            copies[-1].start()
        if k == 11:
            for n in range(2):
                loads[3 + n].wait()
                copies[n].start()
    copies.append(pltpu.make_async_copy(down, grad_down, sem.at[5]))
    copies[-1].start()
    for copy in copies:
        copy.wait()


def run_final(coarse_in, grad_features, total):
    return pl.pallas_call(
        final_kernel,
        out_shape=(
            jax.ShapeDtypeStruct((PEERS, 6 * L), BF16),
            jax.ShapeDtypeStruct((2, C, V), BF16),
            jax.ShapeDtypeStruct((27, C, C), F32),
            jax.ShapeDtypeStruct((8, C, C), F32),
        ),
        in_specs=hbm(3),
        out_specs=tuple(hbm(4)),
        scratch_shapes=[
            pltpu.VMEM((27 * C, L), BF16),
            pltpu.VMEM((27, C, C), F32),
            pltpu.VMEM((8, C, C), F32),
            pltpu.VMEM((PEERS, 6 * L), BF16),
            pltpu.VMEM((2, C, V), BF16),
            pltpu.SemaphoreType.DMA((5,)),
            pltpu.SemaphoreType.DMA((6,)),
        ],
        compiler_params=pltpu.CompilerParams(vmem_limit_bytes=VMEM_LIMIT),
    )(coarse_in, grad_features, total)


def per_device(features, occupancy, neighbours, live_count, w_subm, w_down, grad_coarse):
    return run_final(
        *run_section(neighbours, live_count, occupancy, features, grad_coarse, w_subm, w_down)
    )


def solution(mesh):
    blocks = P(("rep", "space"), None)
    return jax.shard_map(
        per_device,
        mesh=mesh,
        in_specs=(
            P(("rep", "space"), None, None), blocks, blocks, P(("rep", "space")), P(), P(), blocks,
        ),
        out_specs=(
            blocks, P(("rep", "space"), None, None), P("rep", None, None), P("rep", None, None),
        ),
        check_vma=False,
    )
```
